32 devices in a mesh: feat: 4 (over z), dom: 8 (over y, x, core).
Axes of the slice: x: 2, y: 2, z: 4, core: 2. Of those that a mesh axis runs over, the one named last changes fastest.
Arguments:
- features: bfloat16 [8, 512, 768], P('dom', None, 'feat'), may hold values from -6 to 6
- tiles: bfloat16 [8, 12, 128, 128], P('dom')
- tile_ids: int32 [8, 12, 2], P('dom'), may hold values from 0 to 3, as said below
- sources: int32 [8, 8, 4, 16], P('dom'), may hold values from 0 to 511
- targets: int32 [8, 8, 4, 16], P('dom'), may hold values from 0 to 127
- counts: int32 [8, 8, 4], P('dom'), may hold values from 0 to 16, as said below
- edge_weight: bfloat16 [8, 8, 4, 16], P('dom'), may hold values from 0.5 to 2
- self_one: bfloat16 [768, 1024], replicated, may hold values from -0.21875 to 0.21875
- neigh_one: bfloat16 [768, 1024], replicated, may hold values from -0.21875 to 0.21875
- self_out: bfloat16 [1024, 153], replicated, may hold values from -0.1875 to 0.1875
- neigh_out: bfloat16 [1024, 153], replicated, may hold values from -0.1875 to 0.1875
Outputs:
- hidden: bfloat16 [8, 512, 1024], P('dom', 'feat')
- logits: float32 [8, 153, 512], P('dom', None, 'feat')
The draws below stay inside these ranges and needn't reach their ends.
Inputs may be any that keep to these rules, and one draw needn't show every extreme that they name: `tile_ids`: in each partition the 12 (row block, column block) pairs are distinct, and every row block appears in exactly 3 of them, in no fixed order. counts[e, e, g] is 0; in every draw some partition receives 16 live slots from every other partition in every group.
All inputs are finite; a program needn't handle non-finite values.
Results may differ from the reference program's by a relative error of at most 0.003.
Values may be sent and summed in bfloat16 or wider, within the bound.
No kernel may reach another device: no remote copies, remote signals or barrier semaphores. Data moves between devices by JAX's collectives and lax.ppermute only.
A program may use at most 64 MiB of HBM per device.

```python
import math
import jax
import jax.numpy as jnp
from jax import lax

F = 768
HID = 1024
CLASSES = 153
TILE = 128
NODE_BLKS = 1
TILE_ROW = 3
SLOTS = 16
ROWS = 128
PART_NODES = 512
N_FEAT = 4
N_DOM = 8


def draw_tiles(key, part):
    key = jax.random.fold_in(key, 5)
    shape = (N_DOM, TILE_ROW * NODE_BLKS * N_FEAT, TILE, TILE)
    uniform_values = jax.random.uniform(key, shape, jnp.float32)
    entry_values = uniform_values * (2.0 / TILE)
    return entry_values.astype(jnp.bfloat16)


def draw_tile_ids(key, part):
    key = jax.random.fold_in(key, 11)
    key_cols, key_order = jax.random.split(key)
    block_count = NODE_BLKS * N_FEAT
    tile_total = block_count * TILE_ROW
    scores = jax.random.randint(key_cols, (N_DOM, block_count, block_count), 0, 1 << 20)
    scores = scores * block_count + jnp.arange(block_count, dtype=jnp.int32)
    ranked = jnp.argsort(scores, axis=2, stable=True)[:, :, :TILE_ROW].astype(jnp.int32)
    row_ids = jnp.broadcast_to(jnp.arange(block_count, dtype=jnp.int32)[None, :, None], ranked.shape)
    listed = jnp.stack([row_ids, ranked], axis=-1).reshape(N_DOM, tile_total, 2)
    order_scores = jax.random.randint(key_order, (N_DOM, tile_total), 0, 1 << 20) * tile_total
    order_scores = order_scores + jnp.arange(tile_total, dtype=jnp.int32)
    order = jnp.argsort(order_scores, axis=1, stable=True)
    return jnp.take_along_axis(listed, order[:, :, None], axis=1).astype(jnp.int32)


def draw_counts(key, part):
    key = jax.random.fold_in(key, 23)
    key_base, key_crowd, key_pick = jax.random.split(key, 3)
    drawn = jax.random.randint(key_base, (N_DOM, N_DOM, N_FEAT), 0, SLOTS + 1)
    crowded = jax.random.randint(key_crowd, (N_DOM,), 0, 4) == 0
    chosen_one = jax.random.randint(key_pick, (), 0, N_DOM)
    crowded = crowded | (jnp.arange(N_DOM) == chosen_one)
    filled = jnp.where(crowded[:, None, None], SLOTS, drawn)
    diagonal = jnp.arange(N_DOM)[:, None] == jnp.arange(N_DOM)[None, :]
    return jnp.where(diagonal[:, :, None], 0, filled).astype(jnp.int32)


def plant(values, stream_key, smallest, high):
    spot = [jax.random.randint(jax.random.fold_in(stream_key, axis), (), 0, length) for axis, length in enumerate(values.shape)]
    widest = values.shape.index(max(values.shape))
    neighbour = spot[:widest] + [(spot[widest] + 1) % values.shape[widest]] + spot[widest + 1:]
    return values.at[tuple(spot)].set(smallest).at[tuple(neighbour)].set(high)


def shard_levels(own_key, extent, pieces, smallest, largest):
    loudness, own = 1.0, jax.random.fold_in(own_key, 6)
    for dim, blocks in pieces:
        steps = jnp.exp(jax.random.uniform(jax.random.fold_in(own, dim), (blocks,), jnp.float32, smallest / len(pieces), largest / len(pieces)))
        loudness = loudness * jnp.repeat(steps, extent[dim] // blocks).reshape([-1 if axis == dim else 1 for axis in range(len(extent))])
    return loudness


def bell_draw(rng, extent, deviation, bound, cuts=(), kind=jnp.bfloat16):
    array = deviation * jax.random.normal(rng, extent, jnp.float32)
    if cuts:
        array = array * shard_levels(rng, extent, cuts, -0.22, 0.18)
    return jnp.clip(array, -bound, bound).astype(kind)


def setup_inputs(seed: int = 0) -> dict:
    seeds = jax.random.split(jax.random.key(seed), 12)
    features = bell_draw(seeds[0], (N_DOM, PART_NODES, F), 1.0, 6.0, ((0, 8), (2, 4)))
    tiles = draw_tiles(jax.random.fold_in(seeds[11], 71), 0)
    tile_ids = draw_tile_ids(jax.random.fold_in(seeds[11], 71), 0)
    sources = plant(jax.random.randint(seeds[3], (N_DOM, N_DOM, N_FEAT, SLOTS), 0, PART_NODES), jax.random.fold_in(seeds[3], 1), 0, PART_NODES - 1).astype(jnp.int32)
    targets = plant(jax.random.randint(seeds[4], (N_DOM, N_DOM, N_FEAT, SLOTS), 0, ROWS), jax.random.fold_in(seeds[4], 1), 0, ROWS - 1).astype(jnp.int32)
    counts = draw_counts(jax.random.fold_in(seeds[11], 71), 0)
    edge_weight = jnp.clip(jnp.exp(math.log(2.0) - 1.3862944 * jax.random.uniform(seeds[6], (N_DOM, N_DOM, N_FEAT, SLOTS), jnp.float32) ** shard_levels(seeds[6], (N_DOM, N_DOM, N_FEAT, SLOTS), ((0, 8),), -0.2, 0.2)), 0.5, 2.0).astype(jnp.bfloat16)
    self_one = bell_draw(seeds[7], (F, HID), F ** -0.5, 0.21875)
    neigh_one = bell_draw(seeds[8], (F, HID), F ** -0.5, 0.21875)
    self_out = bell_draw(seeds[9], (HID, CLASSES), HID ** -0.5, 0.1875)
    neigh_out = bell_draw(seeds[10], (HID, CLASSES), HID ** -0.5, 0.1875)
    return {"features": features, "tiles": tiles, "tile_ids": tile_ids, "sources": sources, "targets": targets, "counts": counts, "edge_weight": edge_weight, "self_one": self_one, "neigh_one": neigh_one, "self_out": self_out, "neigh_out": neigh_out}


def block_sum(tile_contents, tile_pairs, feature_field_rows):
    block_count = feature_field_rows.shape[0] // TILE
    blocks = feature_field_rows.reshape(block_count, TILE, feature_field_rows.shape[1]).astype(jnp.float32)
    picked = jnp.take(blocks, tile_pairs[:, 1], axis=0)
    products = jnp.einsum("tij,tjc->tic", tile_contents.astype(jnp.float32), picked, precision=lax.Precision.HIGHEST)
    owners = (tile_pairs[:, 0][:, None] == jnp.arange(block_count, dtype=jnp.int32)[None, :]).astype(jnp.float32)
    summed = jnp.einsum("tb,tic->bic", owners, products, precision=lax.Precision.HIGHEST)
    return summed.reshape(feature_field_rows.shape[0], feature_field_rows.shape[1])


def edge_matrix(target_part, count_part, weight_part):
    slot_live = jnp.arange(SLOTS, dtype=jnp.int32)[None, None, :] < count_part[:, :, None]
    kept_weights = jnp.where(slot_live, weight_part.astype(jnp.float32), 0.0)
    target_hits = (target_part[..., None] == jnp.arange(ROWS, dtype=jnp.int32)).astype(jnp.float32)
    return target_hits * kept_weights[..., None]


def reference(features, tiles, tile_ids, sources, targets, counts, edge_weight, self_one, neigh_one, self_out, neigh_out):
    partitions = jnp.arange(N_DOM, dtype=jnp.int32)

    def edge_parts(partition):
        edge_matrices = edge_matrix(targets[partition], counts[partition], edge_weight[partition])
        ones_field = jnp.ones((PART_NODES, 1), jnp.float32)
        tile_degree = block_sum(tiles[partition], tile_ids[partition], ones_field)[:, 0]
        degree = tile_degree + jnp.sum(edge_matrices, axis=(0, 2)).reshape(PART_NODES)
        return edge_matrices, degree

    def boundary_term(edge_matrices, field_all, partition):
        picks = sources[:, partition]
        entry_values = field_all[partitions[:, None, None], picks].astype(jnp.float32)
        summed = jnp.einsum("dgsr,dgsc->grc", edge_matrices, entry_values, precision=lax.Precision.HIGHEST)
        return summed.reshape(PART_NODES, field_all.shape[2])

    def first_layer(partition):
        edge_matrices, degree = edge_parts(partition)
        own_rows = features[partition]
        edge_term = boundary_term(edge_matrices, features, partition)
        local_term = block_sum(tiles[partition], tile_ids[partition], own_rows)
        neighbours = ((local_term + edge_term) / degree[:, None]).astype(jnp.bfloat16)
        preact = jnp.dot(own_rows, self_one, preferred_element_type=jnp.float32) + jnp.dot(neighbours, neigh_one, preferred_element_type=jnp.float32)
        return jnp.maximum(preact, 0.0).astype(jnp.bfloat16)

    hidden = lax.map(first_layer, partitions)

    def last_layer(partition):
        edge_matrices, degree = edge_parts(partition)
        own_rows = hidden[partition]
        edge_term = boundary_term(edge_matrices, hidden, partition)
        local_term = block_sum(tiles[partition], tile_ids[partition], own_rows)
        mean_two = (local_term + edge_term) / degree[:, None]
        scores = jnp.dot(own_rows, self_out, preferred_element_type=jnp.float32)
        scores = scores + jnp.dot(mean_two, neigh_out.astype(jnp.float32), precision=lax.Precision.HIGHEST)
        return scores.T

    logits = lax.map(last_layer, partitions)
    return hidden, logits
```

```python
import functools

import jax
import jax.numpy as jnp
from jax import lax
from jax.experimental import pallas as pl
from jax.experimental.pallas import tpu as pltpu
from jax.sharding import PartitionSpec as P

f32 = jnp.float32
bf16 = jnp.bfloat16
VM = pl.BlockSpec(memory_space=pltpu.VMEM)
SM = pl.BlockSpec(memory_space=pltpu.SMEM)


def call(kernel, out_shape, in_specs, scratch=(), cost=None, limit=24 << 20):
    return pl.pallas_call(
        kernel,
        out_shape=out_shape,
        in_specs=in_specs,
        out_specs=jax.tree.map(lambda _: VM, out_shape),
        scratch_shapes=list(scratch),
        cost_estimate=cost,
        compiler_params=pltpu.CompilerParams(vmem_limit_bytes=limit),
    )


def fill_hits(hits, sources_ref, first, chunk, offset):
    groups, slots = sources_ref.shape[1], sources_ref.shape[2]
    nodes = hits.shape[1]
    lane = lax.broadcasted_iota(jnp.int32, (slots, nodes), 1) + offset
    for e in range(chunk):
        columns = sources_ref[first + e].T
        for g in range(groups):
            row = (g * chunk + e) * slots
            hits[row : row + slots, :] = jnp.where(
                columns[:, g : g + 1] == lane, 1.0, 0.0
            ).astype(bf16)


def send_rows(hits, sources_ref, table, out_ref, chunk, offset):
    groups, parts, slots, width = out_ref.shape

    def step(i, _):
        first = i * chunk
        fill_hits(hits, sources_ref, first, chunk, offset)
        rows = jnp.dot(hits[...], table, preferred_element_type=f32).astype(bf16)
        rows = rows.reshape(groups, chunk, slots, width)
        out_ref[:, pl.ds(first, chunk), :, :] = rows
        return 0

    if parts == chunk:
        step(0, 0)
    else:
        lax.fori_loop(0, parts // chunk, step, 0)


def first_kernel(chunk, me_ref, ids_ref, sources_ref, features_ref, tiles_ref, *rest):
    groups, rows = len(rest) - 3, tiles_ref.shape[1]
    out_ref, locals_, sums, hits = rest[0], rest[1 : 1 + groups], rest[-2], rest[-1]
    send_rows(hits, sources_ref, features_ref[...], out_ref, chunk, 0)
    sums[...] = jnp.zeros_like(sums)

    def add(t, _):
        to = pl.multiple_of(ids_ref[t, 0] * rows, rows)
        at = pl.multiple_of(ids_ref[t, 1] * rows, rows)
        sums[pl.ds(to, rows), :] += jnp.dot(
            tiles_ref[t], features_ref[pl.ds(at, rows), :], preferred_element_type=f32
        )
        return 0

    lax.fori_loop(0, tiles_ref.shape[0], add, 0)
    for k in range(groups):
        group = lax.rem(me_ref[0] + k, groups)
        locals_[k][...] = sums[pl.ds(pl.multiple_of(group * rows, rows), rows), :].astype(bf16)


def graph_kernel(
    me_ref, ids_ref, tiles_ref, targets_ref, counts_ref, weight_ref, band_ref, edges_ref, degree_ref
):
    me = me_ref[0]
    parts, groups, slots = targets_ref.shape
    rows = band_ref.shape[1]
    band_ref[...] = jnp.zeros_like(band_ref)

    def place(t, _):
        @pl.when(ids_ref[t, 0] == me)
        def _():
            band_ref[ids_ref[t, 1]] = tiles_ref[t]

        return 0

    lax.fori_loop(0, tiles_ref.shape[0], place, 0)
    mine = lax.broadcasted_iota(jnp.int32, (parts, groups, slots), 1) == me
    target = jnp.sum(jnp.where(mine, targets_ref[...], 0), axis=1)
    weight = jnp.sum(jnp.where(mine, weight_ref[...].astype(f32), 0.0), axis=1)
    count_mine = lax.broadcasted_iota(jnp.int32, (parts, groups), 1) == me
    count = jnp.sum(jnp.where(count_mine, counts_ref[...], 0), axis=1, keepdims=True)
    live = lax.broadcasted_iota(jnp.int32, (parts, slots), 1) < count
    weight = jnp.where(live, weight, 0.0)
    target, weight = target.T, weight.T
    lane = lax.broadcasted_iota(jnp.int32, (slots, rows), 1)
    pieces = [
        jnp.where(target[:, d : d + 1] == lane, weight[:, d : d + 1], 0.0) for d in range(parts)
    ]
    edges = jnp.concatenate(pieces, axis=0).T
    edges_ref[...] = edges.astype(bf16)
    degree = jnp.sum(edges, axis=1, keepdims=True)
    for b in range(band_ref.shape[0]):
        degree = degree + jnp.sum(band_ref[b].astype(f32), axis=1, keepdims=True)
    degree_ref[...] = jnp.broadcast_to(degree, degree_ref.shape)


def blocks(me, groups, width):
    for k in range(groups):
        source = lax.rem(me + groups - k, groups)
        yield k, source, pl.ds(pl.multiple_of(source * width, width), width)


def self_kernel(me_ref, weight_ref, *rest):
    out_ref, parts = rest[-1], rest[:-1]
    total = None
    for k, _, span in blocks(me_ref[0], len(parts), parts[0].shape[1]):
        term = jnp.dot(parts[k][...], weight_ref[span, :], preferred_element_type=f32)
        total = term if total is None else total + term
    out_ref[...] = total


def hidden_kernel(
    groups,
    chunk,
    me_ref,
    weight_ref,
    out_weight_ref,
    sources_ref,
    own_ref,
    edges_ref,
    degree_ref,
    incoming_ref,
    *rest,
):
    locals_ = rest[:groups]
    hidden_ref, projected_ref, send_ref, hits = rest[groups:]
    rows, width = locals_[0].shape
    me = me_ref[0]
    total = own_ref[...]
    degree = degree_ref[:, :1]
    for k, source, span in blocks(me, groups, width):
        arrived = incoming_ref[source].reshape(edges_ref.shape[1], width)
        mean = jnp.dot(edges_ref[...], arrived, preferred_element_type=f32)
        mean = (mean + locals_[k][...].astype(f32)) / degree
        total = total + jnp.dot(
            mean.astype(bf16), weight_ref[span, :], preferred_element_type=f32
        )
    hidden = jnp.maximum(total, 0.0).astype(bf16)
    hidden_ref[...] = hidden
    projected = jnp.dot(hidden, out_weight_ref[...], preferred_element_type=f32).astype(bf16)
    projected_ref[...] = projected
    send_rows(hits, sources_ref, projected, send_ref, chunk, me * rows)


def own_kernel(hidden_ref, weight_ref, out_ref):
    out_ref[...] = jnp.dot(hidden_ref[...], weight_ref[...], preferred_element_type=f32)


def last_kernel(groups, me_ref, own_ref, band_ref, edges_ref, degree_ref, incoming_ref, *rest):
    projected, out_ref = rest[:groups], rest[groups]
    classes = own_ref.shape[1]
    total = jnp.zeros(own_ref.shape, f32)
    for k, source, _ in blocks(me_ref[0], groups, 1):
        total = total + jnp.dot(band_ref[source], projected[k][...], preferred_element_type=f32)
        arrived = incoming_ref[k].reshape(edges_ref.shape[1], classes)
        total = total + jnp.dot(edges_ref[...], arrived, preferred_element_type=f32)
    out_ref[...] = (own_ref[...] + total / degree_ref[:, :1]).T


def on_device(
    features,
    tiles,
    tile_ids,
    sources,
    targets,
    counts,
    edge_weight,
    self_one,
    neigh_one,
    self_out,
    neigh_out,
):
    feature_cols, tile_contents, tile_pairs = features[0], tiles[0], tile_ids[0]
    groups, parts = lax.axis_size("feat"), lax.axis_size("dom")
    me = lax.axis_index("feat")
    me_array = me.astype(jnp.int32).reshape(1)
    nodes, width = feature_cols.shape
    rows, side, slots = nodes // groups, tile_contents.shape[1], sources.shape[3]
    hid, classes = self_one.shape[1], self_out.shape[1]
    chunk = max(1, min(parts, 512 // (groups * slots)))
    both = ("feat", "dom")

    def shape(*dims, dtype=bf16):
        return jax.ShapeDtypeStruct(dims, dtype)

    def shift(value, k):
        return lax.ppermute(value, "feat", [(i, (i + k) % groups) for i in range(groups)])

    def cost(flops, size):
        return pl.CostEstimate(flops=flops, bytes_accessed=size, transcendentals=0)

    feature_blocks = [
        lax.dynamic_slice_in_dim(feature_cols, lax.rem(me + k, groups) * rows, rows)
        for k in range(groups)
    ]
    feature_blocks = feature_blocks[:1] + [
        shift(feature_blocks[k], k) for k in range(1, groups)
    ]
    sent, *local_blocks = call(
        functools.partial(first_kernel, chunk),
        (shape(groups, parts, slots, width),) + (shape(rows, width),) * groups,
        [SM, SM, VM, VM, VM],
        [pltpu.VMEM((nodes, width), f32), pltpu.VMEM((chunk * groups * slots, nodes), bf16)],
        cost(2 * nodes * nodes * width * 2, 1 << 20),
    )(me_array, tile_pairs, sources[0], feature_cols, tile_contents)
    sent = sent.reshape(groups * parts, slots, width)
    incoming = lax.all_to_all(sent, both, split_axis=0, concat_axis=0, tiled=True)
    incoming = incoming.reshape(groups, parts, slots, width)
    local_blocks = local_blocks[:1] + [shift(local_blocks[k], k) for k in range(1, groups)]
    band, edges, degree = call(
        graph_kernel,
        (shape(groups, rows, side), shape(rows, parts * slots), shape(rows, side, dtype=f32)),
        [SM, SM, VM, VM, VM, VM],
        (),
        cost(1 << 20, 2 << 20),
    )(me_array, tile_pairs, tile_contents, targets[0], counts[0], edge_weight[0])
    own = call(
        self_kernel,
        shape(rows, hid, dtype=f32),
        [SM] + [VM] * (1 + groups),
        (),
        cost(2 * rows * hid * groups * width, 2 << 20),
    )(me_array, self_one, *feature_blocks)
    hidden, projected, sent = call(
        functools.partial(hidden_kernel, groups, chunk),
        (shape(rows, hid), shape(rows, classes), shape(groups, parts, slots, classes)),
        [SM] + [VM] * (7 + groups),
        [pltpu.VMEM((chunk * groups * slots, rows), bf16)],
        cost(2 * rows * hid * groups * width, 3 << 20),
    )(me_array, neigh_one, neigh_out, sources[0], own, edges, degree, incoming, *local_blocks)
    sent = sent.reshape(groups * parts, slots, classes)
    incoming = lax.all_to_all(sent, both, split_axis=0, concat_axis=0, tiled=True)
    incoming = incoming.reshape(groups, parts, slots, classes)
    projected = [projected] + [shift(projected, k) for k in range(1, groups)]
    own = call(
        own_kernel, shape(rows, classes, dtype=f32), [VM, VM], (), cost(2 * rows * hid * classes, 1 << 20)
    )(hidden, self_out)
    logits = call(
        functools.partial(last_kernel, groups),
        shape(classes, rows, dtype=f32),
        [SM] + [VM] * (5 + groups),
        (),
        cost(2 * rows * nodes * classes * 2, 1 << 20),
    )(me_array, own, band, edges, degree, incoming, *projected)
    return hidden[None], logits[None]


def solution(mesh):
    placed = (
        P("dom", None, "feat"),
        P("dom", None, None, None),
        P("dom", None, None),
        P("dom", None, None, None),
        P("dom", None, None, None),
        P("dom", None, None),
        P("dom", None, None, None),
        P(),
        P(),
        P(),
        P(),
    )
    return jax.shard_map(
        on_device,
        mesh=mesh,
        in_specs=placed,
        out_specs=(P("dom", "feat", None), P("dom", None, "feat")),
        check_vma=False,
    )
```

```python
import functools

import jax
import jax.numpy as jnp
from jax import lax
from jax.experimental import pallas as pl
from jax.experimental.pallas import tpu as pltpu
from jax.sharding import PartitionSpec as P

f32 = jnp.float32
bf16 = jnp.bfloat16
VM = pl.BlockSpec(memory_space=pltpu.VMEM)
SM = pl.BlockSpec(memory_space=pltpu.SMEM)
LAST = (((1,), (1,)), ((), ()))
FIRST = (((0,), (0,)), ((), ()))


def call(kernel, out_shape, in_specs, scratch=(), flops=0, size=0):
    return pl.pallas_call(
        kernel,
        out_shape=out_shape,
        in_specs=in_specs,
        out_specs=jax.tree.map(lambda _: VM, out_shape),
        scratch_shapes=list(scratch),
        cost_estimate=pl.CostEstimate(flops=flops, bytes_accessed=size, transcendentals=0),
        compiler_params=pltpu.CompilerParams(vmem_limit_bytes=24 << 20),
    )


def dot(left, right, dims):
    return lax.dot_general(left, right, dims, preferred_element_type=f32)


def behind(me, groups, k):
    return lax.rem(me + groups - k, groups)


def gather_kernel(chunk, me_ref, sources_ref, features_ref, out_ref, *rest):
    blocks, hits = rest[:-1], rest[-1]
    parts, groups, slots = sources_ref.shape
    nodes = hits.shape[1]
    rows = nodes // groups
    table = features_ref[...]
    lane = lax.broadcasted_iota(jnp.int32, (slots, nodes), 1)

    def step(i, _):
        for e in range(chunk):
            columns = sources_ref[i * chunk + e].T
            for g in range(groups):
                row = (e * groups + g) * slots
                hits[row : row + slots, :] = jnp.where(
                    columns[:, g : g + 1] == lane, 1.0, 0.0
                ).astype(bf16)
        picked = dot(hits[...], table, LAST).astype(bf16)
        out_ref[pl.ds(i * chunk, chunk)] = picked.reshape(chunk, groups * slots, -1)
        return 0

    if parts == chunk:
        step(0, 0)
    else:
        lax.fori_loop(0, parts // chunk, step, 0)
    for k in range(groups):
        group = lax.rem(me_ref[0] + k, groups)
        blocks[k][...] = features_ref[:, pl.ds(pl.multiple_of(group * rows, rows), rows)]


def local_kernel(
    me_ref,
    ids_ref,
    counts_ref,
    features_ref,
    tiles_ref,
    targets_ref,
    weight_ref,
    sums_ref,
    edges_ref,
    degree_ref,
    band_ref,
):
    me = me_ref[0]
    parts, groups, slots = targets_ref.shape
    rows = tiles_ref.shape[1]
    sums_ref[...] = jnp.zeros_like(sums_ref)
    degree_ref[...] = jnp.zeros_like(degree_ref)
    band_ref[...] = jnp.zeros_like(band_ref)
    ones = jnp.ones((degree_ref.shape[1], rows), bf16)

    def add(t, _):
        to, at = ids_ref[0, t], ids_ref[1, t]
        tile = tiles_ref[t]
        part = features_ref[:, pl.ds(pl.multiple_of(at * rows, rows), rows)]
        sums_ref[to] += dot(part, tile, LAST)
        degree_ref[to] += dot(ones, tile, LAST)

        @pl.when(to == me)
        def _():
            band_ref[at] = tile

        return 0

    lax.fori_loop(0, tiles_ref.shape[0], add, 0)
    lane = lax.broadcasted_iota(jnp.int32, (slots, rows), 1)
    slot = lax.broadcasted_iota(jnp.int32, (slots, rows), 0)

    def connect(d, _):
        target, weight = targets_ref[d].T, weight_ref[d].astype(f32).T
        for g in range(groups):
            hit = (target[:, g : g + 1] == lane) & (slot < counts_ref[g, d])
            values = jnp.where(hit, weight[:, g : g + 1], 0.0)
            edges_ref[g, d] = values.astype(bf16)
            degree_ref[g] += jnp.sum(values, axis=0, keepdims=True)
        return 0

    lax.fori_loop(0, parts, connect, 0)


def mean_kernel(me_ref, incoming_ref, sums_ref, edges_ref, degree_ref, *outs):
    groups, parts, slots, rows = edges_ref.shape
    width = incoming_ref.shape[2]
    for k in range(groups):
        group = lax.rem(me_ref[0] + k, groups)
        arrived = incoming_ref[:, pl.ds(pl.multiple_of(group * slots, slots), slots), :]
        arrived = arrived.reshape(parts * slots, width)
        total = sums_ref[group] + dot(arrived, edges_ref[group].reshape(parts * slots, rows), FIRST)
        outs[k][...] = (total / degree_ref[group][:1]).astype(bf16)


def self_kernel(me_ref, weight_ref, *rest):
    out_ref, parts = rest[-1], rest[:-1]
    width = parts[0].shape[0]
    total = None
    for k in range(len(parts)):
        source = behind(me_ref[0], len(parts), k)
        span = pl.ds(pl.multiple_of(source * width, width), width)
        term = dot(parts[k][...], weight_ref[span, :], FIRST)
        total = term if total is None else total + term
    out_ref[...] = total


def hidden_kernel(me_ref, weight_ref, out_weight_ref, own_ref, *rest):
    parts, hidden_ref, projected_ref = rest[:-2], rest[-2], rest[-1]
    width = parts[0].shape[0]
    total = own_ref[...]
    for k in range(len(parts)):
        source = behind(me_ref[0], len(parts), k)
        span = pl.ds(pl.multiple_of(source * width, width), width)
        total = total + dot(parts[k][...], weight_ref[span, :], FIRST)
    hidden = jnp.maximum(total, 0.0).astype(bf16)
    hidden_ref[...] = hidden
    projected_ref[...] = dot(out_weight_ref[...], hidden, LAST).astype(bf16)


def own_kernel(hidden_ref, weight_ref, out_ref):
    out_ref[...] = dot(weight_ref[...], hidden_ref[...], LAST)


def pick_kernel(me_ref, sources_ref, *rest):
    projected, out_ref = rest[:-1], rest[-1]
    parts, groups, slots = sources_ref.shape
    me, rows = me_ref[0], projected[0].shape[1]
    mine = lax.broadcasted_iota(jnp.int32, sources_ref.shape, 1) == me
    picks = jnp.sum(jnp.where(mine, sources_ref[...], 0), axis=1).T
    picks = jnp.concatenate(
        [jnp.broadcast_to(picks[:, e : e + 1], (slots, rows)) for e in range(parts)], axis=0
    )
    lane = lax.broadcasted_iota(jnp.int32, picks.shape, 1)
    total = None
    for k in range(groups):
        hits = jnp.where(picks == lane + behind(me, groups, k) * rows, 1.0, 0.0).astype(bf16)
        term = dot(hits, projected[k][...], LAST)
        total = term if total is None else total + term
    out_ref[...] = total.astype(bf16).reshape(out_ref.shape)


def near_kernel(me_ref, band_ref, *rest):
    projected, out_ref = rest[:-1], rest[-1]
    groups = len(projected)
    total = None
    for k in range(groups):
        term = dot(projected[k][...], band_ref[behind(me_ref[0], groups, k)], LAST)
        total = term if total is None else total + term
    out_ref[...] = total


def last_kernel(me_ref, own_ref, near_ref, edges_ref, degree_ref, incoming_ref, out_ref):
    groups, parts, slots, rows = edges_ref.shape
    me = me_ref[0]
    arrived = incoming_ref[...].reshape(parts * slots, -1)
    far = dot(arrived, edges_ref[me].reshape(parts * slots, rows), FIRST)
    total = own_ref[...] + (near_ref[...] + far) / degree_ref[me][:1]
    out_ref[...] = total.reshape(out_ref.shape)


def on_device(
    features,
    tiles,
    tile_ids,
    sources,
    targets,
    counts,
    edge_weight,
    self_one,
    neigh_one,
    self_out,
    neigh_out,
):
    feature_rows, tile_contents = features[0].T, tiles[0]
    groups, parts = lax.axis_size("feat"), lax.axis_size("dom")
    me = lax.axis_index("feat").astype(jnp.int32).reshape(1)
    width, nodes = feature_rows.shape
    rows, slots = nodes // groups, sources.shape[3]
    hid, classes = self_one.shape[1], self_out.shape[1]
    chunk = max(1, min(parts, 512 // (groups * slots)))

    def shape(*dims, dtype=bf16):
        return jax.ShapeDtypeStruct(dims, dtype)

    def shift(blocks):
        return [blocks[0]] + [
            lax.ppermute(blocks[k], "feat", [(i, (i + k) % groups) for i in range(groups)])
            for k in range(1, groups)
        ]

    def swap(value):
        return lax.all_to_all(value, "dom", split_axis=0, concat_axis=0, tiled=True)

    sent, *feature_blocks = call(
        functools.partial(gather_kernel, chunk),
        (shape(parts, groups * slots, width),) + (shape(width, rows),) * groups,
        [SM, VM, VM],
        [pltpu.VMEM((chunk * groups * slots, nodes), bf16)],
        2 * nodes * nodes * width,
        1 << 20,
    )(me, sources[0], feature_rows)
    incoming = swap(sent)
    feature_blocks = shift(feature_blocks)
    sums, edges, degree, band = call(
        local_kernel,
        (
            shape(groups, width, rows, dtype=f32),
            shape(groups, parts, slots, rows),
            shape(groups, 8, rows, dtype=f32),
            shape(groups, rows, rows),
        ),
        [SM, SM, SM, VM, VM, VM, VM],
        (),
        2 * nodes * nodes * width,
        1 << 20,
    )(
        me,
        tile_ids[0].T,
        counts[0].T,
        feature_rows,
        tile_contents,
        targets[0],
        edge_weight[0],
    )
    means = call(
        mean_kernel,
        (shape(width, rows),) * groups,
        [SM, VM, VM, VM, VM],
        (),
        2 * nodes * parts * slots * width,
        1 << 20,
    )(me, incoming, sums, edges, degree)
    means = shift(means)
    own = call(
        self_kernel,
        shape(rows, hid, dtype=f32),
        [SM] + [VM] * (1 + groups),
        (),
        2 * rows * hid * groups * width,
        2 << 20,
    )(me, self_one, *feature_blocks)
    hidden, projected = call(
        hidden_kernel,
        (shape(rows, hid), shape(classes, rows)),
        [SM] + [VM] * (3 + groups),
        (),
        2 * rows * hid * groups * width,
        2 << 20,
    )(me, neigh_one, neigh_out.T, own, *means)
    projected = shift([projected] * groups)
    sent = call(
        pick_kernel,
        shape(parts, slots, classes),
        [SM] + [VM] * (1 + groups),
        (),
        2 * parts * slots * nodes * classes,
        1 << 19,
    )(me, sources[0], *projected)
    incoming = swap(sent)
    own = call(
        own_kernel,
        shape(classes, rows, dtype=f32),
        [VM, VM],
        (),
        2 * rows * hid * classes,
        1 << 20,
    )(hidden, self_out.T)
    near = call(
        near_kernel,
        shape(classes, rows, dtype=f32),
        [SM] + [VM] * (1 + groups),
        (),
        2 * rows * nodes * classes,
        1 << 19,
    )(me, band, *projected)
    logits = call(
        last_kernel,
        shape(classes, 1, rows, dtype=f32),
        [SM] + [VM] * 5,
        (),
        2 * rows * parts * slots * classes,
        1 << 19,
    )(me, own, near, edges, degree, incoming)
    return hidden[None], logits.transpose(1, 0, 2)


def solution(mesh):
    placed = (
        P("dom", None, "feat"),
        P("dom", None, None, None),
        P("dom", None, None),
        P("dom", None, None, None),
        P("dom", None, None, None),
        P("dom", None, None),
        P("dom", None, None, None),
        P(),
        P(),
        P(),
        P(),
    )
    return jax.shard_map(
        on_device,
        mesh=mesh,
        in_specs=placed,
        out_specs=(P("dom", "feat", None), P("dom", None, "feat")),
        check_vma=False,
    )
```

```python
import functools

import jax
import jax.numpy as jnp
from jax import lax
from jax.experimental import pallas as pl
from jax.experimental.pallas import tpu as pltpu
from jax.sharding import PartitionSpec as P

f32 = jnp.float32
bf16 = jnp.bfloat16
VM = pl.BlockSpec(memory_space=pltpu.VMEM)
SM = pl.BlockSpec(memory_space=pltpu.SMEM)
HB = pl.BlockSpec(memory_space=pltpu.HBM)
LAST = (((1,), (1,)), ((), ()))
FIRST = (((0,), (0,)), ((), ()))
EXTRA = 16


def call(kernel, out_shape, in_specs, scratch=(), flops=0, size=0, limit=4, out_specs=None):
    run = pl.pallas_call(
        kernel,
        out_shape=out_shape,
        in_specs=in_specs,
        out_specs=out_specs or jax.tree.map(lambda _: VM, out_shape),
        scratch_shapes=list(scratch),
        cost_estimate=pl.CostEstimate(flops=flops, bytes_accessed=size, transcendentals=0),
        compiler_params=pltpu.CompilerParams(vmem_limit_bytes=limit << 20),
    )

    def placed(*operands):
        return run(
            *(
                pltpu.with_memory_space_constraint(value, pltpu.HBM) if spec is HB else value
                for value, spec in zip(operands, in_specs)
            )
        )

    return placed


def dot(left, right, dims):
    return lax.dot_general(left, right, dims, preferred_element_type=f32)


def send_to(me, groups, k):
    return me ^ k if groups & (groups - 1) == 0 else (me + k) % groups


def ahead(me, groups, k):
    return me ^ k if groups & (groups - 1) == 0 else lax.rem(me + k, groups)


def behind(me, groups, k):
    return me ^ k if groups & (groups - 1) == 0 else lax.rem(me + groups - k, groups)


def fetch(sems, *pairs):
    copies = [pltpu.make_async_copy(a, b, sems.at[i]) for i, (a, b) in enumerate(pairs)]
    for copy in copies:
        copy.start()
    return copies


def columns_of(values):
    return values.reshape(-1, values.shape[-1]).T


def gather_kernel(chunk, me_ref, sources_hbm, features_hbm, out_ref, *rest):
    blocks, (sources_ref, features_ref, hits, sems) = rest[:-4], rest[-4:]
    parts, groups, slots = sources_ref.shape
    nodes = hits.shape[1]
    rows = nodes // groups
    for copy in fetch(sems, (sources_hbm, sources_ref), (features_hbm, features_ref)):
        copy.wait()
    lane = lax.broadcasted_iota(jnp.int32, (slots, nodes), 1)

    def step(i, _):
        columns = columns_of(sources_ref[pl.ds(i * chunk, chunk)])
        for n in range(chunk * groups):
            hits[n * slots : (n + 1) * slots, :] = jnp.where(
                columns[:, n : n + 1] == lane, 1.0, 0.0
            ).astype(bf16)
        picked = dot(hits[...], features_ref[...], LAST).astype(bf16)
        out_ref[pl.ds(i * chunk, chunk)] = picked.reshape(chunk, groups * slots, -1)
        return 0

    if parts == chunk:
        step(0, 0)
    else:
        lax.fori_loop(0, parts // chunk, step, 0)
    for k in range(1, groups):
        group = ahead(me_ref[0], groups, k)
        blocks[k - 1][...] = features_ref[:, pl.ds(pl.multiple_of(group * rows, rows), rows)]


def local_kernel(
    chunk,
    me_ref,
    ids_hbm,
    counts_hbm,
    features_hbm,
    tiles_hbm,
    targets_hbm,
    weight_hbm,
    sources_hbm,
    sums_ref,
    edges_ref,
    band_ref,
    hits_ref,
    ids_ref,
    counts_ref,
    features_ref,
    tiles_ref,
    targets_ref,
    weight_ref,
    sources_ref,
    bands,
    sems,
):
    me = me_ref[0]
    parts, groups, slots = targets_ref.shape
    rows = tiles_ref.shape[1]
    width = features_hbm.shape[0]
    copies = fetch(
        sems,
        (ids_hbm, ids_ref),
        (counts_hbm, counts_ref),
        (features_hbm, features_ref.at[pl.ds(0, width), :]),
        (tiles_hbm, tiles_ref),
        (targets_hbm, targets_ref),
        (weight_hbm, weight_ref),
        (sources_hbm, sources_ref),
    )
    extra = features_ref.shape[0] - width
    features_ref[width:, :] = jnp.ones((extra, features_ref.shape[1]), bf16)
    bands[...] = jnp.zeros_like(bands)
    for copy in copies:
        copy.wait()

    def place(t, _):
        at = pl.multiple_of(ids_ref[1, t] * rows, rows)
        bands[ids_ref[0, t], :, pl.ds(at, rows)] = tiles_ref[t]
        return 0

    lax.fori_loop(0, tiles_ref.shape[0], place, 0, unroll=tiles_ref.shape[0] <= 16)
    for g in range(groups):
        sums_ref[g] = dot(features_ref[...], bands[g], LAST)
    band_ref[...] = bands[me]
    lane = lax.broadcasted_iota(jnp.int32, (slots, rows), 1)
    slot = lax.broadcasted_iota(jnp.int32, (slots, rows), 0)

    def connect(i, _):
        first = i * chunk
        target = columns_of(targets_ref[pl.ds(first, chunk)])
        weight = columns_of(weight_ref[pl.ds(first, chunk)].astype(f32))
        for g in range(groups):
            degree = jnp.zeros((1, rows), f32)
            for e in range(chunk):
                n = e * groups + g
                hit = (target[:, n : n + 1] == lane) & (slot < counts_ref[g, first + e])
                values = jnp.where(hit, weight[:, n : n + 1], 0.0)
                edges_ref[g, first + e] = values.astype(bf16)
                degree = degree + jnp.sum(values, axis=0, keepdims=True)
            sums_ref[g, width : width + 1, :] += degree
        return 0

    if parts == chunk:
        connect(0, 0)
    else:
        lax.fori_loop(0, parts // chunk, connect, 0)
    mine = lax.broadcasted_iota(jnp.int32, sources_ref.shape, 1) == me
    picks = jnp.sum(jnp.where(mine, sources_ref[...], 0), axis=1).T
    lane = lax.broadcasted_iota(jnp.int32, (slots, hits_ref.shape[1]), 1)
    for e in range(parts):
        hits_ref[e * slots : (e + 1) * slots, :] = jnp.where(
            picks[:, e : e + 1] == lane, 1.0, 0.0
        ).astype(bf16)


def mean_kernel(me_ref, incoming_ref, sums_ref, edges_ref, *outs):
    groups, parts, slots, rows = edges_ref.shape
    width = incoming_ref.shape[2]
    for k in range(groups):
        group = ahead(me_ref[0], groups, k)
        arrived = incoming_ref[:, pl.ds(pl.multiple_of(group * slots, slots), slots), :]
        arrived = arrived.reshape(parts * slots, width)
        total = sums_ref[group, :width, :] + dot(
            arrived, edges_ref[group].reshape(parts * slots, rows), FIRST
        )
        outs[k][...] = (total / sums_ref[group, width : width + 1, :]).astype(bf16)


def self_kernel(me_ref, features_hbm, weight_ref, *rest):
    parts, (out_ref, own_ref, sem) = rest[:-3], rest[-3:]
    groups, (width, rows) = len(parts) + 1, own_ref.shape
    me = me_ref[0]
    own = pltpu.make_async_copy(
        features_hbm.at[:, pl.ds(pl.multiple_of(me * rows, rows), rows)], own_ref, sem
    )
    own.start()
    total = jnp.zeros(out_ref.shape, f32)
    for k in range(1, groups):
        span = pl.ds(pl.multiple_of(behind(me, groups, k) * width, width), width)
        total = total + dot(parts[k - 1][...], weight_ref[span, :], FIRST)
    own.wait()
    span = pl.ds(pl.multiple_of(me * width, width), width)
    out_ref[...] = total + dot(own_ref[...], weight_ref[span, :], FIRST)


def hidden_kernel(me_ref, weight_ref, out_weight_ref, own_ref, *rest):
    parts, hidden_ref, projected_ref = rest[:-2], rest[-2], rest[-1]
    width = parts[0].shape[0]
    total = own_ref[...]
    for k in range(len(parts)):
        source = behind(me_ref[0], len(parts), k)
        span = pl.ds(pl.multiple_of(source * width, width), width)
        total = total + dot(parts[k][...], weight_ref[span, :], FIRST)
    hidden = jnp.maximum(total, 0.0).astype(bf16)
    hidden_ref[...] = hidden
    projected_ref[...] = dot(out_weight_ref[...], hidden, LAST).astype(bf16)


def own_kernel(hidden_ref, weight_ref, out_ref, hidden_out, sem):
    copy = pltpu.make_async_copy(hidden_ref, hidden_out, sem)
    copy.start()
    out_ref[...] = dot(weight_ref[...], hidden_ref[...], LAST)
    copy.wait()


def pick_kernel(me_ref, hits_ref, *rest):
    projected, out_ref = rest[:-1], rest[-1]
    groups, rows = len(projected), projected[0].shape[1]
    total = None
    for k in range(groups):
        at = pl.multiple_of(behind(me_ref[0], groups, k) * rows, rows)
        term = dot(hits_ref[:, pl.ds(at, rows)], projected[k][...], LAST)
        total = term if total is None else total + term
    out_ref[...] = total.astype(bf16).reshape(out_ref.shape)


def near_kernel(me_ref, band_ref, *rest):
    projected, out_ref = rest[:-1], rest[-1]
    groups, rows = len(projected), projected[0].shape[1]
    total = None
    for k in range(groups):
        at = pl.multiple_of(behind(me_ref[0], groups, k) * rows, rows)
        term = dot(projected[k][...], band_ref[:, pl.ds(at, rows)], LAST)
        total = term if total is None else total + term
    out_ref[...] = total


def last_kernel(me_ref, own_ref, near_ref, edges_ref, sums_ref, incoming_ref, out_ref):
    groups, parts, slots, rows = edges_ref.shape
    me, width = me_ref[0], sums_ref.shape[1] - EXTRA
    arrived = incoming_ref[...].reshape(parts * slots, -1)
    far = dot(arrived, edges_ref[me].reshape(parts * slots, rows), FIRST)
    total = own_ref[...] + (near_ref[...] + far) / sums_ref[me, width : width + 1, :]
    out_ref[...] = total.reshape(out_ref.shape)


def on_device(
    features,
    tiles,
    tile_ids,
    sources,
    targets,
    counts,
    edge_weight,
    self_one,
    neigh_one,
    self_out,
    neigh_out,
):
    feature_rows, tile_contents = features[0].T, tiles[0]
    groups, parts = lax.axis_size("feat"), lax.axis_size("dom")
    me = lax.axis_index("feat").astype(jnp.int32).reshape(1)
    width, nodes = feature_rows.shape
    rows, slots = nodes // groups, sources.shape[3]
    hid, classes = self_one.shape[1], self_out.shape[1]
    chunk = max(1, min(parts, 512 // (groups * slots)))

    def shape(*dims, dtype=bf16):
        return jax.ShapeDtypeStruct(dims, dtype)

    def shift(blocks):
        return [
            lax.ppermute(
                block, "feat", [(i, send_to(i, groups, k)) for i in range(groups)]
            )
            for k, block in enumerate(blocks, 1)
        ]

    def swap(value):
        return lax.all_to_all(value, "dom", split_axis=0, concat_axis=0, tiled=True)

    sent, *feature_blocks = call(
        functools.partial(gather_kernel, chunk),
        (shape(parts, groups * slots, width),) + (shape(width, rows),) * (groups - 1),
        [SM, HB, HB],
        [
            pltpu.VMEM((parts, groups, slots), jnp.int32),
            pltpu.VMEM((width, nodes), bf16),
            pltpu.VMEM((chunk * groups * slots, nodes), bf16),
            pltpu.SemaphoreType.DMA((2,)),
        ],
        2 * nodes * nodes * width,
        1 << 20,
    )(me, sources[0], feature_rows)
    incoming = swap(sent)
    feature_blocks = shift(feature_blocks)
    sums, edges, band, hits = call(
        functools.partial(local_kernel, chunk),
        (
            shape(groups, width + EXTRA, rows, dtype=f32),
            shape(groups, parts, slots, rows),
            shape(rows, nodes),
            shape(parts * slots, nodes),
        ),
        [SM] + [HB] * 7,
        [
            pltpu.SMEM(tile_ids.shape[:0:-1], jnp.int32),
            pltpu.SMEM(counts.shape[:0:-1], jnp.int32),
            pltpu.VMEM((width + EXTRA, nodes), bf16),
            pltpu.VMEM(tile_contents.shape, bf16),
            pltpu.VMEM((parts, groups, slots), jnp.int32),
            pltpu.VMEM((parts, groups, slots), bf16),
            pltpu.VMEM((parts, groups, slots), jnp.int32),
            pltpu.VMEM((groups, rows, nodes), bf16),
            pltpu.SemaphoreType.DMA((7,)),
        ],
        2 * nodes * nodes * width,
        1 << 20,
        4 if groups <= 4 else 16,
    )(
        me,
        tile_ids[0].T,
        counts[0].T,
        feature_rows,
        tile_contents,
        targets[0],
        edge_weight[0],
        sources[0],
    )
    own_mean, *means = call(
        mean_kernel,
        (shape(width, rows),) * groups,
        [SM, VM, VM, VM],
        (),
        2 * nodes * parts * slots * width,
        1 << 20,
    )(me, incoming, sums, edges)
    means = shift(means)
    own = call(
        self_kernel,
        shape(rows, hid, dtype=f32),
        [SM, HB] + [VM] * groups,
        [pltpu.VMEM((width, rows), bf16), pltpu.SemaphoreType.DMA],
        2 * rows * hid * groups * width,
        2 << 20,
    )(me, feature_rows, self_one, *feature_blocks)
    hidden, projected = call(
        hidden_kernel,
        (shape(rows, hid), shape(classes, rows)),
        [SM] + [VM] * (3 + groups),
        (),
        2 * rows * hid * groups * width,
        2 << 20,
    )(me, neigh_one, neigh_out.T, own, own_mean, *means)
    projected = [projected] + shift([projected] * (groups - 1))
    sent = call(
        pick_kernel,
        shape(parts, slots, classes),
        [SM] + [VM] * (1 + groups),
        (),
        2 * parts * slots * nodes * classes,
        1 << 19,
    )(me, hits, *projected)
    incoming = swap(sent)
    own, hidden = call(
        own_kernel,
        (shape(classes, rows, dtype=f32), shape(rows, hid)),
        [VM, VM],
        [pltpu.SemaphoreType.DMA],
        2 * rows * hid * classes,
        1 << 20,
        out_specs=(VM, HB),
    )(hidden, self_out.T)
    near = call(
        near_kernel,
        shape(classes, rows, dtype=f32),
        [SM] + [VM] * (1 + groups),
        (),
        2 * rows * nodes * classes,
        1 << 19,
    )(me, band, *projected)
    logits = call(
        last_kernel,
        shape(classes, 1, rows, dtype=f32),
        [SM] + [VM] * 5,
        (),
        2 * rows * parts * slots * classes,
        1 << 19,
    )(me, own, near, edges, sums, incoming)
    return hidden[None], logits.transpose(1, 0, 2)


def solution(mesh):
    placed = (
        P("dom", None, "feat"),
        P("dom", None, None, None),
        P("dom", None, None),
        P("dom", None, None, None),
        P("dom", None, None, None),
        P("dom", None, None),
        P("dom", None, None, None),
        P(),
        P(),
        P(),
        P(),
    )
    return jax.shard_map(
        on_device,
        mesh=mesh,
        in_specs=placed,
        out_specs=(P("dom", "feat", None), P("dom", None, "feat")),
        check_vma=False,
    )
```

```python
import functools

import jax
import jax.numpy as jnp
from jax import lax
from jax.experimental import pallas as pl
from jax.experimental.pallas import tpu as pltpu
from jax.sharding import PartitionSpec as P

f32 = jnp.float32
bf16 = jnp.bfloat16
VM = pl.BlockSpec(memory_space=pltpu.VMEM)
SM = pl.BlockSpec(memory_space=pltpu.SMEM)
HB = pl.BlockSpec(memory_space=pltpu.HBM)
LAST = (((1,), (1,)), ((), ()))
FIRST = (((0,), (0,)), ((), ()))
EXTRA = 16


def call(kernel, out_shape, in_specs, scratch=(), flops=0, size=0, limit=4, out_specs=None):
    run = pl.pallas_call(
        kernel,
        out_shape=out_shape,
        in_specs=in_specs,
        out_specs=out_specs or jax.tree.map(lambda _: VM, out_shape),
        scratch_shapes=list(scratch),
        cost_estimate=pl.CostEstimate(flops=flops, bytes_accessed=size, transcendentals=0),
        compiler_params=pltpu.CompilerParams(vmem_limit_bytes=limit << 20),
    )

    def placed(*operands):
        return run(
            *(
                pltpu.with_memory_space_constraint(value, pltpu.HBM) if spec is HB else value
                for value, spec in zip(operands, in_specs)
            )
        )

    return placed


def dot(left, right, dims):
    return lax.dot_general(left, right, dims, preferred_element_type=f32)


def step_of(groups, k):
    return sorted(range(groups), key=lambda d: (d > 0, abs(2 * d - groups - 1)))[k]


def ahead(me, groups, k):
    step = step_of(groups, k)
    return me ^ step if groups & (groups - 1) == 0 else (me + step) % groups


def behind(me, groups, k):
    step = step_of(groups, k)
    return me ^ step if groups & (groups - 1) == 0 else (me + groups - step) % groups


def fetch(sems, *pairs):
    copies = [pltpu.make_async_copy(a, b, sems.at[i]) for i, (a, b) in enumerate(pairs)]
    for copy in copies:
        copy.start()
    return copies


def columns_of(values):
    return values.reshape(-1, values.shape[-1]).T


def gather_kernel(chunk, me_ref, sources_hbm, features_hbm, out_ref, *rest):
    blocks, (sources_ref, features_ref, hits, sems) = rest[:-4], rest[-4:]
    parts, groups, slots = sources_ref.shape
    nodes = hits.shape[1]
    rows = nodes // groups
    indices, table = fetch(sems, (sources_hbm, sources_ref), (features_hbm, features_ref))
    indices.wait()
    lane = lax.broadcasted_iota(jnp.int32, (slots, nodes), 1)

    def step(i, last):
        columns = columns_of(sources_ref[pl.ds(i * chunk, chunk)])
        for n in range(chunk * groups):
            hits[n * slots : (n + 1) * slots, :] = jnp.where(
                columns[:, n : n + 1] == lane, 1.0, 0.0
            ).astype(bf16)
        if last:
            table.wait()
        picked = dot(hits[...], features_ref[...], LAST).astype(bf16)
        out_ref[pl.ds(i * chunk, chunk)] = picked.reshape(chunk, groups * slots, -1)

    if parts == chunk:
        step(0, True)
    else:
        table.wait()
        lax.fori_loop(0, parts // chunk, lambda i, _: step(i, False), None)
    for k in range(1, groups):
        group = ahead(me_ref[0], groups, k)
        blocks[k - 1][...] = features_ref[:, pl.ds(pl.multiple_of(group * rows, rows), rows)]


def local_kernel(
    chunk,
    me_ref,
    ids_hbm,
    counts_hbm,
    features_hbm,
    tiles_hbm,
    targets_hbm,
    weight_hbm,
    sources_hbm,
    sums_ref,
    edges_ref,
    band_ref,
    hits_ref,
    ids_ref,
    counts_ref,
    features_ref,
    tiles_ref,
    targets_ref,
    weight_ref,
    sources_ref,
    bands,
    sems,
):
    me = me_ref[0]
    parts, groups, slots = targets_ref.shape
    rows = tiles_ref.shape[1]
    width = features_hbm.shape[0]
    copies = fetch(
        sems,
        (ids_hbm, ids_ref),
        (counts_hbm, counts_ref),
        (features_hbm, features_ref.at[pl.ds(0, width), :]),
        (tiles_hbm, tiles_ref),
        (targets_hbm, targets_ref),
        (weight_hbm, weight_ref),
        (sources_hbm, sources_ref),
    )
    extra = features_ref.shape[0] - width
    features_ref[width:, :] = jnp.ones((extra, features_ref.shape[1]), bf16)
    bands[...] = jnp.zeros_like(bands)
    for copy in copies:
        copy.wait()

    def place(t, _):
        at = pl.multiple_of(ids_ref[1, t] * rows, rows)
        bands[ids_ref[0, t], :, pl.ds(at, rows)] = tiles_ref[t]
        return 0

    lax.fori_loop(0, tiles_ref.shape[0], place, 0, unroll=tiles_ref.shape[0] <= 16)
    for g in range(groups):
        sums_ref[g] = dot(features_ref[...], bands[g], LAST)
    band_ref[...] = bands[me]
    lane = lax.broadcasted_iota(jnp.int32, (slots, rows), 1)
    slot = lax.broadcasted_iota(jnp.int32, (slots, rows), 0)

    def connect(i, _):
        first = i * chunk
        target = columns_of(targets_ref[pl.ds(first, chunk)])
        weight = columns_of(weight_ref[pl.ds(first, chunk)].astype(f32))
        for g in range(groups):
            degree = jnp.zeros((1, rows), f32)
            for e in range(chunk):
                n = e * groups + g
                hit = (target[:, n : n + 1] == lane) & (slot < counts_ref[g, first + e])
                values = jnp.where(hit, weight[:, n : n + 1], 0.0)
                edges_ref[g, first + e] = values.astype(bf16)
                degree = degree + jnp.sum(values, axis=0, keepdims=True)
            sums_ref[g, width : width + 1, :] += degree
        return 0

    if parts == chunk:
        connect(0, 0)
    else:
        lax.fori_loop(0, parts // chunk, connect, 0)
    mine = lax.broadcasted_iota(jnp.int32, sources_ref.shape, 1) == me
    picks = jnp.sum(jnp.where(mine, sources_ref[...], 0), axis=1).T
    lane = lax.broadcasted_iota(jnp.int32, (slots, hits_ref.shape[1]), 1)
    for e in range(parts):
        hits_ref[e * slots : (e + 1) * slots, :] = jnp.where(
            picks[:, e : e + 1] == lane, 1.0, 0.0
        ).astype(bf16)


def mean_kernel(me_ref, incoming_ref, sums_ref, edges_ref, *outs):
    groups, parts, slots, rows = edges_ref.shape
    width = incoming_ref.shape[2]
    for k in range(groups):
        group = ahead(me_ref[0], groups, k)
        arrived = incoming_ref[:, pl.ds(pl.multiple_of(group * slots, slots), slots), :]
        arrived = arrived.reshape(parts * slots, width)
        total = sums_ref[group, :width, :] + dot(
            arrived, edges_ref[group].reshape(parts * slots, rows), FIRST
        )
        outs[k][...] = (total / sums_ref[group, width : width + 1, :]).astype(bf16)


def self_kernel(me_ref, features_hbm, weight_ref, *rest):
    parts, (out_ref, own_ref, sem) = rest[:-3], rest[-3:]
    groups, (width, rows) = len(parts) + 1, own_ref.shape
    me = me_ref[0]
    own = pltpu.make_async_copy(
        features_hbm.at[:, pl.ds(pl.multiple_of(me * rows, rows), rows)], own_ref, sem
    )
    own.start()
    total = jnp.zeros(out_ref.shape, f32)
    for k in range(1, groups):
        span = pl.ds(pl.multiple_of(behind(me, groups, k) * width, width), width)
        total = total + dot(parts[k - 1][...], weight_ref[span, :], FIRST)
    own.wait()
    span = pl.ds(pl.multiple_of(me * width, width), width)
    out_ref[...] = total + dot(own_ref[...], weight_ref[span, :], FIRST)


def hidden_kernel(me_ref, weight_ref, out_weight_ref, own_ref, *rest):
    groups = len(rest) // 2
    parts, hidden_ref, copies = rest[:groups], rest[groups], rest[groups + 1 :]
    width = parts[0].shape[0]
    total = own_ref[...]
    for k in range(len(parts)):
        source = behind(me_ref[0], len(parts), k)
        span = pl.ds(pl.multiple_of(source * width, width), width)
        total = total + dot(parts[k][...], weight_ref[span, :], FIRST)
    hidden = jnp.maximum(total, 0.0).astype(bf16)
    hidden_ref[...] = hidden
    projected = dot(out_weight_ref[...], hidden, LAST).astype(bf16)
    for copy in copies:
        copy[...] = projected


def own_kernel(hidden_ref, weight_ref, out_ref, hidden_out, sem):
    copy = pltpu.make_async_copy(hidden_ref, hidden_out, sem)
    copy.start()
    out_ref[...] = dot(weight_ref[...], hidden_ref[...], LAST)
    copy.wait()


def pick_kernel(me_ref, hits_ref, *rest):
    projected, out_ref = rest[:-1], rest[-1]
    groups, rows = len(projected), projected[0].shape[1]
    total = None
    for k in range(groups):
        at = pl.multiple_of(behind(me_ref[0], groups, k) * rows, rows)
        term = dot(hits_ref[:, pl.ds(at, rows)], projected[k][...], LAST)
        total = term if total is None else total + term
    out_ref[...] = total.astype(bf16).reshape(out_ref.shape)


def near_kernel(me_ref, band_ref, *rest):
    projected, out_ref = rest[:-1], rest[-1]
    groups, rows = len(projected), projected[0].shape[1]
    total = None
    for k in range(groups):
        at = pl.multiple_of(behind(me_ref[0], groups, k) * rows, rows)
        term = dot(projected[k][...], band_ref[:, pl.ds(at, rows)], LAST)
        total = term if total is None else total + term
    out_ref[...] = total


def last_kernel(me_ref, own_ref, near_ref, edges_ref, sums_ref, incoming_ref, out_ref):
    groups, parts, slots, rows = edges_ref.shape
    me, width = me_ref[0], sums_ref.shape[1] - EXTRA
    arrived = incoming_ref[...].reshape(parts * slots, -1)
    far = dot(arrived, edges_ref[me].reshape(parts * slots, rows), FIRST)
    total = own_ref[...] + (near_ref[...] + far) / sums_ref[me, width : width + 1, :]
    out_ref[...] = total.reshape(out_ref.shape)


def on_device(
    features,
    tiles,
    tile_ids,
    sources,
    targets,
    counts,
    edge_weight,
    self_one,
    neigh_one,
    self_out,
    neigh_out,
):
    feature_rows, tile_contents = features[0].T, tiles[0]
    groups, parts = lax.axis_size("feat"), lax.axis_size("dom")
    me = lax.axis_index("feat").astype(jnp.int32).reshape(1)
    width, nodes = feature_rows.shape
    rows, slots = nodes // groups, sources.shape[3]
    hid, classes = self_one.shape[1], self_out.shape[1]
    chunk = max(1, min(parts, 512 // (groups * slots)))

    def shape(*dims, dtype=bf16):
        return jax.ShapeDtypeStruct(dims, dtype)

    def shift(blocks):
        return [
            lax.ppermute(
                block, "feat", [(i, ahead(i, groups, k)) for i in range(groups)]
            )
            for k, block in enumerate(blocks, 1)
        ]

    def swap(value):
        return lax.all_to_all(value, "dom", split_axis=0, concat_axis=0, tiled=True)

    sent, *feature_blocks = call(
        functools.partial(gather_kernel, chunk),
        (shape(parts, groups * slots, width),) + (shape(width, rows),) * (groups - 1),
        [SM, HB, HB],
        [
            pltpu.VMEM((parts, groups, slots), jnp.int32),
            pltpu.VMEM((width, nodes), bf16),
            pltpu.VMEM((chunk * groups * slots, nodes), bf16),
            pltpu.SemaphoreType.DMA((2,)),
        ],
        2 * nodes * nodes * width,
        1 << 20,
    )(me, sources[0], feature_rows)
    incoming = swap(sent)
    feature_blocks = shift(feature_blocks)
    sums, edges, band, hits = call(
        functools.partial(local_kernel, chunk),
        (
            shape(groups, width + EXTRA, rows, dtype=f32),
            shape(groups, parts, slots, rows),
            shape(rows, nodes),
            shape(parts * slots, nodes),
        ),
        [SM] + [HB] * 7,
        [
            pltpu.SMEM(tile_ids.shape[:0:-1], jnp.int32),
            pltpu.SMEM(counts.shape[:0:-1], jnp.int32),
            pltpu.VMEM((width + EXTRA, nodes), bf16),
            pltpu.VMEM(tile_contents.shape, bf16),
            pltpu.VMEM((parts, groups, slots), jnp.int32),
            pltpu.VMEM((parts, groups, slots), bf16),
            pltpu.VMEM((parts, groups, slots), jnp.int32),
            pltpu.VMEM((groups, rows, nodes), bf16),
            pltpu.SemaphoreType.DMA((7,)),
        ],
        2 * nodes * nodes * width,
        1 << 20,
        4 if groups <= 4 else 16,
    )(
        me,
        tile_ids[0].T,
        counts[0].T,
        feature_rows,
        tile_contents,
        targets[0],
        edge_weight[0],
        sources[0],
    )
    own_mean, *means = call(
        mean_kernel,
        (shape(width, rows),) * groups,
        [SM, VM, VM, VM],
        (),
        2 * nodes * parts * slots * width,
        1 << 20,
    )(me, incoming, sums, edges)
    means = shift(means)
    own = call(
        self_kernel,
        shape(rows, hid, dtype=f32),
        [SM, HB] + [VM] * groups,
        [pltpu.VMEM((width, rows), bf16), pltpu.SemaphoreType.DMA],
        2 * rows * hid * groups * width,
        2 << 20,
    )(me, feature_rows, self_one, *feature_blocks)
    hidden, *projected = call(
        hidden_kernel,
        (shape(rows, hid),) + (shape(classes, rows),) * groups,
        [SM] + [VM] * (3 + groups),
        (),
        2 * rows * hid * groups * width,
        2 << 20,
    )(me, neigh_one, neigh_out.T, own, own_mean, *means)
    projected = projected[:1] + shift(projected[1:])
    sent = call(
        pick_kernel,
        shape(parts, slots, classes),
        [SM] + [VM] * (1 + groups),
        (),
        2 * parts * slots * nodes * classes,
        1 << 19,
    )(me, hits, *projected)
    incoming = swap(sent)
    own, hidden = call(
        own_kernel,
        (shape(classes, rows, dtype=f32), shape(rows, hid)),
        [VM, VM],
        [pltpu.SemaphoreType.DMA],
        2 * rows * hid * classes,
        1 << 20,
        out_specs=(VM, HB),
    )(hidden, self_out.T)
    near = call(
        near_kernel,
        shape(classes, rows, dtype=f32),
        [SM] + [VM] * (1 + groups),
        (),
        2 * rows * nodes * classes,
        1 << 19,
    )(me, band, *projected)
    logits = call(
        last_kernel,
        shape(classes, 1, rows, dtype=f32),
        [SM] + [VM] * 5,
        (),
        2 * rows * parts * slots * classes,
        1 << 19,
    )(me, own, near, edges, sums, incoming)
    return hidden[None], logits.transpose(1, 0, 2)


def solution(mesh):
    placed = (
        P("dom", None, "feat"),
        P("dom", None, None, None),
        P("dom", None, None),
        P("dom", None, None, None),
        P("dom", None, None, None),
        P("dom", None, None),
        P("dom", None, None, None),
        P(),
        P(),
        P(),
        P(),
    )
    return jax.shard_map(
        on_device,
        mesh=mesh,
        in_specs=placed,
        out_specs=(P("dom", "feat", None), P("dom", None, "feat")),
        check_vma=False,
    )
```

```python
import functools

import jax
import jax.numpy as jnp
from jax import lax
from jax.experimental import pallas as pl
from jax.experimental.pallas import tpu as pltpu
from jax.sharding import PartitionSpec as P

f32 = jnp.float32
bf16 = jnp.bfloat16
VM = pl.BlockSpec(memory_space=pltpu.VMEM)
SM = pl.BlockSpec(memory_space=pltpu.SMEM)
HB = pl.BlockSpec(memory_space=pltpu.HBM)
LAST = (((1,), (1,)), ((), ()))
FIRST = (((0,), (0,)), ((), ()))
EXTRA = 16


def call(kernel, out_shape, in_specs, scratch=(), flops=0, size=0, limit=4, out_specs=None):
    run = pl.pallas_call(
        kernel,
        out_shape=out_shape,
        in_specs=in_specs,
        out_specs=out_specs or jax.tree.map(lambda _: VM, out_shape),
        scratch_shapes=list(scratch),
        cost_estimate=pl.CostEstimate(flops=flops, bytes_accessed=size, transcendentals=0),
        compiler_params=pltpu.CompilerParams(vmem_limit_bytes=limit << 20),
    )

    def placed(*operands):
        return run(
            *(
                pltpu.with_memory_space_constraint(value, pltpu.HBM) if spec is HB else value
                for value, spec in zip(operands, in_specs)
            )
        )

    return placed


def dot(left, right, dims):
    return lax.dot_general(left, right, dims, preferred_element_type=f32)


def step_of(groups, k):
    return sorted(range(groups), key=lambda d: (d > 0, abs(2 * d - groups - 1)))[k]


def ahead(me, groups, k):
    step = step_of(groups, k)
    return me ^ step if groups & (groups - 1) == 0 else (me + step) % groups


def behind(me, groups, k):
    step = step_of(groups, k)
    return me ^ step if groups & (groups - 1) == 0 else (me + groups - step) % groups


def step_to(a, b, count):
    return a ^ b if count & (count - 1) == 0 else (b + count - a) % count


def next_to(a, step, count):
    return a ^ step if count & (count - 1) == 0 else (a + step) % count


def fetch(sems, *pairs):
    copies = [pltpu.make_async_copy(a, b, sems.at[i]) for i, (a, b) in enumerate(pairs)]
    for copy in copies:
        copy.start()
    return copies


def columns_of(values):
    return values.reshape(-1, values.shape[-1]).T


def gather_kernel(chunk, me_ref, sources_hbm, features_hbm, out_ref, *rest):
    blocks, (sources_ref, features_ref, hits, sems) = rest[:-4], rest[-4:]
    parts, groups, slots = sources_ref.shape
    nodes = hits.shape[1]
    rows = nodes // groups
    indices, table = fetch(sems, (sources_hbm, sources_ref), (features_hbm, features_ref))
    indices.wait()
    lane = lax.broadcasted_iota(jnp.int32, (slots, nodes), 1)

    def step(i, last):
        columns = columns_of(sources_ref[pl.ds(i * chunk, chunk)])
        for n in range(chunk * groups):
            hits[n * slots : (n + 1) * slots, :] = jnp.where(
                columns[:, n : n + 1] == lane, 1.0, 0.0
            ).astype(bf16)
        if last:
            table.wait()
        picked = dot(hits[...], features_ref[...], LAST).astype(bf16)
        out_ref[pl.ds(i * chunk, chunk)] = picked.reshape(chunk, groups * slots, -1)

    if parts == chunk:
        step(0, True)
    else:
        table.wait()
        lax.fori_loop(0, parts // chunk, lambda i, _: step(i, False), None)
    for k in range(1, groups):
        group = ahead(me_ref[0], groups, k)
        blocks[k - 1][...] = features_ref[:, pl.ds(pl.multiple_of(group * rows, rows), rows)]


def local_kernel(
    chunk,
    me_ref,
    part_ref,
    ids_hbm,
    counts_hbm,
    features_hbm,
    tiles_hbm,
    targets_hbm,
    weight_hbm,
    sources_hbm,
    sums_ref,
    edges_ref,
    band_ref,
    hits_ref,
    far_ref,
    ids_ref,
    counts_ref,
    features_ref,
    tiles_ref,
    targets_ref,
    weight_ref,
    sources_ref,
    bands,
    sems,
):
    me = me_ref[0]
    parts, groups, slots = targets_ref.shape
    rows = tiles_ref.shape[1]
    width = features_hbm.shape[0]
    copies = fetch(
        sems,
        (ids_hbm, ids_ref),
        (counts_hbm, counts_ref),
        (features_hbm, features_ref.at[pl.ds(0, width), :]),
        (tiles_hbm, tiles_ref),
        (targets_hbm, targets_ref),
        (weight_hbm, weight_ref),
        (sources_hbm, sources_ref),
    )
    extra = features_ref.shape[0] - width
    features_ref[width:, :] = jnp.ones((extra, features_ref.shape[1]), bf16)
    bands[...] = jnp.zeros_like(bands)
    for copy in copies:
        copy.wait()

    def place(t, _):
        at = pl.multiple_of(ids_ref[1, t] * rows, rows)
        bands[ids_ref[0, t], :, pl.ds(at, rows)] = tiles_ref[t]
        return 0

    lax.fori_loop(0, tiles_ref.shape[0], place, 0, unroll=tiles_ref.shape[0] <= 16)
    for g in range(groups):
        sums_ref[g] = dot(features_ref[...], bands[g], LAST)
    band_ref[...] = bands[me]
    lane = lax.broadcasted_iota(jnp.int32, (slots, rows), 1)
    slot = lax.broadcasted_iota(jnp.int32, (slots, rows), 0)

    def connect(i, _):
        first = i * chunk
        target = columns_of(targets_ref[pl.ds(first, chunk)])
        weight = columns_of(weight_ref[pl.ds(first, chunk)].astype(f32))
        for g in range(groups):
            degree = jnp.zeros((1, rows), f32)
            for e in range(chunk):
                n = e * groups + g
                hit = (target[:, n : n + 1] == lane) & (slot < counts_ref[g, first + e])
                values = jnp.where(hit, weight[:, n : n + 1], 0.0)
                edges_ref[g, first + e] = values.astype(bf16)
                degree = degree + jnp.sum(values, axis=0, keepdims=True)
            sums_ref[g, width : width + 1, :] += degree
        return 0

    if parts == chunk:
        connect(0, 0)
    else:
        lax.fori_loop(0, parts // chunk, connect, 0)
    mine = lax.broadcasted_iota(jnp.int32, sources_ref.shape, 1) == me
    picks = jnp.sum(jnp.where(mine, sources_ref[...], 0), axis=1).T
    lane = lax.broadcasted_iota(jnp.int32, (slots, hits_ref.shape[1]), 1)
    chips, chip, core = parts // 2, part_ref[0] // 2, part_ref[0] % 2
    for d in range(parts):
        other = (d % 2) ^ core
        to = other * chips + step_to(chip, d // 2, chips)
        hits_ref[pl.ds(pl.multiple_of(to * slots, slots), slots), :] = jnp.where(
            picks[:, d : d + 1] == lane, 1.0, 0.0
        ).astype(bf16)
        at = step_to(d // 2, chip, chips) * 2 + other
        far_ref[pl.ds(pl.multiple_of(at * slots, slots), slots), :] = edges_ref[me, d]


def mean_kernel(me_ref, incoming_ref, sums_ref, edges_ref, *outs):
    groups, parts, slots, rows = edges_ref.shape
    width = incoming_ref.shape[2]
    for k in range(groups):
        group = ahead(me_ref[0], groups, k)
        arrived = incoming_ref[:, pl.ds(pl.multiple_of(group * slots, slots), slots), :]
        arrived = arrived.reshape(parts * slots, width)
        total = sums_ref[group, :width, :] + dot(
            arrived, edges_ref[group].reshape(parts * slots, rows), FIRST
        )
        outs[k][...] = (total / sums_ref[group, width : width + 1, :]).astype(bf16)


def self_kernel(me_ref, features_hbm, weight_ref, *rest):
    parts, (out_ref, own_ref, sem) = rest[:-3], rest[-3:]
    groups, (width, rows) = len(parts) + 1, own_ref.shape
    me = me_ref[0]
    own = pltpu.make_async_copy(
        features_hbm.at[:, pl.ds(pl.multiple_of(me * rows, rows), rows)], own_ref, sem
    )
    own.start()
    total = jnp.zeros(out_ref.shape, f32)
    for k in range(1, groups):
        span = pl.ds(pl.multiple_of(behind(me, groups, k) * width, width), width)
        total = total + dot(parts[k - 1][...], weight_ref[span, :], FIRST)
    own.wait()
    span = pl.ds(pl.multiple_of(me * width, width), width)
    out_ref[...] = total + dot(own_ref[...], weight_ref[span, :], FIRST)


def hidden_kernel(me_ref, weight_ref, out_weight_ref, own_ref, *rest):
    groups = len(rest) // 2
    parts, hidden_ref, copies = rest[:groups], rest[groups], rest[groups + 1 :]
    width = parts[0].shape[0]
    total = own_ref[...]
    for k in range(len(parts)):
        source = behind(me_ref[0], len(parts), k)
        span = pl.ds(pl.multiple_of(source * width, width), width)
        total = total + dot(parts[k][...], weight_ref[span, :], FIRST)
    hidden = jnp.maximum(total, 0.0).astype(bf16)
    hidden_ref[...] = hidden
    projected = dot(out_weight_ref[...], hidden, LAST).astype(bf16)
    for copy in copies:
        copy[...] = projected


def own_kernel(hidden_ref, weight_ref, out_ref, hidden_out, sem):
    copy = pltpu.make_async_copy(hidden_ref, hidden_out, sem)
    copy.start()
    out_ref[...] = dot(weight_ref[...], hidden_ref[...], LAST)
    copy.wait()


def pick_kernel(me_ref, hits_ref, *rest):
    projected, (mine_ref, mate_ref) = rest[:-2], rest[-2:]
    groups, rows = len(projected), projected[0].shape[1]
    total = None
    for k in range(groups):
        at = pl.multiple_of(behind(me_ref[0], groups, k) * rows, rows)
        term = dot(hits_ref[:, pl.ds(at, rows)], projected[k][...], LAST)
        total = term if total is None else total + term
    total = total.astype(bf16)
    half = total.shape[0] // 2
    mine_ref[...] = total[:half].reshape(mine_ref.shape)
    mate_ref[...] = total[half:].reshape(mate_ref.shape)


def pair_kernel(mine_ref, got_ref, *outs):
    for j, out in enumerate(outs):
        out[0] = mine_ref[j]
        out[1] = got_ref[j]


def near_kernel(me_ref, band_ref, *rest):
    projected, out_ref = rest[:-1], rest[-1]
    groups, rows = len(projected), projected[0].shape[1]
    total = None
    for k in range(groups):
        at = pl.multiple_of(behind(me_ref[0], groups, k) * rows, rows)
        term = dot(projected[k][...], band_ref[:, pl.ds(at, rows)], LAST)
        total = term if total is None else total + term
    out_ref[...] = total


def last_kernel(me_ref, own_ref, near_ref, far_ref, sums_ref, *rest):
    arrived, out_ref = rest[:-1], rest[-1]
    width = sums_ref.shape[1] - EXTRA
    arrived = jnp.concatenate([part[...].reshape(-1, part.shape[2]) for part in arrived], axis=0)
    far = dot(arrived, far_ref[...], FIRST)
    total = own_ref[...] + (near_ref[...] + far) / sums_ref[me_ref[0], width : width + 1, :]
    out_ref[...] = total.reshape(out_ref.shape)


def on_device(
    features,
    tiles,
    tile_ids,
    sources,
    targets,
    counts,
    edge_weight,
    self_one,
    neigh_one,
    self_out,
    neigh_out,
):
    feature_rows, tile_contents = features[0].T, tiles[0]
    groups, parts = lax.axis_size("feat"), lax.axis_size("dom")
    me = lax.axis_index("feat").astype(jnp.int32).reshape(1)
    part = lax.axis_index("dom").astype(jnp.int32).reshape(1)
    width, nodes = feature_rows.shape
    rows, slots = nodes // groups, sources.shape[3]
    hid, classes = self_one.shape[1], self_out.shape[1]
    chunk = max(1, min(parts, 512 // (groups * slots)))

    def shape(*dims, dtype=bf16):
        return jax.ShapeDtypeStruct(dims, dtype)

    def shift(blocks):
        return [
            lax.ppermute(
                block, "feat", [(i, ahead(i, groups, k)) for i in range(groups)]
            )
            for k, block in enumerate(blocks, 1)
        ]

    def swap(value):
        return lax.all_to_all(value, "dom", split_axis=0, concat_axis=0, tiled=True)

    sent, *feature_blocks = call(
        functools.partial(gather_kernel, chunk),
        (shape(parts, groups * slots, width),) + (shape(width, rows),) * (groups - 1),
        [SM, HB, HB],
        [
            pltpu.VMEM((parts, groups, slots), jnp.int32),
            pltpu.VMEM((width, nodes), bf16),
            pltpu.VMEM((chunk * groups * slots, nodes), bf16),
            pltpu.SemaphoreType.DMA((2,)),
        ],
        2 * nodes * nodes * width,
        1 << 20,
    )(me, sources[0], feature_rows)
    incoming = swap(sent)
    feature_blocks = shift(feature_blocks)
    sums, edges, band, hits, far = call(
        functools.partial(local_kernel, chunk),
        (
            shape(groups, width + EXTRA, rows, dtype=f32),
            shape(groups, parts, slots, rows),
            shape(rows, nodes),
            shape(parts * slots, nodes),
            shape(parts * slots, rows),
        ),
        [SM, SM] + [HB] * 7,
        [
            pltpu.SMEM(tile_ids.shape[:0:-1], jnp.int32),
            pltpu.SMEM(counts.shape[:0:-1], jnp.int32),
            pltpu.VMEM((width + EXTRA, nodes), bf16),
            pltpu.VMEM(tile_contents.shape, bf16),
            pltpu.VMEM((parts, groups, slots), jnp.int32),
            pltpu.VMEM((parts, groups, slots), bf16),
            pltpu.VMEM((parts, groups, slots), jnp.int32),
            pltpu.VMEM((groups, rows, nodes), bf16),
            pltpu.SemaphoreType.DMA((7,)),
        ],
        2 * nodes * nodes * width,
        1 << 20,
        4 if groups <= 4 else 16,
    )(
        me,
        part,
        tile_ids[0].T,
        counts[0].T,
        feature_rows,
        tile_contents,
        targets[0],
        edge_weight[0],
        sources[0],
    )
    own_mean, *means = call(
        mean_kernel,
        (shape(width, rows),) * groups,
        [SM, VM, VM, VM],
        (),
        2 * nodes * parts * slots * width,
        1 << 20,
    )(me, incoming, sums, edges)
    means = shift(means)
    own = call(
        self_kernel,
        shape(rows, hid, dtype=f32),
        [SM, HB] + [VM] * groups,
        [pltpu.VMEM((width, rows), bf16), pltpu.SemaphoreType.DMA],
        2 * rows * hid * groups * width,
        2 << 20,
    )(me, feature_rows, self_one, *feature_blocks)
    hidden, *projected = call(
        hidden_kernel,
        (shape(rows, hid),) + (shape(classes, rows),) * groups,
        [SM] + [VM] * (3 + groups),
        (),
        2 * rows * hid * groups * width,
        2 << 20,
    )(me, neigh_one, neigh_out.T, own, own_mean, *means)
    projected = projected[:1] + shift(projected[1:])
    chips = parts // 2
    mine, mate = call(
        pick_kernel,
        (shape(chips, slots, classes),) * 2,
        [SM] + [VM] * (1 + groups),
        (),
        2 * parts * slots * nodes * classes,
        1 << 19,
    )(me, hits, *projected)
    mate = lax.ppermute(mate, "dom", [(d, d ^ 1) for d in range(parts)])
    arrived = call(
        pair_kernel, (shape(2, slots, classes),) * chips, [VM, VM], (), 0, 1 << 19
    )(mine, mate)
    arrived = [arrived[0]] + [
        lax.ppermute(
            arrived[j],
            "dom",
            [(d, next_to(d // 2, j, chips) * 2 + d % 2) for d in range(parts)],
        )
        for j in range(1, chips)
    ]
    own, hidden = call(
        own_kernel,
        (shape(classes, rows, dtype=f32), shape(rows, hid)),
        [VM, VM],
        [pltpu.SemaphoreType.DMA],
        2 * rows * hid * classes,
        1 << 20,
        out_specs=(VM, HB),
    )(hidden, self_out.T)
    near = call(
        near_kernel,
        shape(classes, rows, dtype=f32),
        [SM] + [VM] * (1 + groups),
        (),
        2 * rows * nodes * classes,
        1 << 19,
    )(me, band, *projected)
    logits = call(
        last_kernel,
        shape(classes, 1, rows, dtype=f32),
        [SM] + [VM] * (4 + chips),
        (),
        2 * rows * parts * slots * classes,
        1 << 19,
    )(me, own, near, far, sums, *arrived)
    return hidden[None], logits.transpose(1, 0, 2)


def solution(mesh):
    placed = (
        P("dom", None, "feat"),
        P("dom", None, None, None),
        P("dom", None, None),
        P("dom", None, None, None),
        P("dom", None, None, None),
        P("dom", None, None),
        P("dom", None, None, None),
        P(),
        P(),
        P(),
        P(),
    )
    return jax.shard_map(
        on_device,
        mesh=mesh,
        in_specs=placed,
        out_specs=(P("dom", "feat", None), P("dom", None, "feat")),
        check_vma=False,
    )
```

```python
import functools

import jax
import jax.numpy as jnp
from jax import lax
from jax.experimental import pallas as pl
from jax.experimental.pallas import tpu as pltpu
from jax.sharding import PartitionSpec as P

f32 = jnp.float32
bf16 = jnp.bfloat16
VM = pl.BlockSpec(memory_space=pltpu.VMEM)
SM = pl.BlockSpec(memory_space=pltpu.SMEM)
HB = pl.BlockSpec(memory_space=pltpu.HBM)
LAST = (((1,), (1,)), ((), ()))
FIRST = (((0,), (0,)), ((), ()))
EXTRA = 16


def call(kernel, out_shape, in_specs, scratch=(), flops=0, size=0, limit=4, out_specs=None):
    run = pl.pallas_call(
        kernel,
        out_shape=out_shape,
        in_specs=in_specs,
        out_specs=out_specs or jax.tree.map(lambda _: VM, out_shape),
        scratch_shapes=list(scratch),
        cost_estimate=pl.CostEstimate(flops=flops, bytes_accessed=size, transcendentals=0),
        compiler_params=pltpu.CompilerParams(vmem_limit_bytes=limit << 20),
    )

    def placed(*operands):
        return run(
            *(
                pltpu.with_memory_space_constraint(value, pltpu.HBM) if spec is HB else value
                for value, spec in zip(operands, in_specs)
            )
        )

    return placed


def dot(left, right, dims):
    return lax.dot_general(left, right, dims, preferred_element_type=f32)


def step_of(groups, k):
    return (groups - k) % groups


def whole_lanes(count):
    return -(-count // 128) * 128


def ahead(me, groups, k):
    step = step_of(groups, k)
    return me ^ step if groups & (groups - 1) == 0 else (me + step) % groups


def behind(me, groups, k):
    step = step_of(groups, k)
    return me ^ step if groups & (groups - 1) == 0 else (me + groups - step) % groups


def step_to(a, b, count):
    step = a ^ b if count & (count - 1) == 0 else (b + count - a) % count
    return (count - step) % count


def next_to(a, j, count):
    step = step_of(count, j)
    return a ^ step if count & (count - 1) == 0 else (a + step) % count


def fetch(sems, *pairs):
    copies = [pltpu.make_async_copy(a, b, sems.at[i]) for i, (a, b) in enumerate(pairs)]
    for copy in copies:
        copy.start()
    return copies


def columns_of(values):
    return values.reshape(-1, values.shape[-1]).T


def gather_kernel(chunk, me_ref, sources_hbm, features_hbm, out_ref, *rest):
    blocks, (sources_ref, features_ref, hits, sems) = rest[:-4], rest[-4:]
    parts, groups, slots = sources_ref.shape
    nodes = hits.shape[1]
    rows = nodes // groups
    width = features_hbm.shape[0]
    indices, table = fetch(
        sems, (sources_hbm, sources_ref), (features_hbm, features_ref.at[pl.ds(0, width), :])
    )
    if features_ref.shape[0] > width:
        features_ref[width:, :] = jnp.zeros((features_ref.shape[0] - width, nodes), bf16)
    indices.wait()
    lane = lax.broadcasted_iota(jnp.int32, (slots, nodes), 1)

    def step(i, last):
        columns = columns_of(sources_ref[pl.ds(i * chunk, chunk)])
        for n in range(chunk * groups):
            hits[n * slots : (n + 1) * slots, :] = jnp.where(
                columns[:, n : n + 1] == lane, 1.0, 0.0
            ).astype(bf16)
        if last:
            table.wait()
        picked = dot(hits[...], features_ref[...], LAST).astype(bf16)
        out_ref[pl.ds(i * chunk, chunk)] = picked.reshape(chunk, groups * slots, -1)

    if parts == chunk:
        step(0, True)
    else:
        table.wait()
        lax.fori_loop(0, parts // chunk, lambda i, _: step(i, False), None)
    for k in range(1, groups):
        group = ahead(me_ref[0], groups, k)
        blocks[k - 1][...] = features_ref[:width, pl.ds(pl.multiple_of(group * rows, rows), rows)]


def local_kernel(
    chunk,
    me_ref,
    part_ref,
    ids_hbm,
    counts_hbm,
    features_hbm,
    tiles_hbm,
    targets_hbm,
    weight_hbm,
    sources_hbm,
    sums_ref,
    edges_ref,
    band_ref,
    hits_ref,
    far_ref,
    ids_ref,
    counts_ref,
    features_ref,
    tiles_ref,
    targets_ref,
    weight_ref,
    sources_ref,
    bands,
    sems,
):
    me = me_ref[0]
    parts, groups, slots = targets_ref.shape
    rows = tiles_ref.shape[1]
    width = features_hbm.shape[0]
    copies = fetch(
        sems,
        (ids_hbm, ids_ref),
        (counts_hbm, counts_ref),
        (features_hbm, features_ref.at[pl.ds(0, width), :]),
        (tiles_hbm, tiles_ref),
        (targets_hbm, targets_ref),
        (weight_hbm, weight_ref),
        (sources_hbm, sources_ref),
    )
    extra = features_ref.shape[0] - width
    features_ref[width:, :] = jnp.ones((extra, features_ref.shape[1]), bf16)
    bands[...] = jnp.zeros_like(bands)
    for copy in copies:
        copy.wait()

    def place(t, _):
        at = pl.multiple_of(ids_ref[1, t] * rows, rows)
        bands[ids_ref[0, t], :, pl.ds(at, rows)] = tiles_ref[t]
        return 0

    lax.fori_loop(0, tiles_ref.shape[0], place, 0, unroll=tiles_ref.shape[0] <= 16)
    for g in range(groups):
        sums_ref[g] = dot(features_ref[...], bands[g], LAST)
    band_ref[...] = bands[me]
    lane = lax.broadcasted_iota(jnp.int32, (slots, rows), 1)
    slot = lax.broadcasted_iota(jnp.int32, (slots, rows), 0)

    def connect(i, _):
        first = i * chunk
        target = columns_of(targets_ref[pl.ds(first, chunk)])
        weight = columns_of(weight_ref[pl.ds(first, chunk)].astype(f32))
        for g in range(groups):
            degree = jnp.zeros((1, rows), f32)
            for e in range(chunk):
                n = e * groups + g
                hit = (target[:, n : n + 1] == lane) & (slot < counts_ref[g, first + e])
                values = jnp.where(hit, weight[:, n : n + 1], 0.0)
                edges_ref[g, first + e] = values.astype(bf16)
                degree = degree + jnp.sum(values, axis=0, keepdims=True)
            sums_ref[g, width : width + 1, :] += degree
        return 0

    if parts == chunk:
        connect(0, 0)
    else:
        lax.fori_loop(0, parts // chunk, connect, 0)
    mine = lax.broadcasted_iota(jnp.int32, sources_ref.shape, 1) == me
    picks = jnp.sum(jnp.where(mine, sources_ref[...], 0), axis=1).T
    lane = lax.broadcasted_iota(jnp.int32, (slots, hits_ref.shape[1]), 1)
    chips, chip, core = parts // 2, part_ref[0] // 2, part_ref[0] % 2
    for d in range(parts):
        other = (d % 2) ^ core
        to = other * chips + step_to(chip, d // 2, chips)
        hits_ref[pl.ds(pl.multiple_of(to * slots, slots), slots), :] = jnp.where(
            picks[:, d : d + 1] == lane, 1.0, 0.0
        ).astype(bf16)
        at = step_to(d // 2, chip, chips) * 2 + other
        far_ref[pl.ds(pl.multiple_of(at * slots, slots), slots), :] = edges_ref[me, d]


def mean_kernel(me_ref, incoming_ref, sums_ref, edges_ref, *outs):
    groups, parts, slots, rows = edges_ref.shape
    width = outs[0].shape[0]
    for k in range(groups):
        group = ahead(me_ref[0], groups, k)
        arrived = incoming_ref[:, pl.ds(pl.multiple_of(group * slots, slots), slots), :]
        arrived = arrived.reshape(parts * slots, -1)
        far = dot(arrived, edges_ref[group].reshape(parts * slots, rows), FIRST)
        total = sums_ref[group, :width, :] + far[:width]
        outs[k][...] = (total / sums_ref[group, width : width + 1, :]).astype(bf16)


def self_kernel(me_ref, features_hbm, weight_ref, *rest):
    parts, (out_ref, own_ref, sem) = rest[:-3], rest[-3:]
    groups, (width, rows) = len(parts) + 1, own_ref.shape
    me = me_ref[0]
    own = pltpu.make_async_copy(
        features_hbm.at[:, pl.ds(pl.multiple_of(me * rows, rows), rows)], own_ref, sem
    )
    own.start()
    total = jnp.zeros(out_ref.shape, f32)
    for k in range(1, groups):
        span = pl.ds(pl.multiple_of(behind(me, groups, k) * width, width), width)
        total = total + dot(parts[k - 1][...], weight_ref[span, :], FIRST)
    own.wait()
    span = pl.ds(pl.multiple_of(me * width, width), width)
    out_ref[...] = total + dot(own_ref[...], weight_ref[span, :], FIRST)


def hidden_kernel(me_ref, weight_ref, out_weight_ref, own_ref, *rest):
    groups = len(rest) // 2
    parts, hidden_ref, copies = rest[:groups], rest[groups], rest[groups + 1 :]
    width = parts[0].shape[0]
    total = own_ref[...]
    for k in range(len(parts)):
        source = behind(me_ref[0], len(parts), k)
        span = pl.ds(pl.multiple_of(source * width, width), width)
        total = total + dot(parts[k][...], weight_ref[span, :], FIRST)
    hidden = jnp.maximum(total, 0.0).astype(bf16)
    hidden_ref[...] = hidden
    projected = dot(out_weight_ref[...], hidden, LAST).astype(bf16)
    for copy in copies:
        copy[...] = projected


def own_kernel(hidden_ref, weight_ref, out_ref, hidden_out, sem):
    copy = pltpu.make_async_copy(hidden_ref, hidden_out, sem)
    copy.start()
    out_ref[...] = dot(weight_ref[...], hidden_ref[...], LAST)
    copy.wait()


def pick_kernel(me_ref, hits_ref, *rest):
    projected, (mine_ref, mate_ref) = rest[:-2], rest[-2:]
    groups, rows = len(projected), projected[0].shape[1]
    total = None
    for k in range(groups):
        at = pl.multiple_of(behind(me_ref[0], groups, k) * rows, rows)
        term = dot(hits_ref[:, pl.ds(at, rows)], projected[k][...], LAST)
        total = term if total is None else total + term
    gap = mine_ref.shape[2] - total.shape[1]
    total = jnp.concatenate([total, jnp.zeros((total.shape[0], gap), f32)], axis=1).astype(bf16)
    half = total.shape[0] // 2
    mine_ref[...] = total[:half].reshape(mine_ref.shape)
    mate_ref[...] = total[half:].reshape(mate_ref.shape)


def pair_kernel(mine_ref, got_ref, *outs):
    for j, out in enumerate(outs):
        out[0] = mine_ref[j]
        out[1] = got_ref[j]


def near_kernel(me_ref, band_ref, *rest):
    projected, out_ref = rest[:-1], rest[-1]
    groups, rows = len(projected), projected[0].shape[1]
    total = None
    for k in range(groups):
        at = pl.multiple_of(behind(me_ref[0], groups, k) * rows, rows)
        term = dot(projected[k][...], band_ref[:, pl.ds(at, rows)], LAST)
        total = term if total is None else total + term
    out_ref[...] = total


def last_kernel(me_ref, own_ref, near_ref, far_ref, sums_ref, *rest):
    arrived, out_ref = rest[:-1], rest[-1]
    width = sums_ref.shape[1] - EXTRA
    arrived = jnp.concatenate([part[...].reshape(-1, part.shape[2]) for part in arrived], axis=0)
    far = dot(arrived, far_ref[...], FIRST)[: own_ref.shape[0]]
    total = own_ref[...] + (near_ref[...] + far) / sums_ref[me_ref[0], width : width + 1, :]
    out_ref[...] = total.reshape(out_ref.shape)


def on_device(
    features,
    tiles,
    tile_ids,
    sources,
    targets,
    counts,
    edge_weight,
    self_one,
    neigh_one,
    self_out,
    neigh_out,
):
    feature_rows, tile_contents = features[0].T, tiles[0]
    groups, parts = lax.axis_size("feat"), lax.axis_size("dom")
    me = lax.axis_index("feat").astype(jnp.int32).reshape(1)
    part = lax.axis_index("dom").astype(jnp.int32).reshape(1)
    width, nodes = feature_rows.shape
    rows, slots = nodes // groups, sources.shape[3]
    hid, classes = self_one.shape[1], self_out.shape[1]
    chunk = max(1, min(parts, 512 // (groups * slots)))

    def shape(*dims, dtype=bf16):
        return jax.ShapeDtypeStruct(dims, dtype)

    def shift(blocks):
        return [
            lax.ppermute(
                block, "feat", [(i, ahead(i, groups, k)) for i in range(groups)]
            )
            for k, block in enumerate(blocks, 1)
        ]

    def swap(value):
        return lax.all_to_all(value, "dom", split_axis=0, concat_axis=0, tiled=True)

    sent, *feature_blocks = call(
        functools.partial(gather_kernel, chunk),
        (shape(parts, groups * slots, whole_lanes(width)),)
        + (shape(width, rows),) * (groups - 1),
        [SM, HB, HB],
        [
            pltpu.VMEM((parts, groups, slots), jnp.int32),
            pltpu.VMEM((whole_lanes(width), nodes), bf16),
            pltpu.VMEM((chunk * groups * slots, nodes), bf16),
            pltpu.SemaphoreType.DMA((2,)),
        ],
        2 * nodes * nodes * width,
        1 << 20,
    )(me, sources[0], feature_rows)
    incoming = swap(sent)
    feature_blocks = shift(feature_blocks)
    sums, edges, band, hits, far = call(
        functools.partial(local_kernel, chunk),
        (
            shape(groups, width + EXTRA, rows, dtype=f32),
            shape(groups, parts, slots, rows),
            shape(rows, nodes),
            shape(parts * slots, nodes),
            shape(parts * slots, rows),
        ),
        [SM, SM] + [HB] * 7,
        [
            pltpu.SMEM(tile_ids.shape[:0:-1], jnp.int32),
            pltpu.SMEM(counts.shape[:0:-1], jnp.int32),
            pltpu.VMEM((width + EXTRA, nodes), bf16),
            pltpu.VMEM(tile_contents.shape, bf16),
            pltpu.VMEM((parts, groups, slots), jnp.int32),
            pltpu.VMEM((parts, groups, slots), bf16),
            pltpu.VMEM((parts, groups, slots), jnp.int32),
            pltpu.VMEM((groups, rows, nodes), bf16),
            pltpu.SemaphoreType.DMA((7,)),
        ],
        2 * nodes * nodes * width,
        1 << 20,
        4 if groups <= 4 else 16,
    )(
        me,
        part,
        tile_ids[0].T,
        counts[0].T,
        feature_rows,
        tile_contents,
        targets[0],
        edge_weight[0],
        sources[0],
    )
    own_mean, *means = call(
        mean_kernel,
        (shape(width, rows),) * groups,
        [SM, VM, VM, VM],
        (),
        2 * nodes * parts * slots * width,
        1 << 20,
    )(me, incoming, sums, edges)
    means = shift(means)
    own = call(
        self_kernel,
        shape(rows, hid, dtype=f32),
        [SM, HB] + [VM] * groups,
        [pltpu.VMEM((width, rows), bf16), pltpu.SemaphoreType.DMA],
        2 * rows * hid * groups * width,
        2 << 20,
    )(me, feature_rows, self_one, *feature_blocks)
    hidden, *projected = call(
        hidden_kernel,
        (shape(rows, hid),) + (shape(classes, rows),) * groups,
        [SM] + [VM] * (3 + groups),
        (),
        2 * rows * hid * groups * width,
        2 << 20,
    )(me, neigh_one, neigh_out.T, own, own_mean, *means)
    projected = projected[:1] + shift(projected[1:])
    chips = parts // 2
    mine, mate = call(
        pick_kernel,
        (shape(chips, slots, whole_lanes(classes)),) * 2,
        [SM] + [VM] * (1 + groups),
        (),
        2 * parts * slots * nodes * classes,
        1 << 19,
    )(me, hits, *projected)
    mate = lax.ppermute(mate, "dom", [(d, d ^ 1) for d in range(parts)])
    arrived = call(
        pair_kernel, (shape(2, slots, whole_lanes(classes)),) * chips, [VM, VM], (), 0, 1 << 19
    )(mine, mate)
    arrived = [arrived[0]] + [
        lax.ppermute(
            arrived[j],
            "dom",
            [(d, next_to(d // 2, j, chips) * 2 + d % 2) for d in range(parts)],
        )
        for j in range(1, chips)
    ]
    own, hidden = call(
        own_kernel,
        (shape(classes, rows, dtype=f32), shape(rows, hid)),
        [VM, VM],
        [pltpu.SemaphoreType.DMA],
        2 * rows * hid * classes,
        1 << 20,
        out_specs=(VM, HB),
    )(hidden, self_out.T)
    near = call(
        near_kernel,
        shape(classes, rows, dtype=f32),
        [SM] + [VM] * (1 + groups),
        (),
        2 * rows * nodes * classes,
        1 << 19,
    )(me, band, *projected)
    logits = call(
        last_kernel,
        shape(classes, 1, rows, dtype=f32),
        [SM] + [VM] * (4 + chips),
        (),
        2 * rows * parts * slots * classes,
        1 << 19,
    )(me, own, near, far, sums, *arrived)
    return hidden[None], logits.transpose(1, 0, 2)


def solution(mesh):
    placed = (
        P("dom", None, "feat"),
        P("dom", None, None, None),
        P("dom", None, None),
        P("dom", None, None, None),
        P("dom", None, None, None),
        P("dom", None, None),
        P("dom", None, None, None),
        P(),
        P(),
        P(),
        P(),
    )
    return jax.shard_map(
        on_device,
        mesh=mesh,
        in_specs=placed,
        out_specs=(P("dom", "feat", None), P("dom", None, "feat")),
        check_vma=False,
    )
```

```python
import functools

import jax
import jax.numpy as jnp
from jax import lax
from jax.experimental import pallas as pl
from jax.experimental.pallas import tpu as pltpu
from jax.sharding import PartitionSpec as P

f32 = jnp.float32
bf16 = jnp.bfloat16
VM = pl.BlockSpec(memory_space=pltpu.VMEM)
SM = pl.BlockSpec(memory_space=pltpu.SMEM)
HB = pl.BlockSpec(memory_space=pltpu.HBM)
LAST = (((1,), (1,)), ((), ()))
FIRST = (((0,), (0,)), ((), ()))
EXTRA = 16


def call(kernel, out_shape, in_specs, scratch=(), flops=0, size=0, limit=4, out_specs=None):
    run = pl.pallas_call(
        kernel,
        out_shape=out_shape,
        in_specs=in_specs,
        out_specs=out_specs or jax.tree.map(lambda _: VM, out_shape),
        scratch_shapes=list(scratch),
        cost_estimate=pl.CostEstimate(flops=flops, bytes_accessed=size, transcendentals=0),
        compiler_params=pltpu.CompilerParams(vmem_limit_bytes=limit << 20),
    )

    def placed(*operands):
        return run(
            *(
                pltpu.with_memory_space_constraint(value, pltpu.HBM) if spec is HB else value
                for value, spec in zip(operands, in_specs)
            )
        )

    return placed


def dot(left, right, dims):
    return lax.dot_general(left, right, dims, preferred_element_type=f32)


def step_of(groups, k):
    return (groups - k) % groups


def whole_lanes(count):
    return -(-count // 128) * 128


def hop(groups, k, core):
    return k and groups - k + core * (1 if k > 1 else 2 - groups)


def ahead(me, core, groups, k):
    step = hop(groups, k, core)
    return me ^ step if groups & (groups - 1) == 0 else (me + step) % groups


def behind(me, core, groups, k):
    step = hop(groups, k, core)
    return me ^ step if groups & (groups - 1) == 0 else (me + groups - step) % groups


def place_of(me_ref):
    return me_ref[0] // 2, me_ref[0] % 2


def step_to(a, b, count):
    step = a ^ b if count & (count - 1) == 0 else (b + count - a) % count
    return (count - step) % count


def next_to(a, j, count):
    step = step_of(count, j)
    return a ^ step if count & (count - 1) == 0 else (a + step) % count


def fetch(sems, *pairs):
    copies = [pltpu.make_async_copy(a, b, sems.at[i]) for i, (a, b) in enumerate(pairs)]
    for copy in copies:
        copy.start()
    return copies


def columns_of(values):
    return values.reshape(-1, values.shape[-1]).T


def gather_kernel(chunk, me_ref, sources_hbm, features_hbm, out_ref, *rest):
    blocks, (sources_ref, features_ref, hits, sems) = rest[:-4], rest[-4:]
    parts, groups, slots = sources_ref.shape
    nodes = hits.shape[1]
    rows = nodes // groups
    width = features_hbm.shape[0]
    indices, table = fetch(
        sems, (sources_hbm, sources_ref), (features_hbm, features_ref.at[pl.ds(0, width), :])
    )
    if features_ref.shape[0] > width:
        features_ref[width:, :] = jnp.zeros((features_ref.shape[0] - width, nodes), bf16)
    indices.wait()
    lane = lax.broadcasted_iota(jnp.int32, (slots, nodes), 1)

    def step(i, last):
        columns = columns_of(sources_ref[pl.ds(i * chunk, chunk)])
        for n in range(chunk * groups):
            hits[n * slots : (n + 1) * slots, :] = jnp.where(
                columns[:, n : n + 1] == lane, 1.0, 0.0
            ).astype(bf16)
        if last:
            table.wait()
        picked = dot(hits[...], features_ref[...], LAST).astype(bf16)
        out_ref[pl.ds(i * chunk, chunk)] = picked.reshape(chunk, groups * slots, -1)

    if parts == chunk:
        step(0, True)
    else:
        table.wait()
        lax.fori_loop(0, parts // chunk, lambda i, _: step(i, False), None)
    for k in range(1, groups):
        group = ahead(*place_of(me_ref), groups, k)
        blocks[k - 1][...] = features_ref[:width, pl.ds(pl.multiple_of(group * rows, rows), rows)]


def local_kernel(
    chunk,
    me_ref,
    part_ref,
    ids_hbm,
    counts_hbm,
    features_hbm,
    tiles_hbm,
    targets_hbm,
    weight_hbm,
    sources_hbm,
    sums_ref,
    edges_ref,
    band_ref,
    hits_ref,
    far_ref,
    ids_ref,
    counts_ref,
    features_ref,
    tiles_ref,
    targets_ref,
    weight_ref,
    sources_ref,
    bands,
    sems,
):
    me, core = place_of(me_ref)
    parts, groups, slots = targets_ref.shape
    rows = tiles_ref.shape[1]
    width = features_hbm.shape[0]
    copies = fetch(
        sems,
        (ids_hbm, ids_ref),
        (counts_hbm, counts_ref),
        (features_hbm, features_ref.at[pl.ds(0, width), :]),
        (tiles_hbm, tiles_ref),
        (targets_hbm, targets_ref),
        (weight_hbm, weight_ref),
        (sources_hbm, sources_ref),
    )
    extra = features_ref.shape[0] - width
    features_ref[width:, :] = jnp.ones((extra, features_ref.shape[1]), bf16)
    bands[...] = jnp.zeros_like(bands)
    for copy in copies:
        copy.wait()

    def place(t, _):
        at = pl.multiple_of(ids_ref[1, t] * rows, rows)
        bands[ids_ref[0, t], :, pl.ds(at, rows)] = tiles_ref[t]
        return 0

    lax.fori_loop(0, tiles_ref.shape[0], place, 0, unroll=tiles_ref.shape[0] <= 16)
    for g in range(groups):
        sums_ref[g] = dot(features_ref[...], bands[g], LAST)
    band_ref[...] = bands[me]
    lane = lax.broadcasted_iota(jnp.int32, (slots, rows), 1)
    slot = lax.broadcasted_iota(jnp.int32, (slots, rows), 0)

    def connect(i, _):
        first = i * chunk
        target = columns_of(targets_ref[pl.ds(first, chunk)])
        weight = columns_of(weight_ref[pl.ds(first, chunk)].astype(f32))
        for g in range(groups):
            degree = jnp.zeros((1, rows), f32)
            for e in range(chunk):
                n = e * groups + g
                hit = (target[:, n : n + 1] == lane) & (slot < counts_ref[g, first + e])
                values = jnp.where(hit, weight[:, n : n + 1], 0.0)
                edges_ref[g, first + e] = values.astype(bf16)
                degree = degree + jnp.sum(values, axis=0, keepdims=True)
            sums_ref[g, width : width + 1, :] += degree
        return 0

    if parts == chunk:
        connect(0, 0)
    else:
        lax.fori_loop(0, parts // chunk, connect, 0)
    mine = lax.broadcasted_iota(jnp.int32, sources_ref.shape, 1) == me
    picks = jnp.sum(jnp.where(mine, sources_ref[...], 0), axis=1).T
    lane = lax.broadcasted_iota(jnp.int32, (slots, hits_ref.shape[1]), 1)
    chips, chip = parts // 2, part_ref[0] // 2
    for d in range(parts):
        other = (d % 2) ^ core
        to = other * chips + step_to(chip, d // 2, chips)
        hits_ref[pl.ds(pl.multiple_of(to * slots, slots), slots), :] = jnp.where(
            picks[:, d : d + 1] == lane, 1.0, 0.0
        ).astype(bf16)
        at = step_to(d // 2, chip, chips) * 2 + other
        far_ref[pl.ds(pl.multiple_of(at * slots, slots), slots), :] = edges_ref[me, d]


def mean_kernel(me_ref, incoming_ref, sums_ref, edges_ref, *outs):
    groups, parts, slots, rows = edges_ref.shape
    width = outs[0].shape[0]
    for k in range(groups):
        group = ahead(*place_of(me_ref), groups, k)
        arrived = incoming_ref[:, pl.ds(pl.multiple_of(group * slots, slots), slots), :]
        arrived = arrived.reshape(parts * slots, -1)
        far = dot(arrived, edges_ref[group].reshape(parts * slots, rows), FIRST)
        total = sums_ref[group, :width, :] + far[:width]
        outs[k][...] = (total / sums_ref[group, width : width + 1, :]).astype(bf16)


def self_kernel(me_ref, features_hbm, weight_ref, *rest):
    parts, (out_ref, own_ref, sem) = rest[:-3], rest[-3:]
    groups, (width, rows) = len(parts) + 1, own_ref.shape
    me, core = place_of(me_ref)
    own = pltpu.make_async_copy(
        features_hbm.at[:, pl.ds(pl.multiple_of(me * rows, rows), rows)], own_ref, sem
    )
    own.start()
    total = jnp.zeros(out_ref.shape, f32)
    for k in range(1, groups):
        span = pl.ds(pl.multiple_of(behind(me, core, groups, k) * width, width), width)
        total = total + dot(parts[k - 1][...], weight_ref[span, :], FIRST)
    own.wait()
    span = pl.ds(pl.multiple_of(me * width, width), width)
    out_ref[...] = total + dot(own_ref[...], weight_ref[span, :], FIRST)


def hidden_kernel(me_ref, weight_ref, out_weight_ref, own_ref, *rest):
    groups = len(rest) // 2
    parts, hidden_ref, copies = rest[:groups], rest[groups], rest[groups + 1 :]
    width = parts[0].shape[0]
    total = own_ref[...]
    for k in range(len(parts)):
        source = behind(*place_of(me_ref), len(parts), k)
        span = pl.ds(pl.multiple_of(source * width, width), width)
        total = total + dot(parts[k][...], weight_ref[span, :], FIRST)
    hidden = jnp.maximum(total, 0.0).astype(bf16)
    hidden_ref[...] = hidden
    projected = dot(out_weight_ref[...], hidden, LAST).astype(bf16)
    for copy in copies:
        copy[...] = projected


def own_kernel(hidden_ref, weight_ref, out_ref, hidden_out, sem):
    copy = pltpu.make_async_copy(hidden_ref, hidden_out, sem)
    copy.start()
    out_ref[...] = dot(weight_ref[...], hidden_ref[...], LAST)
    copy.wait()


def pick_kernel(me_ref, hits_ref, *rest):
    projected, (mine_ref, mate_ref) = rest[:-2], rest[-2:]
    groups, rows = len(projected), projected[0].shape[1]
    total = None
    for k in range(groups):
        at = pl.multiple_of(behind(*place_of(me_ref), groups, k) * rows, rows)
        term = dot(hits_ref[:, pl.ds(at, rows)], projected[k][...], LAST)
        total = term if total is None else total + term
    gap = mine_ref.shape[2] - total.shape[1]
    total = jnp.concatenate([total, jnp.zeros((total.shape[0], gap), f32)], axis=1).astype(bf16)
    half = total.shape[0] // 2
    mine_ref[...] = total[:half].reshape(mine_ref.shape)
    mate_ref[...] = total[half:].reshape(mate_ref.shape)


def pair_kernel(mine_ref, got_ref, *outs):
    for j, out in enumerate(outs):
        out[0] = mine_ref[j]
        out[1] = got_ref[j]


def near_kernel(me_ref, band_ref, *rest):
    projected, out_ref = rest[:-1], rest[-1]
    groups, rows = len(projected), projected[0].shape[1]
    total = None
    for k in range(groups):
        at = pl.multiple_of(behind(*place_of(me_ref), groups, k) * rows, rows)
        term = dot(projected[k][...], band_ref[:, pl.ds(at, rows)], LAST)
        total = term if total is None else total + term
    out_ref[...] = total


def last_kernel(me_ref, own_ref, near_ref, far_ref, sums_ref, *rest):
    arrived, out_ref = rest[:-1], rest[-1]
    width = sums_ref.shape[1] - EXTRA
    arrived = jnp.concatenate([part[...].reshape(-1, part.shape[2]) for part in arrived], axis=0)
    far = dot(arrived, far_ref[...], FIRST)[: own_ref.shape[0]]
    total = own_ref[...] + (near_ref[...] + far) / sums_ref[me_ref[0] // 2, width : width + 1, :]
    out_ref[...] = total.reshape(out_ref.shape)


def on_device(
    features,
    tiles,
    tile_ids,
    sources,
    targets,
    counts,
    edge_weight,
    self_one,
    neigh_one,
    self_out,
    neigh_out,
):
    feature_rows, tile_contents = features[0].T, tiles[0]
    groups, parts = lax.axis_size("feat"), lax.axis_size("dom")
    part = lax.axis_index("dom").astype(jnp.int32)
    me = (lax.axis_index("feat").astype(jnp.int32) * 2 + part % 2).reshape(1)
    part = part.reshape(1)
    width, nodes = feature_rows.shape
    rows, slots = nodes // groups, sources.shape[3]
    hid, classes = self_one.shape[1], self_out.shape[1]
    chunk = max(1, min(parts, 512 // (groups * slots)))

    def shape(*dims, dtype=bf16):
        return jax.ShapeDtypeStruct(dims, dtype)

    def shift(blocks):
        return [
            lax.ppermute(
                block,
                ("feat", "dom"),
                [
                    (f * parts + d, ahead(f, d % 2, groups, k) * parts + d)
                    for f in range(groups)
                    for d in range(parts)
                ],
            )
            for k, block in enumerate(blocks, 1)
        ]

    def swap(value):
        return lax.all_to_all(value, "dom", split_axis=0, concat_axis=0, tiled=True)

    sent, *feature_blocks = call(
        functools.partial(gather_kernel, chunk),
        (shape(parts, groups * slots, whole_lanes(width)),)
        + (shape(width, rows),) * (groups - 1),
        [SM, HB, HB],
        [
            pltpu.VMEM((parts, groups, slots), jnp.int32),
            pltpu.VMEM((whole_lanes(width), nodes), bf16),
            pltpu.VMEM((chunk * groups * slots, nodes), bf16),
            pltpu.SemaphoreType.DMA((2,)),
        ],
        2 * nodes * nodes * width,
        1 << 20,
    )(me, sources[0], feature_rows)
    incoming = swap(sent)
    feature_blocks = shift(feature_blocks)
    sums, edges, band, hits, far = call(
        functools.partial(local_kernel, chunk),
        (
            shape(groups, width + EXTRA, rows, dtype=f32),
            shape(groups, parts, slots, rows),
            shape(rows, nodes),
            shape(parts * slots, nodes),
            shape(parts * slots, rows),
        ),
        [SM, SM] + [HB] * 7,
        [
            pltpu.SMEM(tile_ids.shape[:0:-1], jnp.int32),
            pltpu.SMEM(counts.shape[:0:-1], jnp.int32),
            pltpu.VMEM((width + EXTRA, nodes), bf16),
            pltpu.VMEM(tile_contents.shape, bf16),
            pltpu.VMEM((parts, groups, slots), jnp.int32),
            pltpu.VMEM((parts, groups, slots), bf16),
            pltpu.VMEM((parts, groups, slots), jnp.int32),
            pltpu.VMEM((groups, rows, nodes), bf16),
            pltpu.SemaphoreType.DMA((7,)),
        ],
        2 * nodes * nodes * width,
        1 << 20,
        4 if groups <= 4 else 16,
    )(
        me,
        part,
        tile_ids[0].T,
        counts[0].T,
        feature_rows,
        tile_contents,
        targets[0],
        edge_weight[0],
        sources[0],
    )
    own_mean, *means = call(
        mean_kernel,
        (shape(width, rows),) * groups,
        [SM, VM, VM, VM],
        (),
        2 * nodes * parts * slots * width,
        1 << 20,
    )(me, incoming, sums, edges)
    means = shift(means)
    own = call(
        self_kernel,
        shape(rows, hid, dtype=f32),
        [SM, HB] + [VM] * groups,
        [pltpu.VMEM((width, rows), bf16), pltpu.SemaphoreType.DMA],
        2 * rows * hid * groups * width,
        2 << 20,
    )(me, feature_rows, self_one, *feature_blocks)
    hidden, *projected = call(
        hidden_kernel,
        (shape(rows, hid),) + (shape(classes, rows),) * groups,
        [SM] + [VM] * (3 + groups),
        (),
        2 * rows * hid * groups * width,
        2 << 20,
    )(me, neigh_one, neigh_out.T, own, own_mean, *means)
    projected = projected[:1] + shift(projected[1:])
    chips = parts // 2
    mine, mate = call(
        pick_kernel,
        (shape(chips, slots, whole_lanes(classes)),) * 2,
        [SM] + [VM] * (1 + groups),
        (),
        2 * parts * slots * nodes * classes,
        1 << 19,
    )(me, hits, *projected)
    mate = lax.ppermute(mate, "dom", [(d, d ^ 1) for d in range(parts)])
    arrived = call(
        pair_kernel, (shape(2, slots, whole_lanes(classes)),) * chips, [VM, VM], (), 0, 1 << 19
    )(mine, mate)
    arrived = [arrived[0]] + [
        lax.ppermute(
            arrived[j],
            "dom",
            [(d, next_to(d // 2, j, chips) * 2 + d % 2) for d in range(parts)],
        )
        for j in range(1, chips)
    ]
    own, hidden = call(
        own_kernel,
        (shape(classes, rows, dtype=f32), shape(rows, hid)),
        [VM, VM],
        [pltpu.SemaphoreType.DMA],
        2 * rows * hid * classes,
        1 << 20,
        out_specs=(VM, HB),
    )(hidden, self_out.T)
    near = call(
        near_kernel,
        shape(classes, rows, dtype=f32),
        [SM] + [VM] * (1 + groups),
        (),
        2 * rows * nodes * classes,
        1 << 19,
    )(me, band, *projected)
    logits = call(
        last_kernel,
        shape(classes, 1, rows, dtype=f32),
        [SM] + [VM] * (4 + chips),
        (),
        2 * rows * parts * slots * classes,
        1 << 19,
    )(me, own, near, far, sums, *arrived)
    return hidden[None], logits.transpose(1, 0, 2)


def solution(mesh):
    placed = (
        P("dom", None, "feat"),
        P("dom", None, None, None),
        P("dom", None, None),
        P("dom", None, None, None),
        P("dom", None, None, None),
        P("dom", None, None),
        P("dom", None, None, None),
        P(),
        P(),
        P(),
        P(),
    )
    return jax.shard_map(
        on_device,
        mesh=mesh,
        in_specs=placed,
        out_specs=(P("dom", "feat", None), P("dom", None, "feat")),
        check_vma=False,
    )
```

```python
import functools

import jax
import jax.numpy as jnp
from jax import lax
from jax.experimental import pallas as pl
from jax.experimental.pallas import tpu as pltpu
from jax.sharding import PartitionSpec as P

f32 = jnp.float32
bf16 = jnp.bfloat16
VM = pl.BlockSpec(memory_space=pltpu.VMEM)
SM = pl.BlockSpec(memory_space=pltpu.SMEM)
HB = pl.BlockSpec(memory_space=pltpu.HBM)
LAST = (((1,), (1,)), ((), ()))
FIRST = (((0,), (0,)), ((), ()))
EXTRA = 16


def call(kernel, out_shape, in_specs, scratch=(), flops=0, size=0, limit=4, out_specs=None):
    run = pl.pallas_call(
        kernel,
        out_shape=out_shape,
        in_specs=in_specs,
        out_specs=out_specs or jax.tree.map(lambda _: VM, out_shape),
        scratch_shapes=list(scratch),
        cost_estimate=pl.CostEstimate(flops=flops, bytes_accessed=size, transcendentals=0),
        compiler_params=pltpu.CompilerParams(vmem_limit_bytes=limit << 20),
    )

    def placed(*operands):
        return run(
            *(
                pltpu.with_memory_space_constraint(value, pltpu.HBM) if spec is HB else value
                for value, spec in zip(operands, in_specs)
            )
        )

    return placed


def dot(left, right, dims):
    return lax.dot_general(left, right, dims, preferred_element_type=f32)


def step_of(groups, k):
    return (groups - k) % groups


def whole_lanes(count):
    return -(-count // 128) * 128


def ahead(me, groups, k):
    step = step_of(groups, k)
    return me ^ step if groups & (groups - 1) == 0 else (me + step) % groups


def behind(me, groups, k):
    step = step_of(groups, k)
    return me ^ step if groups & (groups - 1) == 0 else (me + groups - step) % groups


def step_to(a, b, count):
    step = a ^ b if count & (count - 1) == 0 else (b + count - a) % count
    return (count - step) % count


def next_to(a, j, count):
    step = step_of(count, j)
    return a ^ step if count & (count - 1) == 0 else (a + step) % count


def fetch(sems, *pairs):
    copies = [pltpu.make_async_copy(a, b, sems.at[i]) for i, (a, b) in enumerate(pairs)]
    for copy in copies:
        copy.start()
    return copies


def columns_of(values):
    return values.reshape(-1, values.shape[-1]).T


def gather_kernel(chunk, me_ref, part_ref, sources_hbm, features_hbm, mine_ref, mate_ref, *rest):
    blocks, (sources_ref, features_ref, order, hits, sems) = rest[:-5], rest[-5:]
    parts, groups, slots = sources_ref.shape
    nodes = hits.shape[1]
    rows = nodes // groups
    width = features_hbm.shape[0]
    chips, chip, core = parts // 2, part_ref[0] // 2, part_ref[0] % 2
    indices, table = fetch(
        sems, (sources_hbm, sources_ref), (features_hbm, features_ref.at[pl.ds(0, width), :])
    )
    if features_ref.shape[0] > width:
        features_ref[width:, :] = jnp.zeros((features_ref.shape[0] - width, nodes), bf16)
    indices.wait()
    lane = lax.broadcasted_iota(jnp.int32, (slots, nodes), 1)

    def step(i, out, other, last):
        for j in range(chunk):
            order[j] = sources_ref[next_to(chip, i * chunk + j, chips) * 2 + (core ^ other)]
        columns = columns_of(order[...])
        for n in range(chunk * groups):
            hits[n * slots : (n + 1) * slots, :] = jnp.where(
                columns[:, n : n + 1] == lane, 1.0, 0.0
            ).astype(bf16)
        if last:
            table.wait()
        picked = dot(hits[...], features_ref[...], LAST).astype(bf16)
        out[pl.ds(i * chunk, chunk)] = picked.reshape(chunk, groups * slots, -1)

    if chips == chunk:
        step(0, mate_ref, 1, True)
        step(0, mine_ref, 0, False)
    else:
        table.wait()
        for other, out in enumerate((mine_ref, mate_ref)):
            lax.fori_loop(0, chips // chunk, lambda i, _: step(i, out, other, False), None)
    for k in range(1, groups):
        group = ahead(me_ref[0], groups, k)
        blocks[k - 1][...] = features_ref[:width, pl.ds(pl.multiple_of(group * rows, rows), rows)]


def local_kernel(
    chunk,
    me_ref,
    part_ref,
    ids_hbm,
    counts_hbm,
    features_hbm,
    tiles_hbm,
    targets_hbm,
    weight_hbm,
    sources_hbm,
    sums_ref,
    edges_ref,
    band_ref,
    hits_ref,
    ids_ref,
    counts_ref,
    features_ref,
    tiles_ref,
    targets_ref,
    weight_ref,
    sources_ref,
    bands,
    sems,
):
    me = me_ref[0]
    parts, groups, slots = targets_ref.shape
    rows = tiles_ref.shape[1]
    width = features_hbm.shape[0]
    copies = fetch(
        sems,
        (ids_hbm, ids_ref),
        (counts_hbm, counts_ref),
        (features_hbm, features_ref.at[pl.ds(0, width), :]),
        (tiles_hbm, tiles_ref),
        (targets_hbm, targets_ref),
        (weight_hbm, weight_ref),
        (sources_hbm, sources_ref),
    )
    extra = features_ref.shape[0] - width
    features_ref[width:, :] = jnp.ones((extra, features_ref.shape[1]), bf16)
    bands[...] = jnp.zeros_like(bands)
    for copy in copies:
        copy.wait()

    def place(t, _):
        at = pl.multiple_of(ids_ref[1, t] * rows, rows)
        bands[ids_ref[0, t], :, pl.ds(at, rows)] = tiles_ref[t]
        return 0

    lax.fori_loop(0, tiles_ref.shape[0], place, 0, unroll=tiles_ref.shape[0] <= 16)
    for g in range(groups):
        sums_ref[g] = dot(features_ref[...], bands[g], LAST)
    band_ref[...] = bands[me]
    lane = lax.broadcasted_iota(jnp.int32, (slots, rows), 1)
    slot = lax.broadcasted_iota(jnp.int32, (slots, rows), 0)
    chips, chip, core = parts // 2, part_ref[0] // 2, part_ref[0] % 2

    def connect(i, _):
        first = i * chunk
        target = columns_of(targets_ref[pl.ds(first, chunk)])
        weight = columns_of(weight_ref[pl.ds(first, chunk)].astype(f32))
        for g in range(groups):
            degree = jnp.zeros((1, rows), f32)
            for e in range(chunk):
                n, d = e * groups + g, first + e
                at = step_to(d // 2, chip, chips) * 2 + ((d % 2) ^ core)
                hit = (target[:, n : n + 1] == lane) & (slot < counts_ref[g, first + e])
                values = jnp.where(hit, weight[:, n : n + 1], 0.0)
                edges_ref[g, at] = values.astype(bf16)
                degree = degree + jnp.sum(values, axis=0, keepdims=True)
            sums_ref[g, width : width + 1, :] += degree
        return 0

    if parts == chunk:
        connect(0, 0)
    else:
        lax.fori_loop(0, parts // chunk, connect, 0)
    mine = lax.broadcasted_iota(jnp.int32, sources_ref.shape, 1) == me
    picks = jnp.sum(jnp.where(mine, sources_ref[...], 0), axis=1).T
    lane = lax.broadcasted_iota(jnp.int32, (slots, hits_ref.shape[1]), 1)
    for d in range(parts):
        other = (d % 2) ^ core
        to = other * chips + step_to(chip, d // 2, chips)
        hits_ref[pl.ds(pl.multiple_of(to * slots, slots), slots), :] = jnp.where(
            picks[:, d : d + 1] == lane, 1.0, 0.0
        ).astype(bf16)


def mean_kernel(late, me_ref, sums_ref, edges_ref, *rest):
    groups, parts, slots, rows = edges_ref.shape
    arrived, held, outs = rest[: parts // 2], rest[parts // 2 :][:late], rest[parts // 2 + late :]
    width = outs[0].shape[0]
    for k in range(groups):
        group = ahead(me_ref[0], groups, k)
        span = pl.ds(pl.multiple_of(group * slots, slots), slots)
        far = jnp.concatenate([x[:, span, :].reshape(2 * slots, -1) for x in arrived], axis=0)
        far = dot(far, edges_ref[group].reshape(parts * slots, rows), FIRST)
        total = sums_ref[group, :width, :] + far[:width]
        outs[k][...] = (total / sums_ref[group, width : width + 1, :]).astype(bf16)
    for block, out in zip(held, outs[groups:]):
        out[...] = block[...]


def rows_from(me, groups, k, width):
    return pl.ds(pl.multiple_of(behind(me, groups, k) * width, width), width)


def self_kernel(groups, me_ref, features_hbm, weight_ref, *rest):
    early, (out_ref, own_ref, sem) = rest[:-3], rest[-3:]
    width, rows = own_ref.shape
    me = me_ref[0]
    own = pltpu.make_async_copy(
        features_hbm.at[:, pl.ds(pl.multiple_of(me * rows, rows), rows)], own_ref, sem
    )
    own.start()
    total = jnp.zeros(out_ref.shape, f32)
    for k, block in enumerate(early, 1):
        total = total + dot(block[...], weight_ref[rows_from(me, groups, k, width), :], FIRST)
    own.wait()
    span = pl.ds(pl.multiple_of(me * width, width), width)
    out_ref[...] = total + dot(own_ref[...], weight_ref[span, :], FIRST)


def hidden_kernel(groups, late, me_ref, self_weight_ref, weight_ref, out_weight_ref, own_ref, *rest):
    held, parts, (hidden_ref, *copies) = rest[:late], rest[late:][:groups], rest[late + groups :]
    width = parts[0].shape[0]
    me = me_ref[0]
    total = own_ref[...]
    for k, block in enumerate(held, groups - late):
        span = rows_from(me, groups, k, width)
        total = total + dot(block[...], self_weight_ref[span, :], FIRST)
    for k in range(groups):
        span = rows_from(me, groups, k, width)
        total = total + dot(parts[k][...], weight_ref[span, :], FIRST)
    hidden = jnp.maximum(total, 0.0).astype(bf16)
    hidden_ref[...] = hidden
    projected = dot(out_weight_ref[...], hidden, LAST).astype(bf16)
    for copy in copies:
        copy[...] = projected


def own_kernel(hidden_ref, weight_ref, out_ref, hidden_out, sem):
    copy = pltpu.make_async_copy(hidden_ref, hidden_out, sem)
    copy.start()
    out_ref[...] = dot(weight_ref[...], hidden_ref[...], LAST)
    copy.wait()


def pick_kernel(me_ref, hits_ref, *rest):
    projected, (mine_ref, mate_ref) = rest[:-2], rest[-2:]
    groups, rows = len(projected), projected[0].shape[1]
    total = None
    for k in range(groups):
        at = pl.multiple_of(behind(me_ref[0], groups, k) * rows, rows)
        term = dot(hits_ref[:, pl.ds(at, rows)], projected[k][...], LAST)
        total = term if total is None else total + term
    gap = mine_ref.shape[2] - total.shape[1]
    total = jnp.concatenate([total, jnp.zeros((total.shape[0], gap), f32)], axis=1).astype(bf16)
    half = total.shape[0] // 2
    mine_ref[...] = total[:half].reshape(mine_ref.shape)
    mate_ref[...] = total[half:].reshape(mate_ref.shape)


def pair_kernel(after, mine_ref, got_ref, *rest):
    del after
    chips = mine_ref.shape[0]
    held = (len(rest) - chips) // 2
    for j, out in enumerate(rest[held : held + chips]):
        out[0] = mine_ref[j]
        out[1] = got_ref[j]
    for block, out in zip(rest[:held], rest[held + chips :]):
        out[...] = block[...]


def near_kernel(me_ref, band_ref, *rest):
    projected, out_ref = rest[:-1], rest[-1]
    groups, rows = len(projected), projected[0].shape[1]
    total = None
    for k in range(groups):
        at = pl.multiple_of(behind(me_ref[0], groups, k) * rows, rows)
        term = dot(projected[k][...], band_ref[:, pl.ds(at, rows)], LAST)
        total = term if total is None else total + term
    out_ref[...] = total


def last_kernel(me_ref, own_ref, near_ref, edges_ref, sums_ref, *rest):
    arrived, out_ref = rest[:-1], rest[-1]
    groups, parts, slots, rows = edges_ref.shape
    me, width = me_ref[0], sums_ref.shape[1] - EXTRA
    arrived = jnp.concatenate([x[...].reshape(2 * slots, -1) for x in arrived], axis=0)
    far = dot(arrived, edges_ref[me].reshape(parts * slots, rows), FIRST)
    far = far[: own_ref.shape[0]]
    total = own_ref[...] + (near_ref[...] + far) / sums_ref[me, width : width + 1, :]
    out_ref[...] = total.reshape(out_ref.shape)


def on_device(
    features,
    tiles,
    tile_ids,
    sources,
    targets,
    counts,
    edge_weight,
    self_one,
    neigh_one,
    self_out,
    neigh_out,
):
    feature_rows, tile_contents = features[0].T, tiles[0]
    groups, parts = lax.axis_size("feat"), lax.axis_size("dom")
    me = lax.axis_index("feat").astype(jnp.int32).reshape(1)
    part = lax.axis_index("dom").astype(jnp.int32).reshape(1)
    width, nodes = feature_rows.shape
    rows, slots = nodes // groups, sources.shape[3]
    hid, classes = self_one.shape[1], self_out.shape[1]
    chips, late = parts // 2, 1
    chunk = max(1, min(parts, 512 // (groups * slots)))

    def shape(*dims, dtype=bf16):
        return jax.ShapeDtypeStruct(dims, dtype)

    def shift(blocks, first=1):
        return [
            lax.ppermute(
                block, "feat", [(i, ahead(i, groups, k)) for i in range(groups)]
            )
            for k, block in enumerate(blocks, first)
        ]

    def to_mate(value):
        return lax.ppermute(value, "dom", [(d, d ^ 1) for d in range(parts)])

    def to_chips(blocks):
        return [blocks[0]] + [
            lax.ppermute(
                blocks[j],
                "dom",
                [(d, next_to(d // 2, j, chips) * 2 + d % 2) for d in range(parts)],
            )
            for j in range(1, chips)
        ]

    picked = min(chips, chunk)
    lanes = whole_lanes(width)
    mine, mate, *feature_blocks = call(
        functools.partial(gather_kernel, picked),
        (shape(chips, groups * slots, lanes),) * 2 + (shape(width, rows),) * (groups - 1),
        [SM, SM, HB, HB],
        [
            pltpu.VMEM((parts, groups, slots), jnp.int32),
            pltpu.VMEM((lanes, nodes), bf16),
            pltpu.VMEM((picked, groups, slots), jnp.int32),
            pltpu.VMEM((picked * groups * slots, nodes), bf16),
            pltpu.SemaphoreType.DMA((2,)),
        ],
        2 * nodes * nodes * width,
        1 << 20,
    )(me, part, sources[0], feature_rows)
    mate = to_mate(mate)
    sums, edges, band, hits = call(
        functools.partial(local_kernel, chunk),
        (
            shape(groups, width + EXTRA, rows, dtype=f32),
            shape(groups, parts, slots, rows),
            shape(rows, nodes),
            shape(parts * slots, nodes),
        ),
        [SM, SM] + [HB] * 7,
        [
            pltpu.SMEM(tile_ids.shape[:0:-1], jnp.int32),
            pltpu.SMEM(counts.shape[:0:-1], jnp.int32),
            pltpu.VMEM((width + EXTRA, nodes), bf16),
            pltpu.VMEM(tile_contents.shape, bf16),
            pltpu.VMEM((parts, groups, slots), jnp.int32),
            pltpu.VMEM((parts, groups, slots), bf16),
            pltpu.VMEM((parts, groups, slots), jnp.int32),
            pltpu.VMEM((groups, rows, nodes), bf16),
            pltpu.SemaphoreType.DMA((7,)),
        ],
        2 * nodes * nodes * width,
        1 << 20,
        4 if groups <= 4 else 16,
    )(
        me,
        part,
        tile_ids[0].T,
        counts[0].T,
        feature_rows,
        tile_contents,
        targets[0],
        edge_weight[0],
        sources[0],
    )
    paired = call(
        pair_kernel,
        (shape(2, groups * slots, lanes),) * chips + (shape(width, rows),) * (groups - 1 - late),
        [VM] * (2 + groups - late),
        (),
        0,
        1 << 20,
    )(hits, mine, mate, *feature_blocks[: groups - 1 - late])
    arrived = to_chips(paired[:chips])
    early_blocks = shift(paired[chips:])
    moved = call(
        functools.partial(mean_kernel, late),
        (shape(width, rows),) * (groups + late),
        [SM] + [VM] * (2 + chips + late),
        (),
        2 * nodes * parts * slots * width,
        1 << 20,
    )(me, sums, edges, *arrived, *feature_blocks[groups - 1 - late :])
    means = [moved[0]] + shift(moved[1:groups])
    late_blocks = shift(moved[groups:], groups - late)
    own = call(
        functools.partial(self_kernel, groups),
        shape(rows, hid, dtype=f32),
        [SM, HB] + [VM] * (groups - late),
        [pltpu.VMEM((width, rows), bf16), pltpu.SemaphoreType.DMA],
        2 * rows * hid * groups * width,
        2 << 20,
    )(me, feature_rows, self_one, *early_blocks)
    hidden, *projected = call(
        functools.partial(hidden_kernel, groups, late),
        (shape(rows, hid),) + (shape(classes, rows),) * groups,
        [SM] + [VM] * (4 + late + groups),
        (),
        2 * rows * hid * groups * width,
        2 << 20,
    )(me, self_one, neigh_one, neigh_out.T, own, *late_blocks, *means)
    projected = projected[:1] + shift(projected[1:])
    mine, mate = call(
        pick_kernel,
        (shape(chips, slots, whole_lanes(classes)),) * 2,
        [SM] + [VM] * (1 + groups),
        (),
        2 * parts * slots * nodes * classes,
        1 << 19,
    )(me, hits, *projected)
    mate = to_mate(mate)
    arrived = to_chips(
        call(pair_kernel, (shape(2, slots, whole_lanes(classes)),) * chips, [VM] * 3, (), 0, 1 << 19)(
            hits, mine, mate
        )
    )
    own, hidden = call(
        own_kernel,
        (shape(classes, rows, dtype=f32), shape(rows, hid)),
        [VM, VM],
        [pltpu.SemaphoreType.DMA],
        2 * rows * hid * classes,
        1 << 20,
        out_specs=(VM, HB),
    )(hidden, self_out.T)
    near = call(
        near_kernel,
        shape(classes, rows, dtype=f32),
        [SM] + [VM] * (1 + groups),
        (),
        2 * rows * nodes * classes,
        1 << 19,
    )(me, band, *projected)
    logits = call(
        last_kernel,
        shape(classes, 1, rows, dtype=f32),
        [SM] + [VM] * (4 + chips),
        (),
        2 * rows * parts * slots * classes,
        1 << 19,
    )(me, own, near, edges, sums, *arrived)
    return hidden[None], logits.transpose(1, 0, 2)


def solution(mesh):
    placed = (
        P("dom", None, "feat"),
        P("dom", None, None, None),
        P("dom", None, None),
        P("dom", None, None, None),
        P("dom", None, None, None),
        P("dom", None, None),
        P("dom", None, None, None),
        P(),
        P(),
        P(),
        P(),
    )
    return jax.shard_map(
        on_device,
        mesh=mesh,
        in_specs=placed,
        out_specs=(P("dom", "feat", None), P("dom", None, "feat")),
        check_vma=False,
    )
```

```python
import functools

import jax
import jax.numpy as jnp
from jax import lax
from jax.experimental import pallas as pl
from jax.experimental.pallas import tpu as pltpu
from jax.sharding import PartitionSpec as P

f32 = jnp.float32
bf16 = jnp.bfloat16
VM = pl.BlockSpec(memory_space=pltpu.VMEM)
SM = pl.BlockSpec(memory_space=pltpu.SMEM)
HB = pl.BlockSpec(memory_space=pltpu.HBM)
LAST = (((1,), (1,)), ((), ()))
FIRST = (((0,), (0,)), ((), ()))
EXTRA = 16


def call(kernel, out_shape, in_specs, scratch=(), flops=0, size=0, limit=4, out_specs=None):
    run = pl.pallas_call(
        kernel,
        out_shape=out_shape,
        in_specs=in_specs,
        out_specs=out_specs or jax.tree.map(lambda _: VM, out_shape),
        scratch_shapes=list(scratch),
        cost_estimate=pl.CostEstimate(flops=flops, bytes_accessed=size, transcendentals=0),
        compiler_params=pltpu.CompilerParams(vmem_limit_bytes=limit << 20),
    )

    def placed(*operands):
        return run(
            *(
                pltpu.with_memory_space_constraint(value, pltpu.HBM) if spec is HB else value
                for value, spec in zip(operands, in_specs)
            )
        )

    return placed


def dot(left, right, dims):
    return lax.dot_general(left, right, dims, preferred_element_type=f32)


def step_of(groups, k):
    return (groups - k) % groups


def whole_lanes(count):
    return -(-count // 128) * 128


def ahead(me, groups, k):
    step = step_of(groups, k)
    return me ^ step if groups & (groups - 1) == 0 else (me + step) % groups


def behind(me, groups, k):
    step = step_of(groups, k)
    return me ^ step if groups & (groups - 1) == 0 else (me + groups - step) % groups


def step_to(a, b, count):
    step = a ^ b if count & (count - 1) == 0 else (b + count - a) % count
    return (count - step) % count


def next_to(a, j, count):
    step = step_of(count, j)
    return a ^ step if count & (count - 1) == 0 else (a + step) % count


def fetch(sems, *pairs):
    copies = [pltpu.make_async_copy(a, b, sems.at[i]) for i, (a, b) in enumerate(pairs)]
    for copy in copies:
        copy.start()
    return copies


def columns_of(values):
    return values.reshape(-1, values.shape[-1]).T


def gather_kernel(chunk, me_ref, part_ref, sources_hbm, features_hbm, mine_ref, mate_ref, *rest):
    blocks, (sources_ref, features_ref, order, hits, sems) = rest[:-5], rest[-5:]
    parts, groups, slots = sources_ref.shape
    nodes = hits.shape[1]
    rows = nodes // groups
    width = features_hbm.shape[0]
    chips, chip, core = parts // 2, part_ref[0] // 2, part_ref[0] % 2
    indices, table = fetch(
        sems, (sources_hbm, sources_ref), (features_hbm, features_ref.at[pl.ds(0, width), :])
    )
    if features_ref.shape[0] > width:
        features_ref[width:, :] = jnp.zeros((features_ref.shape[0] - width, nodes), bf16)
    indices.wait()
    lane = lax.broadcasted_iota(jnp.int32, (slots, nodes), 1)

    def step(i, out, other, last):
        for j in range(chunk):
            order[j] = sources_ref[next_to(chip, i * chunk + j, chips) * 2 + (core ^ other)]
        columns = columns_of(order[...])
        for n in range(chunk * groups):
            hits[n * slots : (n + 1) * slots, :] = jnp.where(
                columns[:, n : n + 1] == lane, 1.0, 0.0
            ).astype(bf16)
        if last:
            table.wait()
        picked = dot(hits[...], features_ref[...], LAST).astype(bf16)
        out[pl.ds(i * chunk, chunk)] = picked.reshape(chunk, groups * slots, -1)

    if chips == chunk:
        step(0, mate_ref, 1, True)
        step(0, mine_ref, 0, False)
    else:
        table.wait()
        for other, out in enumerate((mine_ref, mate_ref)):
            lax.fori_loop(0, chips // chunk, lambda i, _: step(i, out, other, False), None)
    for k in range(1, groups):
        group = ahead(me_ref[0], groups, k)
        blocks[k - 1][...] = features_ref[:width, pl.ds(pl.multiple_of(group * rows, rows), rows)]


def local_kernel(
    chunk,
    me_ref,
    part_ref,
    ids_hbm,
    counts_hbm,
    features_hbm,
    tiles_hbm,
    targets_hbm,
    weight_hbm,
    sums_ref,
    edges_ref,
    band_ref,
    ids_ref,
    counts_ref,
    features_ref,
    tiles_ref,
    targets_ref,
    weight_ref,
    bands,
    sems,
):
    me = me_ref[0]
    parts, groups, slots = targets_ref.shape
    rows = tiles_ref.shape[1]
    width = features_hbm.shape[0]
    copies = fetch(
        sems,
        (ids_hbm, ids_ref),
        (counts_hbm, counts_ref),
        (features_hbm, features_ref.at[pl.ds(0, width), :]),
        (tiles_hbm, tiles_ref),
        (targets_hbm, targets_ref),
        (weight_hbm, weight_ref),
    )
    extra = features_ref.shape[0] - width
    features_ref[width:, :] = jnp.ones((extra, features_ref.shape[1]), bf16)
    bands[...] = jnp.zeros_like(bands)
    for copy in copies:
        copy.wait()

    def place(t, _):
        at = pl.multiple_of(ids_ref[1, t] * rows, rows)
        bands[ids_ref[0, t], :, pl.ds(at, rows)] = tiles_ref[t]
        return 0

    lax.fori_loop(0, tiles_ref.shape[0], place, 0, unroll=tiles_ref.shape[0] <= 16)
    for g in range(groups):
        sums_ref[g] = dot(features_ref[...], bands[g], LAST)
    band_ref[...] = bands[me]
    lane = lax.broadcasted_iota(jnp.int32, (slots, rows), 1)
    slot = lax.broadcasted_iota(jnp.int32, (slots, rows), 0)
    chips, chip, core = parts // 2, part_ref[0] // 2, part_ref[0] % 2

    def connect(i, _):
        first = i * chunk
        target = columns_of(targets_ref[pl.ds(first, chunk)])
        weight = columns_of(weight_ref[pl.ds(first, chunk)].astype(f32))
        for g in range(groups):
            degree = jnp.zeros((1, rows), f32)
            for e in range(chunk):
                n, d = e * groups + g, first + e
                at = step_to(d // 2, chip, chips) * 2 + ((d % 2) ^ core)
                hit = (target[:, n : n + 1] == lane) & (slot < counts_ref[g, first + e])
                values = jnp.where(hit, weight[:, n : n + 1], 0.0)
                edges_ref[g, at] = values.astype(bf16)
                degree = degree + jnp.sum(values, axis=0, keepdims=True)
            sums_ref[g, width : width + 1, :] += degree
        return 0

    if parts == chunk:
        connect(0, 0)
    else:
        lax.fori_loop(0, parts // chunk, connect, 0)


def hits_kernel(after, me_ref, part_ref, sources_hbm, hits_ref, sources_ref, sem):
    del after
    copy = pltpu.make_async_copy(sources_hbm, sources_ref, sem)
    copy.start()
    parts, groups, slots = sources_ref.shape
    chips, chip, core = parts // 2, part_ref[0] // 2, part_ref[0] % 2
    mine = lax.broadcasted_iota(jnp.int32, sources_ref.shape, 1) == me_ref[0]
    copy.wait()
    picks = jnp.sum(jnp.where(mine, sources_ref[...], 0), axis=1).T
    lane = lax.broadcasted_iota(jnp.int32, (slots, hits_ref.shape[1]), 1)
    for d in range(parts):
        to = ((d % 2) ^ core) * chips + step_to(chip, d // 2, chips)
        hits_ref[pl.ds(pl.multiple_of(to * slots, slots), slots), :] = jnp.where(
            picks[:, d : d + 1] == lane, 1.0, 0.0
        ).astype(bf16)


def mean_kernel(late, me_ref, sums_ref, edges_ref, *rest):
    groups, parts, slots, rows = edges_ref.shape
    arrived, held, outs = rest[: parts // 2], rest[parts // 2 :][:late], rest[parts // 2 + late :]
    width = outs[0].shape[0]
    for k in range(groups):
        group = ahead(me_ref[0], groups, k)
        span = pl.ds(pl.multiple_of(group * slots, slots), slots)
        far = jnp.concatenate([x[:, span, :].reshape(2 * slots, -1) for x in arrived], axis=0)
        far = dot(far, edges_ref[group].reshape(parts * slots, rows), FIRST)
        total = sums_ref[group, :width, :] + far[:width]
        outs[k][...] = (total / sums_ref[group, width : width + 1, :]).astype(bf16)
    for block, out in zip(held, outs[groups:]):
        out[...] = block[...]


def rows_from(me, groups, k, width):
    return pl.ds(pl.multiple_of(behind(me, groups, k) * width, width), width)


def self_kernel(groups, me_ref, features_hbm, weight_ref, *rest):
    early, (out_ref, own_ref, sem) = rest[:-3], rest[-3:]
    width, rows = own_ref.shape
    me = me_ref[0]
    own = pltpu.make_async_copy(
        features_hbm.at[:, pl.ds(pl.multiple_of(me * rows, rows), rows)], own_ref, sem
    )
    own.start()
    span = pl.ds(pl.multiple_of(me * width, width), width)
    total = jnp.zeros(out_ref.shape, f32)
    for k, block in enumerate(early, 1):
        total = total + dot(block[...], weight_ref[rows_from(me, groups, k, width), :], FIRST)
    own.wait()
    out_ref[...] = total + dot(own_ref[...], weight_ref[span, :], FIRST)


def hidden_kernel(groups, late, me_ref, self_weight_ref, weight_ref, out_weight_ref, own_ref, *rest):
    held, parts, (hidden_ref, *copies) = rest[:late], rest[late:][:groups], rest[late + groups :]
    width = parts[0].shape[0]
    me = me_ref[0]
    total = own_ref[...]
    for k, block in enumerate(held, groups - late):
        span = rows_from(me, groups, k, width)
        total = total + dot(block[...], self_weight_ref[span, :], FIRST)
    for k, block in enumerate(parts):
        span = rows_from(me, groups, k, width)
        total = total + dot(block[...], weight_ref[span, :], FIRST)
    hidden = jnp.maximum(total, 0.0).astype(bf16)
    hidden_ref[...] = hidden
    projected = dot(out_weight_ref[...], hidden, LAST).astype(bf16)
    for copy in copies:
        copy[...] = projected


def own_kernel(hidden_ref, weight_ref, out_ref, hidden_out, sem):
    copy = pltpu.make_async_copy(hidden_ref, hidden_out, sem)
    copy.start()
    out_ref[...] = dot(weight_ref[...], hidden_ref[...], LAST)
    copy.wait()


def pick_kernel(me_ref, hits_ref, *rest):
    projected, (mine_ref, mate_ref) = rest[:-2], rest[-2:]
    groups, rows = len(projected), projected[0].shape[1]
    total = None
    for k in range(groups):
        at = pl.multiple_of(behind(me_ref[0], groups, k) * rows, rows)
        term = dot(hits_ref[:, pl.ds(at, rows)], projected[k][...], LAST)
        total = term if total is None else total + term
    gap = mine_ref.shape[2] - total.shape[1]
    total = jnp.concatenate([total, jnp.zeros((total.shape[0], gap), f32)], axis=1).astype(bf16)
    half = total.shape[0] // 2
    mine_ref[...] = total[:half].reshape(mine_ref.shape)
    mate_ref[...] = total[half:].reshape(mate_ref.shape)


def pair_kernel(after, mine_ref, got_ref, *rest):
    del after
    chips = mine_ref.shape[0]
    held = (len(rest) - chips) // 2
    for j, out in enumerate(rest[held : held + chips]):
        out[0] = mine_ref[j]
        out[1] = got_ref[j]
    for block, out in zip(rest[:held], rest[held + chips :]):
        out[...] = block[...]


def near_kernel(me_ref, own_ref, sums_ref, band_ref, *rest):
    projected, out_ref = rest[:-1], rest[-1]
    groups, rows = len(projected), projected[0].shape[1]
    me, width = me_ref[0], sums_ref.shape[1] - EXTRA
    total = None
    for k in range(groups):
        at = pl.multiple_of(behind(me, groups, k) * rows, rows)
        term = dot(projected[k][...], band_ref[:, pl.ds(at, rows)], LAST)
        total = term if total is None else total + term
    out_ref[...] = own_ref[...] + total / sums_ref[me, width : width + 1, :]


def last_kernel(me_ref, near_ref, edges_ref, sums_ref, *rest):
    arrived, out_ref = rest[:-1], rest[-1]
    groups, parts, slots, rows = edges_ref.shape
    me, width = me_ref[0], sums_ref.shape[1] - EXTRA
    arrived = jnp.concatenate([x[...].reshape(2 * slots, -1) for x in arrived], axis=0)
    far = dot(arrived, edges_ref[me].reshape(parts * slots, rows), FIRST)
    far = far[: near_ref.shape[0]]
    total = near_ref[...] + far / sums_ref[me, width : width + 1, :]
    out_ref[...] = total.reshape(out_ref.shape)


def on_device(
    features,
    tiles,
    tile_ids,
    sources,
    targets,
    counts,
    edge_weight,
    self_one,
    neigh_one,
    self_out,
    neigh_out,
):
    feature_rows, tile_contents = features[0].T, tiles[0]
    groups, parts = lax.axis_size("feat"), lax.axis_size("dom")
    me = lax.axis_index("feat").astype(jnp.int32).reshape(1)
    part = lax.axis_index("dom").astype(jnp.int32).reshape(1)
    width, nodes = feature_rows.shape
    rows, slots = nodes // groups, sources.shape[3]
    hid, classes = self_one.shape[1], self_out.shape[1]
    chips, late = parts // 2, 0
    chunk = max(1, min(parts, 512 // (groups * slots)))

    def shape(*dims, dtype=bf16):
        return jax.ShapeDtypeStruct(dims, dtype)

    def shift(blocks, first=1):
        return [
            lax.ppermute(
                block, "feat", [(i, ahead(i, groups, k)) for i in range(groups)]
            )
            for k, block in enumerate(blocks, first)
        ]

    def to_mate(value):
        return lax.ppermute(value, "dom", [(d, d ^ 1) for d in range(parts)])

    def to_chips(blocks):
        return [blocks[0]] + [
            lax.ppermute(
                blocks[j],
                "dom",
                [(d, next_to(d // 2, j, chips) * 2 + d % 2) for d in range(parts)],
            )
            for j in range(1, chips)
        ]

    picked = min(chips, chunk)
    lanes = whole_lanes(width)
    mine, mate, *feature_blocks = call(
        functools.partial(gather_kernel, picked),
        (shape(chips, groups * slots, lanes),) * 2 + (shape(width, rows),) * (groups - 1),
        [SM, SM, HB, HB],
        [
            pltpu.VMEM((parts, groups, slots), jnp.int32),
            pltpu.VMEM((lanes, nodes), bf16),
            pltpu.VMEM((picked, groups, slots), jnp.int32),
            pltpu.VMEM((picked * groups * slots, nodes), bf16),
            pltpu.SemaphoreType.DMA((2,)),
        ],
        2 * nodes * nodes * width,
        1 << 20,
    )(me, part, sources[0], feature_rows)
    mate = to_mate(mate)
    sums, edges, band = call(
        functools.partial(local_kernel, chunk),
        (
            shape(groups, width + EXTRA, rows, dtype=f32),
            shape(groups, parts, slots, rows),
            shape(rows, nodes),
        ),
        [SM, SM] + [HB] * 6,
        [
            pltpu.SMEM(tile_ids.shape[:0:-1], jnp.int32),
            pltpu.SMEM(counts.shape[:0:-1], jnp.int32),
            pltpu.VMEM((width + EXTRA, nodes), bf16),
            pltpu.VMEM(tile_contents.shape, bf16),
            pltpu.VMEM((parts, groups, slots), jnp.int32),
            pltpu.VMEM((parts, groups, slots), bf16),
            pltpu.VMEM((groups, rows, nodes), bf16),
            pltpu.SemaphoreType.DMA((6,)),
        ],
        2 * nodes * nodes * width,
        1 << 20,
        4 if groups <= 4 else 16,
    )(
        me,
        part,
        tile_ids[0].T,
        counts[0].T,
        feature_rows,
        tile_contents,
        targets[0],
        edge_weight[0],
    )
    paired = call(
        pair_kernel,
        (shape(2, groups * slots, lanes),) * chips + (shape(width, rows),) * (groups - 1 - late),
        [VM] * (2 + groups - late),
        (),
        0,
        1 << 20,
    )(band, mine, mate, *feature_blocks[: groups - 1 - late])
    arrived = to_chips(paired[:chips])
    early_blocks = shift(paired[chips:])
    moved = call(
        functools.partial(mean_kernel, late),
        (shape(width, rows),) * (groups + late),
        [SM] + [VM] * (2 + chips + late),
        (),
        2 * nodes * parts * slots * width,
        1 << 20,
    )(me, sums, edges, *arrived, *feature_blocks[groups - 1 - late :])
    means = [moved[0]] + shift(moved[1:groups])
    late_blocks = shift(moved[groups:], groups - late)
    own = call(
        functools.partial(self_kernel, groups),
        shape(rows, hid, dtype=f32),
        [SM, HB] + [VM] * (groups - late),
        [pltpu.VMEM((width, rows), bf16), pltpu.SemaphoreType.DMA],
        2 * rows * hid * groups * width,
        2 << 20,
    )(me, feature_rows, self_one, *early_blocks)
    hidden, *projected = call(
        functools.partial(hidden_kernel, groups, late),
        (shape(rows, hid),) + (shape(classes, rows),) * groups,
        [SM] + [VM] * (4 + late + groups),
        (),
        2 * rows * hid * groups * width,
        2 << 20,
    )(me, self_one, neigh_one, neigh_out.T, own, *late_blocks, *means)
    hits = call(
        hits_kernel,
        shape(parts * slots, nodes),
        [VM, SM, SM, HB],
        [pltpu.VMEM((parts, groups, slots), jnp.int32), pltpu.SemaphoreType.DMA],
        0,
        1 << 19,
    )(projected[0], me, part, sources[0])
    projected = projected[:1] + shift(projected[1:])
    mine, mate = call(
        pick_kernel,
        (shape(chips, slots, whole_lanes(classes)),) * 2,
        [SM] + [VM] * (1 + groups),
        (),
        2 * parts * slots * nodes * classes,
        1 << 19,
    )(me, hits, *projected)
    mate = to_mate(mate)
    arrived = to_chips(
        call(pair_kernel, (shape(2, slots, whole_lanes(classes)),) * chips, [VM] * 3, (), 0, 1 << 19)(
            hits, mine, mate
        )
    )
    own, hidden = call(
        own_kernel,
        (shape(classes, rows, dtype=f32), shape(rows, hid)),
        [VM, VM],
        [pltpu.SemaphoreType.DMA],
        2 * rows * hid * classes,
        1 << 20,
        out_specs=(VM, HB),
    )(hidden, self_out.T)
    near = call(
        near_kernel,
        shape(classes, rows, dtype=f32),
        [SM] + [VM] * (3 + groups),
        (),
        2 * rows * nodes * classes,
        1 << 19,
    )(me, own, sums, band, *projected)
    logits = call(
        last_kernel,
        shape(classes, 1, rows, dtype=f32),
        [SM] + [VM] * (3 + chips),
        (),
        2 * rows * parts * slots * classes,
        1 << 19,
    )(me, near, edges, sums, *arrived)
    return hidden[None], logits.transpose(1, 0, 2)


def solution(mesh):
    placed = (
        P("dom", None, "feat"),
        P("dom", None, None, None),
        P("dom", None, None),
        P("dom", None, None, None),
        P("dom", None, None, None),
        P("dom", None, None),
        P("dom", None, None, None),
        P(),
        P(),
        P(),
        P(),
    )
    return jax.shard_map(
        on_device,
        mesh=mesh,
        in_specs=placed,
        out_specs=(P("dom", "feat", None), P("dom", None, "feat")),
        check_vma=False,
    )
```

```python
import functools

import jax
import jax.numpy as jnp
from jax import lax
from jax.experimental import pallas as pl
from jax.experimental.pallas import tpu as pltpu
from jax.sharding import PartitionSpec as P

f32 = jnp.float32
bf16 = jnp.bfloat16
VM = pl.BlockSpec(memory_space=pltpu.VMEM)
SM = pl.BlockSpec(memory_space=pltpu.SMEM)
HB = pl.BlockSpec(memory_space=pltpu.HBM)
LAST = (((1,), (1,)), ((), ()))
FIRST = (((0,), (0,)), ((), ()))
EXTRA = 16


def call(kernel, out_shape, in_specs, scratch=(), flops=0, size=0, limit=4, out_specs=None):
    run = pl.pallas_call(
        kernel,
        out_shape=out_shape,
        in_specs=in_specs,
        out_specs=out_specs or jax.tree.map(lambda _: VM, out_shape),
        scratch_shapes=list(scratch),
        cost_estimate=pl.CostEstimate(flops=flops, bytes_accessed=size, transcendentals=0),
        compiler_params=pltpu.CompilerParams(vmem_limit_bytes=limit << 20),
    )

    def placed(*operands):
        return run(
            *(
                pltpu.with_memory_space_constraint(value, pltpu.HBM) if spec is HB else value
                for value, spec in zip(operands, in_specs)
            )
        )

    return placed


def dot(left, right, dims):
    return lax.dot_general(left, right, dims, preferred_element_type=f32)


def step_of(groups, k):
    return (groups - k) % groups


def whole_lanes(count):
    return -(-count // 128) * 128


def ahead(me, groups, k):
    step = step_of(groups, k)
    return me ^ step if groups & (groups - 1) == 0 else (me + step) % groups


def behind(me, groups, k):
    step = step_of(groups, k)
    return me ^ step if groups & (groups - 1) == 0 else (me + groups - step) % groups


def rounds_of(groups):
    if groups == 4:
        pairs = [[(0, 2)], [(0, 3), (1, 2)], [(1, 3)], [(0, 1), (2, 3)]]
        return [dict(p + [(b, a) for a, b in p]) for p in pairs]
    return [{i: ahead(i, groups, k) for i in range(groups)} for k in range(1, groups)]


def look_up(table, me):
    found = -1
    for key, value in table.items():
        found = jnp.where(me == key, value, found)
    return found


def step_to(a, b, count):
    step = a ^ b if count & (count - 1) == 0 else (b + count - a) % count
    return (count - step) % count


def next_to(a, j, count):
    step = step_of(count, j)
    return a ^ step if count & (count - 1) == 0 else (a + step) % count


def fetch(sems, *pairs):
    copies = [pltpu.make_async_copy(a, b, sems.at[i]) for i, (a, b) in enumerate(pairs)]
    for copy in copies:
        copy.start()
    return copies


def columns_of(values):
    return values.reshape(-1, values.shape[-1]).T


def gather_kernel(chunk, me_ref, part_ref, sources_hbm, features_hbm, mine_ref, mate_ref, *rest):
    blocks, (sources_ref, features_ref, order, hits, sems) = rest[:-5], rest[-5:]
    parts, groups, slots = sources_ref.shape
    nodes = hits.shape[1]
    rows = nodes // groups
    width = features_hbm.shape[0]
    chips, chip, core = parts // 2, part_ref[0] // 2, part_ref[0] % 2
    indices, table = fetch(
        sems, (sources_hbm, sources_ref), (features_hbm, features_ref.at[pl.ds(0, width), :])
    )
    if features_ref.shape[0] > width:
        features_ref[width:, :] = jnp.zeros((features_ref.shape[0] - width, nodes), bf16)
    indices.wait()
    lane = lax.broadcasted_iota(jnp.int32, (slots, nodes), 1)

    def step(i, out, other, last):
        for j in range(chunk):
            order[j] = sources_ref[next_to(chip, i * chunk + j, chips) * 2 + (core ^ other)]
        columns = columns_of(order[...])
        for n in range(chunk * groups):
            hits[n * slots : (n + 1) * slots, :] = jnp.where(
                columns[:, n : n + 1] == lane, 1.0, 0.0
            ).astype(bf16)
        if last:
            table.wait()
        picked = dot(hits[...], features_ref[...], LAST).astype(bf16)
        out[pl.ds(i * chunk, chunk)] = picked.reshape(chunk, groups * slots, -1)

    if chips == chunk:
        step(0, mate_ref, 1, True)
        step(0, mine_ref, 0, False)
    else:
        table.wait()
        for other, out in enumerate((mine_ref, mate_ref)):
            lax.fori_loop(0, chips // chunk, lambda i, _: step(i, out, other, False), None)
    for table, block in zip(rounds_of(groups), blocks):
        group = jnp.maximum(look_up(table, me_ref[0]), 0)
        block[...] = features_ref[:width, pl.ds(pl.multiple_of(group * rows, rows), rows)]


def local_kernel(
    chunk,
    me_ref,
    part_ref,
    ids_hbm,
    counts_hbm,
    features_hbm,
    tiles_hbm,
    targets_hbm,
    weight_hbm,
    sums_ref,
    edges_ref,
    band_ref,
    ids_ref,
    counts_ref,
    features_ref,
    tiles_ref,
    targets_ref,
    weight_ref,
    bands,
    sems,
):
    me = me_ref[0]
    parts, groups, slots = targets_ref.shape
    rows = tiles_ref.shape[1]
    width = features_hbm.shape[0]
    copies = fetch(
        sems,
        (ids_hbm, ids_ref),
        (counts_hbm, counts_ref),
        (features_hbm, features_ref.at[pl.ds(0, width), :]),
        (tiles_hbm, tiles_ref),
        (targets_hbm, targets_ref),
        (weight_hbm, weight_ref),
    )
    extra = features_ref.shape[0] - width
    features_ref[width:, :] = jnp.ones((extra, features_ref.shape[1]), bf16)
    bands[...] = jnp.zeros_like(bands)
    for copy in copies:
        copy.wait()

    def place(t, _):
        at = pl.multiple_of(ids_ref[1, t] * rows, rows)
        bands[ids_ref[0, t], :, pl.ds(at, rows)] = tiles_ref[t]
        return 0

    lax.fori_loop(0, tiles_ref.shape[0], place, 0, unroll=tiles_ref.shape[0] <= 16)
    for g in range(groups):
        sums_ref[g] = dot(features_ref[...], bands[g], LAST)
    band_ref[...] = bands[me]
    lane = lax.broadcasted_iota(jnp.int32, (slots, rows), 1)
    slot = lax.broadcasted_iota(jnp.int32, (slots, rows), 0)
    chips, chip, core = parts // 2, part_ref[0] // 2, part_ref[0] % 2

    def connect(i, _):
        first = i * chunk
        target = columns_of(targets_ref[pl.ds(first, chunk)])
        weight = columns_of(weight_ref[pl.ds(first, chunk)].astype(f32))
        for g in range(groups):
            degree = jnp.zeros((1, rows), f32)
            for e in range(chunk):
                n, d = e * groups + g, first + e
                at = step_to(d // 2, chip, chips) * 2 + ((d % 2) ^ core)
                hit = (target[:, n : n + 1] == lane) & (slot < counts_ref[g, first + e])
                values = jnp.where(hit, weight[:, n : n + 1], 0.0)
                edges_ref[g, at] = values.astype(bf16)
                degree = degree + jnp.sum(values, axis=0, keepdims=True)
            sums_ref[g, width : width + 1, :] += degree
        return 0

    if parts == chunk:
        connect(0, 0)
    else:
        lax.fori_loop(0, parts // chunk, connect, 0)


def hits_kernel(after, me_ref, part_ref, sources_hbm, hits_ref, sources_ref, sem):
    del after
    copy = pltpu.make_async_copy(sources_hbm, sources_ref, sem)
    copy.start()
    parts, groups, slots = sources_ref.shape
    chips, chip, core = parts // 2, part_ref[0] // 2, part_ref[0] % 2
    mine = lax.broadcasted_iota(jnp.int32, sources_ref.shape, 1) == me_ref[0]
    copy.wait()
    picks = jnp.sum(jnp.where(mine, sources_ref[...], 0), axis=1).T
    lane = lax.broadcasted_iota(jnp.int32, (slots, hits_ref.shape[1]), 1)
    for d in range(parts):
        to = ((d % 2) ^ core) * chips + step_to(chip, d // 2, chips)
        hits_ref[pl.ds(pl.multiple_of(to * slots, slots), slots), :] = jnp.where(
            picks[:, d : d + 1] == lane, 1.0, 0.0
        ).astype(bf16)


def mean_kernel(me_ref, sums_ref, edges_ref, *rest):
    groups, parts, slots, rows = edges_ref.shape
    arrived, outs = rest[: parts // 2], rest[parts // 2 :]
    width = outs[0].shape[0]
    for k in range(groups):
        group = ahead(me_ref[0], groups, k)
        span = pl.ds(pl.multiple_of(group * slots, slots), slots)
        far = jnp.concatenate([x[:, span, :].reshape(2 * slots, -1) for x in arrived], axis=0)
        far = dot(far, edges_ref[group].reshape(parts * slots, rows), FIRST)
        total = sums_ref[group, :width, :] + far[:width]
        outs[k][...] = (total / sums_ref[group, width : width + 1, :]).astype(bf16)


def self_kernel(groups, me_ref, features_hbm, weight_ref, *rest):
    blocks, (out_ref, own_ref, sem) = rest[:-3], rest[-3:]
    width, rows = own_ref.shape
    me = me_ref[0]
    own = pltpu.make_async_copy(
        features_hbm.at[:, pl.ds(pl.multiple_of(me * rows, rows), rows)], own_ref, sem
    )
    own.start()
    out_ref[...] = jnp.zeros_like(out_ref)

    def add(block, source):
        span = pl.ds(pl.multiple_of(source * width, width), width)
        out_ref[...] += dot(block[...], weight_ref[span, :], FIRST)

    for table, block in zip(rounds_of(groups), blocks):
        source = look_up({b: a for a, b in table.items()}, me)
        pl.when(source >= 0)(functools.partial(add, block, source))
    own.wait()
    add(own_ref, me)


def hidden_kernel(groups, me_ref, weight_ref, out_weight_ref, own_ref, *rest):
    parts, (hidden_ref, *copies) = rest[:groups], rest[groups:]
    width = parts[0].shape[0]
    total = own_ref[...]
    for k, block in enumerate(parts):
        source = behind(me_ref[0], groups, k)
        span = pl.ds(pl.multiple_of(source * width, width), width)
        total = total + dot(block[...], weight_ref[span, :], FIRST)
    hidden = jnp.maximum(total, 0.0).astype(bf16)
    hidden_ref[...] = hidden
    projected = dot(out_weight_ref[...], hidden, LAST).astype(bf16)
    for copy in copies:
        copy[...] = projected


def own_kernel(hidden_ref, weight_ref, out_ref, hidden_out, sem):
    copy = pltpu.make_async_copy(hidden_ref, hidden_out, sem)
    copy.start()
    out_ref[...] = dot(weight_ref[...], hidden_ref[...], LAST)
    copy.wait()


def pick_kernel(me_ref, hits_ref, *rest):
    projected, (mine_ref, mate_ref) = rest[:-2], rest[-2:]
    groups, rows = len(projected), projected[0].shape[1]
    total = None
    for k in range(groups):
        at = pl.multiple_of(behind(me_ref[0], groups, k) * rows, rows)
        term = dot(hits_ref[:, pl.ds(at, rows)], projected[k][...], LAST)
        total = term if total is None else total + term
    gap = mine_ref.shape[2] - total.shape[1]
    total = jnp.concatenate([total, jnp.zeros((total.shape[0], gap), f32)], axis=1).astype(bf16)
    half = total.shape[0] // 2
    mine_ref[...] = total[:half].reshape(mine_ref.shape)
    mate_ref[...] = total[half:].reshape(mate_ref.shape)


def pair_kernel(after, mine_ref, got_ref, *rest):
    del after
    chips = mine_ref.shape[0]
    held = (len(rest) - chips) // 2
    for j, out in enumerate(rest[held : held + chips]):
        out[0] = mine_ref[j]
        out[1] = got_ref[j]
    for block, out in zip(rest[:held], rest[held + chips :]):
        out[...] = block[...]


def near_kernel(me_ref, own_ref, sums_ref, band_ref, *rest):
    projected, out_ref = rest[:-1], rest[-1]
    groups, rows = len(projected), projected[0].shape[1]
    me, width = me_ref[0], sums_ref.shape[1] - EXTRA
    total = None
    for k in range(groups):
        at = pl.multiple_of(behind(me, groups, k) * rows, rows)
        term = dot(projected[k][...], band_ref[:, pl.ds(at, rows)], LAST)
        total = term if total is None else total + term
    out_ref[...] = own_ref[...] + total / sums_ref[me, width : width + 1, :]


def last_kernel(me_ref, near_ref, edges_ref, sums_ref, *rest):
    arrived, out_ref = rest[:-1], rest[-1]
    groups, parts, slots, rows = edges_ref.shape
    me, width = me_ref[0], sums_ref.shape[1] - EXTRA
    arrived = jnp.concatenate([x[...].reshape(2 * slots, -1) for x in arrived], axis=0)
    far = dot(arrived, edges_ref[me].reshape(parts * slots, rows), FIRST)
    far = far[: near_ref.shape[0]]
    total = near_ref[...] + far / sums_ref[me, width : width + 1, :]
    out_ref[...] = total.reshape(out_ref.shape)


def on_device(
    features,
    tiles,
    tile_ids,
    sources,
    targets,
    counts,
    edge_weight,
    self_one,
    neigh_one,
    self_out,
    neigh_out,
):
    feature_rows, tile_contents = features[0].T, tiles[0]
    groups, parts = lax.axis_size("feat"), lax.axis_size("dom")
    me = lax.axis_index("feat").astype(jnp.int32).reshape(1)
    part = lax.axis_index("dom").astype(jnp.int32).reshape(1)
    width, nodes = feature_rows.shape
    rows, slots = nodes // groups, sources.shape[3]
    hid, classes = self_one.shape[1], self_out.shape[1]
    chips, rounds = parts // 2, rounds_of(groups)
    chunk = max(1, min(parts, 512 // (groups * slots)))

    def shape(*dims, dtype=bf16):
        return jax.ShapeDtypeStruct(dims, dtype)

    def shift(blocks):
        return [
            lax.ppermute(
                block, "feat", [(i, ahead(i, groups, k)) for i in range(groups)]
            )
            for k, block in enumerate(blocks, 1)
        ]

    def to_mate(value):
        return lax.ppermute(value, "dom", [(d, d ^ 1) for d in range(parts)])

    def to_chips(blocks):
        return [blocks[0]] + [
            lax.ppermute(
                blocks[j],
                "dom",
                [(d, next_to(d // 2, j, chips) * 2 + d % 2) for d in range(parts)],
            )
            for j in range(1, chips)
        ]

    picked = min(chips, chunk)
    lanes = whole_lanes(width)
    mine, mate, *feature_blocks = call(
        functools.partial(gather_kernel, picked),
        (shape(chips, groups * slots, lanes),) * 2 + (shape(width, rows),) * len(rounds),
        [SM, SM, HB, HB],
        [
            pltpu.VMEM((parts, groups, slots), jnp.int32),
            pltpu.VMEM((lanes, nodes), bf16),
            pltpu.VMEM((picked, groups, slots), jnp.int32),
            pltpu.VMEM((picked * groups * slots, nodes), bf16),
            pltpu.SemaphoreType.DMA((2,)),
        ],
        2 * nodes * nodes * width,
        1 << 20,
    )(me, part, sources[0], feature_rows)
    mate = to_mate(mate)
    sums, edges, band = call(
        functools.partial(local_kernel, chunk),
        (
            shape(groups, width + EXTRA, rows, dtype=f32),
            shape(groups, parts, slots, rows),
            shape(rows, nodes),
        ),
        [SM, SM] + [HB] * 6,
        [
            pltpu.SMEM(tile_ids.shape[:0:-1], jnp.int32),
            pltpu.SMEM(counts.shape[:0:-1], jnp.int32),
            pltpu.VMEM((width + EXTRA, nodes), bf16),
            pltpu.VMEM(tile_contents.shape, bf16),
            pltpu.VMEM((parts, groups, slots), jnp.int32),
            pltpu.VMEM((parts, groups, slots), bf16),
            pltpu.VMEM((groups, rows, nodes), bf16),
            pltpu.SemaphoreType.DMA((6,)),
        ],
        2 * nodes * nodes * width,
        1 << 20,
        4 if groups <= 4 else 16,
    )(
        me,
        part,
        tile_ids[0].T,
        counts[0].T,
        feature_rows,
        tile_contents,
        targets[0],
        edge_weight[0],
    )
    paired = call(
        pair_kernel,
        (shape(2, groups * slots, lanes),) * chips + (shape(width, rows),) * len(rounds),
        [VM] * (3 + len(rounds)),
        (),
        0,
        1 << 20,
    )(band, mine, mate, *feature_blocks)
    arrived = to_chips(paired[:chips])
    feature_blocks = [
        lax.ppermute(block, "feat", list(table.items()))
        for table, block in zip(rounds, paired[chips:])
    ]
    means = call(
        mean_kernel,
        (shape(width, rows),) * groups,
        [SM] + [VM] * (2 + chips),
        (),
        2 * nodes * parts * slots * width,
        1 << 20,
    )(me, sums, edges, *arrived)
    means = [means[0]] + shift(means[1:])
    own = call(
        functools.partial(self_kernel, groups),
        shape(rows, hid, dtype=f32),
        [SM, HB] + [VM] * (1 + len(rounds)),
        [pltpu.VMEM((width, rows), bf16), pltpu.SemaphoreType.DMA],
        2 * rows * hid * groups * width,
        2 << 20,
    )(me, feature_rows, self_one, *feature_blocks)
    hidden, *projected = call(
        functools.partial(hidden_kernel, groups),
        (shape(rows, hid),) + (shape(classes, rows),) * groups,
        [SM] + [VM] * (3 + groups),
        (),
        2 * rows * hid * groups * width,
        2 << 20,
    )(me, neigh_one, neigh_out.T, own, *means)
    hits = call(
        hits_kernel,
        shape(parts * slots, nodes),
        [VM, SM, SM, HB],
        [pltpu.VMEM((parts, groups, slots), jnp.int32), pltpu.SemaphoreType.DMA],
        0,
        1 << 19,
    )(projected[0], me, part, sources[0])
    projected = projected[:1] + shift(projected[1:])
    mine, mate = call(
        pick_kernel,
        (shape(chips, slots, whole_lanes(classes)),) * 2,
        [SM] + [VM] * (1 + groups),
        (),
        2 * parts * slots * nodes * classes,
        1 << 19,
    )(me, hits, *projected)
    mate = to_mate(mate)
    arrived = to_chips(
        call(pair_kernel, (shape(2, slots, whole_lanes(classes)),) * chips, [VM] * 3, (), 0, 1 << 19)(
            hits, mine, mate
        )
    )
    own, hidden = call(
        own_kernel,
        (shape(classes, rows, dtype=f32), shape(rows, hid)),
        [VM, VM],
        [pltpu.SemaphoreType.DMA],
        2 * rows * hid * classes,
        1 << 20,
        out_specs=(VM, HB),
    )(hidden, self_out.T)
    near = call(
        near_kernel,
        shape(classes, rows, dtype=f32),
        [SM] + [VM] * (3 + groups),
        (),
        2 * rows * nodes * classes,
        1 << 19,
    )(me, own, sums, band, *projected)
    logits = call(
        last_kernel,
        shape(classes, 1, rows, dtype=f32),
        [SM] + [VM] * (3 + chips),
        (),
        2 * rows * parts * slots * classes,
        1 << 19,
    )(me, near, edges, sums, *arrived)
    return hidden[None], logits.transpose(1, 0, 2)


def solution(mesh):
    placed = (
        P("dom", None, "feat"),
        P("dom", None, None, None),
        P("dom", None, None),
        P("dom", None, None, None),
        P("dom", None, None, None),
        P("dom", None, None),
        P("dom", None, None, None),
        P(),
        P(),
        P(),
        P(),
    )
    return jax.shard_map(
        on_device,
        mesh=mesh,
        in_specs=placed,
        out_specs=(P("dom", "feat", None), P("dom", None, "feat")),
        check_vma=False,
    )
```

```python
import functools

import jax
import jax.numpy as jnp
from jax import lax
from jax.experimental import pallas as pl
from jax.experimental.pallas import tpu as pltpu
from jax.sharding import PartitionSpec as P

f32 = jnp.float32
bf16 = jnp.bfloat16
VM = pl.BlockSpec(memory_space=pltpu.VMEM)
SM = pl.BlockSpec(memory_space=pltpu.SMEM)
HB = pl.BlockSpec(memory_space=pltpu.HBM)
LAST = (((1,), (1,)), ((), ()))
FIRST = (((0,), (0,)), ((), ()))
EXTRA = 16


def call(kernel, out_shape, in_specs, scratch=(), flops=0, size=0, limit=4, out_specs=None):
    run = pl.pallas_call(
        kernel,
        out_shape=out_shape,
        in_specs=in_specs,
        out_specs=out_specs or jax.tree.map(lambda _: VM, out_shape),
        scratch_shapes=list(scratch),
        cost_estimate=pl.CostEstimate(flops=flops, bytes_accessed=size, transcendentals=0),
        compiler_params=pltpu.CompilerParams(vmem_limit_bytes=limit << 20),
    )

    def placed(*operands):
        return run(
            *(
                pltpu.with_memory_space_constraint(value, pltpu.HBM) if spec is HB else value
                for value, spec in zip(operands, in_specs)
            )
        )

    return placed


def dot(left, right, dims):
    return lax.dot_general(left, right, dims, preferred_element_type=f32)


def step_of(groups, k):
    return (groups - k) % groups


def whole_lanes(count):
    return -(-count // 128) * 128


def ahead(me, groups, k):
    step = step_of(groups, k)
    return me ^ step if groups & (groups - 1) == 0 else (me + step) % groups


def behind(me, groups, k):
    step = step_of(groups, k)
    return me ^ step if groups & (groups - 1) == 0 else (me + groups - step) % groups


def step_to(a, b, count):
    step = a ^ b if count & (count - 1) == 0 else (b + count - a) % count
    return (count - step) % count


def next_to(a, j, count):
    step = step_of(count, j)
    return a ^ step if count & (count - 1) == 0 else (a + step) % count


def fetch(sems, *pairs):
    copies = [pltpu.make_async_copy(a, b, sems.at[i]) for i, (a, b) in enumerate(pairs)]
    for copy in copies:
        copy.start()
    return copies


def columns_of(values):
    return values.reshape(-1, values.shape[-1]).T


def gather_kernel(
    chunk,
    part_ref,
    sources_hbm,
    features_hbm,
    mine_ref,
    mate_ref,
    blocks_ref,
    sources_ref,
    features_ref,
    order,
    hits,
    sems,
):
    parts, groups, slots = sources_ref.shape
    nodes = hits.shape[1]
    rows = nodes // groups
    width = features_hbm.shape[0]
    chips, chip, core = parts // 2, part_ref[0] // 2, part_ref[0] % 2
    indices, table = fetch(
        sems, (sources_hbm, sources_ref), (features_hbm, features_ref.at[pl.ds(0, width), :])
    )
    if features_ref.shape[0] > width:
        features_ref[width:, :] = jnp.zeros((features_ref.shape[0] - width, nodes), bf16)
    indices.wait()
    lane = lax.broadcasted_iota(jnp.int32, (slots, nodes), 1)

    def step(i, out, other, last):
        for j in range(chunk):
            order[j] = sources_ref[next_to(chip, i * chunk + j, chips) * 2 + (core ^ other)]
        columns = columns_of(order[...])
        for n in range(chunk * groups):
            hits[n * slots : (n + 1) * slots, :] = jnp.where(
                columns[:, n : n + 1] == lane, 1.0, 0.0
            ).astype(bf16)
        if last:
            table.wait()
        picked = dot(hits[...], features_ref[...], LAST).astype(bf16)
        out[pl.ds(i * chunk, chunk)] = picked.reshape(chunk, groups * slots, -1)

    if chips == chunk:
        step(0, mate_ref, 1, True)
        step(0, mine_ref, 0, False)
    else:
        table.wait()
        for other, out in enumerate((mine_ref, mate_ref)):
            lax.fori_loop(0, chips // chunk, lambda i, _: step(i, out, other, False), None)
    for g in range(groups):
        blocks_ref[g] = features_ref[:width, g * rows : (g + 1) * rows]


def local_kernel(
    chunk,
    me_ref,
    part_ref,
    ids_hbm,
    counts_hbm,
    features_hbm,
    tiles_hbm,
    targets_hbm,
    weight_hbm,
    sums_ref,
    edges_ref,
    band_ref,
    ids_ref,
    counts_ref,
    features_ref,
    tiles_ref,
    targets_ref,
    weight_ref,
    bands,
    degree_ref,
    sems,
):
    me = me_ref[0]
    parts, groups, slots = targets_ref.shape
    rows = tiles_ref.shape[1]
    width = features_hbm.shape[0]
    copies = fetch(
        sems,
        (counts_hbm, counts_ref),
        (targets_hbm, targets_ref),
        (weight_hbm, weight_ref),
        (ids_hbm, ids_ref),
        (features_hbm, features_ref.at[pl.ds(0, width), :]),
        (tiles_hbm, tiles_ref),
    )
    extra = features_ref.shape[0] - width
    features_ref[width:, :] = jnp.ones((extra, features_ref.shape[1]), bf16)
    bands[...] = jnp.zeros_like(bands)
    degree_ref[...] = jnp.zeros_like(degree_ref)
    for copy in copies[:3]:
        copy.wait()
    lane = lax.broadcasted_iota(jnp.int32, (slots, rows), 1)
    slot = lax.broadcasted_iota(jnp.int32, (slots, rows), 0)
    chips, chip, core = parts // 2, part_ref[0] // 2, part_ref[0] % 2

    def connect(i, _):
        first = i * chunk
        target = columns_of(targets_ref[pl.ds(first, chunk)])
        weight = columns_of(weight_ref[pl.ds(first, chunk)].astype(f32))
        for g in range(groups):
            degree = jnp.zeros((1, rows), f32)
            for e in range(chunk):
                n, d = e * groups + g, first + e
                at = step_to(d // 2, chip, chips) * 2 + ((d % 2) ^ core)
                hit = (target[:, n : n + 1] == lane) & (slot < counts_ref[g, first + e])
                values = jnp.where(hit, weight[:, n : n + 1], 0.0)
                edges_ref[g, at] = values.astype(bf16)
                degree = degree + jnp.sum(values, axis=0, keepdims=True)
            degree_ref[g] += degree
        return 0

    if parts == chunk:
        connect(0, 0)
    else:
        lax.fori_loop(0, parts // chunk, connect, 0)
    for copy in copies[3:]:
        copy.wait()

    def place(t, _):
        at = pl.multiple_of(ids_ref[1, t] * rows, rows)
        bands[ids_ref[0, t], :, pl.ds(at, rows)] = tiles_ref[t]
        return 0

    lax.fori_loop(0, tiles_ref.shape[0], place, 0, unroll=tiles_ref.shape[0] <= 16)
    for g in range(groups):
        sums_ref[g] = dot(features_ref[...], bands[g], LAST)
        sums_ref[g, width : width + 1, :] += degree_ref[g, :1]
    band_ref[...] = bands[me]


def hits_kernel(after, me_ref, part_ref, sources_hbm, hits_ref, sources_ref, sem):
    del after
    copy = pltpu.make_async_copy(sources_hbm, sources_ref, sem)
    copy.start()
    parts, groups, slots = sources_ref.shape
    chips, chip, core = parts // 2, part_ref[0] // 2, part_ref[0] % 2
    mine = lax.broadcasted_iota(jnp.int32, sources_ref.shape, 1) == me_ref[0]
    copy.wait()
    picks = jnp.sum(jnp.where(mine, sources_ref[...], 0), axis=1).T
    lane = lax.broadcasted_iota(jnp.int32, (slots, hits_ref.shape[1]), 1)
    for d in range(parts):
        to = ((d % 2) ^ core) * chips + step_to(chip, d // 2, chips)
        hits_ref[pl.ds(pl.multiple_of(to * slots, slots), slots), :] = jnp.where(
            picks[:, d : d + 1] == lane, 1.0, 0.0
        ).astype(bf16)


def mean_kernel(me_ref, sums_ref, edges_ref, *rest):
    groups, parts, slots, rows = edges_ref.shape
    arrived, outs = rest[: parts // 2], rest[parts // 2 :]
    width = outs[0].shape[0]
    for k in range(groups):
        group = ahead(me_ref[0], groups, k)
        span = pl.ds(pl.multiple_of(group * slots, slots), slots)
        far = jnp.concatenate([x[:, span, :].reshape(2 * slots, -1) for x in arrived], axis=0)
        far = dot(far, edges_ref[group].reshape(parts * slots, rows), FIRST)
        total = sums_ref[group, :width, :] + far[:width]
        outs[k][...] = (total / sums_ref[group, width : width + 1, :]).astype(bf16)


def self_kernel(weight_ref, blocks_ref, out_ref):
    groups, width, _ = blocks_ref.shape
    total = jnp.zeros(out_ref.shape, f32)
    for g in range(groups):
        weight = weight_ref[g * width : (g + 1) * width, :]
        total = total + dot(blocks_ref[g], weight, FIRST)
    out_ref[...] = total


def hidden_kernel(groups, me_ref, weight_ref, out_weight_ref, own_ref, *rest):
    parts, (hidden_ref, *copies) = rest[:groups], rest[groups:]
    width = parts[0].shape[0]
    total = own_ref[...]
    for k, block in enumerate(parts):
        source = behind(me_ref[0], groups, k)
        span = pl.ds(pl.multiple_of(source * width, width), width)
        total = total + dot(block[...], weight_ref[span, :], FIRST)
    hidden = jnp.maximum(total, 0.0).astype(bf16)
    hidden_ref[...] = hidden
    projected = dot(out_weight_ref[...], hidden, LAST).astype(bf16)
    for copy in copies:
        copy[...] = projected


def own_kernel(hidden_ref, weight_ref, out_ref, hidden_out, sem):
    copy = pltpu.make_async_copy(hidden_ref, hidden_out, sem)
    copy.start()
    out_ref[...] = dot(weight_ref[...], hidden_ref[...], LAST)
    copy.wait()


def pick_kernel(me_ref, hits_ref, *rest):
    projected, (mine_ref, mate_ref) = rest[:-2], rest[-2:]
    groups, rows = len(projected), projected[0].shape[1]
    total = None
    for k in range(groups):
        at = pl.multiple_of(behind(me_ref[0], groups, k) * rows, rows)
        term = dot(hits_ref[:, pl.ds(at, rows)], projected[k][...], LAST)
        total = term if total is None else total + term
    gap = mine_ref.shape[2] - total.shape[1]
    total = jnp.concatenate([total, jnp.zeros((total.shape[0], gap), f32)], axis=1).astype(bf16)
    half = total.shape[0] // 2
    mine_ref[...] = total[:half].reshape(mine_ref.shape)
    mate_ref[...] = total[half:].reshape(mate_ref.shape)


def pair_kernel(after, mine_ref, got_ref, *rest):
    del after
    chips = mine_ref.shape[0]
    held = (len(rest) - chips) // 2
    for j, out in enumerate(rest[held : held + chips]):
        out[0] = mine_ref[j]
        out[1] = got_ref[j]
    for block, out in zip(rest[:held], rest[held + chips :]):
        out[...] = block[...]


def near_kernel(me_ref, own_ref, sums_ref, band_ref, *rest):
    projected, out_ref = rest[:-1], rest[-1]
    groups, rows = len(projected), projected[0].shape[1]
    me, width = me_ref[0], sums_ref.shape[1] - EXTRA
    total = None
    for k in range(groups):
        at = pl.multiple_of(behind(me, groups, k) * rows, rows)
        term = dot(projected[k][...], band_ref[:, pl.ds(at, rows)], LAST)
        total = term if total is None else total + term
    out_ref[...] = own_ref[...] + total / sums_ref[me, width : width + 1, :]


def last_kernel(me_ref, near_ref, edges_ref, sums_ref, *rest):
    arrived, out_ref = rest[:-1], rest[-1]
    groups, parts, slots, rows = edges_ref.shape
    me, width = me_ref[0], sums_ref.shape[1] - EXTRA
    arrived = jnp.concatenate([x[...].reshape(2 * slots, -1) for x in arrived], axis=0)
    far = dot(arrived, edges_ref[me].reshape(parts * slots, rows), FIRST)
    far = far[: near_ref.shape[0]]
    total = near_ref[...] + far / sums_ref[me, width : width + 1, :]
    out_ref[...] = total.reshape(out_ref.shape)


def on_device(
    features,
    tiles,
    tile_ids,
    sources,
    targets,
    counts,
    edge_weight,
    self_one,
    neigh_one,
    self_out,
    neigh_out,
):
    feature_rows, tile_contents = features[0].T, tiles[0]
    groups, parts = lax.axis_size("feat"), lax.axis_size("dom")
    me = lax.axis_index("feat").astype(jnp.int32).reshape(1)
    part = lax.axis_index("dom").astype(jnp.int32).reshape(1)
    width, nodes = feature_rows.shape
    rows, slots = nodes // groups, sources.shape[3]
    hid, classes = self_one.shape[1], self_out.shape[1]
    chips = parts // 2
    chunk = max(1, min(parts, 512 // (groups * slots)))

    def shape(*dims, dtype=bf16):
        return jax.ShapeDtypeStruct(dims, dtype)

    def shift(blocks):
        return [
            lax.ppermute(
                block, "feat", [(i, ahead(i, groups, k)) for i in range(groups)]
            )
            for k, block in enumerate(blocks, 1)
        ]

    def to_mate(value):
        return lax.ppermute(value, "dom", [(d, d ^ 1) for d in range(parts)])

    def to_chips(blocks):
        return [blocks[0]] + [
            lax.ppermute(
                blocks[j],
                "dom",
                [(d, next_to(d // 2, j, chips) * 2 + d % 2) for d in range(parts)],
            )
            for j in range(1, chips)
        ]

    picked = min(chips, chunk)
    lanes = whole_lanes(width)
    mine, mate, feature_blocks = call(
        functools.partial(gather_kernel, picked),
        (shape(chips, groups * slots, lanes),) * 2 + (shape(groups, width, rows),),
        [SM, HB, HB],
        [
            pltpu.VMEM((parts, groups, slots), jnp.int32),
            pltpu.VMEM((lanes, nodes), bf16),
            pltpu.VMEM((picked, groups, slots), jnp.int32),
            pltpu.VMEM((picked * groups * slots, nodes), bf16),
            pltpu.SemaphoreType.DMA((2,)),
        ],
        2 * nodes * nodes * width,
        1 << 20,
    )(part, sources[0], feature_rows)
    mate = to_mate(mate)
    sums, edges, band = call(
        functools.partial(local_kernel, chunk),
        (
            shape(groups, width + EXTRA, rows, dtype=f32),
            shape(groups, parts, slots, rows),
            shape(rows, nodes),
        ),
        [SM, SM] + [HB] * 6,
        [
            pltpu.SMEM(tile_ids.shape[:0:-1], jnp.int32),
            pltpu.SMEM(counts.shape[:0:-1], jnp.int32),
            pltpu.VMEM((width + EXTRA, nodes), bf16),
            pltpu.VMEM(tile_contents.shape, bf16),
            pltpu.VMEM((parts, groups, slots), jnp.int32),
            pltpu.VMEM((parts, groups, slots), bf16),
            pltpu.VMEM((groups, rows, nodes), bf16),
            pltpu.VMEM((groups, 8, rows), f32),
            pltpu.SemaphoreType.DMA((6,)),
        ],
        2 * nodes * nodes * width,
        1 << 20,
        4 if groups <= 4 else 16,
    )(
        me,
        part,
        tile_ids[0].T,
        counts[0].T,
        feature_rows,
        tile_contents,
        targets[0],
        edge_weight[0],
    )
    *paired, feature_blocks = call(
        pair_kernel,
        (shape(2, groups * slots, lanes),) * chips + (shape(groups, width, rows),),
        [VM] * 4,
        (),
        0,
        1 << 20,
    )(band, mine, mate, feature_blocks)
    arrived = to_chips(paired)
    feature_blocks = lax.all_to_all(
        feature_blocks, "feat", split_axis=0, concat_axis=0, tiled=True
    )
    means = call(
        mean_kernel,
        (shape(width, rows),) * groups,
        [SM] + [VM] * (2 + chips),
        (),
        2 * nodes * parts * slots * width,
        1 << 20,
    )(me, sums, edges, *arrived)
    means = [means[0]] + shift(means[1:])
    own = call(
        self_kernel,
        shape(rows, hid, dtype=f32),
        [VM, VM],
        (),
        2 * rows * hid * groups * width,
        2 << 20,
    )(self_one, feature_blocks)
    hidden, *projected = call(
        functools.partial(hidden_kernel, groups),
        (shape(rows, hid),) + (shape(classes, rows),) * groups,
        [SM] + [VM] * (3 + groups),
        (),
        2 * rows * hid * groups * width,
        2 << 20,
    )(me, neigh_one, neigh_out.T, own, *means)
    hits = call(
        hits_kernel,
        shape(parts * slots, nodes),
        [VM, SM, SM, HB],
        [pltpu.VMEM((parts, groups, slots), jnp.int32), pltpu.SemaphoreType.DMA],
        0,
        1 << 19,
    )(projected[0], me, part, sources[0])
    projected = projected[:1] + shift(projected[1:])
    mine, mate = call(
        pick_kernel,
        (shape(chips, slots, whole_lanes(classes)),) * 2,
        [SM] + [VM] * (1 + groups),
        (),
        2 * parts * slots * nodes * classes,
        1 << 19,
    )(me, hits, *projected)
    mate = to_mate(mate)
    arrived = to_chips(
        call(pair_kernel, (shape(2, slots, whole_lanes(classes)),) * chips, [VM] * 3, (), 0, 1 << 19)(
            hits, mine, mate
        )
    )
    own, hidden = call(
        own_kernel,
        (shape(classes, rows, dtype=f32), shape(rows, hid)),
        [VM, VM],
        [pltpu.SemaphoreType.DMA],
        2 * rows * hid * classes,
        1 << 20,
        out_specs=(VM, HB),
    )(hidden, self_out.T)
    near = call(
        near_kernel,
        shape(classes, rows, dtype=f32),
        [SM] + [VM] * (3 + groups),
        (),
        2 * rows * nodes * classes,
        1 << 19,
    )(me, own, sums, band, *projected)
    logits = call(
        last_kernel,
        shape(classes, 1, rows, dtype=f32),
        [SM] + [VM] * (3 + chips),
        (),
        2 * rows * parts * slots * classes,
        1 << 19,
    )(me, near, edges, sums, *arrived)
    return hidden[None], logits.transpose(1, 0, 2)


def solution(mesh):
    placed = (
        P("dom", None, "feat"),
        P("dom", None, None, None),
        P("dom", None, None),
        P("dom", None, None, None),
        P("dom", None, None, None),
        P("dom", None, None),
        P("dom", None, None, None),
        P(),
        P(),
        P(),
        P(),
    )
    return jax.shard_map(
        on_device,
        mesh=mesh,
        in_specs=placed,
        out_specs=(P("dom", "feat", None), P("dom", None, "feat")),
        check_vma=False,
    )
```

```python
import functools

import jax
import jax.numpy as jnp
from jax import lax
from jax.experimental import pallas as pl
from jax.experimental.pallas import tpu as pltpu
from jax.sharding import PartitionSpec as P

f32 = jnp.float32
bf16 = jnp.bfloat16
VM = pl.BlockSpec(memory_space=pltpu.VMEM)
SM = pl.BlockSpec(memory_space=pltpu.SMEM)
HB = pl.BlockSpec(memory_space=pltpu.HBM)
LAST = (((1,), (1,)), ((), ()))
FIRST = (((0,), (0,)), ((), ()))
EXTRA = 16


def call(kernel, out_shape, in_specs, scratch=(), flops=0, size=0, limit=4, out_specs=None):
    run = pl.pallas_call(
        kernel,
        out_shape=out_shape,
        in_specs=in_specs,
        out_specs=out_specs or jax.tree.map(lambda _: VM, out_shape),
        scratch_shapes=list(scratch),
        cost_estimate=pl.CostEstimate(flops=flops, bytes_accessed=size, transcendentals=0),
        compiler_params=pltpu.CompilerParams(vmem_limit_bytes=limit << 20),
    )

    def placed(*operands):
        return run(
            *(
                pltpu.with_memory_space_constraint(value, pltpu.HBM) if spec is HB else value
                for value, spec in zip(operands, in_specs)
            )
        )

    return placed


def dot(left, right, dims):
    return lax.dot_general(left, right, dims, preferred_element_type=f32)


def step_of(groups, k, near=False):
    if near and k:
        return 1 if k == 1 else groups - k + 1
    return (groups - k) % groups


def whole_lanes(count):
    return -(-count // 128) * 128


def ahead(me, groups, k, near=False):
    step = step_of(groups, k, near)
    return me ^ step if groups & (groups - 1) == 0 else (me + step) % groups


def behind(me, groups, k, near=False):
    step = step_of(groups, k, near)
    return me ^ step if groups & (groups - 1) == 0 else (me + groups - step) % groups


def step_to(a, b, count):
    step = a ^ b if count & (count - 1) == 0 else (b + count - a) % count
    return (count - step) % count


def next_to(a, j, count):
    step = step_of(count, j)
    return a ^ step if count & (count - 1) == 0 else (a + step) % count


def fetch(sems, *pairs):
    copies = [pltpu.make_async_copy(a, b, sems.at[i]) for i, (a, b) in enumerate(pairs)]
    for copy in copies:
        copy.start()
    return copies


def columns_of(values):
    return values.reshape(-1, values.shape[-1]).T


def gather_kernel(chunk, me_ref, part_ref, sources_hbm, features_hbm, mine_ref, mate_ref, *rest):
    blocks, (sources_ref, features_ref, order, hits, sems) = rest[:-5], rest[-5:]
    parts, groups, slots = sources_ref.shape
    nodes = hits.shape[1]
    rows = nodes // groups
    width = features_hbm.shape[0]
    chips, chip, core = parts // 2, part_ref[0] // 2, part_ref[0] % 2
    indices, table = fetch(
        sems, (sources_hbm, sources_ref), (features_hbm, features_ref.at[pl.ds(0, width), :])
    )
    if features_ref.shape[0] > width:
        features_ref[width:, :] = jnp.zeros((features_ref.shape[0] - width, nodes), bf16)
    indices.wait()
    lane = lax.broadcasted_iota(jnp.int32, (slots, nodes), 1)

    def step(i, out, other, last):
        for j in range(chunk):
            order[j] = sources_ref[next_to(chip, i * chunk + j, chips) * 2 + (core ^ other)]
        columns = columns_of(order[...])
        for n in range(chunk * groups):
            hits[n * slots : (n + 1) * slots, :] = jnp.where(
                columns[:, n : n + 1] == lane, 1.0, 0.0
            ).astype(bf16)
        if last:
            table.wait()
        picked = dot(hits[...], features_ref[...], LAST).astype(bf16)
        out[pl.ds(i * chunk, chunk)] = picked.reshape(chunk, groups * slots, -1)

    if chips == chunk:
        step(0, mate_ref, 1, True)
        step(0, mine_ref, 0, False)
    else:
        table.wait()
        for other, out in enumerate((mine_ref, mate_ref)):
            lax.fori_loop(0, chips // chunk, lambda i, _: step(i, out, other, False), None)
    for k in range(1, groups):
        group = ahead(me_ref[0], groups, k, True)
        blocks[k - 1][...] = features_ref[:width, pl.ds(pl.multiple_of(group * rows, rows), rows)]


def local_kernel(
    chunk,
    me_ref,
    part_ref,
    ids_hbm,
    counts_hbm,
    features_hbm,
    tiles_hbm,
    targets_hbm,
    weight_hbm,
    sums_ref,
    edges_ref,
    band_ref,
    ids_ref,
    counts_ref,
    features_ref,
    tiles_ref,
    targets_ref,
    weight_ref,
    bands,
    sems,
):
    me = me_ref[0]
    parts, groups, slots = targets_ref.shape
    rows = tiles_ref.shape[1]
    width = features_hbm.shape[0]
    copies = fetch(
        sems,
        (ids_hbm, ids_ref),
        (counts_hbm, counts_ref),
        (features_hbm, features_ref.at[pl.ds(0, width), :]),
        (tiles_hbm, tiles_ref),
        (targets_hbm, targets_ref),
        (weight_hbm, weight_ref),
    )
    extra = features_ref.shape[0] - width
    features_ref[width:, :] = jnp.ones((extra, features_ref.shape[1]), bf16)
    bands[...] = jnp.zeros_like(bands)
    for copy in copies:
        copy.wait()

    def place(t, _):
        at = pl.multiple_of(ids_ref[1, t] * rows, rows)
        bands[ids_ref[0, t], :, pl.ds(at, rows)] = tiles_ref[t]
        return 0

    lax.fori_loop(0, tiles_ref.shape[0], place, 0, unroll=tiles_ref.shape[0] <= 16)
    for g in range(groups):
        sums_ref[g] = dot(features_ref[...], bands[g], LAST)
    band_ref[...] = bands[me]
    lane = lax.broadcasted_iota(jnp.int32, (slots, rows), 1)
    slot = lax.broadcasted_iota(jnp.int32, (slots, rows), 0)
    chips, chip, core = parts // 2, part_ref[0] // 2, part_ref[0] % 2

    def connect(i, _):
        first = i * chunk
        target = columns_of(targets_ref[pl.ds(first, chunk)])
        weight = columns_of(weight_ref[pl.ds(first, chunk)].astype(f32))
        for g in range(groups):
            degree = jnp.zeros((1, rows), f32)
            for e in range(chunk):
                n, d = e * groups + g, first + e
                at = step_to(d // 2, chip, chips) * 2 + ((d % 2) ^ core)
                hit = (target[:, n : n + 1] == lane) & (slot < counts_ref[g, first + e])
                values = jnp.where(hit, weight[:, n : n + 1], 0.0)
                edges_ref[g, at] = values.astype(bf16)
                degree = degree + jnp.sum(values, axis=0, keepdims=True)
            sums_ref[g, width : width + 1, :] += degree
        return 0

    if parts == chunk:
        connect(0, 0)
    else:
        lax.fori_loop(0, parts // chunk, connect, 0)


def hits_kernel(after, me_ref, part_ref, sources_hbm, hits_ref, sources_ref, sem):
    del after
    copy = pltpu.make_async_copy(sources_hbm, sources_ref, sem)
    copy.start()
    parts, groups, slots = sources_ref.shape
    chips, chip, core = parts // 2, part_ref[0] // 2, part_ref[0] % 2
    mine = lax.broadcasted_iota(jnp.int32, sources_ref.shape, 1) == me_ref[0]
    copy.wait()
    picks = jnp.sum(jnp.where(mine, sources_ref[...], 0), axis=1).T
    lane = lax.broadcasted_iota(jnp.int32, (slots, hits_ref.shape[1]), 1)
    for d in range(parts):
        to = ((d % 2) ^ core) * chips + step_to(chip, d // 2, chips)
        hits_ref[pl.ds(pl.multiple_of(to * slots, slots), slots), :] = jnp.where(
            picks[:, d : d + 1] == lane, 1.0, 0.0
        ).astype(bf16)


def mean_kernel(me_ref, sums_ref, edges_ref, *rest):
    groups, parts, slots, rows = edges_ref.shape
    arrived, outs = rest[: parts // 2], rest[parts // 2 :]
    width = outs[0].shape[0]
    for k in range(groups):
        group = ahead(me_ref[0], groups, k)
        span = pl.ds(pl.multiple_of(group * slots, slots), slots)
        far = jnp.concatenate([x[:, span, :].reshape(2 * slots, -1) for x in arrived], axis=0)
        far = dot(far, edges_ref[group].reshape(parts * slots, rows), FIRST)
        total = sums_ref[group, :width, :] + far[:width]
        outs[k][...] = (total / sums_ref[group, width : width + 1, :]).astype(bf16)


def rows_from(me, groups, k, width, near=False):
    return pl.ds(pl.multiple_of(behind(me, groups, k, near) * width, width), width)


def self_kernel(me_ref, features_hbm, weight_ref, *rest):
    blocks, (out_ref, own_ref, sem) = rest[:-3], rest[-3:]
    groups, (width, rows) = len(blocks) + 1, own_ref.shape
    me = me_ref[0]
    own = pltpu.make_async_copy(
        features_hbm.at[:, pl.ds(pl.multiple_of(me * rows, rows), rows)], own_ref, sem
    )
    own.start()
    total = jnp.zeros(out_ref.shape, f32)
    for k, block in enumerate(blocks, 1):
        span = rows_from(me, groups, k, width, True)
        total = total + dot(block[...], weight_ref[span, :], FIRST)
    own.wait()
    span = pl.ds(pl.multiple_of(me * width, width), width)
    out_ref[...] = total + dot(own_ref[...], weight_ref[span, :], FIRST)


def hidden_kernel(me_ref, weight_ref, out_weight_ref, own_ref, *rest):
    groups = (len(rest) - 1) // 2
    parts, (hidden_ref, *copies) = rest[:groups], rest[groups:]
    width = parts[0].shape[0]
    total = own_ref[...]
    for k, block in enumerate(parts):
        span = rows_from(me_ref[0], groups, k, width)
        total = total + dot(block[...], weight_ref[span, :], FIRST)
    hidden = jnp.maximum(total, 0.0).astype(bf16)
    hidden_ref[...] = hidden
    projected = dot(out_weight_ref[...], hidden, LAST).astype(bf16)
    for copy in copies:
        copy[...] = projected


def own_kernel(hidden_ref, weight_ref, out_ref, hidden_out, sem):
    copy = pltpu.make_async_copy(hidden_ref, hidden_out, sem)
    copy.start()
    out_ref[...] = dot(weight_ref[...], hidden_ref[...], LAST)
    copy.wait()


def pick_kernel(me_ref, hits_ref, *rest):
    projected, (mine_ref, mate_ref) = rest[:-2], rest[-2:]
    groups, rows = len(projected), projected[0].shape[1]
    total = None
    for k in range(groups):
        at = pl.multiple_of(behind(me_ref[0], groups, k) * rows, rows)
        term = dot(hits_ref[:, pl.ds(at, rows)], projected[k][...], LAST)
        total = term if total is None else total + term
    gap = mine_ref.shape[2] - total.shape[1]
    total = jnp.concatenate([total, jnp.zeros((total.shape[0], gap), f32)], axis=1).astype(bf16)
    half = total.shape[0] // 2
    mine_ref[...] = total[:half].reshape(mine_ref.shape)
    mate_ref[...] = total[half:].reshape(mate_ref.shape)


def pair_kernel(after, mine_ref, got_ref, *rest):
    del after
    chips = mine_ref.shape[0]
    held = (len(rest) - chips) // 2
    for j, out in enumerate(rest[held : held + chips]):
        out[0] = mine_ref[j]
        out[1] = got_ref[j]
    for block, out in zip(rest[:held], rest[held + chips :]):
        out[...] = block[...]


def near_kernel(me_ref, own_ref, sums_ref, band_ref, *rest):
    projected, out_ref = rest[:-1], rest[-1]
    groups, rows = len(projected), projected[0].shape[1]
    me, width = me_ref[0], sums_ref.shape[1] - EXTRA
    total = None
    for k in range(groups):
        at = pl.multiple_of(behind(me, groups, k) * rows, rows)
        term = dot(projected[k][...], band_ref[:, pl.ds(at, rows)], LAST)
        total = term if total is None else total + term
    out_ref[...] = own_ref[...] + total / sums_ref[me, width : width + 1, :]


def last_kernel(me_ref, near_ref, edges_ref, sums_ref, *rest):
    arrived, out_ref = rest[:-1], rest[-1]
    groups, parts, slots, rows = edges_ref.shape
    me, width = me_ref[0], sums_ref.shape[1] - EXTRA
    arrived = jnp.concatenate([x[...].reshape(2 * slots, -1) for x in arrived], axis=0)
    far = dot(arrived, edges_ref[me].reshape(parts * slots, rows), FIRST)
    far = far[: near_ref.shape[0]]
    total = near_ref[...] + far / sums_ref[me, width : width + 1, :]
    out_ref[...] = total.reshape(out_ref.shape)


def on_device(
    features,
    tiles,
    tile_ids,
    sources,
    targets,
    counts,
    edge_weight,
    self_one,
    neigh_one,
    self_out,
    neigh_out,
):
    feature_rows, tile_contents = features[0].T, tiles[0]
    groups, parts = lax.axis_size("feat"), lax.axis_size("dom")
    me = lax.axis_index("feat").astype(jnp.int32).reshape(1)
    part = lax.axis_index("dom").astype(jnp.int32).reshape(1)
    width, nodes = feature_rows.shape
    rows, slots = nodes // groups, sources.shape[3]
    hid, classes = self_one.shape[1], self_out.shape[1]
    chips = parts // 2
    chunk = max(1, min(parts, 512 // (groups * slots)))

    def shape(*dims, dtype=bf16):
        return jax.ShapeDtypeStruct(dims, dtype)

    def shift(blocks, near=False):
        return [
            lax.ppermute(block, "feat", [(i, ahead(i, groups, k, near)) for i in range(groups)])
            for k, block in enumerate(blocks, 1)
        ]

    def to_mate(value):
        return lax.ppermute(value, "dom", [(d, d ^ 1) for d in range(parts)])

    def to_chips(blocks):
        return [blocks[0]] + [
            lax.ppermute(
                blocks[j],
                "dom",
                [(d, next_to(d // 2, j, chips) * 2 + d % 2) for d in range(parts)],
            )
            for j in range(1, chips)
        ]

    picked = min(chips, chunk)
    lanes = whole_lanes(width)
    mine, mate, *feature_blocks = call(
        functools.partial(gather_kernel, picked),
        (shape(chips, groups * slots, lanes),) * 2 + (shape(width, rows),) * (groups - 1),
        [SM, SM, HB, HB],
        [
            pltpu.VMEM((parts, groups, slots), jnp.int32),
            pltpu.VMEM((lanes, nodes), bf16),
            pltpu.VMEM((picked, groups, slots), jnp.int32),
            pltpu.VMEM((picked * groups * slots, nodes), bf16),
            pltpu.SemaphoreType.DMA((2,)),
        ],
        2 * nodes * nodes * width,
        1 << 20,
    )(me, part, sources[0], feature_rows)
    mate = to_mate(mate)
    sums, edges, band = call(
        functools.partial(local_kernel, chunk),
        (
            shape(groups, width + EXTRA, rows, dtype=f32),
            shape(groups, parts, slots, rows),
            shape(rows, nodes),
        ),
        [SM, SM] + [HB] * 6,
        [
            pltpu.SMEM(tile_ids.shape[:0:-1], jnp.int32),
            pltpu.SMEM(counts.shape[:0:-1], jnp.int32),
            pltpu.VMEM((width + EXTRA, nodes), bf16),
            pltpu.VMEM(tile_contents.shape, bf16),
            pltpu.VMEM((parts, groups, slots), jnp.int32),
            pltpu.VMEM((parts, groups, slots), bf16),
            pltpu.VMEM((groups, rows, nodes), bf16),
            pltpu.SemaphoreType.DMA((6,)),
        ],
        2 * nodes * nodes * width,
        1 << 20,
        4 if groups <= 4 else 16,
    )(
        me,
        part,
        tile_ids[0].T,
        counts[0].T,
        feature_rows,
        tile_contents,
        targets[0],
        edge_weight[0],
    )
    paired = call(
        pair_kernel,
        (shape(2, groups * slots, lanes),) * chips + (shape(width, rows),) * (groups - 1),
        [VM] * (2 + groups),
        (),
        0,
        1 << 20,
    )(band, mine, mate, *feature_blocks)
    arrived = to_chips(paired[:chips])
    feature_blocks = shift(paired[chips:], near=True)
    means = call(
        mean_kernel,
        (shape(width, rows),) * groups,
        [SM] + [VM] * (2 + chips),
        (),
        2 * nodes * parts * slots * width,
        1 << 20,
    )(me, sums, edges, *arrived)
    means = [means[0]] + shift(means[1:])
    own = call(
        self_kernel,
        shape(rows, hid, dtype=f32),
        [SM, HB] + [VM] * groups,
        [pltpu.VMEM((width, rows), bf16), pltpu.SemaphoreType.DMA],
        2 * rows * hid * groups * width,
        2 << 20,
    )(me, feature_rows, self_one, *feature_blocks)
    hidden, *projected = call(
        hidden_kernel,
        (shape(rows, hid),) + (shape(classes, rows),) * groups,
        [SM] + [VM] * (3 + groups),
        (),
        2 * rows * hid * groups * width,
        2 << 20,
    )(me, neigh_one, neigh_out.T, own, *means)
    hits = call(
        hits_kernel,
        shape(parts * slots, nodes),
        [VM, SM, SM, HB],
        [pltpu.VMEM((parts, groups, slots), jnp.int32), pltpu.SemaphoreType.DMA],
        0,
        1 << 19,
    )(projected[0], me, part, sources[0])
    projected = projected[:1] + shift(projected[1:])
    mine, mate = call(
        pick_kernel,
        (shape(chips, slots, whole_lanes(classes)),) * 2,
        [SM] + [VM] * (1 + groups),
        (),
        2 * parts * slots * nodes * classes,
        1 << 19,
    )(me, hits, *projected)
    mate = to_mate(mate)
    arrived = to_chips(
        call(pair_kernel, (shape(2, slots, whole_lanes(classes)),) * chips, [VM] * 3, (), 0, 1 << 19)(
            hits, mine, mate
        )
    )
    own, hidden = call(
        own_kernel,
        (shape(classes, rows, dtype=f32), shape(rows, hid)),
        [VM, VM],
        [pltpu.SemaphoreType.DMA],
        2 * rows * hid * classes,
        1 << 20,
        out_specs=(VM, HB),
    )(hidden, self_out.T)
    near = call(
        near_kernel,
        shape(classes, rows, dtype=f32),
        [SM] + [VM] * (3 + groups),
        (),
        2 * rows * nodes * classes,
        1 << 19,
    )(me, own, sums, band, *projected)
    logits = call(
        last_kernel,
        shape(classes, 1, rows, dtype=f32),
        [SM] + [VM] * (3 + chips),
        (),
        2 * rows * parts * slots * classes,
        1 << 19,
    )(me, near, edges, sums, *arrived)
    return hidden[None], logits.transpose(1, 0, 2)


def solution(mesh):
    placed = (
        P("dom", None, "feat"),
        P("dom", None, None, None),
        P("dom", None, None),
        P("dom", None, None, None),
        P("dom", None, None, None),
        P("dom", None, None),
        P("dom", None, None, None),
        P(),
        P(),
        P(),
        P(),
    )
    return jax.shard_map(
        on_device,
        mesh=mesh,
        in_specs=placed,
        out_specs=(P("dom", "feat", None), P("dom", None, "feat")),
        check_vma=False,
    )
```

```python
import functools

import jax
import jax.numpy as jnp
from jax import lax
from jax.experimental import pallas as pl
from jax.experimental.pallas import tpu as pltpu
from jax.sharding import PartitionSpec as P

f32 = jnp.float32
bf16 = jnp.bfloat16
VM = pl.BlockSpec(memory_space=pltpu.VMEM)
SM = pl.BlockSpec(memory_space=pltpu.SMEM)
HB = pl.BlockSpec(memory_space=pltpu.HBM)
LAST = (((1,), (1,)), ((), ()))
FIRST = (((0,), (0,)), ((), ()))
EXTRA = 16


def call(kernel, out_shape, in_specs, scratch=(), flops=0, size=0, limit=4, out_specs=None):
    run = pl.pallas_call(
        kernel,
        out_shape=out_shape,
        in_specs=in_specs,
        out_specs=out_specs or jax.tree.map(lambda _: VM, out_shape),
        scratch_shapes=list(scratch),
        cost_estimate=pl.CostEstimate(flops=flops, bytes_accessed=size, transcendentals=0),
        compiler_params=pltpu.CompilerParams(vmem_limit_bytes=limit << 20),
    )

    def placed(*operands):
        return run(
            *(
                pltpu.with_memory_space_constraint(value, pltpu.HBM) if spec is HB else value
                for value, spec in zip(operands, in_specs)
            )
        )

    return placed


def dot(left, right, dims):
    return lax.dot_general(left, right, dims, preferred_element_type=f32)


def step_of(groups, k, near=False):
    if near and groups > 2 and k in (1, 2):
        return groups - 3 + k
    return (groups - k) % groups


def whole_lanes(count):
    return -(-count // 128) * 128


def ahead(me, groups, k, near=False):
    step = step_of(groups, k, near)
    return me ^ step if groups & (groups - 1) == 0 else (me + step) % groups


def behind(me, groups, k, near=False):
    step = step_of(groups, k, near)
    return me ^ step if groups & (groups - 1) == 0 else (me + groups - step) % groups


def step_to(a, b, count):
    step = a ^ b if count & (count - 1) == 0 else (b + count - a) % count
    return (count - step) % count


def next_to(a, j, count):
    step = step_of(count, j)
    return a ^ step if count & (count - 1) == 0 else (a + step) % count


def fetch(sems, *pairs):
    copies = [pltpu.make_async_copy(a, b, sems.at[i]) for i, (a, b) in enumerate(pairs)]
    for copy in copies:
        copy.start()
    return copies


def columns_of(values):
    return values.reshape(-1, values.shape[-1]).T


def gather_kernel(chunk, me_ref, part_ref, sources_hbm, features_hbm, mine_ref, mate_ref, *rest):
    blocks, (sources_ref, features_ref, order, hits, sems) = rest[:-5], rest[-5:]
    parts, groups, slots = sources_ref.shape
    nodes = hits.shape[1]
    rows = nodes // groups
    width = features_hbm.shape[0]
    chips, chip, core = parts // 2, part_ref[0] // 2, part_ref[0] % 2
    indices, table = fetch(
        sems, (sources_hbm, sources_ref), (features_hbm, features_ref.at[pl.ds(0, width), :])
    )
    if features_ref.shape[0] > width:
        features_ref[width:, :] = jnp.zeros((features_ref.shape[0] - width, nodes), bf16)
    indices.wait()
    lane = lax.broadcasted_iota(jnp.int32, (slots, nodes), 1)

    def step(i, out, other, last):
        for j in range(chunk):
            order[j] = sources_ref[next_to(chip, i * chunk + j, chips) * 2 + (core ^ other)]
        columns = columns_of(order[...])
        for n in range(chunk * groups):
            hits[n * slots : (n + 1) * slots, :] = jnp.where(
                columns[:, n : n + 1] == lane, 1.0, 0.0
            ).astype(bf16)
        if last:
            table.wait()
        picked = dot(hits[...], features_ref[...], LAST).astype(bf16)
        out[pl.ds(i * chunk, chunk)] = picked.reshape(chunk, groups * slots, -1)

    if chips == chunk:
        step(0, mate_ref, 1, True)
        step(0, mine_ref, 0, False)
    else:
        table.wait()
        for other, out in enumerate((mine_ref, mate_ref)):
            lax.fori_loop(0, chips // chunk, lambda i, _: step(i, out, other, False), None)
    for k in range(1, groups):
        group = ahead(me_ref[0], groups, k, True)
        blocks[k - 1][...] = features_ref[:width, pl.ds(pl.multiple_of(group * rows, rows), rows)]


def local_kernel(
    chunk,
    me_ref,
    part_ref,
    ids_hbm,
    counts_hbm,
    features_hbm,
    tiles_hbm,
    targets_hbm,
    weight_hbm,
    sums_ref,
    edges_ref,
    band_ref,
    ids_ref,
    counts_ref,
    features_ref,
    tiles_ref,
    targets_ref,
    weight_ref,
    bands,
    sems,
):
    me = me_ref[0]
    parts, groups, slots = targets_ref.shape
    rows = tiles_ref.shape[1]
    width = features_hbm.shape[0]
    copies = fetch(
        sems,
        (ids_hbm, ids_ref),
        (counts_hbm, counts_ref),
        (features_hbm, features_ref.at[pl.ds(0, width), :]),
        (tiles_hbm, tiles_ref),
        (targets_hbm, targets_ref),
        (weight_hbm, weight_ref),
    )
    extra = features_ref.shape[0] - width
    features_ref[width:, :] = jnp.ones((extra, features_ref.shape[1]), bf16)
    bands[...] = jnp.zeros_like(bands)
    for copy in copies:
        copy.wait()

    def place(t, _):
        at = pl.multiple_of(ids_ref[1, t] * rows, rows)
        bands[ids_ref[0, t], :, pl.ds(at, rows)] = tiles_ref[t]
        return 0

    lax.fori_loop(0, tiles_ref.shape[0], place, 0, unroll=tiles_ref.shape[0] <= 16)
    for g in range(groups):
        sums_ref[g] = dot(features_ref[...], bands[g], LAST)
    band_ref[...] = bands[me]
    lane = lax.broadcasted_iota(jnp.int32, (slots, rows), 1)
    slot = lax.broadcasted_iota(jnp.int32, (slots, rows), 0)
    chips, chip, core = parts // 2, part_ref[0] // 2, part_ref[0] % 2

    def connect(i, _):
        first = i * chunk
        target = columns_of(targets_ref[pl.ds(first, chunk)])
        weight = columns_of(weight_ref[pl.ds(first, chunk)].astype(f32))
        for g in range(groups):
            degree = jnp.zeros((1, rows), f32)
            for e in range(chunk):
                n, d = e * groups + g, first + e
                at = step_to(d // 2, chip, chips) * 2 + ((d % 2) ^ core)
                hit = (target[:, n : n + 1] == lane) & (slot < counts_ref[g, first + e])
                values = jnp.where(hit, weight[:, n : n + 1], 0.0)
                edges_ref[g, at] = values.astype(bf16)
                degree = degree + jnp.sum(values, axis=0, keepdims=True)
            sums_ref[g, width : width + 1, :] += degree
        return 0

    if parts == chunk:
        connect(0, 0)
    else:
        lax.fori_loop(0, parts // chunk, connect, 0)


def hits_kernel(after, me_ref, part_ref, sources_hbm, hits_ref, sources_ref, sem):
    del after
    copy = pltpu.make_async_copy(sources_hbm, sources_ref, sem)
    copy.start()
    parts, groups, slots = sources_ref.shape
    chips, chip, core = parts // 2, part_ref[0] // 2, part_ref[0] % 2
    mine = lax.broadcasted_iota(jnp.int32, sources_ref.shape, 1) == me_ref[0]
    copy.wait()
    picks = jnp.sum(jnp.where(mine, sources_ref[...], 0), axis=1).T
    lane = lax.broadcasted_iota(jnp.int32, (slots, hits_ref.shape[1]), 1)
    for d in range(parts):
        to = ((d % 2) ^ core) * chips + step_to(chip, d // 2, chips)
        hits_ref[pl.ds(pl.multiple_of(to * slots, slots), slots), :] = jnp.where(
            picks[:, d : d + 1] == lane, 1.0, 0.0
        ).astype(bf16)


def mean_kernel(me_ref, sums_ref, edges_ref, *rest):
    groups, parts, slots, rows = edges_ref.shape
    arrived, outs = rest[: parts // 2], rest[parts // 2 :]
    width = outs[0].shape[0]
    for k in range(groups):
        group = ahead(me_ref[0], groups, k)
        span = pl.ds(pl.multiple_of(group * slots, slots), slots)
        far = jnp.concatenate([x[:, span, :].reshape(2 * slots, -1) for x in arrived], axis=0)
        far = dot(far, edges_ref[group].reshape(parts * slots, rows), FIRST)
        total = sums_ref[group, :width, :] + far[:width]
        outs[k][...] = (total / sums_ref[group, width : width + 1, :]).astype(bf16)


def rows_from(me, groups, k, width, near=False):
    return pl.ds(pl.multiple_of(behind(me, groups, k, near) * width, width), width)


def self_kernel(me_ref, features_hbm, weight_ref, *rest):
    blocks, (out_ref, own_ref, sem) = rest[:-3], rest[-3:]
    groups, (width, rows) = len(blocks) + 1, own_ref.shape
    me = me_ref[0]
    own = pltpu.make_async_copy(
        features_hbm.at[:, pl.ds(pl.multiple_of(me * rows, rows), rows)], own_ref, sem
    )
    own.start()
    total = jnp.zeros(out_ref.shape, f32)
    for k, block in enumerate(blocks, 1):
        span = rows_from(me, groups, k, width, True)
        total = total + dot(block[...], weight_ref[span, :], FIRST)
    own.wait()
    span = pl.ds(pl.multiple_of(me * width, width), width)
    out_ref[...] = total + dot(own_ref[...], weight_ref[span, :], FIRST)


def hidden_kernel(me_ref, weight_ref, out_weight_ref, own_ref, *rest):
    groups = (len(rest) - 1) // 2
    parts, (hidden_ref, *copies) = rest[:groups], rest[groups:]
    width = parts[0].shape[0]
    total = own_ref[...]
    for k, block in enumerate(parts):
        span = rows_from(me_ref[0], groups, k, width)
        total = total + dot(block[...], weight_ref[span, :], FIRST)
    hidden = jnp.maximum(total, 0.0).astype(bf16)
    hidden_ref[...] = hidden
    projected = dot(out_weight_ref[...], hidden, LAST).astype(bf16)
    for copy in copies:
        copy[...] = projected


def own_kernel(hidden_ref, weight_ref, out_ref, hidden_out, sem):
    copy = pltpu.make_async_copy(hidden_ref, hidden_out, sem)
    copy.start()
    out_ref[...] = dot(weight_ref[...], hidden_ref[...], LAST)
    copy.wait()


def pick_kernel(me_ref, hits_ref, *rest):
    projected, (mine_ref, mate_ref) = rest[:-2], rest[-2:]
    groups, rows = len(projected), projected[0].shape[1]
    total = None
    for k in range(groups):
        at = pl.multiple_of(behind(me_ref[0], groups, k) * rows, rows)
        term = dot(hits_ref[:, pl.ds(at, rows)], projected[k][...], LAST)
        total = term if total is None else total + term
    gap = mine_ref.shape[2] - total.shape[1]
    total = jnp.concatenate([total, jnp.zeros((total.shape[0], gap), f32)], axis=1).astype(bf16)
    half = total.shape[0] // 2
    mine_ref[...] = total[:half].reshape(mine_ref.shape)
    mate_ref[...] = total[half:].reshape(mate_ref.shape)


def pair_kernel(after, mine_ref, got_ref, *rest):
    del after
    chips = mine_ref.shape[0]
    held = (len(rest) - chips) // 2
    for j, out in enumerate(rest[held : held + chips]):
        out[0] = mine_ref[j]
        out[1] = got_ref[j]
    for block, out in zip(rest[:held], rest[held + chips :]):
        out[...] = block[...]


def near_kernel(me_ref, own_ref, sums_ref, band_ref, *rest):
    projected, out_ref = rest[:-1], rest[-1]
    groups, rows = len(projected), projected[0].shape[1]
    me, width = me_ref[0], sums_ref.shape[1] - EXTRA
    total = None
    for k in range(groups):
        at = pl.multiple_of(behind(me, groups, k) * rows, rows)
        term = dot(projected[k][...], band_ref[:, pl.ds(at, rows)], LAST)
        total = term if total is None else total + term
    out_ref[...] = own_ref[...] + total / sums_ref[me, width : width + 1, :]


def last_kernel(me_ref, near_ref, edges_ref, sums_ref, *rest):
    arrived, out_ref = rest[:-1], rest[-1]
    groups, parts, slots, rows = edges_ref.shape
    me, width = me_ref[0], sums_ref.shape[1] - EXTRA
    arrived = jnp.concatenate([x[...].reshape(2 * slots, -1) for x in arrived], axis=0)
    far = dot(arrived, edges_ref[me].reshape(parts * slots, rows), FIRST)
    far = far[: near_ref.shape[0]]
    total = near_ref[...] + far / sums_ref[me, width : width + 1, :]
    out_ref[...] = total.reshape(out_ref.shape)


def on_device(
    features,
    tiles,
    tile_ids,
    sources,
    targets,
    counts,
    edge_weight,
    self_one,
    neigh_one,
    self_out,
    neigh_out,
):
    feature_rows, tile_contents = features[0].T, tiles[0]
    groups, parts = lax.axis_size("feat"), lax.axis_size("dom")
    me = lax.axis_index("feat").astype(jnp.int32).reshape(1)
    part = lax.axis_index("dom").astype(jnp.int32).reshape(1)
    width, nodes = feature_rows.shape
    rows, slots = nodes // groups, sources.shape[3]
    hid, classes = self_one.shape[1], self_out.shape[1]
    chips = parts // 2
    chunk = max(1, min(parts, 512 // (groups * slots)))

    def shape(*dims, dtype=bf16):
        return jax.ShapeDtypeStruct(dims, dtype)

    def shift(blocks, near=False):
        return [
            lax.ppermute(block, "feat", [(i, ahead(i, groups, k, near)) for i in range(groups)])
            for k, block in enumerate(blocks, 1)
        ]

    def to_mate(value):
        return lax.ppermute(value, "dom", [(d, d ^ 1) for d in range(parts)])

    def to_chips(blocks):
        return [blocks[0]] + [
            lax.ppermute(
                blocks[j],
                "dom",
                [(d, next_to(d // 2, j, chips) * 2 + d % 2) for d in range(parts)],
            )
            for j in range(1, chips)
        ]

    picked = min(chips, chunk)
    lanes = whole_lanes(width)
    mine, mate, *feature_blocks = call(
        functools.partial(gather_kernel, picked),
        (shape(chips, groups * slots, lanes),) * 2 + (shape(width, rows),) * (groups - 1),
        [SM, SM, HB, HB],
        [
            pltpu.VMEM((parts, groups, slots), jnp.int32),
            pltpu.VMEM((lanes, nodes), bf16),
            pltpu.VMEM((picked, groups, slots), jnp.int32),
            pltpu.VMEM((picked * groups * slots, nodes), bf16),
            pltpu.SemaphoreType.DMA((2,)),
        ],
        2 * nodes * nodes * width,
        1 << 20,
    )(me, part, sources[0], feature_rows)
    mate = to_mate(mate)
    sums, edges, band = call(
        functools.partial(local_kernel, chunk),
        (
            shape(groups, width + EXTRA, rows, dtype=f32),
            shape(groups, parts, slots, rows),
            shape(rows, nodes),
        ),
        [SM, SM] + [HB] * 6,
        [
            pltpu.SMEM(tile_ids.shape[:0:-1], jnp.int32),
            pltpu.SMEM(counts.shape[:0:-1], jnp.int32),
            pltpu.VMEM((width + EXTRA, nodes), bf16),
            pltpu.VMEM(tile_contents.shape, bf16),
            pltpu.VMEM((parts, groups, slots), jnp.int32),
            pltpu.VMEM((parts, groups, slots), bf16),
            pltpu.VMEM((groups, rows, nodes), bf16),
            pltpu.SemaphoreType.DMA((6,)),
        ],
        2 * nodes * nodes * width,
        1 << 20,
        4 if groups <= 4 else 16,
    )(
        me,
        part,
        tile_ids[0].T,
        counts[0].T,
        feature_rows,
        tile_contents,
        targets[0],
        edge_weight[0],
    )
    paired = call(
        pair_kernel,
        (shape(2, groups * slots, lanes),) * chips + (shape(width, rows),) * (groups - 1),
        [VM] * (2 + groups),
        (),
        0,
        1 << 20,
    )(band, mine, mate, *feature_blocks)
    arrived = to_chips(paired[:chips])
    feature_blocks = shift(paired[chips:], near=True)
    means = call(
        mean_kernel,
        (shape(width, rows),) * groups,
        [SM] + [VM] * (2 + chips),
        (),
        2 * nodes * parts * slots * width,
        1 << 20,
    )(me, sums, edges, *arrived)
    means = [means[0]] + shift(means[1:])
    own = call(
        self_kernel,
        shape(rows, hid, dtype=f32),
        [SM, HB] + [VM] * groups,
        [pltpu.VMEM((width, rows), bf16), pltpu.SemaphoreType.DMA],
        2 * rows * hid * groups * width,
        2 << 20,
    )(me, feature_rows, self_one, *feature_blocks)
    hidden, *projected = call(
        hidden_kernel,
        (shape(rows, hid),) + (shape(classes, rows),) * groups,
        [SM] + [VM] * (3 + groups),
        (),
        2 * rows * hid * groups * width,
        2 << 20,
    )(me, neigh_one, neigh_out.T, own, *means)
    hits = call(
        hits_kernel,
        shape(parts * slots, nodes),
        [VM, SM, SM, HB],
        [pltpu.VMEM((parts, groups, slots), jnp.int32), pltpu.SemaphoreType.DMA],
        0,
        1 << 19,
    )(projected[0], me, part, sources[0])
    projected = projected[:1] + shift(projected[1:])
    mine, mate = call(
        pick_kernel,
        (shape(chips, slots, whole_lanes(classes)),) * 2,
        [SM] + [VM] * (1 + groups),
        (),
        2 * parts * slots * nodes * classes,
        1 << 19,
    )(me, hits, *projected)
    mate = to_mate(mate)
    arrived = to_chips(
        call(pair_kernel, (shape(2, slots, whole_lanes(classes)),) * chips, [VM] * 3, (), 0, 1 << 19)(
            hits, mine, mate
        )
    )
    own, hidden = call(
        own_kernel,
        (shape(classes, rows, dtype=f32), shape(rows, hid)),
        [VM, VM],
        [pltpu.SemaphoreType.DMA],
        2 * rows * hid * classes,
        1 << 20,
        out_specs=(VM, HB),
    )(hidden, self_out.T)
    near = call(
        near_kernel,
        shape(classes, rows, dtype=f32),
        [SM] + [VM] * (3 + groups),
        (),
        2 * rows * nodes * classes,
        1 << 19,
    )(me, own, sums, band, *projected)
    logits = call(
        last_kernel,
        shape(classes, 1, rows, dtype=f32),
        [SM] + [VM] * (3 + chips),
        (),
        2 * rows * parts * slots * classes,
        1 << 19,
    )(me, near, edges, sums, *arrived)
    return hidden[None], logits.transpose(1, 0, 2)


def solution(mesh):
    placed = (
        P("dom", None, "feat"),
        P("dom", None, None, None),
        P("dom", None, None),
        P("dom", None, None, None),
        P("dom", None, None, None),
        P("dom", None, None),
        P("dom", None, None, None),
        P(),
        P(),
        P(),
        P(),
    )
    return jax.shard_map(
        on_device,
        mesh=mesh,
        in_specs=placed,
        out_specs=(P("dom", "feat", None), P("dom", None, "feat")),
        check_vma=False,
    )
```

```python
import functools

import jax
import jax.numpy as jnp
from jax import lax
from jax.experimental import pallas as pl
from jax.experimental.pallas import tpu as pltpu
from jax.sharding import PartitionSpec as P

f32 = jnp.float32
bf16 = jnp.bfloat16
VM = pl.BlockSpec(memory_space=pltpu.VMEM)
SM = pl.BlockSpec(memory_space=pltpu.SMEM)
HB = pl.BlockSpec(memory_space=pltpu.HBM)
LAST = (((1,), (1,)), ((), ()))
FIRST = (((0,), (0,)), ((), ()))
EXTRA = 16


def call(kernel, out_shape, in_specs, scratch=(), flops=0, size=0, limit=4, out_specs=None):
    run = pl.pallas_call(
        kernel,
        out_shape=out_shape,
        in_specs=in_specs,
        out_specs=out_specs or jax.tree.map(lambda _: VM, out_shape),
        scratch_shapes=list(scratch),
        cost_estimate=pl.CostEstimate(flops=flops, bytes_accessed=size, transcendentals=0),
        compiler_params=pltpu.CompilerParams(vmem_limit_bytes=limit << 20),
    )

    def placed(*operands):
        return run(
            *(
                pltpu.with_memory_space_constraint(value, pltpu.HBM) if spec is HB else value
                for value, spec in zip(operands, in_specs)
            )
        )

    return placed


def dot(left, right, dims):
    return lax.dot_general(left, right, dims, preferred_element_type=f32)


def step_of(groups, k, near=False):
    if near and groups > 2 and k in (1, 2):
        return groups - 3 + k
    return (groups - k) % groups


def whole_lanes(count):
    return -(-count // 128) * 128


def ahead(me, groups, k, near=False):
    step = step_of(groups, k, near)
    return me ^ step if groups & (groups - 1) == 0 else (me + step) % groups


def behind(me, groups, k, near=False):
    step = step_of(groups, k, near)
    return me ^ step if groups & (groups - 1) == 0 else (me + groups - step) % groups


def step_to(a, b, count):
    step = a ^ b if count & (count - 1) == 0 else (b + count - a) % count
    return (count - step) % count


def next_to(a, j, count):
    step = step_of(count, j)
    return a ^ step if count & (count - 1) == 0 else (a + step) % count


def fetch(sems, *pairs):
    copies = [pltpu.make_async_copy(a, b, sems.at[i]) for i, (a, b) in enumerate(pairs)]
    for copy in copies:
        copy.start()
    return copies


def columns_of(values):
    return values.reshape(-1, values.shape[-1]).T


def gather_kernel(
    chunk,
    me_ref,
    part_ref,
    sources_hbm,
    ids_hbm,
    features_hbm,
    tiles_hbm,
    mine_ref,
    mate_ref,
    table_ref,
    bands_ref,
    *rest,
):
    blocks, (sources_ref, ids_ref, order, hits, sems, tile_sems) = rest[:-6], rest[-6:]
    parts, groups, slots = sources_ref.shape
    tiles, rows = tiles_hbm.shape[:2]
    width, nodes = features_hbm.shape
    lanes = mine_ref.shape[2]
    chips, chip, core = parts // 2, part_ref[0] // 2, part_ref[0] % 2
    indices, ids, table = fetch(
        sems,
        (sources_hbm, sources_ref),
        (ids_hbm, ids_ref),
        (features_hbm, table_ref.at[pl.ds(0, width), :]),
    )
    table_ref[width : width + EXTRA, :] = jnp.ones((EXTRA, nodes), bf16)
    if table_ref.shape[0] > width + EXTRA:
        table_ref[width + EXTRA :, :] = jnp.zeros(
            (table_ref.shape[0] - width - EXTRA, nodes), bf16
        )
    bands_ref[...] = jnp.zeros_like(bands_ref)

    def tile_copy(t):
        at = pl.multiple_of(ids_ref[1, t] * rows, rows)
        to = bands_ref.at[ids_ref[0, t], :, pl.ds(at, rows)]
        return pltpu.make_async_copy(tiles_hbm.at[t], to, tile_sems.at[t])

    def each_tile(run):
        lax.fori_loop(0, tiles, lambda t, _: run(tile_copy(t)), None, unroll=tiles <= 16)

    ids.wait()
    each_tile(lambda copy: copy.start())
    indices.wait()
    lane = lax.broadcasted_iota(jnp.int32, (slots, nodes), 1)

    def step(i, out, other, last):
        for j in range(chunk):
            order[j] = sources_ref[next_to(chip, i * chunk + j, chips) * 2 + (core ^ other)]
        columns = columns_of(order[...])
        for n in range(chunk * groups):
            hits[n * slots : (n + 1) * slots, :] = jnp.where(
                columns[:, n : n + 1] == lane, 1.0, 0.0
            ).astype(bf16)
        if last:
            table.wait()
        picked = dot(hits[...], table_ref[:lanes, :], LAST).astype(bf16)
        out[pl.ds(i * chunk, chunk)] = picked.reshape(chunk, groups * slots, -1)

    if chips == chunk:
        step(0, mate_ref, 1, True)
        step(0, mine_ref, 0, False)
    else:
        table.wait()
        for other, out in enumerate((mine_ref, mate_ref)):
            lax.fori_loop(0, chips // chunk, lambda i, _: step(i, out, other, False), None)
    for k in range(1, groups):
        group = ahead(me_ref[0], groups, k, True)
        blocks[k - 1][...] = table_ref[:width, pl.ds(pl.multiple_of(group * rows, rows), rows)]
    each_tile(lambda copy: copy.wait())


def local_kernel(
    chunk,
    me_ref,
    part_ref,
    table_ref,
    bands_ref,
    counts_hbm,
    targets_hbm,
    weight_hbm,
    sums_ref,
    edges_ref,
    band_ref,
    counts_ref,
    targets_ref,
    weight_ref,
    sems,
):
    parts, groups, slots = targets_ref.shape
    rows = edges_ref.shape[3]
    high = sums_ref.shape[1]
    copies = fetch(
        sems, (counts_hbm, counts_ref), (targets_hbm, targets_ref), (weight_hbm, weight_ref)
    )
    for g in range(groups):
        sums_ref[g] = dot(table_ref[:high, :], bands_ref[g], LAST)
    band_ref[...] = bands_ref[me_ref[0]]
    lane = lax.broadcasted_iota(jnp.int32, (slots, rows), 1)
    slot = lax.broadcasted_iota(jnp.int32, (slots, rows), 0)
    chips, chip, core = parts // 2, part_ref[0] // 2, part_ref[0] % 2
    for copy in copies:
        copy.wait()

    def connect(i, _):
        first = i * chunk
        target = columns_of(targets_ref[pl.ds(first, chunk)])
        weight = columns_of(weight_ref[pl.ds(first, chunk)].astype(f32))
        for g in range(groups):
            degree = jnp.zeros((1, rows), f32)
            for e in range(chunk):
                n, d = e * groups + g, first + e
                at = step_to(d // 2, chip, chips) * 2 + ((d % 2) ^ core)
                hit = (target[:, n : n + 1] == lane) & (slot < counts_ref[g, d])
                values = jnp.where(hit, weight[:, n : n + 1], 0.0)
                edges_ref[g, at] = values.astype(bf16)
                degree = degree + jnp.sum(values, axis=0, keepdims=True)
            sums_ref[g, high - EXTRA : high - EXTRA + 1, :] += degree
        return 0

    if parts == chunk:
        connect(0, 0)
    else:
        lax.fori_loop(0, parts // chunk, connect, 0)


def hits_kernel(after, me_ref, part_ref, sources_hbm, hits_ref, sources_ref, sem):
    del after
    copy = pltpu.make_async_copy(sources_hbm, sources_ref, sem)
    copy.start()
    parts, groups, slots = sources_ref.shape
    chips, chip, core = parts // 2, part_ref[0] // 2, part_ref[0] % 2
    mine = lax.broadcasted_iota(jnp.int32, sources_ref.shape, 1) == me_ref[0]
    copy.wait()
    picks = jnp.sum(jnp.where(mine, sources_ref[...], 0), axis=1).T
    lane = lax.broadcasted_iota(jnp.int32, (slots, hits_ref.shape[1]), 1)
    for d in range(parts):
        to = ((d % 2) ^ core) * chips + step_to(chip, d // 2, chips)
        hits_ref[pl.ds(pl.multiple_of(to * slots, slots), slots), :] = jnp.where(
            picks[:, d : d + 1] == lane, 1.0, 0.0
        ).astype(bf16)


def mean_kernel(me_ref, sums_ref, edges_ref, *rest):
    groups, parts, slots, rows = edges_ref.shape
    arrived, outs = rest[: parts // 2], rest[parts // 2 :]
    width = outs[0].shape[0]
    for k in range(groups):
        group = ahead(me_ref[0], groups, k)
        span = pl.ds(pl.multiple_of(group * slots, slots), slots)
        far = jnp.concatenate([x[:, span, :].reshape(2 * slots, -1) for x in arrived], axis=0)
        far = dot(far, edges_ref[group].reshape(parts * slots, rows), FIRST)
        total = sums_ref[group, :width, :] + far[:width]
        outs[k][...] = (total / sums_ref[group, width : width + 1, :]).astype(bf16)


def rows_from(me, groups, k, width, near=False):
    return pl.ds(pl.multiple_of(behind(me, groups, k, near) * width, width), width)


def self_kernel(me_ref, features_hbm, weight_ref, *rest):
    blocks, (out_ref, own_ref, sem) = rest[:-3], rest[-3:]
    groups, (width, rows) = len(blocks) + 1, own_ref.shape
    me = me_ref[0]
    own = pltpu.make_async_copy(
        features_hbm.at[:, pl.ds(pl.multiple_of(me * rows, rows), rows)], own_ref, sem
    )
    own.start()
    total = jnp.zeros(out_ref.shape, f32)
    for k, block in enumerate(blocks, 1):
        span = rows_from(me, groups, k, width, True)
        total = total + dot(block[...], weight_ref[span, :], FIRST)
    own.wait()
    span = pl.ds(pl.multiple_of(me * width, width), width)
    out_ref[...] = total + dot(own_ref[...], weight_ref[span, :], FIRST)


def add_blocks(total, me, groups, first, blocks, weight_ref):
    width = blocks[0].shape[0]
    for k, block in enumerate(blocks, first):
        total = total + dot(block[...], weight_ref[rows_from(me, groups, k, width), :], FIRST)
    return total


def early_kernel(groups, me_ref, weight_ref, own_ref, *rest):
    blocks, out_ref = rest[:-1], rest[-1]
    out_ref[...] = add_blocks(own_ref[...], me_ref[0], groups, 0, blocks, weight_ref)


def hidden_kernel(groups, me_ref, weight_ref, out_weight_ref, early_ref, *rest):
    blocks, (hidden_ref, *copies) = rest[: groups - 2], rest[groups - 2 :]
    total = add_blocks(early_ref[...], me_ref[0], groups, 2, blocks, weight_ref)
    hidden = jnp.maximum(total, 0.0).astype(bf16)
    hidden_ref[...] = hidden
    projected = dot(out_weight_ref[...], hidden, LAST).astype(bf16)
    for copy in copies:
        copy[...] = projected


def own_kernel(hidden_ref, weight_ref, out_ref, hidden_out, sem):
    copy = pltpu.make_async_copy(hidden_ref, hidden_out, sem)
    copy.start()
    out_ref[...] = dot(weight_ref[...], hidden_ref[...], LAST)
    copy.wait()


def pick_kernel(me_ref, hits_ref, *rest):
    projected, (mine_ref, mate_ref) = rest[:-2], rest[-2:]
    groups, rows = len(projected), projected[0].shape[1]
    total = None
    for k in range(groups):
        at = pl.multiple_of(behind(me_ref[0], groups, k) * rows, rows)
        term = dot(hits_ref[:, pl.ds(at, rows)], projected[k][...], LAST)
        total = term if total is None else total + term
    gap = mine_ref.shape[2] - total.shape[1]
    total = jnp.concatenate([total, jnp.zeros((total.shape[0], gap), f32)], axis=1).astype(bf16)
    half = total.shape[0] // 2
    mine_ref[...] = total[:half].reshape(mine_ref.shape)
    mate_ref[...] = total[half:].reshape(mate_ref.shape)


def pair_kernel(after, mine_ref, got_ref, *rest):
    del after
    chips = mine_ref.shape[0]
    held = (len(rest) - chips) // 2
    for j, out in enumerate(rest[held : held + chips]):
        out[0] = mine_ref[j]
        out[1] = got_ref[j]
    for block, out in zip(rest[:held], rest[held + chips :]):
        out[...] = block[...]


def near_kernel(me_ref, own_ref, sums_ref, band_ref, *rest):
    projected, out_ref = rest[:-1], rest[-1]
    groups, rows = len(projected), projected[0].shape[1]
    me, width = me_ref[0], sums_ref.shape[1] - EXTRA
    total = None
    for k in range(groups):
        at = pl.multiple_of(behind(me, groups, k) * rows, rows)
        term = dot(projected[k][...], band_ref[:, pl.ds(at, rows)], LAST)
        total = term if total is None else total + term
    out_ref[...] = own_ref[...] + total / sums_ref[me, width : width + 1, :]


def last_kernel(me_ref, near_ref, edges_ref, sums_ref, *rest):
    arrived, out_ref = rest[:-1], rest[-1]
    groups, parts, slots, rows = edges_ref.shape
    me, width = me_ref[0], sums_ref.shape[1] - EXTRA
    arrived = jnp.concatenate([x[...].reshape(2 * slots, -1) for x in arrived], axis=0)
    far = dot(arrived, edges_ref[me].reshape(parts * slots, rows), FIRST)
    far = far[: near_ref.shape[0]]
    total = near_ref[...] + far / sums_ref[me, width : width + 1, :]
    out_ref[...] = total.reshape(out_ref.shape)


def on_device(
    features,
    tiles,
    tile_ids,
    sources,
    targets,
    counts,
    edge_weight,
    self_one,
    neigh_one,
    self_out,
    neigh_out,
):
    feature_rows, tile_contents = features[0].T, tiles[0]
    groups, parts = lax.axis_size("feat"), lax.axis_size("dom")
    me = lax.axis_index("feat").astype(jnp.int32).reshape(1)
    part = lax.axis_index("dom").astype(jnp.int32).reshape(1)
    width, nodes = feature_rows.shape
    rows, slots = nodes // groups, sources.shape[3]
    hid, classes = self_one.shape[1], self_out.shape[1]
    chips = parts // 2
    chunk = max(1, min(parts, 512 // (groups * slots)))

    def shape(*dims, dtype=bf16):
        return jax.ShapeDtypeStruct(dims, dtype)

    def shift(blocks, near=False):
        return [
            lax.ppermute(block, "feat", [(i, ahead(i, groups, k, near)) for i in range(groups)])
            for k, block in enumerate(blocks, 1)
        ]

    def to_mate(value):
        return lax.ppermute(value, "dom", [(d, d ^ 1) for d in range(parts)])

    def to_chips(blocks):
        return [blocks[0]] + [
            lax.ppermute(
                blocks[j],
                "dom",
                [(d, next_to(d // 2, j, chips) * 2 + d % 2) for d in range(parts)],
            )
            for j in range(1, chips)
        ]

    picked = min(chips, chunk)
    lanes = whole_lanes(width)
    table_rows = max(lanes, width + EXTRA)
    mine, mate, table, bands, *feature_blocks = call(
        functools.partial(gather_kernel, picked),
        (shape(chips, groups * slots, lanes),) * 2
        + (shape(table_rows, nodes), shape(groups, rows, nodes))
        + (shape(width, rows),) * (groups - 1),
        [SM, SM, HB, HB, HB, HB],
        [
            pltpu.VMEM((parts, groups, slots), jnp.int32),
            pltpu.SMEM(tile_ids.shape[:0:-1], jnp.int32),
            pltpu.VMEM((picked, groups, slots), jnp.int32),
            pltpu.VMEM((picked * groups * slots, nodes), bf16),
            pltpu.SemaphoreType.DMA((3,)),
            pltpu.SemaphoreType.DMA((tile_contents.shape[0],)),
        ],
        2 * nodes * nodes * width,
        1 << 20,
        4 if groups <= 4 else 16,
    )(me, part, sources[0], tile_ids[0].T, feature_rows, tile_contents)
    mate = to_mate(mate)
    sums, edges, band = call(
        functools.partial(local_kernel, chunk),
        (
            shape(groups, width + EXTRA, rows, dtype=f32),
            shape(groups, parts, slots, rows),
            shape(rows, nodes),
        ),
        [SM, SM, VM, VM] + [HB] * 3,
        [
            pltpu.SMEM(counts.shape[:0:-1], jnp.int32),
            pltpu.VMEM((parts, groups, slots), jnp.int32),
            pltpu.VMEM((parts, groups, slots), bf16),
            pltpu.SemaphoreType.DMA((3,)),
        ],
        2 * nodes * nodes * width,
        1 << 20,
        4 if groups <= 4 else 16,
    )(me, part, table, bands, counts[0].T, targets[0], edge_weight[0])
    paired = call(
        pair_kernel,
        (shape(2, groups * slots, lanes),) * chips + (shape(width, rows),) * (groups - 1),
        [VM] * (2 + groups),
        (),
        0,
        1 << 20,
    )(band, mine, mate, *feature_blocks)
    arrived = to_chips(paired[:chips])
    feature_blocks = shift(paired[chips:], near=True)
    means = call(
        mean_kernel,
        (shape(width, rows),) * groups,
        [SM] + [VM] * (2 + chips),
        (),
        2 * nodes * parts * slots * width,
        1 << 20,
    )(me, sums, edges, *arrived)
    means = [means[0]] + shift(means[1:])
    own = call(
        self_kernel,
        shape(rows, hid, dtype=f32),
        [SM, HB] + [VM] * groups,
        [pltpu.VMEM((width, rows), bf16), pltpu.SemaphoreType.DMA],
        2 * rows * hid * groups * width,
        2 << 20,
    )(me, feature_rows, self_one, *feature_blocks)
    early = call(
        functools.partial(early_kernel, groups),
        shape(rows, hid, dtype=f32),
        [SM] + [VM] * 4,
        (),
        rows * hid * groups * width,
        2 << 20,
    )(me, neigh_one, own, *means[:2])
    hidden, *projected = call(
        functools.partial(hidden_kernel, groups),
        (shape(rows, hid),) + (shape(classes, rows),) * groups,
        [SM] + [VM] * (1 + groups),
        (),
        rows * hid * groups * width,
        2 << 20,
    )(me, neigh_one, neigh_out.T, early, *means[2:])
    hits = call(
        hits_kernel,
        shape(parts * slots, nodes),
        [VM, SM, SM, HB],
        [pltpu.VMEM((parts, groups, slots), jnp.int32), pltpu.SemaphoreType.DMA],
        0,
        1 << 19,
    )(projected[0], me, part, sources[0])
    projected = projected[:1] + shift(projected[1:])
    mine, mate = call(
        pick_kernel,
        (shape(chips, slots, whole_lanes(classes)),) * 2,
        [SM] + [VM] * (1 + groups),
        (),
        2 * parts * slots * nodes * classes,
        1 << 19,
    )(me, hits, *projected)
    mate = to_mate(mate)
    arrived = to_chips(
        call(pair_kernel, (shape(2, slots, whole_lanes(classes)),) * chips, [VM] * 3, (), 0, 1 << 19)(
            hits, mine, mate
        )
    )
    own, hidden = call(
        own_kernel,
        (shape(classes, rows, dtype=f32), shape(rows, hid)),
        [VM, VM],
        [pltpu.SemaphoreType.DMA],
        2 * rows * hid * classes,
        1 << 20,
        out_specs=(VM, HB),
    )(hidden, self_out.T)
    near = call(
        near_kernel,
        shape(classes, rows, dtype=f32),
        [SM] + [VM] * (3 + groups),
        (),
        2 * rows * nodes * classes,
        1 << 19,
    )(me, own, sums, band, *projected)
    logits = call(
        last_kernel,
        shape(classes, 1, rows, dtype=f32),
        [SM] + [VM] * (3 + chips),
        (),
        2 * rows * parts * slots * classes,
        1 << 19,
    )(me, near, edges, sums, *arrived)
    return hidden[None], logits.transpose(1, 0, 2)


def solution(mesh):
    placed = (
        P("dom", None, "feat"),
        P("dom", None, None, None),
        P("dom", None, None),
        P("dom", None, None, None),
        P("dom", None, None, None),
        P("dom", None, None),
        P("dom", None, None, None),
        P(),
        P(),
        P(),
        P(),
    )
    return jax.shard_map(
        on_device,
        mesh=mesh,
        in_specs=placed,
        out_specs=(P("dom", "feat", None), P("dom", None, "feat")),
        check_vma=False,
    )
```

```python
import functools

import jax
import jax.numpy as jnp
from jax import lax
from jax.experimental import pallas as pl
from jax.experimental.pallas import tpu as pltpu
from jax.sharding import PartitionSpec as P

f32 = jnp.float32
bf16 = jnp.bfloat16
VM = pl.BlockSpec(memory_space=pltpu.VMEM)
SM = pl.BlockSpec(memory_space=pltpu.SMEM)
HB = pl.BlockSpec(memory_space=pltpu.HBM)
LAST = (((1,), (1,)), ((), ()))
FIRST = (((0,), (0,)), ((), ()))
EXTRA = 16
PASSED = 5


def call(kernel, out_shape, in_specs, scratch=(), flops=0, size=0, limit=4, out_specs=None):
    run = pl.pallas_call(
        kernel,
        out_shape=out_shape,
        in_specs=in_specs,
        out_specs=out_specs or jax.tree.map(lambda _: VM, out_shape),
        scratch_shapes=list(scratch),
        cost_estimate=pl.CostEstimate(flops=flops, bytes_accessed=size, transcendentals=0),
        compiler_params=pltpu.CompilerParams(vmem_limit_bytes=limit << 20),
    )

    def placed(*operands):
        return run(
            *(
                pltpu.with_memory_space_constraint(value, pltpu.HBM) if spec is HB else value
                for value, spec in zip(operands, in_specs)
            )
        )

    return placed


def dot(left, right, dims):
    return lax.dot_general(left, right, dims, preferred_element_type=f32)


def step_of(groups, k, near=False):
    if near and groups > 2 and k in (1, 2):
        return groups - 3 + k
    return (groups - k) % groups


def whole_lanes(count):
    return -(-count // 128) * 128


def ahead(me, groups, k, near=False):
    step = step_of(groups, k, near)
    return me ^ step if groups & (groups - 1) == 0 else (me + step) % groups


def behind(me, groups, k, near=False):
    step = step_of(groups, k, near)
    return me ^ step if groups & (groups - 1) == 0 else (me + groups - step) % groups


def step_to(a, b, count):
    step = a ^ b if count & (count - 1) == 0 else (b + count - a) % count
    return (count - step) % count


def next_to(a, j, count):
    step = step_of(count, j)
    return a ^ step if count & (count - 1) == 0 else (a + step) % count


def fetch(sems, *pairs):
    copies = [pltpu.make_async_copy(a, b, sems.at[i]) for i, (a, b) in enumerate(pairs)]
    for copy in copies:
        copy.start()
    return copies


def columns_of(values):
    return values.reshape(-1, values.shape[-1]).T


def gather_kernel(
    chunk,
    me_ref,
    part_ref,
    sources_hbm,
    features_hbm,
    *rest,
):
    extras, (mine_ref, mate_ref, table_ref, *outs) = rest[:PASSED], rest[PASSED:]
    passed, blocks = outs[:PASSED], outs[PASSED:-4]
    sources_ref, order, hits, sems = outs[-4:]
    parts, groups, slots = sources_ref.shape
    width, nodes = features_hbm.shape
    rows = nodes // groups
    lanes = mine_ref.shape[2]
    chips, chip, core = parts // 2, part_ref[0] // 2, part_ref[0] % 2
    indices, table, *others = fetch(
        sems,
        (sources_hbm, sources_ref),
        (features_hbm, table_ref.at[pl.ds(0, width), :]),
        *zip(extras, passed),
    )
    table_ref[width : width + EXTRA, :] = jnp.ones((EXTRA, nodes), bf16)
    if table_ref.shape[0] > width + EXTRA:
        table_ref[width + EXTRA :, :] = jnp.zeros(
            (table_ref.shape[0] - width - EXTRA, nodes), bf16
        )
    indices.wait()
    lane = lax.broadcasted_iota(jnp.int32, (slots, nodes), 1)

    def step(i, out, other, last):
        for j in range(chunk):
            order[j] = sources_ref[next_to(chip, i * chunk + j, chips) * 2 + (core ^ other)]
        columns = columns_of(order[...])
        for n in range(chunk * groups):
            hits[n * slots : (n + 1) * slots, :] = jnp.where(
                columns[:, n : n + 1] == lane, 1.0, 0.0
            ).astype(bf16)
        if last:
            table.wait()
        picked = dot(hits[...], table_ref[:lanes, :], LAST).astype(bf16)
        out[pl.ds(i * chunk, chunk)] = picked.reshape(chunk, groups * slots, -1)

    if chips == chunk:
        step(0, mate_ref, 1, True)
        step(0, mine_ref, 0, False)
    else:
        table.wait()
        for other, out in enumerate((mine_ref, mate_ref)):
            lax.fori_loop(0, chips // chunk, lambda i, _: step(i, out, other, False), None)
    for k in range(1, groups):
        group = ahead(me_ref[0], groups, k, True)
        blocks[k - 1][...] = table_ref[:width, pl.ds(pl.multiple_of(group * rows, rows), rows)]
    for copy in others:
        copy.wait()


def local_kernel(
    chunk,
    me_ref,
    part_ref,
    table_ref,
    tiles_ref,
    targets_ref,
    weight_ref,
    ids_vmem,
    counts_vmem,
    sums_ref,
    edges_ref,
    band_ref,
    ids_ref,
    counts_ref,
    bands_ref,
    sems,
):
    parts, groups, slots = targets_ref.shape
    rows = edges_ref.shape[3]
    high = sums_ref.shape[1]
    copies = fetch(sems, (ids_vmem, ids_ref), (counts_vmem, counts_ref))
    bands_ref[...] = jnp.zeros_like(bands_ref)
    for copy in copies:
        copy.wait()

    def place(t, _):
        at = pl.multiple_of(ids_ref[1, t] * rows, rows)
        bands_ref[ids_ref[0, t], :, pl.ds(at, rows)] = tiles_ref[t]
        return 0

    lax.fori_loop(0, tiles_ref.shape[0], place, 0, unroll=tiles_ref.shape[0] <= 16)
    for g in range(groups):
        sums_ref[g] = dot(table_ref[:high, :], bands_ref[g], LAST)
    band_ref[...] = bands_ref[me_ref[0]]
    lane = lax.broadcasted_iota(jnp.int32, (slots, rows), 1)
    slot = lax.broadcasted_iota(jnp.int32, (slots, rows), 0)
    chips, chip, core = parts // 2, part_ref[0] // 2, part_ref[0] % 2

    def connect(i, _):
        first = i * chunk
        target = columns_of(targets_ref[pl.ds(first, chunk)])
        weight = columns_of(weight_ref[pl.ds(first, chunk)].astype(f32))
        for g in range(groups):
            degree = jnp.zeros((1, rows), f32)
            for e in range(chunk):
                n, d = e * groups + g, first + e
                at = step_to(d // 2, chip, chips) * 2 + ((d % 2) ^ core)
                hit = (target[:, n : n + 1] == lane) & (slot < counts_ref[g, d])
                values = jnp.where(hit, weight[:, n : n + 1], 0.0)
                edges_ref[g, at] = values.astype(bf16)
                degree = degree + jnp.sum(values, axis=0, keepdims=True)
            sums_ref[g, high - EXTRA : high - EXTRA + 1, :] += degree
        return 0

    if parts == chunk:
        connect(0, 0)
    else:
        lax.fori_loop(0, parts // chunk, connect, 0)


def hits_kernel(after, me_ref, part_ref, sources_hbm, hits_ref, sources_ref, sem):
    del after
    copy = pltpu.make_async_copy(sources_hbm, sources_ref, sem)
    copy.start()
    parts, groups, slots = sources_ref.shape
    chips, chip, core = parts // 2, part_ref[0] // 2, part_ref[0] % 2
    mine = lax.broadcasted_iota(jnp.int32, sources_ref.shape, 1) == me_ref[0]
    copy.wait()
    picks = jnp.sum(jnp.where(mine, sources_ref[...], 0), axis=1).T
    lane = lax.broadcasted_iota(jnp.int32, (slots, hits_ref.shape[1]), 1)
    for d in range(parts):
        to = ((d % 2) ^ core) * chips + step_to(chip, d // 2, chips)
        hits_ref[pl.ds(pl.multiple_of(to * slots, slots), slots), :] = jnp.where(
            picks[:, d : d + 1] == lane, 1.0, 0.0
        ).astype(bf16)


def mean_kernel(me_ref, sums_ref, edges_ref, *rest):
    groups, parts, slots, rows = edges_ref.shape
    arrived, outs = rest[: parts // 2], rest[parts // 2 :]
    width = outs[0].shape[0]
    for k in range(groups):
        group = ahead(me_ref[0], groups, k)
        span = pl.ds(pl.multiple_of(group * slots, slots), slots)
        far = jnp.concatenate([x[:, span, :].reshape(2 * slots, -1) for x in arrived], axis=0)
        far = dot(far, edges_ref[group].reshape(parts * slots, rows), FIRST)
        total = sums_ref[group, :width, :] + far[:width]
        outs[k][...] = (total / sums_ref[group, width : width + 1, :]).astype(bf16)


def rows_from(me, groups, k, width, near=False):
    return pl.ds(pl.multiple_of(behind(me, groups, k, near) * width, width), width)


def self_kernel(me_ref, features_hbm, weight_ref, *rest):
    blocks, (out_ref, own_ref, sem) = rest[:-3], rest[-3:]
    groups, (width, rows) = len(blocks) + 1, own_ref.shape
    me = me_ref[0]
    own = pltpu.make_async_copy(
        features_hbm.at[:, pl.ds(pl.multiple_of(me * rows, rows), rows)], own_ref, sem
    )
    own.start()
    total = jnp.zeros(out_ref.shape, f32)
    for k, block in enumerate(blocks, 1):
        span = rows_from(me, groups, k, width, True)
        total = total + dot(block[...], weight_ref[span, :], FIRST)
    own.wait()
    span = pl.ds(pl.multiple_of(me * width, width), width)
    out_ref[...] = total + dot(own_ref[...], weight_ref[span, :], FIRST)


def add_blocks(total, me, groups, first, blocks, weight_ref):
    width = blocks[0].shape[0]
    for k, block in enumerate(blocks, first):
        total = total + dot(block[...], weight_ref[rows_from(me, groups, k, width), :], FIRST)
    return total


def early_kernel(groups, me_ref, weight_ref, own_ref, *rest):
    blocks, out_ref = rest[:-1], rest[-1]
    out_ref[...] = add_blocks(own_ref[...], me_ref[0], groups, 0, blocks, weight_ref)


def hidden_kernel(groups, me_ref, weight_ref, out_weight_ref, early_ref, *rest):
    blocks, (hidden_ref, *copies) = rest[: groups - 2], rest[groups - 2 :]
    total = add_blocks(early_ref[...], me_ref[0], groups, 2, blocks, weight_ref)
    hidden = jnp.maximum(total, 0.0).astype(bf16)
    hidden_ref[...] = hidden
    projected = dot(out_weight_ref[...], hidden, LAST).astype(bf16)
    for copy in copies:
        copy[...] = projected


def own_kernel(hidden_ref, weight_ref, out_ref, hidden_out, sem):
    copy = pltpu.make_async_copy(hidden_ref, hidden_out, sem)
    copy.start()
    out_ref[...] = dot(weight_ref[...], hidden_ref[...], LAST)
    copy.wait()


def pick_kernel(me_ref, hits_ref, *rest):
    projected, (mine_ref, mate_ref) = rest[:-2], rest[-2:]
    groups, rows = len(projected), projected[0].shape[1]
    total = None
    for k in range(groups):
        at = pl.multiple_of(behind(me_ref[0], groups, k) * rows, rows)
        term = dot(hits_ref[:, pl.ds(at, rows)], projected[k][...], LAST)
        total = term if total is None else total + term
    gap = mine_ref.shape[2] - total.shape[1]
    total = jnp.concatenate([total, jnp.zeros((total.shape[0], gap), f32)], axis=1).astype(bf16)
    half = total.shape[0] // 2
    mine_ref[...] = total[:half].reshape(mine_ref.shape)
    mate_ref[...] = total[half:].reshape(mate_ref.shape)


def pair_kernel(after, mine_ref, got_ref, *rest):
    del after
    chips = mine_ref.shape[0]
    held = (len(rest) - chips) // 2
    for j, out in enumerate(rest[held : held + chips]):
        out[0] = mine_ref[j]
        out[1] = got_ref[j]
    for block, out in zip(rest[:held], rest[held + chips :]):
        out[...] = block[...]


def near_kernel(me_ref, own_ref, sums_ref, band_ref, *rest):
    projected, out_ref = rest[:-1], rest[-1]
    groups, rows = len(projected), projected[0].shape[1]
    me, width = me_ref[0], sums_ref.shape[1] - EXTRA
    total = None
    for k in range(groups):
        at = pl.multiple_of(behind(me, groups, k) * rows, rows)
        term = dot(projected[k][...], band_ref[:, pl.ds(at, rows)], LAST)
        total = term if total is None else total + term
    out_ref[...] = own_ref[...] + total / sums_ref[me, width : width + 1, :]


def last_kernel(me_ref, near_ref, edges_ref, sums_ref, *rest):
    arrived, out_ref = rest[:-1], rest[-1]
    groups, parts, slots, rows = edges_ref.shape
    me, width = me_ref[0], sums_ref.shape[1] - EXTRA
    arrived = jnp.concatenate([x[...].reshape(2 * slots, -1) for x in arrived], axis=0)
    far = dot(arrived, edges_ref[me].reshape(parts * slots, rows), FIRST)
    far = far[: near_ref.shape[0]]
    total = near_ref[...] + far / sums_ref[me, width : width + 1, :]
    out_ref[...] = total.reshape(out_ref.shape)


def on_device(
    features,
    tiles,
    tile_ids,
    sources,
    targets,
    counts,
    edge_weight,
    self_one,
    neigh_one,
    self_out,
    neigh_out,
):
    feature_rows, tile_contents = features[0].T, tiles[0]
    groups, parts = lax.axis_size("feat"), lax.axis_size("dom")
    me = lax.axis_index("feat").astype(jnp.int32).reshape(1)
    part = lax.axis_index("dom").astype(jnp.int32).reshape(1)
    width, nodes = feature_rows.shape
    rows, slots = nodes // groups, sources.shape[3]
    hid, classes = self_one.shape[1], self_out.shape[1]
    chips = parts // 2
    chunk = max(1, min(parts, 512 // (groups * slots)))

    def shape(*dims, dtype=bf16):
        return jax.ShapeDtypeStruct(dims, dtype)

    def shift(blocks, near=False):
        return [
            lax.ppermute(block, "feat", [(i, ahead(i, groups, k, near)) for i in range(groups)])
            for k, block in enumerate(blocks, 1)
        ]

    def to_mate(value):
        return lax.ppermute(value, "dom", [(d, d ^ 1) for d in range(parts)])

    def to_chips(blocks):
        return [blocks[0]] + [
            lax.ppermute(
                blocks[j],
                "dom",
                [(d, next_to(d // 2, j, chips) * 2 + d % 2) for d in range(parts)],
            )
            for j in range(1, chips)
        ]

    picked = min(chips, chunk)
    lanes = whole_lanes(width)
    table_rows = max(lanes, width + EXTRA)
    extras = (tile_contents, targets[0], edge_weight[0], tile_ids[0].T, counts[0].T)
    mine, mate, table, *rest = call(
        functools.partial(gather_kernel, picked),
        (shape(chips, groups * slots, lanes),) * 2
        + (shape(table_rows, nodes),)
        + tuple(shape(*value.shape, dtype=value.dtype) for value in extras)
        + (shape(width, rows),) * (groups - 1),
        [SM, SM, HB, HB] + [HB] * PASSED,
        [
            pltpu.VMEM((parts, groups, slots), jnp.int32),
            pltpu.VMEM((picked, groups, slots), jnp.int32),
            pltpu.VMEM((picked * groups * slots, nodes), bf16),
            pltpu.SemaphoreType.DMA((2 + PASSED,)),
        ],
        2 * nodes * nodes * width,
        1 << 20,
    )(me, part, sources[0], feature_rows, *extras)
    passed, feature_blocks = rest[:PASSED], rest[PASSED:]
    mate = to_mate(mate)
    sums, edges, band = call(
        functools.partial(local_kernel, chunk),
        (
            shape(groups, width + EXTRA, rows, dtype=f32),
            shape(groups, parts, slots, rows),
            shape(rows, nodes),
        ),
        [SM, SM, VM] + [VM] * PASSED,
        [
            pltpu.SMEM(tile_ids.shape[:0:-1], jnp.int32),
            pltpu.SMEM(counts.shape[:0:-1], jnp.int32),
            pltpu.VMEM((groups, rows, nodes), bf16),
            pltpu.SemaphoreType.DMA((2,)),
        ],
        2 * nodes * nodes * width,
        1 << 20,
        4 if groups <= 4 else 16,
    )(me, part, table, *passed)
    paired = call(
        pair_kernel,
        (shape(2, groups * slots, lanes),) * chips + (shape(width, rows),) * (groups - 1),
        [VM] * (2 + groups),
        (),
        0,
        1 << 20,
    )(band, mine, mate, *feature_blocks)
    arrived = to_chips(paired[:chips])
    feature_blocks = shift(paired[chips:], near=True)
    means = call(
        mean_kernel,
        (shape(width, rows),) * groups,
        [SM] + [VM] * (2 + chips),
        (),
        2 * nodes * parts * slots * width,
        1 << 20,
    )(me, sums, edges, *arrived)
    means = [means[0]] + shift(means[1:])
    own = call(
        self_kernel,
        shape(rows, hid, dtype=f32),
        [SM, HB] + [VM] * groups,
        [pltpu.VMEM((width, rows), bf16), pltpu.SemaphoreType.DMA],
        2 * rows * hid * groups * width,
        2 << 20,
    )(me, feature_rows, self_one, *feature_blocks)
    early = call(
        functools.partial(early_kernel, groups),
        shape(rows, hid, dtype=f32),
        [SM] + [VM] * 4,
        (),
        rows * hid * groups * width,
        2 << 20,
    )(me, neigh_one, own, *means[:2])
    hidden, *projected = call(
        functools.partial(hidden_kernel, groups),
        (shape(rows, hid),) + (shape(classes, rows),) * groups,
        [SM] + [VM] * (1 + groups),
        (),
        rows * hid * groups * width,
        2 << 20,
    )(me, neigh_one, neigh_out.T, early, *means[2:])
    hits = call(
        hits_kernel,
        shape(parts * slots, nodes),
        [VM, SM, SM, HB],
        [pltpu.VMEM((parts, groups, slots), jnp.int32), pltpu.SemaphoreType.DMA],
        0,
        1 << 19,
    )(projected[0], me, part, sources[0])
    projected = projected[:1] + shift(projected[1:])
    mine, mate = call(
        pick_kernel,
        (shape(chips, slots, whole_lanes(classes)),) * 2,
        [SM] + [VM] * (1 + groups),
        (),
        2 * parts * slots * nodes * classes,
        1 << 19,
    )(me, hits, *projected)
    mate = to_mate(mate)
    arrived = to_chips(
        call(pair_kernel, (shape(2, slots, whole_lanes(classes)),) * chips, [VM] * 3, (), 0, 1 << 19)(
            hits, mine, mate
        )
    )
    own, hidden = call(
        own_kernel,
        (shape(classes, rows, dtype=f32), shape(rows, hid)),
        [VM, VM],
        [pltpu.SemaphoreType.DMA],
        2 * rows * hid * classes,
        1 << 20,
        out_specs=(VM, HB),
    )(hidden, self_out.T)
    near = call(
        near_kernel,
        shape(classes, rows, dtype=f32),
        [SM] + [VM] * (3 + groups),
        (),
        2 * rows * nodes * classes,
        1 << 19,
    )(me, own, sums, band, *projected)
    logits = call(
        last_kernel,
        shape(classes, 1, rows, dtype=f32),
        [SM] + [VM] * (3 + chips),
        (),
        2 * rows * parts * slots * classes,
        1 << 19,
    )(me, near, edges, sums, *arrived)
    return hidden[None], logits.transpose(1, 0, 2)


def solution(mesh):
    placed = (
        P("dom", None, "feat"),
        P("dom", None, None, None),
        P("dom", None, None),
        P("dom", None, None, None),
        P("dom", None, None, None),
        P("dom", None, None),
        P("dom", None, None, None),
        P(),
        P(),
        P(),
        P(),
    )
    return jax.shard_map(
        on_device,
        mesh=mesh,
        in_specs=placed,
        out_specs=(P("dom", "feat", None), P("dom", None, "feat")),
        check_vma=False,
    )
```

```python
import functools

import jax
import jax.numpy as jnp
from jax import lax
from jax.experimental import pallas as pl
from jax.experimental.pallas import tpu as pltpu
from jax.sharding import PartitionSpec as P

f32 = jnp.float32
bf16 = jnp.bfloat16
VM = pl.BlockSpec(memory_space=pltpu.VMEM)
SM = pl.BlockSpec(memory_space=pltpu.SMEM)
HB = pl.BlockSpec(memory_space=pltpu.HBM)
LAST = (((1,), (1,)), ((), ()))
FIRST = (((0,), (0,)), ((), ()))
EXTRA = 16
PASSED = 5


def call(kernel, out_shape, in_specs, scratch=(), flops=0, size=0, limit=4, out_specs=None):
    run = pl.pallas_call(
        kernel,
        out_shape=out_shape,
        in_specs=in_specs,
        out_specs=out_specs or jax.tree.map(lambda _: VM, out_shape),
        scratch_shapes=list(scratch),
        cost_estimate=pl.CostEstimate(flops=flops, bytes_accessed=size, transcendentals=0),
        compiler_params=pltpu.CompilerParams(vmem_limit_bytes=limit << 20),
    )

    def placed(*operands):
        return run(
            *(
                pltpu.with_memory_space_constraint(value, pltpu.HBM) if spec is HB else value
                for value, spec in zip(operands, in_specs)
            )
        )

    return placed


def dot(left, right, dims):
    return lax.dot_general(left, right, dims, preferred_element_type=f32)


def step_of(groups, k, near=False):
    if near and groups > 2 and k in (1, 2):
        return groups - 3 + k
    return (groups - k) % groups


def whole_lanes(count):
    return -(-count // 128) * 128


def ahead(me, groups, k, near=False):
    step = step_of(groups, k, near)
    return me ^ step if groups & (groups - 1) == 0 else (me + step) % groups


def behind(me, groups, k, near=False):
    step = step_of(groups, k, near)
    return me ^ step if groups & (groups - 1) == 0 else (me + groups - step) % groups


def step_to(a, b, count):
    step = a ^ b if count & (count - 1) == 0 else (b + count - a) % count
    return (count - step) % count


def next_to(a, j, count):
    step = step_of(count, j)
    return a ^ step if count & (count - 1) == 0 else (a + step) % count


def fetch(sems, *pairs):
    copies = [pltpu.make_async_copy(a, b, sems.at[i]) for i, (a, b) in enumerate(pairs)]
    for copy in copies:
        copy.start()
    return copies


def columns_of(values):
    return values.reshape(-1, values.shape[-1]).T


def pick_rows(chunk, other, part_ref, sources_ref, table_ref, out_ref, order, hits, ready):
    chips, lanes = out_ref.shape[0], out_ref.shape[2]
    _, groups, slots = sources_ref.shape
    nodes = table_ref.shape[1]
    chip, core = part_ref[0] // 2, part_ref[0] % 2
    lane = lax.broadcasted_iota(jnp.int32, (slots, nodes), 1)

    def step(i, last):
        for j in range(chunk):
            order[j] = sources_ref[next_to(chip, i * chunk + j, chips) * 2 + (core ^ other)]
        columns = columns_of(order[...])
        for n in range(chunk * groups):
            hits[n * slots : (n + 1) * slots, :] = jnp.where(
                columns[:, n : n + 1] == lane, 1.0, 0.0
            ).astype(bf16)
        if last:
            ready()
        picked = dot(hits[...], table_ref[:lanes, :], LAST).astype(bf16)
        out_ref[pl.ds(i * chunk, chunk)] = picked.reshape(chunk, groups * slots, -1)

    if chips == chunk:
        step(0, True)
    else:
        ready()
        lax.fori_loop(0, chips // chunk, lambda i, _: step(i, False), None)


def gather_kernel(chunk, part_ref, sources_hbm, features_hbm, *rest):
    extras, (mate_ref, table_ref, sources_ref, *rest) = rest[:PASSED], rest[PASSED:]
    passed, (order, hits, sems) = rest[:PASSED], rest[PASSED:]
    width, nodes = features_hbm.shape
    indices, table, *others = fetch(
        sems,
        (sources_hbm, sources_ref),
        (features_hbm, table_ref.at[pl.ds(0, width), :]),
        *zip(extras, passed),
    )
    table_ref[width : width + EXTRA, :] = jnp.ones((EXTRA, nodes), bf16)
    if table_ref.shape[0] > width + EXTRA:
        table_ref[width + EXTRA :, :] = jnp.zeros(
            (table_ref.shape[0] - width - EXTRA, nodes), bf16
        )
    indices.wait()
    pick_rows(chunk, 1, part_ref, sources_ref, table_ref, mate_ref, order, hits, table.wait)
    for copy in others:
        copy.wait()


def local_kernel(
    chunk,
    me_ref,
    part_ref,
    table_ref,
    sources_ref,
    tiles_ref,
    targets_ref,
    weight_ref,
    ids_vmem,
    counts_vmem,
    sums_ref,
    edges_ref,
    band_ref,
    mine_ref,
    *rest,
):
    blocks, (ids_ref, counts_ref, bands_ref, order, hits, sems) = rest[:-6], rest[-6:]
    parts, groups, slots = targets_ref.shape
    rows = edges_ref.shape[3]
    high = sums_ref.shape[1]
    width = high - EXTRA
    copies = fetch(sems, (ids_vmem, ids_ref), (counts_vmem, counts_ref))
    bands_ref[...] = jnp.zeros_like(bands_ref)
    picked = order.shape[0]
    pick_rows(picked, 0, part_ref, sources_ref, table_ref, mine_ref, order, hits, lambda: None)
    for k in range(1, groups):
        group = ahead(me_ref[0], groups, k, True)
        blocks[k - 1][...] = table_ref[:width, pl.ds(pl.multiple_of(group * rows, rows), rows)]
    for copy in copies:
        copy.wait()

    def place(t, _):
        at = pl.multiple_of(ids_ref[1, t] * rows, rows)
        bands_ref[ids_ref[0, t], :, pl.ds(at, rows)] = tiles_ref[t]
        return 0

    lax.fori_loop(0, tiles_ref.shape[0], place, 0, unroll=tiles_ref.shape[0] <= 16)
    for g in range(groups):
        sums_ref[g] = dot(table_ref[:high, :], bands_ref[g], LAST)
    band_ref[...] = bands_ref[me_ref[0]]
    lane = lax.broadcasted_iota(jnp.int32, (slots, rows), 1)
    slot = lax.broadcasted_iota(jnp.int32, (slots, rows), 0)
    chips, chip, core = parts // 2, part_ref[0] // 2, part_ref[0] % 2

    def connect(i, _):
        first = i * chunk
        target = columns_of(targets_ref[pl.ds(first, chunk)])
        weight = columns_of(weight_ref[pl.ds(first, chunk)].astype(f32))
        for g in range(groups):
            degree = jnp.zeros((1, rows), f32)
            for e in range(chunk):
                n, d = e * groups + g, first + e
                at = step_to(d // 2, chip, chips) * 2 + ((d % 2) ^ core)
                hit = (target[:, n : n + 1] == lane) & (slot < counts_ref[g, d])
                values = jnp.where(hit, weight[:, n : n + 1], 0.0)
                edges_ref[g, at] = values.astype(bf16)
                degree = degree + jnp.sum(values, axis=0, keepdims=True)
            sums_ref[g, width : width + 1, :] += degree
        return 0

    if parts == chunk:
        connect(0, 0)
    else:
        lax.fori_loop(0, parts // chunk, connect, 0)


def hits_kernel(after, me_ref, part_ref, sources_hbm, hits_ref, sources_ref, sem):
    del after
    copy = pltpu.make_async_copy(sources_hbm, sources_ref, sem)
    copy.start()
    parts, groups, slots = sources_ref.shape
    chips, chip, core = parts // 2, part_ref[0] // 2, part_ref[0] % 2
    mine = lax.broadcasted_iota(jnp.int32, sources_ref.shape, 1) == me_ref[0]
    copy.wait()
    picks = jnp.sum(jnp.where(mine, sources_ref[...], 0), axis=1).T
    lane = lax.broadcasted_iota(jnp.int32, (slots, hits_ref.shape[1]), 1)
    for d in range(parts):
        to = ((d % 2) ^ core) * chips + step_to(chip, d // 2, chips)
        hits_ref[pl.ds(pl.multiple_of(to * slots, slots), slots), :] = jnp.where(
            picks[:, d : d + 1] == lane, 1.0, 0.0
        ).astype(bf16)


def mean_kernel(me_ref, sums_ref, edges_ref, *rest):
    groups, parts, slots, rows = edges_ref.shape
    arrived, outs = rest[: parts // 2], rest[parts // 2 :]
    width = outs[0].shape[0]
    for k in range(groups):
        group = ahead(me_ref[0], groups, k)
        span = pl.ds(pl.multiple_of(group * slots, slots), slots)
        far = jnp.concatenate([x[:, span, :].reshape(2 * slots, -1) for x in arrived], axis=0)
        far = dot(far, edges_ref[group].reshape(parts * slots, rows), FIRST)
        total = sums_ref[group, :width, :] + far[:width]
        outs[k][...] = (total / sums_ref[group, width : width + 1, :]).astype(bf16)


def rows_from(me, groups, k, width, near=False):
    return pl.ds(pl.multiple_of(behind(me, groups, k, near) * width, width), width)


def self_kernel(me_ref, features_hbm, weight_hbm, *rest):
    blocks, (out_ref, own_ref, weight_ref, sems) = rest[:-4], rest[-4:]
    groups, (width, rows) = len(blocks) + 1, own_ref.shape
    me = me_ref[0]
    spans = [rows_from(me, groups, k, width, True) for k in range(groups)]
    own, *weights = fetch(
        sems,
        (features_hbm.at[:, pl.ds(pl.multiple_of(me * rows, rows), rows)], own_ref),
        *[(weight_hbm.at[span, :], weight_ref.at[span, :]) for span in spans],
    )
    own.wait()
    total = jnp.zeros(out_ref.shape, f32)
    for block, span, weight in zip((own_ref, *blocks), spans, weights):
        weight.wait()
        total = total + dot(block[...], weight_ref[span, :], FIRST)
    out_ref[...] = total


def add_blocks(total, me, groups, first, blocks, weight_ref):
    width = blocks[0].shape[0]
    for k, block in enumerate(blocks, first):
        total = total + dot(block[...], weight_ref[rows_from(me, groups, k, width), :], FIRST)
    return total


def early_kernel(groups, me_ref, weight_ref, own_ref, *rest):
    blocks, out_ref = rest[:-1], rest[-1]
    out_ref[...] = add_blocks(own_ref[...], me_ref[0], groups, 0, blocks, weight_ref)


def hidden_kernel(groups, me_ref, weight_ref, out_weight_ref, early_ref, *rest):
    blocks, (hidden_ref, *copies) = rest[: groups - 2], rest[groups - 2 :]
    total = add_blocks(early_ref[...], me_ref[0], groups, 2, blocks, weight_ref)
    hidden = jnp.maximum(total, 0.0).astype(bf16)
    hidden_ref[...] = hidden
    projected = dot(out_weight_ref[...], hidden, LAST).astype(bf16)
    for copy in copies:
        copy[...] = projected


def own_kernel(hidden_ref, weight_ref, out_ref, hidden_out, sem):
    copy = pltpu.make_async_copy(hidden_ref, hidden_out, sem)
    copy.start()
    out_ref[...] = dot(weight_ref[...], hidden_ref[...], LAST)
    copy.wait()


def pick_kernel(me_ref, hits_ref, *rest):
    projected, (mine_ref, mate_ref) = rest[:-2], rest[-2:]
    groups, rows = len(projected), projected[0].shape[1]
    total = None
    for k in range(groups):
        at = pl.multiple_of(behind(me_ref[0], groups, k) * rows, rows)
        term = dot(hits_ref[:, pl.ds(at, rows)], projected[k][...], LAST)
        total = term if total is None else total + term
    gap = mine_ref.shape[2] - total.shape[1]
    total = jnp.concatenate([total, jnp.zeros((total.shape[0], gap), f32)], axis=1).astype(bf16)
    half = total.shape[0] // 2
    mine_ref[...] = total[:half].reshape(mine_ref.shape)
    mate_ref[...] = total[half:].reshape(mate_ref.shape)


def pair_kernel(after, mine_ref, got_ref, *rest):
    del after
    chips = mine_ref.shape[0]
    held = (len(rest) - chips) // 2
    for j, out in enumerate(rest[held : held + chips]):
        out[0] = mine_ref[j]
        out[1] = got_ref[j]
    for block, out in zip(rest[:held], rest[held + chips :]):
        out[...] = block[...]


def near_kernel(me_ref, own_ref, sums_ref, band_ref, *rest):
    projected, out_ref = rest[:-1], rest[-1]
    groups, rows = len(projected), projected[0].shape[1]
    me, width = me_ref[0], sums_ref.shape[1] - EXTRA
    total = None
    for k in range(groups):
        at = pl.multiple_of(behind(me, groups, k) * rows, rows)
        term = dot(projected[k][...], band_ref[:, pl.ds(at, rows)], LAST)
        total = term if total is None else total + term
    out_ref[...] = own_ref[...] + total / sums_ref[me, width : width + 1, :]


def last_kernel(me_ref, near_ref, edges_ref, sums_ref, *rest):
    arrived, out_ref = rest[:-1], rest[-1]
    groups, parts, slots, rows = edges_ref.shape
    me, width = me_ref[0], sums_ref.shape[1] - EXTRA
    arrived = jnp.concatenate([x[...].reshape(2 * slots, -1) for x in arrived], axis=0)
    far = dot(arrived, edges_ref[me].reshape(parts * slots, rows), FIRST)
    far = far[: near_ref.shape[0]]
    total = near_ref[...] + far / sums_ref[me, width : width + 1, :]
    out_ref[...] = total.reshape(out_ref.shape)


def on_device(
    features,
    tiles,
    tile_ids,
    sources,
    targets,
    counts,
    edge_weight,
    self_one,
    neigh_one,
    self_out,
    neigh_out,
):
    feature_rows, tile_contents = features[0].T, tiles[0]
    groups, parts = lax.axis_size("feat"), lax.axis_size("dom")
    me = lax.axis_index("feat").astype(jnp.int32).reshape(1)
    part = lax.axis_index("dom").astype(jnp.int32).reshape(1)
    width, nodes = feature_rows.shape
    rows, slots = nodes // groups, sources.shape[3]
    hid, classes = self_one.shape[1], self_out.shape[1]
    chips = parts // 2
    chunk = max(1, min(parts, 512 // (groups * slots)))

    def shape(*dims, dtype=bf16):
        return jax.ShapeDtypeStruct(dims, dtype)

    def shift(blocks, near=False):
        return [
            lax.ppermute(block, "feat", [(i, ahead(i, groups, k, near)) for i in range(groups)])
            for k, block in enumerate(blocks, 1)
        ]

    def to_mate(value):
        return lax.ppermute(value, "dom", [(d, d ^ 1) for d in range(parts)])

    def to_chips(blocks):
        return [blocks[0]] + [
            lax.ppermute(
                blocks[j],
                "dom",
                [(d, next_to(d // 2, j, chips) * 2 + d % 2) for d in range(parts)],
            )
            for j in range(1, chips)
        ]

    picked = min(chips, chunk)
    lanes = whole_lanes(width)
    table_rows = max(lanes, width + EXTRA)
    extras = (tile_contents, targets[0], edge_weight[0], tile_ids[0].T, counts[0].T)
    picking = [
        pltpu.VMEM((picked, groups, slots), jnp.int32),
        pltpu.VMEM((picked * groups * slots, nodes), bf16),
    ]
    mate, table, *passed = call(
        functools.partial(gather_kernel, picked),
        (
            shape(chips, groups * slots, lanes),
            shape(table_rows, nodes),
            shape(parts, groups, slots, dtype=jnp.int32),
        )
        + tuple(shape(*value.shape, dtype=value.dtype) for value in extras),
        [SM, HB, HB] + [HB] * PASSED,
        picking + [pltpu.SemaphoreType.DMA((2 + PASSED,))],
        2 * nodes * nodes * width,
        1 << 20,
    )(part, sources[0], feature_rows, *extras)
    mate = to_mate(mate)
    sums, edges, band, mine, *feature_blocks = call(
        functools.partial(local_kernel, chunk),
        (
            shape(groups, width + EXTRA, rows, dtype=f32),
            shape(groups, parts, slots, rows),
            shape(rows, nodes),
            shape(chips, groups * slots, lanes),
        )
        + (shape(width, rows),) * (groups - 1),
        [SM, SM, VM, VM] + [VM] * PASSED,
        [
            pltpu.SMEM(tile_ids.shape[:0:-1], jnp.int32),
            pltpu.SMEM(counts.shape[:0:-1], jnp.int32),
            pltpu.VMEM((groups, rows, nodes), bf16),
        ]
        + picking
        + [pltpu.SemaphoreType.DMA((2,))],
        2 * nodes * nodes * width,
        1 << 20,
        4 if groups <= 4 else 16,
    )(me, part, table, *passed)
    paired = call(
        pair_kernel,
        (shape(2, groups * slots, lanes),) * chips + (shape(width, rows),) * (groups - 1),
        [VM] * (2 + groups),
        (),
        0,
        1 << 20,
    )(band, mine, mate, *feature_blocks)
    arrived = to_chips(paired[:chips])
    feature_blocks = shift(paired[chips:], near=True)
    means = call(
        mean_kernel,
        (shape(width, rows),) * groups,
        [SM] + [VM] * (2 + chips),
        (),
        2 * nodes * parts * slots * width,
        1 << 20,
    )(me, sums, edges, *arrived)
    means = [means[0]] + shift(means[1:])
    own = call(
        self_kernel,
        shape(rows, hid, dtype=f32),
        [SM, HB, HB] + [VM] * (groups - 1),
        [
            pltpu.VMEM((width, rows), bf16),
            pltpu.VMEM(self_one.shape, bf16),
            pltpu.SemaphoreType.DMA((1 + groups,)),
        ],
        2 * rows * hid * groups * width,
        2 << 20,
    )(me, feature_rows, self_one, *feature_blocks)
    early = call(
        functools.partial(early_kernel, groups),
        shape(rows, hid, dtype=f32),
        [SM] + [VM] * 4,
        (),
        rows * hid * groups * width,
        2 << 20,
    )(me, neigh_one, own, *means[:2])
    hidden, *projected = call(
        functools.partial(hidden_kernel, groups),
        (shape(rows, hid),) + (shape(classes, rows),) * groups,
        [SM] + [VM] * (1 + groups),
        (),
        rows * hid * groups * width,
        2 << 20,
    )(me, neigh_one, neigh_out.T, early, *means[2:])
    hits = call(
        hits_kernel,
        shape(parts * slots, nodes),
        [VM, SM, SM, HB],
        [pltpu.VMEM((parts, groups, slots), jnp.int32), pltpu.SemaphoreType.DMA],
        0,
        1 << 19,
    )(projected[0], me, part, sources[0])
    projected = projected[:1] + shift(projected[1:])
    mine, mate = call(
        pick_kernel,
        (shape(chips, slots, whole_lanes(classes)),) * 2,
        [SM] + [VM] * (1 + groups),
        (),
        2 * parts * slots * nodes * classes,
        1 << 19,
    )(me, hits, *projected)
    mate = to_mate(mate)
    arrived = to_chips(
        call(pair_kernel, (shape(2, slots, whole_lanes(classes)),) * chips, [VM] * 3, (), 0, 1 << 19)(
            hits, mine, mate
        )
    )
    own, hidden = call(
        own_kernel,
        (shape(classes, rows, dtype=f32), shape(rows, hid)),
        [VM, VM],
        [pltpu.SemaphoreType.DMA],
        2 * rows * hid * classes,
        1 << 20,
        out_specs=(VM, HB),
    )(hidden, self_out.T)
    near = call(
        near_kernel,
        shape(classes, rows, dtype=f32),
        [SM] + [VM] * (3 + groups),
        (),
        2 * rows * nodes * classes,
        1 << 19,
    )(me, own, sums, band, *projected)
    logits = call(
        last_kernel,
        shape(classes, 1, rows, dtype=f32),
        [SM] + [VM] * (3 + chips),
        (),
        2 * rows * parts * slots * classes,
        1 << 19,
    )(me, near, edges, sums, *arrived)
    return hidden[None], logits.transpose(1, 0, 2)


def solution(mesh):
    placed = (
        P("dom", None, "feat"),
        P("dom", None, None, None),
        P("dom", None, None),
        P("dom", None, None, None),
        P("dom", None, None, None),
        P("dom", None, None),
        P("dom", None, None, None),
        P(),
        P(),
        P(),
        P(),
    )
    return jax.shard_map(
        on_device,
        mesh=mesh,
        in_specs=placed,
        out_specs=(P("dom", "feat", None), P("dom", None, "feat")),
        check_vma=False,
    )
```

```python
import functools

import jax
import jax.numpy as jnp
from jax import lax
from jax.experimental import pallas as pl
from jax.experimental.pallas import tpu as pltpu
from jax.sharding import PartitionSpec as P

f32 = jnp.float32
bf16 = jnp.bfloat16
VM = pl.BlockSpec(memory_space=pltpu.VMEM)
SM = pl.BlockSpec(memory_space=pltpu.SMEM)
HB = pl.BlockSpec(memory_space=pltpu.HBM)
LAST = (((1,), (1,)), ((), ()))
FIRST = (((0,), (0,)), ((), ()))
EXTRA = 16
PASSED = 5


def call(kernel, out_shape, in_specs, scratch=(), flops=0, size=0, limit=4, out_specs=None):
    run = pl.pallas_call(
        kernel,
        out_shape=out_shape,
        in_specs=in_specs,
        out_specs=out_specs or jax.tree.map(lambda _: VM, out_shape),
        scratch_shapes=list(scratch),
        cost_estimate=pl.CostEstimate(flops=flops, bytes_accessed=size, transcendentals=0),
        compiler_params=pltpu.CompilerParams(vmem_limit_bytes=limit << 20),
    )

    def placed(*operands):
        return run(
            *(
                pltpu.with_memory_space_constraint(value, pltpu.HBM) if spec is HB else value
                for value, spec in zip(operands, in_specs)
            )
        )

    return placed


def dot(left, right, dims):
    return lax.dot_general(left, right, dims, preferred_element_type=f32)


def step_of(groups, k, near=False):
    if near and groups > 2 and k in (1, 2):
        return groups - 3 + k
    return (groups - k) % groups


def whole_lanes(count):
    return -(-count // 128) * 128


def ahead(me, groups, k, near=False):
    step = step_of(groups, k, near)
    return me ^ step if groups & (groups - 1) == 0 else (me + step) % groups


def behind(me, groups, k, near=False):
    step = step_of(groups, k, near)
    return me ^ step if groups & (groups - 1) == 0 else (me + groups - step) % groups


def step_to(a, b, count):
    step = a ^ b if count & (count - 1) == 0 else (b + count - a) % count
    return (count - step) % count


def next_to(a, j, count):
    step = step_of(count, j)
    return a ^ step if count & (count - 1) == 0 else (a + step) % count


def fetch(sems, *pairs):
    copies = [pltpu.make_async_copy(a, b, sems.at[i]) for i, (a, b) in enumerate(pairs)]
    for copy in copies:
        copy.start()
    return copies


def columns_of(values):
    return values.reshape(-1, values.shape[-1]).T


def pick_rows(chunk, other, part_ref, sources_ref, table_ref, out_ref, order, hits, ready):
    chips, lanes = out_ref.shape[0], out_ref.shape[2]
    _, groups, slots = sources_ref.shape
    nodes = table_ref.shape[1]
    chip, core = part_ref[0] // 2, part_ref[0] % 2
    lane = lax.broadcasted_iota(jnp.int32, (slots, nodes), 1)

    def step(i, last):
        for j in range(chunk):
            order[j] = sources_ref[next_to(chip, i * chunk + j, chips) * 2 + (core ^ other)]
        columns = columns_of(order[...])
        for n in range(chunk * groups):
            hits[n * slots : (n + 1) * slots, :] = jnp.where(
                columns[:, n : n + 1] == lane, 1.0, 0.0
            ).astype(bf16)
        if last:
            ready()
        picked = dot(hits[...], table_ref[:lanes, :], LAST).astype(bf16)
        out_ref[pl.ds(i * chunk, chunk)] = picked.reshape(chunk, groups * slots, -1)

    if chips == chunk:
        step(0, True)
    else:
        ready()
        lax.fori_loop(0, chips // chunk, lambda i, _: step(i, False), None)


def gather_kernel(chunk, part_ref, sources_hbm, features_hbm, *rest):
    extras, (mate_ref, table_ref, sources_ref, *rest) = rest[:PASSED], rest[PASSED:]
    passed, (order, hits, sems) = rest[:PASSED], rest[PASSED:]
    width, nodes = features_hbm.shape
    indices, table, *others = fetch(
        sems,
        (sources_hbm, sources_ref),
        (features_hbm, table_ref.at[pl.ds(0, width), :]),
        *zip(extras, passed),
    )
    table_ref[width : width + EXTRA, :] = jnp.ones((EXTRA, nodes), bf16)
    if table_ref.shape[0] > width + EXTRA:
        table_ref[width + EXTRA :, :] = jnp.zeros(
            (table_ref.shape[0] - width - EXTRA, nodes), bf16
        )
    indices.wait()
    pick_rows(chunk, 1, part_ref, sources_ref, table_ref, mate_ref, order, hits, table.wait)
    for copy in others:
        copy.wait()


def local_kernel(
    chunk,
    me_ref,
    part_ref,
    table_ref,
    sources_ref,
    tiles_ref,
    targets_ref,
    weight_ref,
    ids_vmem,
    counts_vmem,
    sums_ref,
    edges_ref,
    band_ref,
    mine_ref,
    *rest,
):
    blocks, (ids_ref, counts_ref, bands_ref, order, hits, sems) = rest[:-6], rest[-6:]
    parts, groups, slots = targets_ref.shape
    rows = edges_ref.shape[3]
    high = sums_ref.shape[1]
    width = high - EXTRA
    copies = fetch(sems, (ids_vmem, ids_ref), (counts_vmem, counts_ref))
    bands_ref[...] = jnp.zeros_like(bands_ref)
    picked = order.shape[0]
    pick_rows(picked, 0, part_ref, sources_ref, table_ref, mine_ref, order, hits, lambda: None)
    for k in range(1, groups):
        group = ahead(me_ref[0], groups, k, True)
        blocks[k - 1][...] = table_ref[:width, pl.ds(pl.multiple_of(group * rows, rows), rows)]
    for copy in copies:
        copy.wait()

    def place(t, _):
        at = pl.multiple_of(ids_ref[1, t] * rows, rows)
        bands_ref[ids_ref[0, t], :, pl.ds(at, rows)] = tiles_ref[t]
        return 0

    lax.fori_loop(0, tiles_ref.shape[0], place, 0, unroll=tiles_ref.shape[0] <= 16)
    for g in range(groups):
        sums_ref[g] = dot(table_ref[:high, :], bands_ref[g], LAST)
    band_ref[...] = bands_ref[me_ref[0]]
    lane = lax.broadcasted_iota(jnp.int32, (slots, rows), 1)
    slot = lax.broadcasted_iota(jnp.int32, (slots, rows), 0)
    chips, chip, core = parts // 2, part_ref[0] // 2, part_ref[0] % 2

    def connect(i, _):
        first = i * chunk
        target = columns_of(targets_ref[pl.ds(first, chunk)])
        weight = columns_of(weight_ref[pl.ds(first, chunk)].astype(f32))
        for g in range(groups):
            degree = jnp.zeros((1, rows), f32)
            for e in range(chunk):
                n, d = e * groups + g, first + e
                at = step_to(d // 2, chip, chips) * 2 + ((d % 2) ^ core)
                hit = (target[:, n : n + 1] == lane) & (slot < counts_ref[g, d])
                values = jnp.where(hit, weight[:, n : n + 1], 0.0)
                edges_ref[g, at] = values.astype(bf16)
                degree = degree + jnp.sum(values, axis=0, keepdims=True)
            sums_ref[g, width : width + 1, :] += degree
        return 0

    if parts == chunk:
        connect(0, 0)
    else:
        lax.fori_loop(0, parts // chunk, connect, 0)


def hits_kernel(after, me_ref, part_ref, sources_hbm, hits_ref, sources_ref, sem):
    del after
    copy = pltpu.make_async_copy(sources_hbm, sources_ref, sem)
    copy.start()
    parts, groups, slots = sources_ref.shape
    chips, chip, core = parts // 2, part_ref[0] // 2, part_ref[0] % 2
    mine = lax.broadcasted_iota(jnp.int32, sources_ref.shape, 1) == me_ref[0]
    copy.wait()
    picks = jnp.sum(jnp.where(mine, sources_ref[...], 0), axis=1).T
    lane = lax.broadcasted_iota(jnp.int32, (slots, hits_ref.shape[1]), 1)
    for d in range(parts):
        to = ((d % 2) ^ core) * chips + step_to(chip, d // 2, chips)
        hits_ref[pl.ds(pl.multiple_of(to * slots, slots), slots), :] = jnp.where(
            picks[:, d : d + 1] == lane, 1.0, 0.0
        ).astype(bf16)


def mean_kernel(me_ref, sums_ref, edges_ref, held_ref, *rest):
    groups, parts, slots, rows = edges_ref.shape
    arrived, outs = rest[: parts // 2], rest[parts // 2 :]
    width = held_ref.shape[0]
    for k in range(groups):
        group = ahead(me_ref[0], groups, k)
        span = pl.ds(pl.multiple_of(group * slots, slots), slots)
        far = jnp.concatenate([x[:, span, :].reshape(2 * slots, -1) for x in arrived], axis=0)
        far = dot(far, edges_ref[group].reshape(parts * slots, rows), FIRST)
        total = sums_ref[group, :width, :] + far[:width]
        outs[k][:width, :] = (total / sums_ref[group, width : width + 1, :]).astype(bf16)
    outs[groups - 1][width:, :] = held_ref[...]


def rows_from(me, groups, k, width, near=False):
    return pl.ds(pl.multiple_of(behind(me, groups, k, near) * width, width), width)


def self_kernel(me_ref, features_hbm, weight_hbm, *rest):
    blocks, (out_ref, near_ref, own_ref, weight_ref, sems) = rest[:-5], rest[-5:]
    groups, (width, rows) = len(blocks) + 2, own_ref.shape
    me = me_ref[0]
    spans = [rows_from(me, groups, k, width, True) for k in range(groups)]
    own, *weights, near = fetch(
        sems,
        (features_hbm.at[:, pl.ds(pl.multiple_of(me * rows, rows), rows)], own_ref),
        *[(weight_hbm.at[span, :], weight_ref.at[span, :]) for span in spans[:-1]],
        (weight_hbm.at[spans[-1], :], near_ref),
    )
    own.wait()
    total = jnp.zeros(out_ref.shape, f32)
    for block, span, weight in zip((own_ref, *blocks), spans, weights):
        weight.wait()
        total = total + dot(block[...], weight_ref[span, :], FIRST)
    out_ref[...] = total
    near.wait()


def add_blocks(total, me, groups, first, blocks, weight_ref, width):
    for k, block in enumerate(blocks, first):
        span = rows_from(me, groups, k, width)
        total = total + dot(block[:width, :], weight_ref[span, :], FIRST)
    return total


def early_kernel(groups, me_ref, weight_ref, own_ref, *rest):
    blocks, out_ref = rest[:-1], rest[-1]
    width = blocks[0].shape[0]
    out_ref[...] = add_blocks(own_ref[...], me_ref[0], groups, 0, blocks, weight_ref, width)


def hidden_kernel(groups, me_ref, weight_ref, near_ref, out_weight_ref, early_ref, *rest):
    blocks, (hidden_ref, *copies) = rest[: groups - 2], rest[groups - 2 :]
    width = near_ref.shape[0]
    total = add_blocks(early_ref[...], me_ref[0], groups, 2, blocks, weight_ref, width)
    total = total + dot(blocks[-1][width:, :], near_ref[...], FIRST)
    hidden = jnp.maximum(total, 0.0).astype(bf16)
    hidden_ref[...] = hidden
    projected = dot(out_weight_ref[...], hidden, LAST).astype(bf16)
    for copy in copies:
        copy[...] = projected


def own_kernel(hidden_ref, weight_ref, out_ref, hidden_out, sem):
    copy = pltpu.make_async_copy(hidden_ref, hidden_out, sem)
    copy.start()
    out_ref[...] = dot(weight_ref[...], hidden_ref[...], LAST)
    copy.wait()


def pick_kernel(me_ref, hits_ref, *rest):
    projected, (mine_ref, mate_ref) = rest[:-2], rest[-2:]
    groups, rows = len(projected), projected[0].shape[1]
    total = None
    for k in range(groups):
        at = pl.multiple_of(behind(me_ref[0], groups, k) * rows, rows)
        term = dot(hits_ref[:, pl.ds(at, rows)], projected[k][...], LAST)
        total = term if total is None else total + term
    gap = mine_ref.shape[2] - total.shape[1]
    total = jnp.concatenate([total, jnp.zeros((total.shape[0], gap), f32)], axis=1).astype(bf16)
    half = total.shape[0] // 2
    mine_ref[...] = total[:half].reshape(mine_ref.shape)
    mate_ref[...] = total[half:].reshape(mate_ref.shape)


def pair_kernel(after, mine_ref, got_ref, *rest):
    del after
    chips = mine_ref.shape[0]
    held = (len(rest) - chips) // 2
    for j, out in enumerate(rest[held : held + chips]):
        out[0] = mine_ref[j]
        out[1] = got_ref[j]
    for block, out in zip(rest[:held], rest[held + chips :]):
        out[...] = block[...]


def near_kernel(me_ref, own_ref, sums_ref, band_ref, *rest):
    projected, out_ref = rest[:-1], rest[-1]
    groups, rows = len(projected), projected[0].shape[1]
    me, width = me_ref[0], sums_ref.shape[1] - EXTRA
    total = None
    for k in range(groups):
        at = pl.multiple_of(behind(me, groups, k) * rows, rows)
        term = dot(projected[k][...], band_ref[:, pl.ds(at, rows)], LAST)
        total = term if total is None else total + term
    out_ref[...] = own_ref[...] + total / sums_ref[me, width : width + 1, :]


def last_kernel(me_ref, near_ref, edges_ref, sums_ref, *rest):
    arrived, out_ref = rest[:-1], rest[-1]
    groups, parts, slots, rows = edges_ref.shape
    me, width = me_ref[0], sums_ref.shape[1] - EXTRA
    arrived = jnp.concatenate([x[...].reshape(2 * slots, -1) for x in arrived], axis=0)
    far = dot(arrived, edges_ref[me].reshape(parts * slots, rows), FIRST)
    far = far[: near_ref.shape[0]]
    total = near_ref[...] + far / sums_ref[me, width : width + 1, :]
    out_ref[...] = total.reshape(out_ref.shape)


def on_device(
    features,
    tiles,
    tile_ids,
    sources,
    targets,
    counts,
    edge_weight,
    self_one,
    neigh_one,
    self_out,
    neigh_out,
):
    feature_rows, tile_contents = features[0].T, tiles[0]
    groups, parts = lax.axis_size("feat"), lax.axis_size("dom")
    me = lax.axis_index("feat").astype(jnp.int32).reshape(1)
    part = lax.axis_index("dom").astype(jnp.int32).reshape(1)
    width, nodes = feature_rows.shape
    rows, slots = nodes // groups, sources.shape[3]
    hid, classes = self_one.shape[1], self_out.shape[1]
    chips = parts // 2
    chunk = max(1, min(parts, 512 // (groups * slots)))

    def shape(*dims, dtype=bf16):
        return jax.ShapeDtypeStruct(dims, dtype)

    def shift(blocks, near=False):
        return [
            lax.ppermute(block, "feat", [(i, ahead(i, groups, k, near)) for i in range(groups)])
            for k, block in enumerate(blocks, 1)
        ]

    def to_mate(value):
        return lax.ppermute(value, "dom", [(d, d ^ 1) for d in range(parts)])

    def to_chips(blocks):
        return [blocks[0]] + [
            lax.ppermute(
                blocks[j],
                "dom",
                [(d, next_to(d // 2, j, chips) * 2 + d % 2) for d in range(parts)],
            )
            for j in range(1, chips)
        ]

    picked = min(chips, chunk)
    lanes = whole_lanes(width)
    table_rows = max(lanes, width + EXTRA)
    extras = (tile_contents, targets[0], edge_weight[0], tile_ids[0].T, counts[0].T)
    picking = [
        pltpu.VMEM((picked, groups, slots), jnp.int32),
        pltpu.VMEM((picked * groups * slots, nodes), bf16),
    ]
    mate, table, *passed = call(
        functools.partial(gather_kernel, picked),
        (
            shape(chips, groups * slots, lanes),
            shape(table_rows, nodes),
            shape(parts, groups, slots, dtype=jnp.int32),
        )
        + tuple(shape(*value.shape, dtype=value.dtype) for value in extras),
        [SM, HB, HB] + [HB] * PASSED,
        picking + [pltpu.SemaphoreType.DMA((2 + PASSED,))],
        2 * nodes * nodes * width,
        1 << 20,
    )(part, sources[0], feature_rows, *extras)
    mate = to_mate(mate)
    sums, edges, band, mine, *feature_blocks = call(
        functools.partial(local_kernel, chunk),
        (
            shape(groups, width + EXTRA, rows, dtype=f32),
            shape(groups, parts, slots, rows),
            shape(rows, nodes),
            shape(chips, groups * slots, lanes),
        )
        + (shape(width, rows),) * (groups - 1),
        [SM, SM, VM, VM] + [VM] * PASSED,
        [
            pltpu.SMEM(tile_ids.shape[:0:-1], jnp.int32),
            pltpu.SMEM(counts.shape[:0:-1], jnp.int32),
            pltpu.VMEM((groups, rows, nodes), bf16),
        ]
        + picking
        + [pltpu.SemaphoreType.DMA((2,))],
        2 * nodes * nodes * width,
        1 << 20,
        4 if groups <= 4 else 16,
    )(me, part, table, *passed)
    *feature_blocks, near_block = feature_blocks
    paired = call(
        pair_kernel,
        (shape(2, groups * slots, lanes),) * chips + (shape(width, rows),) * (groups - 2),
        [VM] * (1 + groups),
        (),
        0,
        1 << 20,
    )(band, mine, mate, *feature_blocks)
    arrived = to_chips(paired[:chips])
    feature_blocks = shift(paired[chips:], near=True)
    means = call(
        mean_kernel,
        (shape(width, rows),) * (groups - 1) + (shape(2 * width, rows),),
        [SM] + [VM] * (3 + chips),
        (),
        2 * nodes * parts * slots * width,
        1 << 20,
    )(me, sums, edges, near_block, *arrived)
    means = [means[0]] + shift(means[1:])
    own, near_weight = call(
        self_kernel,
        (shape(rows, hid, dtype=f32), shape(width, hid)),
        [SM, HB, HB] + [VM] * (groups - 2),
        [
            pltpu.VMEM((width, rows), bf16),
            pltpu.VMEM(self_one.shape, bf16),
            pltpu.SemaphoreType.DMA((1 + groups,)),
        ],
        100 * rows * hid * groups * width,
        100 << 20,
    )(me, feature_rows, self_one, *feature_blocks)
    early = call(
        functools.partial(early_kernel, groups),
        shape(rows, hid, dtype=f32),
        [SM] + [VM] * 4,
        (),
        rows * hid * groups * width,
        2 << 20,
    )(me, neigh_one, own, *means[:2])
    hidden, *projected = call(
        functools.partial(hidden_kernel, groups),
        (shape(rows, hid),) + (shape(classes, rows),) * groups,
        [SM] + [VM] * (2 + groups),
        (),
        rows * hid * groups * width,
        2 << 20,
    )(me, neigh_one, near_weight, neigh_out.T, early, *means[2:])
    hits = call(
        hits_kernel,
        shape(parts * slots, nodes),
        [VM, SM, SM, HB],
        [pltpu.VMEM((parts, groups, slots), jnp.int32), pltpu.SemaphoreType.DMA],
        0,
        1 << 19,
    )(projected[0], me, part, sources[0])
    projected = projected[:1] + shift(projected[1:])
    mine, mate = call(
        pick_kernel,
        (shape(chips, slots, whole_lanes(classes)),) * 2,
        [SM] + [VM] * (1 + groups),
        (),
        2 * parts * slots * nodes * classes,
        1 << 19,
    )(me, hits, *projected)
    mate = to_mate(mate)
    arrived = to_chips(
        call(pair_kernel, (shape(2, slots, whole_lanes(classes)),) * chips, [VM] * 3, (), 0, 1 << 19)(
            hits, mine, mate
        )
    )
    own, hidden = call(
        own_kernel,
        (shape(classes, rows, dtype=f32), shape(rows, hid)),
        [VM, VM],
        [pltpu.SemaphoreType.DMA],
        2 * rows * hid * classes,
        1 << 20,
        out_specs=(VM, HB),
    )(hidden, self_out.T)
    near = call(
        near_kernel,
        shape(classes, rows, dtype=f32),
        [SM] + [VM] * (3 + groups),
        (),
        2 * rows * nodes * classes,
        1 << 19,
    )(me, own, sums, band, *projected)
    logits = call(
        last_kernel,
        shape(classes, 1, rows, dtype=f32),
        [SM] + [VM] * (3 + chips),
        (),
        2 * rows * parts * slots * classes,
        1 << 19,
    )(me, near, edges, sums, *arrived)
    return hidden[None], logits.transpose(1, 0, 2)


def solution(mesh):
    placed = (
        P("dom", None, "feat"),
        P("dom", None, None, None),
        P("dom", None, None),
        P("dom", None, None, None),
        P("dom", None, None, None),
        P("dom", None, None),
        P("dom", None, None, None),
        P(),
        P(),
        P(),
        P(),
    )
    return jax.shard_map(
        on_device,
        mesh=mesh,
        in_specs=placed,
        out_specs=(P("dom", "feat", None), P("dom", None, "feat")),
        check_vma=False,
    )
```

```python
import functools

import jax
import jax.numpy as jnp
from jax import lax
from jax.experimental import pallas as pl
from jax.experimental.pallas import tpu as pltpu
from jax.sharding import PartitionSpec as P

f32 = jnp.float32
bf16 = jnp.bfloat16
VM = pl.BlockSpec(memory_space=pltpu.VMEM)
SM = pl.BlockSpec(memory_space=pltpu.SMEM)
HB = pl.BlockSpec(memory_space=pltpu.HBM)
LAST = (((1,), (1,)), ((), ()))
FIRST = (((0,), (0,)), ((), ()))
EXTRA = 16
PASSED = 5


def call(kernel, out_shape, in_specs, scratch=(), flops=0, size=0, limit=4, out_specs=None):
    run = pl.pallas_call(
        kernel,
        out_shape=out_shape,
        in_specs=in_specs,
        out_specs=out_specs or jax.tree.map(lambda _: VM, out_shape),
        scratch_shapes=list(scratch),
        cost_estimate=pl.CostEstimate(flops=flops, bytes_accessed=size, transcendentals=0),
        compiler_params=pltpu.CompilerParams(vmem_limit_bytes=limit << 20),
    )

    def placed(*operands):
        return run(
            *(
                pltpu.with_memory_space_constraint(value, pltpu.HBM) if spec is HB else value
                for value, spec in zip(operands, in_specs)
            )
        )

    return placed


def dot(left, right, dims):
    return lax.dot_general(left, right, dims, preferred_element_type=f32)


def step_of(groups, k, near=False):
    if near and groups > 2 and k in (1, 2):
        return groups - 3 + k
    return (groups - k) % groups


def whole_lanes(count):
    return -(-count // 128) * 128


def ahead(me, groups, k, near=False):
    step = step_of(groups, k, near)
    return me ^ step if groups & (groups - 1) == 0 else (me + step) % groups


def behind(me, groups, k, near=False):
    step = step_of(groups, k, near)
    return me ^ step if groups & (groups - 1) == 0 else (me + groups - step) % groups


def step_to(a, b, count):
    step = a ^ b if count & (count - 1) == 0 else (b + count - a) % count
    return (count - step) % count


def next_to(a, j, count):
    step = step_of(count, j)
    return a ^ step if count & (count - 1) == 0 else (a + step) % count


def fetch(sems, *pairs):
    copies = [pltpu.make_async_copy(a, b, sems.at[i]) for i, (a, b) in enumerate(pairs)]
    for copy in copies:
        copy.start()
    return copies


def columns_of(values):
    return values.reshape(-1, values.shape[-1]).T


def pick_rows(chunk, other, part_ref, sources_ref, table_ref, out_ref, order, hits, ready):
    chips, lanes = out_ref.shape[0], out_ref.shape[2]
    _, groups, slots = sources_ref.shape
    nodes = table_ref.shape[1]
    chip, core = part_ref[0] // 2, part_ref[0] % 2
    lane = lax.broadcasted_iota(jnp.int32, (slots, nodes), 1)

    def step(i, last):
        for j in range(chunk):
            order[j] = sources_ref[next_to(chip, i * chunk + j, chips) * 2 + (core ^ other)]
        columns = columns_of(order[...])
        for n in range(chunk * groups):
            hits[n * slots : (n + 1) * slots, :] = jnp.where(
                columns[:, n : n + 1] == lane, 1.0, 0.0
            ).astype(bf16)
        if last:
            ready()
        picked = dot(hits[...], table_ref[:lanes, :], LAST).astype(bf16)
        out_ref[pl.ds(i * chunk, chunk)] = picked.reshape(chunk, groups * slots, -1)

    if chips == chunk:
        step(0, True)
    else:
        ready()
        lax.fori_loop(0, chips // chunk, lambda i, _: step(i, False), None)


def gather_kernel(chunk, part_ref, sources_hbm, features_hbm, *rest):
    extras, (mate_ref, table_ref, sources_ref, *rest) = rest[:PASSED], rest[PASSED:]
    passed, (order, hits, sems) = rest[:PASSED], rest[PASSED:]
    width, nodes = features_hbm.shape
    indices, table, *others = fetch(
        sems,
        (sources_hbm, sources_ref),
        (features_hbm, table_ref.at[pl.ds(0, width), :]),
        *zip(extras, passed),
    )
    table_ref[width : width + EXTRA, :] = jnp.ones((EXTRA, nodes), bf16)
    if table_ref.shape[0] > width + EXTRA:
        table_ref[width + EXTRA :, :] = jnp.zeros(
            (table_ref.shape[0] - width - EXTRA, nodes), bf16
        )
    indices.wait()
    pick_rows(chunk, 1, part_ref, sources_ref, table_ref, mate_ref, order, hits, table.wait)
    for copy in others:
        copy.wait()


def local_kernel(
    chunk,
    me_ref,
    part_ref,
    table_ref,
    sources_ref,
    tiles_ref,
    targets_ref,
    weight_ref,
    ids_vmem,
    counts_vmem,
    sums_ref,
    edges_ref,
    band_ref,
    mine_ref,
    *rest,
):
    blocks, (ids_ref, counts_ref, bands_ref, order, hits, sems) = rest[:-6], rest[-6:]
    parts, groups, slots = targets_ref.shape
    rows = edges_ref.shape[3]
    high = sums_ref.shape[1]
    width = high - EXTRA
    copies = fetch(sems, (ids_vmem, ids_ref), (counts_vmem, counts_ref))
    bands_ref[...] = jnp.zeros_like(bands_ref)
    picked = order.shape[0]
    pick_rows(picked, 0, part_ref, sources_ref, table_ref, mine_ref, order, hits, lambda: None)
    for k in range(1, groups):
        group = ahead(me_ref[0], groups, k, True)
        blocks[k - 1][...] = table_ref[:width, pl.ds(pl.multiple_of(group * rows, rows), rows)]
    for copy in copies:
        copy.wait()

    def place(t, _):
        at = pl.multiple_of(ids_ref[1, t] * rows, rows)
        bands_ref[ids_ref[0, t], :, pl.ds(at, rows)] = tiles_ref[t]
        return 0

    lax.fori_loop(0, tiles_ref.shape[0], place, 0, unroll=tiles_ref.shape[0] <= 16)
    for g in range(groups):
        sums_ref[g] = dot(table_ref[:high, :], bands_ref[g], LAST)
    band_ref[...] = bands_ref[me_ref[0]]
    lane = lax.broadcasted_iota(jnp.int32, (slots, rows), 1)
    slot = lax.broadcasted_iota(jnp.int32, (slots, rows), 0)
    chips, chip, core = parts // 2, part_ref[0] // 2, part_ref[0] % 2

    def connect(i, _):
        first = i * chunk
        target = columns_of(targets_ref[pl.ds(first, chunk)])
        weight = columns_of(weight_ref[pl.ds(first, chunk)].astype(f32))
        for g in range(groups):
            degree = jnp.zeros((1, rows), f32)
            for e in range(chunk):
                n, d = e * groups + g, first + e
                at = step_to(d // 2, chip, chips) * 2 + ((d % 2) ^ core)
                hit = (target[:, n : n + 1] == lane) & (slot < counts_ref[g, d])
                values = jnp.where(hit, weight[:, n : n + 1], 0.0)
                edges_ref[g, at] = values.astype(bf16)
                degree = degree + jnp.sum(values, axis=0, keepdims=True)
            sums_ref[g, width : width + 1, :] += degree
        return 0

    if parts == chunk:
        connect(0, 0)
    else:
        lax.fori_loop(0, parts // chunk, connect, 0)


def hits_kernel(after, me_ref, part_ref, sources_hbm, hits_ref, sources_ref, sem):
    del after
    copy = pltpu.make_async_copy(sources_hbm, sources_ref, sem)
    copy.start()
    parts, groups, slots = sources_ref.shape
    chips, chip, core = parts // 2, part_ref[0] // 2, part_ref[0] % 2
    mine = lax.broadcasted_iota(jnp.int32, sources_ref.shape, 1) == me_ref[0]
    copy.wait()
    picks = jnp.sum(jnp.where(mine, sources_ref[...], 0), axis=1).T
    lane = lax.broadcasted_iota(jnp.int32, (slots, hits_ref.shape[1]), 1)
    for d in range(parts):
        to = ((d % 2) ^ core) * chips + step_to(chip, d // 2, chips)
        hits_ref[pl.ds(pl.multiple_of(to * slots, slots), slots), :] = jnp.where(
            picks[:, d : d + 1] == lane, 1.0, 0.0
        ).astype(bf16)


def mean_kernel(first, me_ref, sums_ref, edges_ref, *rest):
    groups, parts, slots, rows = edges_ref.shape
    arrived, outs = rest[: parts // 2], rest[parts // 2 :]
    width = outs[0].shape[0]
    for k, out in enumerate(outs, first):
        group = ahead(me_ref[0], groups, k)
        span = pl.ds(pl.multiple_of(group * slots, slots), slots)
        far = jnp.concatenate([x[:, span, :].reshape(2 * slots, -1) for x in arrived], axis=0)
        far = dot(far, edges_ref[group].reshape(parts * slots, rows), FIRST)
        total = sums_ref[group, :width, :] + far[:width]
        out[...] = (total / sums_ref[group, width : width + 1, :]).astype(bf16)


def own_mean_kernel(after, *rest):
    del after
    mean_kernel(0, *rest)


def rows_from(me, groups, k, width, near=False):
    return pl.ds(pl.multiple_of(behind(me, groups, k, near) * width, width), width)


def self_kernel(me_ref, features_hbm, weight_hbm, *rest):
    blocks, (out_ref, own_ref, weight_ref, sems) = rest[:-4], rest[-4:]
    groups, (width, rows) = len(blocks) + 1, own_ref.shape
    me = me_ref[0]
    spans = [rows_from(me, groups, k, width, True) for k in range(groups)]
    own, *weights = fetch(
        sems,
        (features_hbm.at[:, pl.ds(pl.multiple_of(me * rows, rows), rows)], own_ref),
        *[(weight_hbm.at[span, :], weight_ref.at[span, :]) for span in spans],
    )
    own.wait()
    total = jnp.zeros(out_ref.shape, f32)
    for block, span, weight in zip((own_ref, *blocks), spans, weights):
        weight.wait()
        total = total + dot(block[...], weight_ref[span, :], FIRST)
    out_ref[...] = total


def add_blocks(total, me, groups, first, blocks, weight_ref):
    width = blocks[0].shape[0]
    for k, block in enumerate(blocks, first):
        total = total + dot(block[...], weight_ref[rows_from(me, groups, k, width), :], FIRST)
    return total


def early_kernel(groups, me_ref, weight_ref, own_ref, *rest):
    blocks, out_ref = rest[:-1], rest[-1]
    out_ref[...] = add_blocks(own_ref[...], me_ref[0], groups, 0, blocks, weight_ref)


def hidden_kernel(groups, me_ref, weight_ref, out_weight_ref, early_ref, *rest):
    blocks, (hidden_ref, *copies) = rest[: groups - 2], rest[groups - 2 :]
    total = add_blocks(early_ref[...], me_ref[0], groups, 2, blocks, weight_ref)
    hidden = jnp.maximum(total, 0.0).astype(bf16)
    hidden_ref[...] = hidden
    projected = dot(out_weight_ref[...], hidden, LAST).astype(bf16)
    for copy in copies:
        copy[...] = projected


def own_kernel(hidden_ref, weight_ref, out_ref, hidden_out, sem):
    copy = pltpu.make_async_copy(hidden_ref, hidden_out, sem)
    copy.start()
    out_ref[...] = dot(weight_ref[...], hidden_ref[...], LAST)
    copy.wait()


def pick_blocks(groups, first, me_ref, hits_ref, blocks):
    rows = blocks[0].shape[1]
    total = None
    for k, block in enumerate(blocks, first):
        at = pl.multiple_of(behind(me_ref[0], groups, k) * rows, rows)
        term = dot(hits_ref[:, pl.ds(at, rows)], block[...], LAST)
        total = term if total is None else total + term
    return total


def early_pick_kernel(groups, me_ref, hits_ref, *rest):
    rest[-1][...] = pick_blocks(groups, 0, me_ref, hits_ref, rest[:-1])


def pick_kernel(groups, me_ref, hits_ref, early_ref, *rest):
    projected, (mine_ref, mate_ref) = rest[:-2], rest[-2:]
    total = early_ref[...] + pick_blocks(groups, 2, me_ref, hits_ref, projected)
    gap = mine_ref.shape[2] - total.shape[1]
    total = jnp.concatenate([total, jnp.zeros((total.shape[0], gap), f32)], axis=1).astype(bf16)
    half = total.shape[0] // 2
    mine_ref[...] = total[:half].reshape(mine_ref.shape)
    mate_ref[...] = total[half:].reshape(mate_ref.shape)


def pair_kernel(after, mine_ref, got_ref, *rest):
    del after
    chips = mine_ref.shape[0]
    held = (len(rest) - chips) // 2
    for j, out in enumerate(rest[held : held + chips]):
        out[0] = mine_ref[j]
        out[1] = got_ref[j]
    for block, out in zip(rest[:held], rest[held + chips :]):
        out[...] = block[...]


def near_kernel(me_ref, own_ref, sums_ref, band_ref, *rest):
    projected, out_ref = rest[:-1], rest[-1]
    groups, rows = len(projected), projected[0].shape[1]
    me, width = me_ref[0], sums_ref.shape[1] - EXTRA
    total = None
    for k in range(groups):
        at = pl.multiple_of(behind(me, groups, k) * rows, rows)
        term = dot(projected[k][...], band_ref[:, pl.ds(at, rows)], LAST)
        total = term if total is None else total + term
    out_ref[...] = own_ref[...] + total / sums_ref[me, width : width + 1, :]


def last_kernel(first, me_ref, near_ref, edges_ref, sums_ref, *rest):
    arrived, out_ref = rest[:-1], rest[-1]
    _, _, slots, rows = edges_ref.shape
    me, width = me_ref[0], sums_ref.shape[1] - EXTRA
    count = 2 * len(arrived)
    arrived = jnp.concatenate([x[...].reshape(2 * slots, -1) for x in arrived], axis=0)
    edges = edges_ref[me, 2 * first : 2 * first + count].reshape(count * slots, rows)
    far = dot(arrived, edges, FIRST)[: near_ref.shape[0]]
    total = near_ref[...] + far / sums_ref[me, width : width + 1, :]
    out_ref[...] = total.reshape(out_ref.shape)


def on_device(
    features,
    tiles,
    tile_ids,
    sources,
    targets,
    counts,
    edge_weight,
    self_one,
    neigh_one,
    self_out,
    neigh_out,
):
    feature_rows, tile_contents = features[0].T, tiles[0]
    groups, parts = lax.axis_size("feat"), lax.axis_size("dom")
    me = lax.axis_index("feat").astype(jnp.int32).reshape(1)
    part = lax.axis_index("dom").astype(jnp.int32).reshape(1)
    width, nodes = feature_rows.shape
    rows, slots = nodes // groups, sources.shape[3]
    hid, classes = self_one.shape[1], self_out.shape[1]
    chips = parts // 2
    chunk = max(1, min(parts, 512 // (groups * slots)))

    def shape(*dims, dtype=bf16):
        return jax.ShapeDtypeStruct(dims, dtype)

    def shift(blocks, near=False):
        return [
            lax.ppermute(block, "feat", [(i, ahead(i, groups, k, near)) for i in range(groups)])
            for k, block in enumerate(blocks, 1)
        ]

    def to_mate(value):
        return lax.ppermute(value, "dom", [(d, d ^ 1) for d in range(parts)])

    def to_chips(blocks):
        return [blocks[0]] + [
            lax.ppermute(
                blocks[j],
                "dom",
                [(d, next_to(d // 2, j, chips) * 2 + d % 2) for d in range(parts)],
            )
            for j in range(1, chips)
        ]

    picked = min(chips, chunk)
    lanes = whole_lanes(width)
    table_rows = max(lanes, width + EXTRA)
    extras = (tile_contents, targets[0], edge_weight[0], tile_ids[0].T, counts[0].T)
    picking = [
        pltpu.VMEM((picked, groups, slots), jnp.int32),
        pltpu.VMEM((picked * groups * slots, nodes), bf16),
    ]
    mate, table, *passed = call(
        functools.partial(gather_kernel, picked),
        (
            shape(chips, groups * slots, lanes),
            shape(table_rows, nodes),
            shape(parts, groups, slots, dtype=jnp.int32),
        )
        + tuple(shape(*value.shape, dtype=value.dtype) for value in extras),
        [SM, HB, HB] + [HB] * PASSED,
        picking + [pltpu.SemaphoreType.DMA((2 + PASSED,))],
        2 * nodes * nodes * width,
        1 << 20,
    )(part, sources[0], feature_rows, *extras)
    mate = to_mate(mate)
    sums, edges, band, mine, *feature_blocks = call(
        functools.partial(local_kernel, chunk),
        (
            shape(groups, width + EXTRA, rows, dtype=f32),
            shape(groups, parts, slots, rows),
            shape(rows, nodes),
            shape(chips, groups * slots, lanes),
        )
        + (shape(width, rows),) * (groups - 1),
        [SM, SM, VM, VM] + [VM] * PASSED,
        [
            pltpu.SMEM(tile_ids.shape[:0:-1], jnp.int32),
            pltpu.SMEM(counts.shape[:0:-1], jnp.int32),
            pltpu.VMEM((groups, rows, nodes), bf16),
        ]
        + picking
        + [pltpu.SemaphoreType.DMA((2,))],
        2 * nodes * nodes * width,
        1 << 20,
        4 if groups <= 4 else 16,
    )(me, part, table, *passed)
    paired = call(
        pair_kernel,
        (shape(2, groups * slots, lanes),) * chips + (shape(width, rows),) * (groups - 1),
        [VM] * (2 + groups),
        (),
        0,
        1 << 20,
    )(band, mine, mate, *feature_blocks)
    arrived = to_chips(paired[:chips])
    feature_blocks = shift(paired[chips:], near=True)
    means = call(
        functools.partial(mean_kernel, 1),
        (shape(width, rows),) * (groups - 1),
        [SM] + [VM] * (2 + chips),
        (),
        2 * nodes * parts * slots * width,
        1 << 20,
    )(me, sums, edges, *arrived)
    means = shift(means)
    own = call(
        self_kernel,
        shape(rows, hid, dtype=f32),
        [SM, HB, HB] + [VM] * (groups - 1),
        [
            pltpu.VMEM((width, rows), bf16),
            pltpu.VMEM(self_one.shape, bf16),
            pltpu.SemaphoreType.DMA((1 + groups,)),
        ],
        2 * rows * hid * groups * width,
        2 << 20,
    )(me, feature_rows, self_one, *feature_blocks)
    own_mean = call(
        own_mean_kernel,
        (shape(width, rows),),
        [VM, SM] + [VM] * (2 + chips),
        (),
        2 * rows * parts * slots * width,
        1 << 18,
    )(own, me, sums, edges, *arrived)
    means = [*own_mean, *means]
    early = call(
        functools.partial(early_kernel, groups),
        shape(rows, hid, dtype=f32),
        [SM] + [VM] * 4,
        (),
        rows * hid * groups * width,
        2 << 20,
    )(me, neigh_one, own, *means[:2])
    hidden, *projected = call(
        functools.partial(hidden_kernel, groups),
        (shape(rows, hid),) + (shape(classes, rows),) * groups,
        [SM] + [VM] * (1 + groups),
        (),
        rows * hid * groups * width,
        2 << 20,
    )(me, neigh_one, neigh_out.T, early, *means[2:])
    hits = call(
        hits_kernel,
        shape(parts * slots, nodes),
        [VM, SM, SM, HB],
        [pltpu.VMEM((parts, groups, slots), jnp.int32), pltpu.SemaphoreType.DMA],
        0,
        1 << 19,
    )(projected[0], me, part, sources[0])
    projected = projected[:1] + shift(projected[1:])
    early = call(
        functools.partial(early_pick_kernel, groups),
        shape(parts * slots, classes, dtype=f32),
        [SM] + [VM] * 3,
        (),
        parts * slots * nodes * classes,
        1 << 18,
    )(me, hits, *projected[:2])
    mine, mate = call(
        functools.partial(pick_kernel, groups),
        (shape(chips, slots, whole_lanes(classes)),) * 2,
        [SM] + [VM] * groups,
        (),
        parts * slots * nodes * classes,
        1 << 18,
    )(me, hits, early, *projected[2:])
    mate = to_mate(mate)
    arrived = to_chips(
        call(pair_kernel, (shape(2, slots, whole_lanes(classes)),) * chips, [VM] * 3, (), 0, 1 << 19)(
            hits, mine, mate
        )
    )
    own, hidden = call(
        own_kernel,
        (shape(classes, rows, dtype=f32), shape(rows, hid)),
        [VM, VM],
        [pltpu.SemaphoreType.DMA],
        2 * rows * hid * classes,
        1 << 20,
        out_specs=(VM, HB),
    )(hidden, self_out.T)
    near = call(
        near_kernel,
        shape(classes, rows, dtype=f32),
        [SM] + [VM] * (3 + groups),
        (),
        2 * rows * nodes * classes,
        1 << 19,
    )(me, own, sums, band, *projected)
    half = chips // 2
    near = call(
        functools.partial(last_kernel, 0),
        shape(classes, rows, dtype=f32),
        [SM] + [VM] * (3 + half),
        (),
        rows * parts * slots * classes,
        1 << 18,
    )(me, near, edges, sums, *arrived[:half])
    logits = call(
        functools.partial(last_kernel, half),
        shape(classes, 1, rows, dtype=f32),
        [SM] + [VM] * (3 + chips - half),
        (),
        rows * parts * slots * classes,
        1 << 19,
    )(me, near, edges, sums, *arrived[half:])
    return hidden[None], logits.transpose(1, 0, 2)


def solution(mesh):
    placed = (
        P("dom", None, "feat"),
        P("dom", None, None, None),
        P("dom", None, None),
        P("dom", None, None, None),
        P("dom", None, None, None),
        P("dom", None, None),
        P("dom", None, None, None),
        P(),
        P(),
        P(),
        P(),
    )
    return jax.shard_map(
        on_device,
        mesh=mesh,
        in_specs=placed,
        out_specs=(P("dom", "feat", None), P("dom", None, "feat")),
        check_vma=False,
    )
```

```python
import functools

import jax
import jax.numpy as jnp
from jax import lax
from jax.experimental import pallas as pl
from jax.experimental.pallas import tpu as pltpu
from jax.sharding import PartitionSpec as P

f32 = jnp.float32
bf16 = jnp.bfloat16
VM = pl.BlockSpec(memory_space=pltpu.VMEM)
SM = pl.BlockSpec(memory_space=pltpu.SMEM)
HB = pl.BlockSpec(memory_space=pltpu.HBM)
LAST = (((1,), (1,)), ((), ()))
FIRST = (((0,), (0,)), ((), ()))
EXTRA = 16
PASSED = 5


def call(kernel, out_shape, in_specs, scratch=(), flops=0, size=0, limit=4, out_specs=None):
    run = pl.pallas_call(
        kernel,
        out_shape=out_shape,
        in_specs=in_specs,
        out_specs=out_specs or jax.tree.map(lambda _: VM, out_shape),
        scratch_shapes=list(scratch),
        cost_estimate=pl.CostEstimate(flops=flops, bytes_accessed=size, transcendentals=0),
        compiler_params=pltpu.CompilerParams(vmem_limit_bytes=limit << 20),
    )

    def placed(*operands):
        return run(
            *(
                pltpu.with_memory_space_constraint(value, pltpu.HBM) if spec is HB else value
                for value, spec in zip(operands, in_specs)
            )
        )

    return placed


def dot(left, right, dims):
    return lax.dot_general(left, right, dims, preferred_element_type=f32)


def step_of(groups, k, near=False):
    if near and groups > 2 and k in (1, 2):
        return groups - 3 + k
    return (groups - k) % groups


def whole_lanes(count):
    return -(-count // 128) * 128


def ahead(me, groups, k, near=False):
    step = step_of(groups, k, near)
    return me ^ step if groups & (groups - 1) == 0 else (me + step) % groups


def behind(me, groups, k, near=False):
    step = step_of(groups, k, near)
    return me ^ step if groups & (groups - 1) == 0 else (me + groups - step) % groups


def step_to(a, b, count):
    step = a ^ b if count & (count - 1) == 0 else (b + count - a) % count
    return (count - step) % count


def next_to(a, j, count):
    step = step_of(count, j)
    return a ^ step if count & (count - 1) == 0 else (a + step) % count


def fetch(sems, *pairs):
    copies = [pltpu.make_async_copy(a, b, sems.at[i]) for i, (a, b) in enumerate(pairs)]
    for copy in copies:
        copy.start()
    return copies


def columns_of(values):
    return values.reshape(-1, values.shape[-1]).T


def pick_rows(chunk, other, part_ref, sources_ref, table_ref, out_ref, order, hits, ready):
    chips, lanes = out_ref.shape[0], out_ref.shape[2]
    _, groups, slots = sources_ref.shape
    nodes = table_ref.shape[1]
    chip, core = part_ref[0] // 2, part_ref[0] % 2
    lane = lax.broadcasted_iota(jnp.int32, (slots, nodes), 1)

    def step(i, last):
        for j in range(chunk):
            order[j] = sources_ref[next_to(chip, i * chunk + j, chips) * 2 + (core ^ other)]
        columns = columns_of(order[...])
        for n in range(chunk * groups):
            hits[n * slots : (n + 1) * slots, :] = jnp.where(
                columns[:, n : n + 1] == lane, 1.0, 0.0
            ).astype(bf16)
        if last:
            ready()
        picked = dot(hits[...], table_ref[:lanes, :], LAST).astype(bf16)
        out_ref[pl.ds(i * chunk, chunk)] = picked.reshape(chunk, groups * slots, -1)

    if chips == chunk:
        step(0, True)
    else:
        ready()
        lax.fori_loop(0, chips // chunk, lambda i, _: step(i, False), None)


def gather_kernel(chunk, part_ref, sources_hbm, features_hbm, *rest):
    extras, (mate_ref, table_ref, sources_ref, *rest) = rest[:PASSED], rest[PASSED:]
    passed, (order, hits, sems) = rest[:PASSED], rest[PASSED:]
    width, nodes = features_hbm.shape
    indices, table, *others = fetch(
        sems,
        (sources_hbm, sources_ref),
        (features_hbm, table_ref.at[pl.ds(0, width), :]),
        *zip(extras, passed),
    )
    table_ref[width : width + EXTRA, :] = jnp.ones((EXTRA, nodes), bf16)
    if table_ref.shape[0] > width + EXTRA:
        table_ref[width + EXTRA :, :] = jnp.zeros(
            (table_ref.shape[0] - width - EXTRA, nodes), bf16
        )
    indices.wait()
    pick_rows(chunk, 1, part_ref, sources_ref, table_ref, mate_ref, order, hits, table.wait)
    for copy in others:
        copy.wait()


def local_kernel(
    chunk,
    me_ref,
    part_ref,
    table_ref,
    sources_ref,
    tiles_ref,
    targets_ref,
    weight_ref,
    ids_vmem,
    counts_vmem,
    sums_ref,
    edges_ref,
    band_ref,
    mine_ref,
    *rest,
):
    blocks, (ids_ref, counts_ref, bands_ref, order, hits, sems) = rest[:-6], rest[-6:]
    parts, groups, slots = targets_ref.shape
    rows = edges_ref.shape[3]
    high = sums_ref.shape[1]
    width = high - EXTRA
    copies = fetch(sems, (ids_vmem, ids_ref), (counts_vmem, counts_ref))
    bands_ref[...] = jnp.zeros_like(bands_ref)
    picked = order.shape[0]
    pick_rows(picked, 0, part_ref, sources_ref, table_ref, mine_ref, order, hits, lambda: None)
    for k in range(1, groups):
        group = ahead(me_ref[0], groups, k, True)
        blocks[k - 1][...] = table_ref[:width, pl.ds(pl.multiple_of(group * rows, rows), rows)]
    for copy in copies:
        copy.wait()

    def place(t, _):
        at = pl.multiple_of(ids_ref[1, t] * rows, rows)
        bands_ref[ids_ref[0, t], :, pl.ds(at, rows)] = tiles_ref[t]
        return 0

    lax.fori_loop(0, tiles_ref.shape[0], place, 0, unroll=tiles_ref.shape[0] <= 16)
    for g in range(groups):
        sums_ref[g] = dot(table_ref[:high, :], bands_ref[g], LAST)
    band_ref[...] = bands_ref[me_ref[0]]
    lane = lax.broadcasted_iota(jnp.int32, (slots, rows), 1)
    slot = lax.broadcasted_iota(jnp.int32, (slots, rows), 0)
    chips, chip, core = parts // 2, part_ref[0] // 2, part_ref[0] % 2

    def connect(i, _):
        first = i * chunk
        target = columns_of(targets_ref[pl.ds(first, chunk)])
        weight = columns_of(weight_ref[pl.ds(first, chunk)].astype(f32))
        for g in range(groups):
            degree = jnp.zeros((1, rows), f32)
            for e in range(chunk):
                n, d = e * groups + g, first + e
                at = step_to(d // 2, chip, chips) * 2 + ((d % 2) ^ core)
                hit = (target[:, n : n + 1] == lane) & (slot < counts_ref[g, d])
                values = jnp.where(hit, weight[:, n : n + 1], 0.0)
                edges_ref[g, at] = values.astype(bf16)
                degree = degree + jnp.sum(values, axis=0, keepdims=True)
            sums_ref[g, width : width + 1, :] += degree
        return 0

    if parts == chunk:
        connect(0, 0)
    else:
        lax.fori_loop(0, parts // chunk, connect, 0)


def hits_kernel(after, me_ref, part_ref, sources_hbm, hits_ref, sources_ref, sem):
    del after
    copy = pltpu.make_async_copy(sources_hbm, sources_ref, sem)
    copy.start()
    parts, groups, slots = sources_ref.shape
    chips, chip, core = parts // 2, part_ref[0] // 2, part_ref[0] % 2
    mine = lax.broadcasted_iota(jnp.int32, sources_ref.shape, 1) == me_ref[0]
    copy.wait()
    picks = jnp.sum(jnp.where(mine, sources_ref[...], 0), axis=1).T
    lane = lax.broadcasted_iota(jnp.int32, (slots, hits_ref.shape[1]), 1)
    for d in range(parts):
        to = ((d % 2) ^ core) * chips + step_to(chip, d // 2, chips)
        hits_ref[pl.ds(pl.multiple_of(to * slots, slots), slots), :] = jnp.where(
            picks[:, d : d + 1] == lane, 1.0, 0.0
        ).astype(bf16)


def mean_kernel(first, me_ref, sums_ref, edges_ref, *rest):
    groups, parts, slots, rows = edges_ref.shape
    arrived, outs = rest[: parts // 2], rest[parts // 2 :]
    width = outs[0].shape[0]
    for k, out in enumerate(outs, first):
        group = ahead(me_ref[0], groups, k)
        span = pl.ds(pl.multiple_of(group * slots, slots), slots)
        far = jnp.concatenate([x[:, span, :].reshape(2 * slots, -1) for x in arrived], axis=0)
        far = dot(far, edges_ref[group].reshape(parts * slots, rows), FIRST)
        total = sums_ref[group, :width, :] + far[:width]
        out[...] = (total / sums_ref[group, width : width + 1, :]).astype(bf16)


def own_mean_kernel(after, *rest):
    del after
    mean_kernel(0, *rest)


def rows_from(me, groups, k, width, near=False):
    return pl.ds(pl.multiple_of(behind(me, groups, k, near) * width, width), width)


def self_kernel(me_ref, features_hbm, weight_hbm, *rest):
    blocks, (out_ref, own_ref, weight_ref, sems) = rest[:-4], rest[-4:]
    groups, (width, rows) = len(blocks) + 1, own_ref.shape
    me = me_ref[0]
    spans = [rows_from(me, groups, k, width, True) for k in range(groups)]
    own, *weights = fetch(
        sems,
        (features_hbm.at[:, pl.ds(pl.multiple_of(me * rows, rows), rows)], own_ref),
        *[(weight_hbm.at[span, :], weight_ref.at[span, :]) for span in spans],
    )
    own.wait()
    total = jnp.zeros(out_ref.shape, f32)
    for block, span, weight in zip((own_ref, *blocks), spans, weights):
        weight.wait()
        total = total + dot(block[...], weight_ref[span, :], FIRST)
    out_ref[...] = total


def add_blocks(total, me, groups, first, blocks, weight_ref):
    width = blocks[0].shape[0]
    for k, block in enumerate(blocks, first):
        total = total + dot(block[...], weight_ref[rows_from(me, groups, k, width), :], FIRST)
    return total


def early_kernel(groups, me_ref, weight_ref, own_ref, *rest):
    blocks, out_ref = rest[:-1], rest[-1]
    out_ref[...] = add_blocks(own_ref[...], me_ref[0], groups, 0, blocks, weight_ref)


def hidden_kernel(groups, me_ref, weight_ref, out_weight_ref, early_ref, *rest):
    blocks, (hidden_ref, *copies) = rest[: groups - 2], rest[groups - 2 :]
    total = add_blocks(early_ref[...], me_ref[0], groups, 2, blocks, weight_ref)
    hidden = jnp.maximum(total, 0.0).astype(bf16)
    hidden_ref[...] = hidden
    projected = dot(out_weight_ref[...], hidden, LAST).astype(bf16)
    for copy in copies:
        copy[...] = projected


def own_kernel(hidden_ref, weight_ref, out_ref, hidden_out, sem):
    copy = pltpu.make_async_copy(hidden_ref, hidden_out, sem)
    copy.start()
    out_ref[...] = dot(weight_ref[...], hidden_ref[...], LAST)
    copy.wait()


def pick_blocks(groups, first, me_ref, hits_ref, blocks):
    rows = blocks[0].shape[1]
    total = None
    for k, block in enumerate(blocks, first):
        at = pl.multiple_of(behind(me_ref[0], groups, k) * rows, rows)
        term = dot(hits_ref[:, pl.ds(at, rows)], block[...], LAST)
        total = term if total is None else total + term
    return total


def early_pick_kernel(groups, me_ref, hits_ref, *rest):
    rest[-1][...] = pick_blocks(groups, 0, me_ref, hits_ref, rest[:-1])


def pick_kernel(groups, me_ref, hits_ref, early_ref, *rest):
    projected, (mine_ref, mate_ref) = rest[:-2], rest[-2:]
    total = early_ref[...] + pick_blocks(groups, 2, me_ref, hits_ref, projected)
    gap = mine_ref.shape[2] - total.shape[1]
    total = jnp.concatenate([total, jnp.zeros((total.shape[0], gap), f32)], axis=1).astype(bf16)
    half = total.shape[0] // 2
    mine_ref[...] = total[:half].reshape(mine_ref.shape)
    mate_ref[...] = total[half:].reshape(mate_ref.shape)


def pair_kernel(after, mine_ref, got_ref, *rest):
    del after
    chips = mine_ref.shape[0]
    held = (len(rest) - chips) // 2
    for j, out in enumerate(rest[held : held + chips]):
        out[0] = mine_ref[j]
        out[1] = got_ref[j]
    for block, out in zip(rest[:held], rest[held + chips :]):
        out[...] = block[...]


def near_kernel(me_ref, own_ref, sums_ref, band_ref, *rest):
    projected, out_ref = rest[:-1], rest[-1]
    groups, rows = len(projected), projected[0].shape[1]
    me, width = me_ref[0], sums_ref.shape[1] - EXTRA
    total = None
    for k in range(groups):
        at = pl.multiple_of(behind(me, groups, k) * rows, rows)
        term = dot(projected[k][...], band_ref[:, pl.ds(at, rows)], LAST)
        total = term if total is None else total + term
    out_ref[...] = own_ref[...] + total / sums_ref[me, width : width + 1, :]


def last_kernel(first, me_ref, near_ref, edges_ref, sums_ref, *rest):
    arrived, out_ref = rest[:-1], rest[-1]
    _, _, slots, rows = edges_ref.shape
    me, width = me_ref[0], sums_ref.shape[1] - EXTRA
    count = 2 * len(arrived)
    arrived = jnp.concatenate([x[...].reshape(2 * slots, -1) for x in arrived], axis=0)
    edges = edges_ref[me, 2 * first : 2 * first + count].reshape(count * slots, rows)
    far = dot(arrived, edges, FIRST)[: near_ref.shape[0]]
    out_ref[...] = near_ref[...] + far / sums_ref[me, width : width + 1, :]


def scores_kernel(first, me_ref, *rest):
    rest, (out_hbm, scores_ref, sem) = rest[:-3], rest[-3:]
    last_kernel(first, me_ref, *rest, scores_ref)
    copy = pltpu.make_async_copy(scores_ref, out_hbm.at[:, 0, :], sem)
    copy.start()
    copy.wait()


def on_device(
    features,
    tiles,
    tile_ids,
    sources,
    targets,
    counts,
    edge_weight,
    self_one,
    neigh_one,
    self_out,
    neigh_out,
):
    feature_rows, tile_contents = features[0].T, tiles[0]
    groups, parts = lax.axis_size("feat"), lax.axis_size("dom")
    me = lax.axis_index("feat").astype(jnp.int32).reshape(1)
    part = lax.axis_index("dom").astype(jnp.int32).reshape(1)
    width, nodes = feature_rows.shape
    rows, slots = nodes // groups, sources.shape[3]
    hid, classes = self_one.shape[1], self_out.shape[1]
    chips = parts // 2
    chunk = max(1, min(parts, 512 // (groups * slots)))

    def shape(*dims, dtype=bf16):
        return jax.ShapeDtypeStruct(dims, dtype)

    def shift(blocks, near=False):
        return [
            lax.ppermute(block, "feat", [(i, ahead(i, groups, k, near)) for i in range(groups)])
            for k, block in enumerate(blocks, 1)
        ]

    def to_mate(value):
        return lax.ppermute(value, "dom", [(d, d ^ 1) for d in range(parts)])

    def to_chips(blocks):
        return [blocks[0]] + [
            lax.ppermute(
                blocks[j],
                "dom",
                [(d, next_to(d // 2, j, chips) * 2 + d % 2) for d in range(parts)],
            )
            for j in range(1, chips)
        ]

    picked = min(chips, chunk)
    lanes = whole_lanes(width)
    table_rows = max(lanes, width + EXTRA)
    extras = (tile_contents, targets[0], edge_weight[0], tile_ids[0].T, counts[0].T)
    picking = [
        pltpu.VMEM((picked, groups, slots), jnp.int32),
        pltpu.VMEM((picked * groups * slots, nodes), bf16),
    ]
    mate, table, *passed = call(
        functools.partial(gather_kernel, picked),
        (
            shape(chips, groups * slots, lanes),
            shape(table_rows, nodes),
            shape(parts, groups, slots, dtype=jnp.int32),
        )
        + tuple(shape(*value.shape, dtype=value.dtype) for value in extras),
        [SM, HB, HB] + [HB] * PASSED,
        picking + [pltpu.SemaphoreType.DMA((2 + PASSED,))],
        2 * nodes * nodes * width,
        1 << 20,
    )(part, sources[0], feature_rows, *extras)
    mate = to_mate(mate)
    sums, edges, band, mine, *feature_blocks = call(
        functools.partial(local_kernel, chunk),
        (
            shape(groups, width + EXTRA, rows, dtype=f32),
            shape(groups, parts, slots, rows),
            shape(rows, nodes),
            shape(chips, groups * slots, lanes),
        )
        + (shape(width, rows),) * (groups - 1),
        [SM, SM, VM, VM] + [VM] * PASSED,
        [
            pltpu.SMEM(tile_ids.shape[:0:-1], jnp.int32),
            pltpu.SMEM(counts.shape[:0:-1], jnp.int32),
            pltpu.VMEM((groups, rows, nodes), bf16),
        ]
        + picking
        + [pltpu.SemaphoreType.DMA((2,))],
        2 * nodes * nodes * width,
        1 << 20,
        4 if groups <= 4 else 16,
    )(me, part, table, *passed)
    paired = call(
        pair_kernel,
        (shape(2, groups * slots, lanes),) * chips + (shape(width, rows),) * (groups - 1),
        [VM] * (2 + groups),
        (),
        0,
        1 << 20,
    )(band, mine, mate, *feature_blocks)
    arrived = to_chips(paired[:chips])
    feature_blocks = shift(paired[chips:], near=True)
    means = call(
        functools.partial(mean_kernel, 1),
        (shape(width, rows),) * (groups - 1),
        [SM] + [VM] * (2 + chips),
        (),
        2 * nodes * parts * slots * width,
        1 << 20,
    )(me, sums, edges, *arrived)
    means = shift(means)
    own = call(
        self_kernel,
        shape(rows, hid, dtype=f32),
        [SM, HB, HB] + [VM] * (groups - 1),
        [
            pltpu.VMEM((width, rows), bf16),
            pltpu.VMEM(self_one.shape, bf16),
            pltpu.SemaphoreType.DMA((1 + groups,)),
        ],
        2 * rows * hid * groups * width,
        2 << 20,
    )(me, feature_rows, self_one, *feature_blocks)
    own_mean = call(
        own_mean_kernel,
        (shape(width, rows),),
        [VM, SM] + [VM] * (2 + chips),
        (),
        2 * rows * parts * slots * width,
        1 << 18,
    )(own, me, sums, edges, *arrived)
    means = [*own_mean, *means]
    early = call(
        functools.partial(early_kernel, groups),
        shape(rows, hid, dtype=f32),
        [SM] + [VM] * 4,
        (),
        rows * hid * groups * width,
        2 << 20,
    )(me, neigh_one, own, *means[:2])
    hidden, *projected = call(
        functools.partial(hidden_kernel, groups),
        (shape(rows, hid),) + (shape(classes, rows),) * groups,
        [SM] + [VM] * (1 + groups),
        (),
        rows * hid * groups * width,
        2 << 20,
    )(me, neigh_one, neigh_out.T, early, *means[2:])
    hits = call(
        hits_kernel,
        shape(parts * slots, nodes),
        [VM, SM, SM, HB],
        [pltpu.VMEM((parts, groups, slots), jnp.int32), pltpu.SemaphoreType.DMA],
        0,
        1 << 19,
    )(projected[0], me, part, sources[0])
    projected = projected[:1] + shift(projected[1:])
    early = call(
        functools.partial(early_pick_kernel, groups),
        shape(parts * slots, classes, dtype=f32),
        [SM] + [VM] * 3,
        (),
        parts * slots * nodes * classes,
        1 << 18,
    )(me, hits, *projected[:2])
    mine, mate = call(
        functools.partial(pick_kernel, groups),
        (shape(chips, slots, whole_lanes(classes)),) * 2,
        [SM] + [VM] * groups,
        (),
        parts * slots * nodes * classes,
        1 << 18,
    )(me, hits, early, *projected[2:])
    mate = to_mate(mate)
    arrived = to_chips(
        call(pair_kernel, (shape(2, slots, whole_lanes(classes)),) * chips, [VM] * 3, (), 0, 1 << 19)(
            hits, mine, mate
        )
    )
    own, hidden = call(
        own_kernel,
        (shape(classes, rows, dtype=f32), shape(rows, hid)),
        [VM, VM],
        [pltpu.SemaphoreType.DMA],
        2 * rows * hid * classes,
        1 << 20,
        out_specs=(VM, HB),
    )(hidden, self_out.T)
    near = call(
        near_kernel,
        shape(classes, rows, dtype=f32),
        [SM] + [VM] * (3 + groups),
        (),
        2 * rows * nodes * classes,
        1 << 19,
    )(me, own, sums, band, *projected)
    half = chips // 2
    near = call(
        functools.partial(last_kernel, 0),
        shape(classes, rows, dtype=f32),
        [SM] + [VM] * (3 + half),
        (),
        rows * parts * slots * classes,
        1 << 18,
    )(me, near, edges, sums, *arrived[:half])
    logits = call(
        functools.partial(scores_kernel, half),
        shape(classes, 1, rows, dtype=f32),
        [SM] + [VM] * (3 + chips - half),
        [pltpu.VMEM((classes, rows), f32), pltpu.SemaphoreType.DMA],
        rows * parts * slots * classes,
        1 << 19,
        out_specs=HB,
    )(me, near, edges, sums, *arrived[half:])
    return hidden[None], logits.transpose(1, 0, 2)


def solution(mesh):
    placed = (
        P("dom", None, "feat"),
        P("dom", None, None, None),
        P("dom", None, None),
        P("dom", None, None, None),
        P("dom", None, None, None),
        P("dom", None, None),
        P("dom", None, None, None),
        P(),
        P(),
        P(),
        P(),
    )
    return jax.shard_map(
        on_device,
        mesh=mesh,
        in_specs=placed,
        out_specs=(P("dom", "feat", None), P("dom", None, "feat")),
        check_vma=False,
    )
```

```python
import functools

import jax
import jax.numpy as jnp
from jax import lax
from jax.experimental import pallas as pl
from jax.experimental.pallas import tpu as pltpu
from jax.sharding import PartitionSpec as P

f32 = jnp.float32
bf16 = jnp.bfloat16
VM = pl.BlockSpec(memory_space=pltpu.VMEM)
SM = pl.BlockSpec(memory_space=pltpu.SMEM)
HB = pl.BlockSpec(memory_space=pltpu.HBM)
LAST = (((1,), (1,)), ((), ()))
FIRST = (((0,), (0,)), ((), ()))
EXTRA = 16
PASSED = 5


class Place:
    def __init__(self, axis):
        self.axis = axis

    def __getitem__(self, _):
        return lax.axis_index(self.axis).astype(jnp.int32)


def call(kernel, out_shape, in_specs, scratch=(), flops=0, size=0, limit=4, out_specs=None):
    def placed(*operands):
        places = [value if isinstance(value, Place) else None for value in operands]
        arrays = [
            pltpu.with_memory_space_constraint(value, pltpu.HBM) if spec is HB else value
            for value, spec in zip(operands, in_specs)
            if spec is not SM
        ]

        def body(*refs):
            rest = iter(refs)
            first = [place if place is not None else next(rest) for place in places]
            kernel(*first, *rest)

        return pl.pallas_call(
            body,
            out_shape=out_shape,
            in_specs=[spec for spec in in_specs if spec is not SM],
            out_specs=out_specs or jax.tree.map(lambda _: VM, out_shape),
            scratch_shapes=list(scratch),
            cost_estimate=pl.CostEstimate(flops=flops, bytes_accessed=size, transcendentals=0),
            compiler_params=pltpu.CompilerParams(vmem_limit_bytes=limit << 20),
        )(*arrays)

    return placed


def dot(left, right, dims):
    return lax.dot_general(left, right, dims, preferred_element_type=f32)


def step_of(groups, k, near=False):
    if near and groups > 2 and k in (1, 2):
        return groups - 3 + k
    return (groups - k) % groups


def whole_lanes(count):
    return -(-count // 128) * 128


def ahead(me, groups, k, near=False):
    step = step_of(groups, k, near)
    return me ^ step if groups & (groups - 1) == 0 else (me + step) % groups


def behind(me, groups, k, near=False):
    step = step_of(groups, k, near)
    return me ^ step if groups & (groups - 1) == 0 else (me + groups - step) % groups


def step_to(a, b, count):
    step = a ^ b if count & (count - 1) == 0 else (b + count - a) % count
    return (count - step) % count


def next_to(a, j, count):
    step = step_of(count, j)
    return a ^ step if count & (count - 1) == 0 else (a + step) % count


def fetch(sems, *pairs):
    copies = [pltpu.make_async_copy(a, b, sems.at[i]) for i, (a, b) in enumerate(pairs)]
    for copy in copies:
        copy.start()
    return copies


def columns_of(values):
    return values.reshape(-1, values.shape[-1]).T


def pick_rows(chunk, other, part_ref, sources_ref, table_ref, out_ref, order, hits, ready):
    chips, lanes = out_ref.shape[0], out_ref.shape[2]
    _, groups, slots = sources_ref.shape
    nodes = table_ref.shape[1]
    chip, core = part_ref[0] // 2, part_ref[0] % 2
    lane = lax.broadcasted_iota(jnp.int32, (slots, nodes), 1)

    def step(i, last):
        for j in range(chunk):
            order[j] = sources_ref[next_to(chip, i * chunk + j, chips) * 2 + (core ^ other)]
        columns = columns_of(order[...])
        for n in range(chunk * groups):
            hits[n * slots : (n + 1) * slots, :] = jnp.where(
                columns[:, n : n + 1] == lane, 1.0, 0.0
            ).astype(bf16)
        if last:
            ready()
        picked = dot(hits[...], table_ref[:lanes, :], LAST).astype(bf16)
        out_ref[pl.ds(i * chunk, chunk)] = picked.reshape(chunk, groups * slots, -1)

    if chips == chunk:
        step(0, True)
    else:
        ready()
        lax.fori_loop(0, chips // chunk, lambda i, _: step(i, False), None)


def gather_kernel(chunk, part_ref, sources_hbm, features_hbm, *rest):
    extras, (mate_ref, table_ref, sources_ref, *rest) = rest[:PASSED], rest[PASSED:]
    passed, (order, hits, sems) = rest[:PASSED], rest[PASSED:]
    width, nodes = features_hbm.shape
    indices, table, *others = fetch(
        sems,
        (sources_hbm, sources_ref),
        (features_hbm, table_ref.at[pl.ds(0, width), :]),
        *zip(extras, passed),
    )
    table_ref[width : width + EXTRA, :] = jnp.ones((EXTRA, nodes), bf16)
    if table_ref.shape[0] > width + EXTRA:
        table_ref[width + EXTRA :, :] = jnp.zeros(
            (table_ref.shape[0] - width - EXTRA, nodes), bf16
        )
    indices.wait()
    pick_rows(chunk, 1, part_ref, sources_ref, table_ref, mate_ref, order, hits, table.wait)
    for copy in others:
        copy.wait()


def local_kernel(
    chunk,
    me_ref,
    part_ref,
    table_ref,
    sources_ref,
    tiles_ref,
    targets_ref,
    weight_ref,
    ids_vmem,
    counts_vmem,
    sums_ref,
    edges_ref,
    band_ref,
    mine_ref,
    *rest,
):
    blocks, (ids_ref, counts_ref, bands_ref, order, hits, sems) = rest[:-6], rest[-6:]
    parts, groups, slots = targets_ref.shape
    rows = edges_ref.shape[3]
    high = sums_ref.shape[1]
    width = high - EXTRA
    copies = fetch(sems, (ids_vmem, ids_ref), (counts_vmem, counts_ref))
    bands_ref[...] = jnp.zeros_like(bands_ref)
    picked = order.shape[0]
    pick_rows(picked, 0, part_ref, sources_ref, table_ref, mine_ref, order, hits, lambda: None)
    for k in range(1, groups):
        group = ahead(me_ref[0], groups, k, True)
        blocks[k - 1][...] = table_ref[:width, pl.ds(pl.multiple_of(group * rows, rows), rows)]
    for copy in copies:
        copy.wait()

    def place(t, _):
        at = pl.multiple_of(ids_ref[1, t] * rows, rows)
        bands_ref[ids_ref[0, t], :, pl.ds(at, rows)] = tiles_ref[t]
        return 0

    lax.fori_loop(0, tiles_ref.shape[0], place, 0, unroll=tiles_ref.shape[0] <= 16)
    for g in range(groups):
        sums_ref[g] = dot(table_ref[:high, :], bands_ref[g], LAST)
    band_ref[...] = bands_ref[me_ref[0]]
    lane = lax.broadcasted_iota(jnp.int32, (slots, rows), 1)
    slot = lax.broadcasted_iota(jnp.int32, (slots, rows), 0)
    chips, chip, core = parts // 2, part_ref[0] // 2, part_ref[0] % 2

    def connect(i, _):
        first = i * chunk
        target = columns_of(targets_ref[pl.ds(first, chunk)])
        weight = columns_of(weight_ref[pl.ds(first, chunk)].astype(f32))
        for g in range(groups):
            degree = jnp.zeros((1, rows), f32)
            for e in range(chunk):
                n, d = e * groups + g, first + e
                at = step_to(d // 2, chip, chips) * 2 + ((d % 2) ^ core)
                hit = (target[:, n : n + 1] == lane) & (slot < counts_ref[g, d])
                values = jnp.where(hit, weight[:, n : n + 1], 0.0)
                edges_ref[g, at] = values.astype(bf16)
                degree = degree + jnp.sum(values, axis=0, keepdims=True)
            sums_ref[g, width : width + 1, :] += degree
        return 0

    if parts == chunk:
        connect(0, 0)
    else:
        lax.fori_loop(0, parts // chunk, connect, 0)


def hits_kernel(after, me_ref, part_ref, sources_hbm, hits_ref, sources_ref, sem):
    del after
    copy = pltpu.make_async_copy(sources_hbm, sources_ref, sem)
    copy.start()
    parts, groups, slots = sources_ref.shape
    chips, chip, core = parts // 2, part_ref[0] // 2, part_ref[0] % 2
    mine = lax.broadcasted_iota(jnp.int32, sources_ref.shape, 1) == me_ref[0]
    copy.wait()
    picks = jnp.sum(jnp.where(mine, sources_ref[...], 0), axis=1).T
    lane = lax.broadcasted_iota(jnp.int32, (slots, hits_ref.shape[1]), 1)
    for d in range(parts):
        to = ((d % 2) ^ core) * chips + step_to(chip, d // 2, chips)
        hits_ref[pl.ds(pl.multiple_of(to * slots, slots), slots), :] = jnp.where(
            picks[:, d : d + 1] == lane, 1.0, 0.0
        ).astype(bf16)


def mean_kernel(first, me_ref, sums_ref, edges_ref, *rest):
    groups, parts, slots, rows = edges_ref.shape
    arrived, outs = rest[: parts // 2], rest[parts // 2 :]
    width = outs[0].shape[0]
    for k, out in enumerate(outs, first):
        group = ahead(me_ref[0], groups, k)
        span = pl.ds(pl.multiple_of(group * slots, slots), slots)
        far = jnp.concatenate([x[:, span, :].reshape(2 * slots, -1) for x in arrived], axis=0)
        far = dot(far, edges_ref[group].reshape(parts * slots, rows), FIRST)
        total = sums_ref[group, :width, :] + far[:width]
        out[...] = (total / sums_ref[group, width : width + 1, :]).astype(bf16)


def own_mean_kernel(after, *rest):
    del after
    mean_kernel(0, *rest)


def rows_from(me, groups, k, width, near=False):
    return pl.ds(pl.multiple_of(behind(me, groups, k, near) * width, width), width)


def self_kernel(me_ref, features_hbm, weight_hbm, *rest):
    blocks, (out_ref, own_ref, weight_ref, sems) = rest[:-4], rest[-4:]
    groups, (width, rows) = len(blocks) + 1, own_ref.shape
    me = me_ref[0]
    spans = [rows_from(me, groups, k, width, True) for k in range(groups)]
    own, *weights = fetch(
        sems,
        (features_hbm.at[:, pl.ds(pl.multiple_of(me * rows, rows), rows)], own_ref),
        *[(weight_hbm.at[span, :], weight_ref.at[span, :]) for span in spans],
    )
    own.wait()
    total = jnp.zeros(out_ref.shape, f32)
    for block, span, weight in zip((own_ref, *blocks), spans, weights):
        weight.wait()
        total = total + dot(block[...], weight_ref[span, :], FIRST)
    out_ref[...] = total


def add_blocks(total, me, groups, first, blocks, weight_ref):
    width = blocks[0].shape[0]
    for k, block in enumerate(blocks, first):
        total = total + dot(block[...], weight_ref[rows_from(me, groups, k, width), :], FIRST)
    return total


def early_kernel(groups, me_ref, weight_ref, own_ref, *rest):
    blocks, out_ref = rest[:-1], rest[-1]
    out_ref[...] = add_blocks(own_ref[...], me_ref[0], groups, 0, blocks, weight_ref)


def hidden_kernel(groups, me_ref, weight_ref, out_weight_ref, early_ref, *rest):
    blocks, (hidden_ref, *copies) = rest[: groups - 2], rest[groups - 2 :]
    total = add_blocks(early_ref[...], me_ref[0], groups, 2, blocks, weight_ref)
    hidden = jnp.maximum(total, 0.0).astype(bf16)
    hidden_ref[...] = hidden
    projected = dot(out_weight_ref[...], hidden, LAST).astype(bf16)
    for copy in copies:
        copy[...] = projected


def own_kernel(hidden_ref, weight_ref, out_ref, hidden_out, sem):
    copy = pltpu.make_async_copy(hidden_ref, hidden_out, sem)
    copy.start()
    out_ref[...] = dot(weight_ref[...], hidden_ref[...], LAST)
    copy.wait()


def pick_blocks(groups, first, me_ref, hits_ref, blocks):
    rows = blocks[0].shape[1]
    total = None
    for k, block in enumerate(blocks, first):
        at = pl.multiple_of(behind(me_ref[0], groups, k) * rows, rows)
        term = dot(hits_ref[:, pl.ds(at, rows)], block[...], LAST)
        total = term if total is None else total + term
    return total


def early_pick_kernel(groups, me_ref, hits_ref, *rest):
    rest[-1][...] = pick_blocks(groups, 0, me_ref, hits_ref, rest[:-1])


def pick_kernel(groups, me_ref, hits_ref, early_ref, *rest):
    projected, (mine_ref, mate_ref) = rest[:-2], rest[-2:]
    total = early_ref[...] + pick_blocks(groups, 2, me_ref, hits_ref, projected)
    gap = mine_ref.shape[2] - total.shape[1]
    total = jnp.concatenate([total, jnp.zeros((total.shape[0], gap), f32)], axis=1).astype(bf16)
    half = total.shape[0] // 2
    mine_ref[...] = total[:half].reshape(mine_ref.shape)
    mate_ref[...] = total[half:].reshape(mate_ref.shape)


def pair_kernel(after, mine_ref, got_ref, *rest):
    del after
    chips = mine_ref.shape[0]
    held = (len(rest) - chips) // 2
    for j, out in enumerate(rest[held : held + chips]):
        out[0] = mine_ref[j]
        out[1] = got_ref[j]
    for block, out in zip(rest[:held], rest[held + chips :]):
        out[...] = block[...]


def near_kernel(me_ref, own_ref, sums_ref, band_ref, *rest):
    projected, out_ref = rest[:-1], rest[-1]
    groups, rows = len(projected), projected[0].shape[1]
    me, width = me_ref[0], sums_ref.shape[1] - EXTRA
    total = None
    for k in range(groups):
        at = pl.multiple_of(behind(me, groups, k) * rows, rows)
        term = dot(projected[k][...], band_ref[:, pl.ds(at, rows)], LAST)
        total = term if total is None else total + term
    out_ref[...] = own_ref[...] + total / sums_ref[me, width : width + 1, :]


def last_kernel(first, me_ref, near_ref, edges_ref, sums_ref, *rest):
    arrived, out_ref = rest[:-1], rest[-1]
    _, _, slots, rows = edges_ref.shape
    me, width = me_ref[0], sums_ref.shape[1] - EXTRA
    count = 2 * len(arrived)
    arrived = jnp.concatenate([x[...].reshape(2 * slots, -1) for x in arrived], axis=0)
    edges = edges_ref[me, 2 * first : 2 * first + count].reshape(count * slots, rows)
    far = dot(arrived, edges, FIRST)[: near_ref.shape[0]]
    out_ref[...] = near_ref[...] + far / sums_ref[me, width : width + 1, :]


def scores_kernel(first, me_ref, *rest):
    rest, (out_hbm, scores_ref, sem) = rest[:-3], rest[-3:]
    last_kernel(first, me_ref, *rest, scores_ref)
    copy = pltpu.make_async_copy(scores_ref, out_hbm.at[:, 0, :], sem)
    copy.start()
    copy.wait()


def on_device(
    features,
    tiles,
    tile_ids,
    sources,
    targets,
    counts,
    edge_weight,
    self_one,
    neigh_one,
    self_out,
    neigh_out,
):
    feature_rows, tile_contents = features[0].T, tiles[0]
    groups, parts = lax.axis_size("feat"), lax.axis_size("dom")
    me, part = Place("feat"), Place("dom")
    width, nodes = feature_rows.shape
    rows, slots = nodes // groups, sources.shape[3]
    hid, classes = self_one.shape[1], self_out.shape[1]
    chips = parts // 2
    chunk = max(1, min(parts, 512 // (groups * slots)))

    def shape(*dims, dtype=bf16):
        return jax.ShapeDtypeStruct(dims, dtype)

    def shift(blocks, near=False):
        return [
            lax.ppermute(block, "feat", [(i, ahead(i, groups, k, near)) for i in range(groups)])
            for k, block in enumerate(blocks, 1)
        ]

    def to_mate(value):
        return lax.ppermute(value, "dom", [(d, d ^ 1) for d in range(parts)])

    def to_chips(blocks):
        return [blocks[0]] + [
            lax.ppermute(
                blocks[j],
                "dom",
                [(d, next_to(d // 2, j, chips) * 2 + d % 2) for d in range(parts)],
            )
            for j in range(1, chips)
        ]

    picked = min(chips, chunk)
    lanes = whole_lanes(width)
    table_rows = max(lanes, width + EXTRA)
    extras = (tile_contents, targets[0], edge_weight[0], tile_ids[0].T, counts[0].T)
    picking = [
        pltpu.VMEM((picked, groups, slots), jnp.int32),
        pltpu.VMEM((picked * groups * slots, nodes), bf16),
    ]
    mate, table, *passed = call(
        functools.partial(gather_kernel, picked),
        (
            shape(chips, groups * slots, lanes),
            shape(table_rows, nodes),
            shape(parts, groups, slots, dtype=jnp.int32),
        )
        + tuple(shape(*value.shape, dtype=value.dtype) for value in extras),
        [SM, HB, HB] + [HB] * PASSED,
        picking + [pltpu.SemaphoreType.DMA((2 + PASSED,))],
        2 * nodes * nodes * width,
        1 << 20,
    )(part, sources[0], feature_rows, *extras)
    mate = to_mate(mate)
    sums, edges, band, mine, *feature_blocks = call(
        functools.partial(local_kernel, chunk),
        (
            shape(groups, width + EXTRA, rows, dtype=f32),
            shape(groups, parts, slots, rows),
            shape(rows, nodes),
            shape(chips, groups * slots, lanes),
        )
        + (shape(width, rows),) * (groups - 1),
        [SM, SM, VM, VM] + [VM] * PASSED,
        [
            pltpu.SMEM(tile_ids.shape[:0:-1], jnp.int32),
            pltpu.SMEM(counts.shape[:0:-1], jnp.int32),
            pltpu.VMEM((groups, rows, nodes), bf16),
        ]
        + picking
        + [pltpu.SemaphoreType.DMA((2,))],
        2 * nodes * nodes * width,
        1 << 20,
        4 if groups <= 4 else 16,
    )(me, part, table, *passed)
    paired = call(
        pair_kernel,
        (shape(2, groups * slots, lanes),) * chips + (shape(width, rows),) * (groups - 1),
        [VM] * (2 + groups),
        (),
        0,
        1 << 20,
    )(band, mine, mate, *feature_blocks)
    arrived = to_chips(paired[:chips])
    feature_blocks = shift(paired[chips:], near=True)
    means = call(
        functools.partial(mean_kernel, 1),
        (shape(width, rows),) * (groups - 1),
        [SM] + [VM] * (2 + chips),
        (),
        2 * nodes * parts * slots * width,
        1 << 20,
    )(me, sums, edges, *arrived)
    means = shift(means)
    own = call(
        self_kernel,
        shape(rows, hid, dtype=f32),
        [SM, HB, HB] + [VM] * (groups - 1),
        [
            pltpu.VMEM((width, rows), bf16),
            pltpu.VMEM(self_one.shape, bf16),
            pltpu.SemaphoreType.DMA((1 + groups,)),
        ],
        2 * rows * hid * groups * width,
        2 << 20,
    )(me, feature_rows, self_one, *feature_blocks)
    own_mean = call(
        own_mean_kernel,
        (shape(width, rows),),
        [VM, SM] + [VM] * (2 + chips),
        (),
        2 * rows * parts * slots * width,
        1 << 18,
    )(own, me, sums, edges, *arrived)
    means = [*own_mean, *means]
    early = call(
        functools.partial(early_kernel, groups),
        shape(rows, hid, dtype=f32),
        [SM] + [VM] * 4,
        (),
        rows * hid * groups * width,
        2 << 20,
    )(me, neigh_one, own, *means[:2])
    hidden, *projected = call(
        functools.partial(hidden_kernel, groups),
        (shape(rows, hid),) + (shape(classes, rows),) * groups,
        [SM] + [VM] * (1 + groups),
        (),
        rows * hid * groups * width,
        2 << 20,
    )(me, neigh_one, neigh_out.T, early, *means[2:])
    hits = call(
        hits_kernel,
        shape(parts * slots, nodes),
        [VM, SM, SM, HB],
        [pltpu.VMEM((parts, groups, slots), jnp.int32), pltpu.SemaphoreType.DMA],
        0,
        1 << 19,
    )(projected[0], me, part, sources[0])
    projected = projected[:1] + shift(projected[1:])
    early = call(
        functools.partial(early_pick_kernel, groups),
        shape(parts * slots, classes, dtype=f32),
        [SM] + [VM] * 3,
        (),
        parts * slots * nodes * classes,
        1 << 18,
    )(me, hits, *projected[:2])
    mine, mate = call(
        functools.partial(pick_kernel, groups),
        (shape(chips, slots, whole_lanes(classes)),) * 2,
        [SM] + [VM] * groups,
        (),
        parts * slots * nodes * classes,
        1 << 18,
    )(me, hits, early, *projected[2:])
    mate = to_mate(mate)
    arrived = to_chips(
        call(pair_kernel, (shape(2, slots, whole_lanes(classes)),) * chips, [VM] * 3, (), 0, 1 << 19)(
            hits, mine, mate
        )
    )
    own, hidden = call(
        own_kernel,
        (shape(classes, rows, dtype=f32), shape(rows, hid)),
        [VM, VM],
        [pltpu.SemaphoreType.DMA],
        2 * rows * hid * classes,
        1 << 20,
        out_specs=(VM, HB),
    )(hidden, self_out.T)
    near = call(
        near_kernel,
        shape(classes, rows, dtype=f32),
        [SM] + [VM] * (3 + groups),
        (),
        2 * rows * nodes * classes,
        1 << 19,
    )(me, own, sums, band, *projected)
    half = chips // 2
    near = call(
        functools.partial(last_kernel, 0),
        shape(classes, rows, dtype=f32),
        [SM] + [VM] * (3 + half),
        (),
        rows * parts * slots * classes,
        1 << 18,
    )(me, near, edges, sums, *arrived[:half])
    logits = call(
        functools.partial(scores_kernel, half),
        shape(classes, 1, rows, dtype=f32),
        [SM] + [VM] * (3 + chips - half),
        [pltpu.VMEM((classes, rows), f32), pltpu.SemaphoreType.DMA],
        rows * parts * slots * classes,
        1 << 19,
        out_specs=HB,
    )(me, near, edges, sums, *arrived[half:])
    return hidden[None], logits.transpose(1, 0, 2)


def solution(mesh):
    placed = (
        P("dom", None, "feat"),
        P("dom", None, None, None),
        P("dom", None, None),
        P("dom", None, None, None),
        P("dom", None, None, None),
        P("dom", None, None),
        P("dom", None, None, None),
        P(),
        P(),
        P(),
        P(),
    )
    return jax.shard_map(
        on_device,
        mesh=mesh,
        in_specs=placed,
        out_specs=(P("dom", "feat", None), P("dom", None, "feat")),
        check_vma=False,
    )
```

```python
import functools

import jax
import jax.numpy as jnp
from jax import lax
from jax.experimental import pallas as pl
from jax.experimental.pallas import tpu as pltpu
from jax.sharding import PartitionSpec as P

f32 = jnp.float32
bf16 = jnp.bfloat16
VM = pl.BlockSpec(memory_space=pltpu.VMEM)
SM = pl.BlockSpec(memory_space=pltpu.SMEM)
HB = pl.BlockSpec(memory_space=pltpu.HBM)
LAST = (((1,), (1,)), ((), ()))
FIRST = (((0,), (0,)), ((), ()))
EXTRA = 16
PASSED = 5


def call(kernel, out_shape, in_specs, scratch=(), flops=0, size=0, limit=4, out_specs=None):
    run = pl.pallas_call(
        kernel,
        out_shape=out_shape,
        in_specs=in_specs,
        out_specs=out_specs or jax.tree.map(lambda _: VM, out_shape),
        scratch_shapes=list(scratch),
        cost_estimate=pl.CostEstimate(flops=flops, bytes_accessed=size, transcendentals=0),
        compiler_params=pltpu.CompilerParams(vmem_limit_bytes=limit << 20),
    )

    def placed(*operands):
        return run(
            *(
                pltpu.with_memory_space_constraint(value, pltpu.HBM) if spec is HB else value
                for value, spec in zip(operands, in_specs)
            )
        )

    return placed


def dot(left, right, dims):
    return lax.dot_general(left, right, dims, preferred_element_type=f32)


MEANS, FEATURES, SCORES = range(3)


def step_of(count, k):
    return (count - k) % count


def shift_of(groups, k, what):
    if what == SCORES or k < 2:
        return k
    return groups - 1 if k == 2 else groups - k + 1


def whole_lanes(count):
    return -(-count // 128) * 128


def ahead(me, groups, k, what=MEANS):
    if what != MEANS:
        return (me + shift_of(groups, k, what)) % groups
    return next_to(me, k, groups)


def behind(me, groups, k, what=MEANS):
    if what != MEANS:
        return (me + groups - shift_of(groups, k, what)) % groups
    step = step_of(groups, k)
    return me ^ step if groups & (groups - 1) == 0 else (me + groups - step) % groups


def step_to(a, b, count):
    step = a ^ b if count & (count - 1) == 0 else (b + count - a) % count
    return (count - step) % count


def next_to(a, j, count):
    step = step_of(count, j)
    return a ^ step if count & (count - 1) == 0 else (a + step) % count


def fetch(sems, *pairs):
    copies = [pltpu.make_async_copy(a, b, sems.at[i]) for i, (a, b) in enumerate(pairs)]
    for copy in copies:
        copy.start()
    return copies


def columns_of(values):
    return values.reshape(-1, values.shape[-1]).T


def pick_rows(chunk, other, part_ref, sources_ref, table_ref, out_ref, order, hits, ready):
    chips, lanes = out_ref.shape[0], out_ref.shape[2]
    _, groups, slots = sources_ref.shape
    nodes = table_ref.shape[1]
    chip, core = part_ref[0] // 2, part_ref[0] % 2
    lane = lax.broadcasted_iota(jnp.int32, (slots, nodes), 1)

    def step(i, last):
        for j in range(chunk):
            order[j] = sources_ref[next_to(chip, i * chunk + j, chips) * 2 + (core ^ other)]
        columns = columns_of(order[...])
        for n in range(chunk * groups):
            hits[n * slots : (n + 1) * slots, :] = jnp.where(
                columns[:, n : n + 1] == lane, 1.0, 0.0
            ).astype(bf16)
        if last:
            ready()
        picked = dot(hits[...], table_ref[:lanes, :], LAST).astype(bf16)
        out_ref[pl.ds(i * chunk, chunk)] = picked.reshape(chunk, groups * slots, -1)

    if chips == chunk:
        step(0, True)
    else:
        ready()
        lax.fori_loop(0, chips // chunk, lambda i, _: step(i, False), None)


def gather_kernel(chunk, part_ref, sources_hbm, features_hbm, *rest):
    extras, (mate_ref, table_ref, sources_ref, *rest) = rest[:PASSED], rest[PASSED:]
    passed, (order, hits, sems) = rest[:PASSED], rest[PASSED:]
    width, nodes = features_hbm.shape
    indices, table, *others = fetch(
        sems,
        (sources_hbm, sources_ref),
        (features_hbm, table_ref.at[pl.ds(0, width), :]),
        *zip(extras, passed),
    )
    table_ref[width : width + EXTRA, :] = jnp.ones((EXTRA, nodes), bf16)
    if table_ref.shape[0] > width + EXTRA:
        table_ref[width + EXTRA :, :] = jnp.zeros(
            (table_ref.shape[0] - width - EXTRA, nodes), bf16
        )
    indices.wait()
    pick_rows(chunk, 1, part_ref, sources_ref, table_ref, mate_ref, order, hits, table.wait)
    for copy in others:
        copy.wait()


def local_kernel(
    chunk,
    me_ref,
    part_ref,
    table_ref,
    sources_ref,
    tiles_ref,
    targets_ref,
    weight_ref,
    ids_vmem,
    counts_vmem,
    sums_ref,
    edges_ref,
    band_ref,
    mine_ref,
    *rest,
):
    blocks, (ids_ref, counts_ref, bands_ref, order, hits, sems) = rest[:-6], rest[-6:]
    parts, groups, slots = targets_ref.shape
    rows = edges_ref.shape[3]
    high = sums_ref.shape[1]
    width = high - EXTRA
    copies = fetch(sems, (ids_vmem, ids_ref), (counts_vmem, counts_ref))
    bands_ref[...] = jnp.zeros_like(bands_ref)
    picked = order.shape[0]
    pick_rows(picked, 0, part_ref, sources_ref, table_ref, mine_ref, order, hits, lambda: None)
    for k in range(1, groups):
        group = ahead(me_ref[0], groups, k, FEATURES)
        blocks[k - 1][...] = table_ref[:width, pl.ds(pl.multiple_of(group * rows, rows), rows)]
    for copy in copies:
        copy.wait()

    def place(t, _):
        at = pl.multiple_of(ids_ref[1, t] * rows, rows)
        bands_ref[ids_ref[0, t], :, pl.ds(at, rows)] = tiles_ref[t]
        return 0

    lax.fori_loop(0, tiles_ref.shape[0], place, 0, unroll=tiles_ref.shape[0] <= 16)
    for g in range(groups):
        sums_ref[g] = dot(table_ref[:high, :], bands_ref[g], LAST)
    band_ref[...] = bands_ref[me_ref[0]]
    lane = lax.broadcasted_iota(jnp.int32, (slots, rows), 1)
    slot = lax.broadcasted_iota(jnp.int32, (slots, rows), 0)
    chips, chip, core = parts // 2, part_ref[0] // 2, part_ref[0] % 2

    def connect(i, _):
        first = i * chunk
        target = columns_of(targets_ref[pl.ds(first, chunk)])
        weight = columns_of(weight_ref[pl.ds(first, chunk)].astype(f32))
        for g in range(groups):
            degree = jnp.zeros((1, rows), f32)
            for e in range(chunk):
                n, d = e * groups + g, first + e
                at = step_to(d // 2, chip, chips) * 2 + ((d % 2) ^ core)
                hit = (target[:, n : n + 1] == lane) & (slot < counts_ref[g, d])
                values = jnp.where(hit, weight[:, n : n + 1], 0.0)
                edges_ref[g, at] = values.astype(bf16)
                degree = degree + jnp.sum(values, axis=0, keepdims=True)
            sums_ref[g, width : width + 1, :] += degree
        return 0

    if parts == chunk:
        connect(0, 0)
    else:
        lax.fori_loop(0, parts // chunk, connect, 0)


def hits_kernel(after, me_ref, part_ref, sources_hbm, hits_ref, sources_ref, sem):
    del after
    copy = pltpu.make_async_copy(sources_hbm, sources_ref, sem)
    copy.start()
    parts, groups, slots = sources_ref.shape
    chips, chip, core = parts // 2, part_ref[0] // 2, part_ref[0] % 2
    mine = lax.broadcasted_iota(jnp.int32, sources_ref.shape, 1) == me_ref[0]
    copy.wait()
    picks = jnp.sum(jnp.where(mine, sources_ref[...], 0), axis=1).T
    lane = lax.broadcasted_iota(jnp.int32, (slots, hits_ref.shape[1]), 1)
    for d in range(parts):
        to = ((d % 2) ^ core) * chips + step_to(chip, d // 2, chips)
        hits_ref[pl.ds(pl.multiple_of(to * slots, slots), slots), :] = jnp.where(
            picks[:, d : d + 1] == lane, 1.0, 0.0
        ).astype(bf16)


def mean_kernel(first, me_ref, sums_ref, edges_ref, *rest):
    groups, parts, slots, rows = edges_ref.shape
    arrived, outs = rest[: parts // 2], rest[parts // 2 :]
    width = outs[0].shape[0]
    for k, out in enumerate(outs, first):
        group = ahead(me_ref[0], groups, k)
        span = pl.ds(pl.multiple_of(group * slots, slots), slots)
        far = jnp.concatenate([x[:, span, :].reshape(2 * slots, -1) for x in arrived], axis=0)
        far = dot(far, edges_ref[group].reshape(parts * slots, rows), FIRST)
        total = sums_ref[group, :width, :] + far[:width]
        out[...] = (total / sums_ref[group, width : width + 1, :]).astype(bf16)


def own_mean_kernel(after, *rest):
    del after
    mean_kernel(0, *rest)


def rows_from(me, groups, k, width, what=MEANS):
    return pl.ds(pl.multiple_of(behind(me, groups, k, what) * width, width), width)


def self_kernel(me_ref, features_hbm, weight_hbm, *rest):
    blocks, (out_ref, own_ref, weight_ref, sems) = rest[:-4], rest[-4:]
    groups, (width, rows) = len(blocks) + 1, own_ref.shape
    me = me_ref[0]
    spans = [rows_from(me, groups, k, width, FEATURES) for k in range(groups)]
    own, *weights = fetch(
        sems,
        (features_hbm.at[:, pl.ds(pl.multiple_of(me * rows, rows), rows)], own_ref),
        *[(weight_hbm.at[span, :], weight_ref.at[span, :]) for span in spans],
    )
    own.wait()
    total = jnp.zeros(out_ref.shape, f32)
    for block, span, weight in zip((own_ref, *blocks), spans, weights):
        weight.wait()
        total = total + dot(block[...], weight_ref[span, :], FIRST)
    out_ref[...] = total


def add_blocks(total, me, groups, first, blocks, weight_ref):
    width = blocks[0].shape[0]
    for k, block in enumerate(blocks, first):
        total = total + dot(block[...], weight_ref[rows_from(me, groups, k, width), :], FIRST)
    return total


def early_kernel(groups, me_ref, weight_ref, own_ref, *rest):
    blocks, out_ref = rest[:-1], rest[-1]
    out_ref[...] = add_blocks(own_ref[...], me_ref[0], groups, 0, blocks, weight_ref)


def hidden_kernel(groups, me_ref, weight_ref, out_weight_ref, early_ref, *rest):
    blocks, (hidden_ref, *copies) = rest[: groups - 2], rest[groups - 2 :]
    total = add_blocks(early_ref[...], me_ref[0], groups, 2, blocks, weight_ref)
    hidden = jnp.maximum(total, 0.0).astype(bf16)
    hidden_ref[...] = hidden
    projected = dot(out_weight_ref[...], hidden, LAST).astype(bf16)
    for copy in copies:
        copy[...] = projected


def own_kernel(hidden_ref, weight_ref, out_ref, hidden_out, sem):
    copy = pltpu.make_async_copy(hidden_ref, hidden_out, sem)
    copy.start()
    out_ref[...] = dot(weight_ref[...], hidden_ref[...], LAST)
    copy.wait()


def pick_blocks(groups, first, me_ref, hits_ref, blocks):
    rows = blocks[0].shape[1]
    total = None
    for k, block in enumerate(blocks, first):
        at = pl.multiple_of(behind(me_ref[0], groups, k, SCORES) * rows, rows)
        term = dot(hits_ref[:, pl.ds(at, rows)], block[...], LAST)
        total = term if total is None else total + term
    return total


def early_pick_kernel(groups, me_ref, hits_ref, *rest):
    rest[-1][...] = pick_blocks(groups, 0, me_ref, hits_ref, rest[:-1])


def pick_kernel(groups, me_ref, hits_ref, early_ref, *rest):
    projected, (mine_ref, mate_ref) = rest[:-2], rest[-2:]
    total = early_ref[...] + pick_blocks(groups, 2, me_ref, hits_ref, projected)
    gap = mine_ref.shape[2] - total.shape[1]
    total = jnp.concatenate([total, jnp.zeros((total.shape[0], gap), f32)], axis=1).astype(bf16)
    half = total.shape[0] // 2
    mine_ref[...] = total[:half].reshape(mine_ref.shape)
    mate_ref[...] = total[half:].reshape(mate_ref.shape)


def pair_kernel(after, mine_ref, got_ref, *rest):
    del after
    chips = mine_ref.shape[0]
    held = (len(rest) - chips) // 2
    for j, out in enumerate(rest[held : held + chips]):
        out[0] = mine_ref[j]
        out[1] = got_ref[j]
    for block, out in zip(rest[:held], rest[held + chips :]):
        out[...] = block[...]


def near_kernel(me_ref, own_ref, sums_ref, band_ref, *rest):
    projected, out_ref = rest[:-1], rest[-1]
    groups, rows = len(projected), projected[0].shape[1]
    me, width = me_ref[0], sums_ref.shape[1] - EXTRA
    total = None
    for k in range(groups):
        at = pl.multiple_of(behind(me, groups, k, SCORES) * rows, rows)
        term = dot(projected[k][...], band_ref[:, pl.ds(at, rows)], LAST)
        total = term if total is None else total + term
    out_ref[...] = own_ref[...] + total / sums_ref[me, width : width + 1, :]


def last_kernel(first, me_ref, near_ref, edges_ref, sums_ref, *rest):
    arrived, out_ref = rest[:-1], rest[-1]
    _, _, slots, rows = edges_ref.shape
    me, width = me_ref[0], sums_ref.shape[1] - EXTRA
    count = 2 * len(arrived)
    arrived = jnp.concatenate([x[...].reshape(2 * slots, -1) for x in arrived], axis=0)
    edges = edges_ref[me, 2 * first : 2 * first + count].reshape(count * slots, rows)
    far = dot(arrived, edges, FIRST)[: near_ref.shape[0]]
    out_ref[...] = near_ref[...] + far / sums_ref[me, width : width + 1, :]


def scores_kernel(first, me_ref, *rest):
    rest, (out_hbm, scores_ref, sem) = rest[:-3], rest[-3:]
    last_kernel(first, me_ref, *rest, scores_ref)
    copy = pltpu.make_async_copy(scores_ref, out_hbm.at[:, 0, :], sem)
    copy.start()
    copy.wait()


def on_device(
    features,
    tiles,
    tile_ids,
    sources,
    targets,
    counts,
    edge_weight,
    self_one,
    neigh_one,
    self_out,
    neigh_out,
):
    feature_rows, tile_contents = features[0].T, tiles[0]
    groups, parts = lax.axis_size("feat"), lax.axis_size("dom")
    me = lax.axis_index("feat").astype(jnp.int32).reshape(1)
    part = lax.axis_index("dom").astype(jnp.int32).reshape(1)
    width, nodes = feature_rows.shape
    rows, slots = nodes // groups, sources.shape[3]
    hid, classes = self_one.shape[1], self_out.shape[1]
    chips = parts // 2
    chunk = max(1, min(parts, 512 // (groups * slots)))

    def shape(*dims, dtype=bf16):
        return jax.ShapeDtypeStruct(dims, dtype)

    def shift(blocks, what=MEANS):
        return [
            lax.ppermute(block, "feat", [(i, ahead(i, groups, k, what)) for i in range(groups)])
            for k, block in enumerate(blocks, 1)
        ]

    def to_mate(value):
        return lax.ppermute(value, "dom", [(d, d ^ 1) for d in range(parts)])

    def to_chips(blocks):
        return [blocks[0]] + [
            lax.ppermute(
                blocks[j],
                "dom",
                [(d, next_to(d // 2, j, chips) * 2 + d % 2) for d in range(parts)],
            )
            for j in range(1, chips)
        ]

    picked = min(chips, chunk)
    lanes = whole_lanes(width)
    table_rows = max(lanes, width + EXTRA)
    extras = (tile_contents, targets[0], edge_weight[0], tile_ids[0].T, counts[0].T)
    picking = [
        pltpu.VMEM((picked, groups, slots), jnp.int32),
        pltpu.VMEM((picked * groups * slots, nodes), bf16),
    ]
    mate, table, *passed = call(
        functools.partial(gather_kernel, picked),
        (
            shape(chips, groups * slots, lanes),
            shape(table_rows, nodes),
            shape(parts, groups, slots, dtype=jnp.int32),
        )
        + tuple(shape(*value.shape, dtype=value.dtype) for value in extras),
        [SM, HB, HB] + [HB] * PASSED,
        picking + [pltpu.SemaphoreType.DMA((2 + PASSED,))],
        2 * nodes * nodes * width,
        1 << 20,
    )(part, sources[0], feature_rows, *extras)
    mate = to_mate(mate)
    sums, edges, band, mine, *feature_blocks = call(
        functools.partial(local_kernel, chunk),
        (
            shape(groups, width + EXTRA, rows, dtype=f32),
            shape(groups, parts, slots, rows),
            shape(rows, nodes),
            shape(chips, groups * slots, lanes),
        )
        + (shape(width, rows),) * (groups - 1),
        [SM, SM, VM, VM] + [VM] * PASSED,
        [
            pltpu.SMEM(tile_ids.shape[:0:-1], jnp.int32),
            pltpu.SMEM(counts.shape[:0:-1], jnp.int32),
            pltpu.VMEM((groups, rows, nodes), bf16),
        ]
        + picking
        + [pltpu.SemaphoreType.DMA((2,))],
        2 * nodes * nodes * width,
        1 << 20,
        4 if groups <= 4 else 16,
    )(me, part, table, *passed)
    paired = call(
        pair_kernel,
        (shape(2, groups * slots, lanes),) * chips + (shape(width, rows),) * (groups - 1),
        [VM] * (2 + groups),
        (),
        0,
        1 << 20,
    )(band, mine, mate, *feature_blocks)
    arrived = to_chips(paired[:chips])
    feature_blocks = shift(paired[chips:], FEATURES)
    means = call(
        functools.partial(mean_kernel, 1),
        (shape(width, rows),) * (groups - 1),
        [SM] + [VM] * (2 + chips),
        (),
        2 * nodes * parts * slots * width,
        1 << 20,
    )(me, sums, edges, *arrived)
    means = shift(means)
    own = call(
        self_kernel,
        shape(rows, hid, dtype=f32),
        [SM, HB, HB] + [VM] * (groups - 1),
        [
            pltpu.VMEM((width, rows), bf16),
            pltpu.VMEM(self_one.shape, bf16),
            pltpu.SemaphoreType.DMA((1 + groups,)),
        ],
        2 * rows * hid * groups * width,
        2 << 20,
    )(me, feature_rows, self_one, *feature_blocks)
    own_mean = call(
        own_mean_kernel,
        (shape(width, rows),),
        [VM, SM] + [VM] * (2 + chips),
        (),
        2 * rows * parts * slots * width,
        1 << 18,
    )(own, me, sums, edges, *arrived)
    means = [*own_mean, *means]
    early = call(
        functools.partial(early_kernel, groups),
        shape(rows, hid, dtype=f32),
        [SM] + [VM] * 4,
        (),
        rows * hid * groups * width,
        2 << 20,
    )(me, neigh_one, own, *means[:2])
    hidden, *projected = call(
        functools.partial(hidden_kernel, groups),
        (shape(rows, hid),) + (shape(classes, rows),) * groups,
        [SM] + [VM] * (1 + groups),
        (),
        rows * hid * groups * width,
        2 << 20,
    )(me, neigh_one, neigh_out.T, early, *means[2:])
    hits = call(
        hits_kernel,
        shape(parts * slots, nodes),
        [VM, SM, SM, HB],
        [pltpu.VMEM((parts, groups, slots), jnp.int32), pltpu.SemaphoreType.DMA],
        0,
        1 << 19,
    )(projected[0], me, part, sources[0])
    projected = projected[:1] + shift(projected[1:], SCORES)
    early = call(
        functools.partial(early_pick_kernel, groups),
        shape(parts * slots, classes, dtype=f32),
        [SM] + [VM] * 3,
        (),
        parts * slots * nodes * classes,
        1 << 18,
    )(me, hits, *projected[:2])
    mine, mate = call(
        functools.partial(pick_kernel, groups),
        (shape(chips, slots, whole_lanes(classes)),) * 2,
        [SM] + [VM] * groups,
        (),
        parts * slots * nodes * classes,
        1 << 18,
    )(me, hits, early, *projected[2:])
    mate = to_mate(mate)
    arrived = to_chips(
        call(pair_kernel, (shape(2, slots, whole_lanes(classes)),) * chips, [VM] * 3, (), 0, 1 << 19)(
            hits, mine, mate
        )
    )
    own, hidden = call(
        own_kernel,
        (shape(classes, rows, dtype=f32), shape(rows, hid)),
        [VM, VM],
        [pltpu.SemaphoreType.DMA],
        2 * rows * hid * classes,
        1 << 20,
        out_specs=(VM, HB),
    )(hidden, self_out.T)
    near = call(
        near_kernel,
        shape(classes, rows, dtype=f32),
        [SM] + [VM] * (3 + groups),
        (),
        2 * rows * nodes * classes,
        1 << 19,
    )(me, own, sums, band, *projected)
    half = chips // 2
    near = call(
        functools.partial(last_kernel, 0),
        shape(classes, rows, dtype=f32),
        [SM] + [VM] * (3 + half),
        (),
        rows * parts * slots * classes,
        1 << 18,
    )(me, near, edges, sums, *arrived[:half])
    logits = call(
        functools.partial(scores_kernel, half),
        shape(classes, 1, rows, dtype=f32),
        [SM] + [VM] * (3 + chips - half),
        [pltpu.VMEM((classes, rows), f32), pltpu.SemaphoreType.DMA],
        rows * parts * slots * classes,
        1 << 19,
        out_specs=HB,
    )(me, near, edges, sums, *arrived[half:])
    return hidden[None], logits.transpose(1, 0, 2)


def solution(mesh):
    placed = (
        P("dom", None, "feat"),
        P("dom", None, None, None),
        P("dom", None, None),
        P("dom", None, None, None),
        P("dom", None, None, None),
        P("dom", None, None),
        P("dom", None, None, None),
        P(),
        P(),
        P(),
        P(),
    )
    return jax.shard_map(
        on_device,
        mesh=mesh,
        in_specs=placed,
        out_specs=(P("dom", "feat", None), P("dom", None, "feat")),
        check_vma=False,
    )
```

```python
import functools

import jax
import jax.numpy as jnp
from jax import lax
from jax.experimental import pallas as pl
from jax.experimental.pallas import tpu as pltpu
from jax.sharding import PartitionSpec as P

f32 = jnp.float32
bf16 = jnp.bfloat16
VM = pl.BlockSpec(memory_space=pltpu.VMEM)
SM = pl.BlockSpec(memory_space=pltpu.SMEM)
HB = pl.BlockSpec(memory_space=pltpu.HBM)
LAST = (((1,), (1,)), ((), ()))
FIRST = (((0,), (0,)), ((), ()))
EXTRA = 16
PASSED = 5


def call(kernel, out_shape, in_specs, scratch=(), flops=0, size=0, limit=4, out_specs=None):
    run = pl.pallas_call(
        kernel,
        out_shape=out_shape,
        in_specs=in_specs,
        out_specs=out_specs or jax.tree.map(lambda _: VM, out_shape),
        scratch_shapes=list(scratch),
        cost_estimate=pl.CostEstimate(flops=flops, bytes_accessed=size, transcendentals=0),
        compiler_params=pltpu.CompilerParams(vmem_limit_bytes=limit << 20),
    )

    def placed(*operands):
        return run(
            *(
                pltpu.with_memory_space_constraint(value, pltpu.HBM) if spec is HB else value
                for value, spec in zip(operands, in_specs)
            )
        )

    return placed


def dot(left, right, dims):
    return lax.dot_general(left, right, dims, preferred_element_type=f32)


def step_of(groups, k, near=False):
    if near and groups > 2 and k in (1, 2):
        return groups - 3 + k
    return (groups - k) % groups


def whole_lanes(count):
    return -(-count // 128) * 128


def ahead(me, groups, k, near=False):
    step = step_of(groups, k, near)
    return me ^ step if groups & (groups - 1) == 0 else (me + step) % groups


def behind(me, groups, k, near=False):
    step = step_of(groups, k, near)
    return me ^ step if groups & (groups - 1) == 0 else (me + groups - step) % groups


def step_to(a, b, count):
    step = a ^ b if count & (count - 1) == 0 else (b + count - a) % count
    return (count - step) % count


def next_to(a, j, count):
    step = step_of(count, j)
    return a ^ step if count & (count - 1) == 0 else (a + step) % count


def fetch(sems, *pairs):
    copies = [pltpu.make_async_copy(a, b, sems.at[i]) for i, (a, b) in enumerate(pairs)]
    for copy in copies:
        copy.start()
    return copies


def columns_of(values):
    return values.reshape(-1, values.shape[-1]).T


def pick_rows(chunk, other, part_ref, sources_ref, table_ref, out_ref, order, hits, ready):
    chips, lanes = out_ref.shape[0], out_ref.shape[2]
    _, groups, slots = sources_ref.shape
    nodes = table_ref.shape[1]
    chip, core = part_ref[0] // 2, part_ref[0] % 2
    lane = lax.broadcasted_iota(jnp.int32, (slots, nodes), 1)

    def step(i, last):
        for j in range(chunk):
            order[j] = sources_ref[next_to(chip, i * chunk + j, chips) * 2 + (core ^ other)]
        columns = columns_of(order[...])
        for n in range(chunk * groups):
            hits[n * slots : (n + 1) * slots, :] = jnp.where(
                columns[:, n : n + 1] == lane, 1.0, 0.0
            ).astype(bf16)
        if last:
            ready()
        picked = dot(hits[...], table_ref[:lanes, :], LAST).astype(bf16)
        out_ref[pl.ds(i * chunk, chunk)] = picked.reshape(chunk, groups * slots, -1)

    if chips == chunk:
        step(0, True)
    else:
        ready()
        lax.fori_loop(0, chips // chunk, lambda i, _: step(i, False), None)


def gather_kernel(chunk, part_ref, sources_hbm, features_hbm, *rest):
    extras, (mate_ref, table_ref, sources_ref, *rest) = rest[:PASSED], rest[PASSED:]
    passed, (order, hits, sems) = rest[:PASSED], rest[PASSED:]
    width, nodes = features_hbm.shape
    indices, table, *others = fetch(
        sems,
        (sources_hbm, sources_ref),
        (features_hbm, table_ref.at[pl.ds(0, width), :]),
        *zip(extras, passed),
    )
    table_ref[width : width + EXTRA, :] = jnp.ones((EXTRA, nodes), bf16)
    if table_ref.shape[0] > width + EXTRA:
        table_ref[width + EXTRA :, :] = jnp.zeros(
            (table_ref.shape[0] - width - EXTRA, nodes), bf16
        )
    indices.wait()
    pick_rows(chunk, 1, part_ref, sources_ref, table_ref, mate_ref, order, hits, table.wait)
    for copy in others:
        copy.wait()


def local_kernel(
    chunk,
    me_ref,
    part_ref,
    table_ref,
    sources_ref,
    tiles_ref,
    targets_ref,
    weight_ref,
    ids_vmem,
    counts_vmem,
    sums_ref,
    edges_ref,
    band_ref,
    mine_ref,
    *rest,
):
    blocks, (ids_ref, counts_ref, bands_ref, order, hits, sems) = rest[:-6], rest[-6:]
    parts, groups, slots = targets_ref.shape
    rows = edges_ref.shape[3]
    high = sums_ref.shape[1]
    width = high - EXTRA
    copies = fetch(sems, (ids_vmem, ids_ref), (counts_vmem, counts_ref))
    bands_ref[...] = jnp.zeros_like(bands_ref)
    picked = order.shape[0]
    pick_rows(picked, 0, part_ref, sources_ref, table_ref, mine_ref, order, hits, lambda: None)
    for k in range(1, groups):
        group = ahead(me_ref[0], groups, k, True)
        blocks[k - 1][...] = table_ref[:width, pl.ds(pl.multiple_of(group * rows, rows), rows)]
    for copy in copies:
        copy.wait()

    def place(t, _):
        at = pl.multiple_of(ids_ref[1, t] * rows, rows)
        bands_ref[ids_ref[0, t], :, pl.ds(at, rows)] = tiles_ref[t]
        return 0

    lax.fori_loop(0, tiles_ref.shape[0], place, 0, unroll=tiles_ref.shape[0] <= 16)
    for g in range(groups):
        sums_ref[g] = dot(table_ref[:high, :], bands_ref[g], LAST)
    band_ref[...] = bands_ref[me_ref[0]]
    lane = lax.broadcasted_iota(jnp.int32, (slots, rows), 1)
    slot = lax.broadcasted_iota(jnp.int32, (slots, rows), 0)
    chips, chip, core = parts // 2, part_ref[0] // 2, part_ref[0] % 2

    def connect(i, _):
        first = i * chunk
        target = columns_of(targets_ref[pl.ds(first, chunk)])
        weight = columns_of(weight_ref[pl.ds(first, chunk)].astype(f32))
        for g in range(groups):
            degree = jnp.zeros((1, rows), f32)
            for e in range(chunk):
                n, d = e * groups + g, first + e
                at = step_to(d // 2, chip, chips) * 2 + ((d % 2) ^ core)
                hit = (target[:, n : n + 1] == lane) & (slot < counts_ref[g, d])
                values = jnp.where(hit, weight[:, n : n + 1], 0.0)
                edges_ref[g, at] = values.astype(bf16)
                degree = degree + jnp.sum(values, axis=0, keepdims=True)
            sums_ref[g, width : width + 1, :] += degree
        return 0

    if parts == chunk:
        connect(0, 0)
    else:
        lax.fori_loop(0, parts // chunk, connect, 0)


def hits_kernel(after, me_ref, part_ref, sources_hbm, hits_ref, sources_ref, sem):
    del after
    copy = pltpu.make_async_copy(sources_hbm, sources_ref, sem)
    copy.start()
    parts, groups, slots = sources_ref.shape
    chips, chip, core = parts // 2, part_ref[0] // 2, part_ref[0] % 2
    mine = lax.broadcasted_iota(jnp.int32, sources_ref.shape, 1) == me_ref[0]
    copy.wait()
    picks = jnp.sum(jnp.where(mine, sources_ref[...], 0), axis=1).T
    lane = lax.broadcasted_iota(jnp.int32, (slots, hits_ref.shape[1]), 1)
    for d in range(parts):
        to = ((d % 2) ^ core) * chips + step_to(chip, d // 2, chips)
        hits_ref[pl.ds(pl.multiple_of(to * slots, slots), slots), :] = jnp.where(
            picks[:, d : d + 1] == lane, 1.0, 0.0
        ).astype(bf16)


def mean_kernel(first, me_ref, sums_ref, edges_ref, *rest):
    groups, parts, slots, rows = edges_ref.shape
    arrived, outs = rest[: parts // 2], rest[parts // 2 :]
    width = outs[0].shape[0]
    for k, out in enumerate(outs, first):
        group = ahead(me_ref[0], groups, k)
        span = pl.ds(pl.multiple_of(group * slots, slots), slots)
        far = jnp.concatenate([x[:, span, :].reshape(2 * slots, -1) for x in arrived], axis=0)
        far = dot(far, edges_ref[group].reshape(parts * slots, rows), FIRST)
        total = sums_ref[group, :width, :] + far[:width]
        out[...] = (total / sums_ref[group, width : width + 1, :]).astype(bf16)


def own_mean_kernel(after, *rest):
    del after
    mean_kernel(0, *rest)


def rows_from(me, groups, k, width, near=False):
    return pl.ds(pl.multiple_of(behind(me, groups, k, near) * width, width), width)


def self_kernel(me_ref, features_hbm, weight_hbm, *rest):
    blocks, (out_ref, own_ref, weight_ref, sems) = rest[:-4], rest[-4:]
    groups, (width, rows) = len(blocks) + 1, own_ref.shape
    me = me_ref[0]
    spans = [rows_from(me, groups, k, width, True) for k in range(groups)]
    own, *weights = fetch(
        sems,
        (features_hbm.at[:, pl.ds(pl.multiple_of(me * rows, rows), rows)], own_ref),
        *[(weight_hbm.at[span, :], weight_ref.at[span, :]) for span in spans],
    )
    own.wait()
    total = jnp.zeros(out_ref.shape, f32)
    for block, span, weight in zip((own_ref, *blocks), spans, weights):
        weight.wait()
        total = total + dot(block[...], weight_ref[span, :], FIRST)
    out_ref[...] = total


def add_blocks(total, me, groups, first, blocks, weight_ref):
    width = blocks[0].shape[0]
    for k, block in enumerate(blocks, first):
        total = total + dot(block[...], weight_ref[rows_from(me, groups, k, width), :], FIRST)
    return total


def early_kernel(groups, first, me_ref, weight_ref, own_ref, *rest):
    blocks, out_ref = rest[:-1], rest[-1]
    out_ref[...] = add_blocks(own_ref[...], me_ref[0], groups, first, blocks, weight_ref)


def hidden_kernel(groups, me_ref, weight_ref, out_weight_ref, early_ref, *rest):
    last_ref, hidden_ref, *copies = rest
    total = add_blocks(early_ref[...], me_ref[0], groups, groups - 1, [last_ref], weight_ref)
    hidden = jnp.maximum(total, 0.0).astype(bf16)
    hidden_ref[...] = hidden
    projected = dot(out_weight_ref[...], hidden, LAST).astype(bf16)
    for copy in copies:
        copy[...] = projected


def own_kernel(hidden_ref, weight_ref, out_ref, hidden_out, sem):
    copy = pltpu.make_async_copy(hidden_ref, hidden_out, sem)
    copy.start()
    out_ref[...] = dot(weight_ref[...], hidden_ref[...], LAST)
    copy.wait()


def pick_blocks(groups, first, me_ref, hits_ref, blocks):
    rows = blocks[0].shape[1]
    total = None
    for k, block in enumerate(blocks, first):
        at = pl.multiple_of(behind(me_ref[0], groups, k) * rows, rows)
        term = dot(hits_ref[:, pl.ds(at, rows)], block[...], LAST)
        total = term if total is None else total + term
    return total


def early_pick_kernel(groups, me_ref, hits_ref, *rest):
    rest[-1][...] = pick_blocks(groups, 0, me_ref, hits_ref, rest[:-1])


def more_pick_kernel(groups, me_ref, hits_ref, early_ref, *rest):
    rest[-1][...] = early_ref[...] + pick_blocks(groups, 2, me_ref, hits_ref, rest[:-1])


def pick_kernel(groups, me_ref, hits_ref, early_ref, *rest):
    last_ref, mine_ref, mate_ref = rest
    total = early_ref[...] + pick_blocks(groups, groups - 1, me_ref, hits_ref, [last_ref])
    gap = mine_ref.shape[2] - total.shape[1]
    total = jnp.concatenate([total, jnp.zeros((total.shape[0], gap), f32)], axis=1).astype(bf16)
    half = total.shape[0] // 2
    mine_ref[...] = total[:half].reshape(mine_ref.shape)
    mate_ref[...] = total[half:].reshape(mate_ref.shape)


def pair_kernel(after, mine_ref, got_ref, *rest):
    del after
    chips = mine_ref.shape[0]
    held = (len(rest) - chips) // 2
    for j, out in enumerate(rest[held : held + chips]):
        out[0] = mine_ref[j]
        out[1] = got_ref[j]
    for block, out in zip(rest[:held], rest[held + chips :]):
        out[...] = block[...]


def near_kernel(me_ref, own_ref, sums_ref, band_ref, *rest):
    projected, out_ref = rest[:-1], rest[-1]
    groups, rows = len(projected), projected[0].shape[1]
    me, width = me_ref[0], sums_ref.shape[1] - EXTRA
    total = None
    for k in range(groups):
        at = pl.multiple_of(behind(me, groups, k) * rows, rows)
        term = dot(projected[k][...], band_ref[:, pl.ds(at, rows)], LAST)
        total = term if total is None else total + term
    out_ref[...] = own_ref[...] + total / sums_ref[me, width : width + 1, :]


def last_kernel(first, me_ref, near_ref, edges_ref, sums_ref, *rest):
    arrived, out_ref = rest[:-1], rest[-1]
    _, _, slots, rows = edges_ref.shape
    me, width = me_ref[0], sums_ref.shape[1] - EXTRA
    count = 2 * len(arrived)
    arrived = jnp.concatenate([x[...].reshape(2 * slots, -1) for x in arrived], axis=0)
    edges = edges_ref[me, 2 * first : 2 * first + count].reshape(count * slots, rows)
    far = dot(arrived, edges, FIRST)[: near_ref.shape[0]]
    out_ref[...] = near_ref[...] + far / sums_ref[me, width : width + 1, :]


def scores_kernel(first, me_ref, *rest):
    rest, (out_hbm, scores_ref, sem) = rest[:-3], rest[-3:]
    last_kernel(first, me_ref, *rest, scores_ref)
    copy = pltpu.make_async_copy(scores_ref, out_hbm.at[:, 0, :], sem)
    copy.start()
    copy.wait()


def on_device(
    features,
    tiles,
    tile_ids,
    sources,
    targets,
    counts,
    edge_weight,
    self_one,
    neigh_one,
    self_out,
    neigh_out,
):
    feature_rows, tile_contents = features[0].T, tiles[0]
    groups, parts = lax.axis_size("feat"), lax.axis_size("dom")
    me = lax.axis_index("feat").astype(jnp.int32).reshape(1)
    part = lax.axis_index("dom").astype(jnp.int32).reshape(1)
    width, nodes = feature_rows.shape
    rows, slots = nodes // groups, sources.shape[3]
    hid, classes = self_one.shape[1], self_out.shape[1]
    chips = parts // 2
    chunk = max(1, min(parts, 512 // (groups * slots)))

    def shape(*dims, dtype=bf16):
        return jax.ShapeDtypeStruct(dims, dtype)

    def shift(blocks, near=False):
        return [
            lax.ppermute(block, "feat", [(i, ahead(i, groups, k, near)) for i in range(groups)])
            for k, block in enumerate(blocks, 1)
        ]

    def to_mate(value):
        return lax.ppermute(value, "dom", [(d, d ^ 1) for d in range(parts)])

    def to_chips(blocks):
        return [blocks[0]] + [
            lax.ppermute(
                blocks[j],
                "dom",
                [(d, next_to(d // 2, j, chips) * 2 + d % 2) for d in range(parts)],
            )
            for j in range(1, chips)
        ]

    picked = min(chips, chunk)
    lanes = whole_lanes(width)
    table_rows = max(lanes, width + EXTRA)
    extras = (tile_contents, targets[0], edge_weight[0], tile_ids[0].T, counts[0].T)
    picking = [
        pltpu.VMEM((picked, groups, slots), jnp.int32),
        pltpu.VMEM((picked * groups * slots, nodes), bf16),
    ]
    mate, table, *passed = call(
        functools.partial(gather_kernel, picked),
        (
            shape(chips, groups * slots, lanes),
            shape(table_rows, nodes),
            shape(parts, groups, slots, dtype=jnp.int32),
        )
        + tuple(shape(*value.shape, dtype=value.dtype) for value in extras),
        [SM, HB, HB] + [HB] * PASSED,
        picking + [pltpu.SemaphoreType.DMA((2 + PASSED,))],
        2 * nodes * nodes * width,
        1 << 20,
    )(part, sources[0], feature_rows, *extras)
    mate = to_mate(mate)
    sums, edges, band, mine, *feature_blocks = call(
        functools.partial(local_kernel, chunk),
        (
            shape(groups, width + EXTRA, rows, dtype=f32),
            shape(groups, parts, slots, rows),
            shape(rows, nodes),
            shape(chips, groups * slots, lanes),
        )
        + (shape(width, rows),) * (groups - 1),
        [SM, SM, VM, VM] + [VM] * PASSED,
        [
            pltpu.SMEM(tile_ids.shape[:0:-1], jnp.int32),
            pltpu.SMEM(counts.shape[:0:-1], jnp.int32),
            pltpu.VMEM((groups, rows, nodes), bf16),
        ]
        + picking
        + [pltpu.SemaphoreType.DMA((2,))],
        2 * nodes * nodes * width,
        1 << 20,
        4 if groups <= 4 else 16,
    )(me, part, table, *passed)
    paired = call(
        pair_kernel,
        (shape(2, groups * slots, lanes),) * chips + (shape(width, rows),) * (groups - 1),
        [VM] * (2 + groups),
        (),
        0,
        1 << 20,
    )(band, mine, mate, *feature_blocks)
    arrived = to_chips(paired[:chips])
    feature_blocks = shift(paired[chips:], near=True)
    means = call(
        functools.partial(mean_kernel, 1),
        (shape(width, rows),) * (groups - 1),
        [SM] + [VM] * (2 + chips),
        (),
        2 * nodes * parts * slots * width,
        1 << 20,
    )(me, sums, edges, *arrived)
    means = shift(means)
    own = call(
        self_kernel,
        shape(rows, hid, dtype=f32),
        [SM, HB, HB] + [VM] * (groups - 1),
        [
            pltpu.VMEM((width, rows), bf16),
            pltpu.VMEM(self_one.shape, bf16),
            pltpu.SemaphoreType.DMA((1 + groups,)),
        ],
        2 * rows * hid * groups * width,
        2 << 20,
    )(me, feature_rows, self_one, *feature_blocks)
    own_mean = call(
        own_mean_kernel,
        (shape(width, rows),),
        [VM, SM] + [VM] * (2 + chips),
        (),
        2 * rows * parts * slots * width,
        1 << 18,
    )(own, me, sums, edges, *arrived)
    means = [*own_mean, *means]
    early = own
    for first, last in ((0, 2), (2, groups - 1)):
        early = call(
            functools.partial(early_kernel, groups, first),
            shape(rows, hid, dtype=f32),
            [SM] + [VM] * (2 + last - first),
            (),
            rows * hid * groups * width,
            2 << 20,
        )(me, neigh_one, early, *means[first:last])
    hidden, *projected = call(
        functools.partial(hidden_kernel, groups),
        (shape(rows, hid),) + (shape(classes, rows),) * groups,
        [SM] + [VM] * 4,
        (),
        rows * hid * groups * width,
        2 << 20,
    )(me, neigh_one, neigh_out.T, early, means[-1])
    hits = call(
        hits_kernel,
        shape(parts * slots, nodes),
        [VM, SM, SM, HB],
        [pltpu.VMEM((parts, groups, slots), jnp.int32), pltpu.SemaphoreType.DMA],
        0,
        1 << 19,
    )(projected[0], me, part, sources[0])
    projected = projected[:1] + shift(projected[1:])
    early = call(
        functools.partial(early_pick_kernel, groups),
        shape(parts * slots, classes, dtype=f32),
        [SM] + [VM] * 3,
        (),
        parts * slots * nodes * classes,
        1 << 18,
    )(me, hits, *projected[:2])
    early = call(
        functools.partial(more_pick_kernel, groups),
        shape(parts * slots, classes, dtype=f32),
        [SM] + [VM] * (groups - 1),
        (),
        parts * slots * nodes * classes,
        1 << 18,
    )(me, hits, early, *projected[2:-1])
    mine, mate = call(
        functools.partial(pick_kernel, groups),
        (shape(chips, slots, whole_lanes(classes)),) * 2,
        [SM] + [VM] * 3,
        (),
        parts * slots * nodes * classes,
        1 << 18,
    )(me, hits, early, projected[-1])
    mate = to_mate(mate)
    arrived = to_chips(
        call(pair_kernel, (shape(2, slots, whole_lanes(classes)),) * chips, [VM] * 3, (), 0, 1 << 19)(
            hits, mine, mate
        )
    )
    own, hidden = call(
        own_kernel,
        (shape(classes, rows, dtype=f32), shape(rows, hid)),
        [VM, VM],
        [pltpu.SemaphoreType.DMA],
        2 * rows * hid * classes,
        1 << 20,
        out_specs=(VM, HB),
    )(hidden, self_out.T)
    near = call(
        near_kernel,
        shape(classes, rows, dtype=f32),
        [SM] + [VM] * (3 + groups),
        (),
        2 * rows * nodes * classes,
        1 << 19,
    )(me, own, sums, band, *projected)
    half = chips // 2
    near = call(
        functools.partial(last_kernel, 0),
        shape(classes, rows, dtype=f32),
        [SM] + [VM] * (3 + half),
        (),
        rows * parts * slots * classes,
        1 << 18,
    )(me, near, edges, sums, *arrived[:half])
    logits = call(
        functools.partial(scores_kernel, half),
        shape(classes, 1, rows, dtype=f32),
        [SM] + [VM] * (3 + chips - half),
        [pltpu.VMEM((classes, rows), f32), pltpu.SemaphoreType.DMA],
        rows * parts * slots * classes,
        1 << 19,
        out_specs=HB,
    )(me, near, edges, sums, *arrived[half:])
    return hidden[None], logits.transpose(1, 0, 2)


def solution(mesh):
    placed = (
        P("dom", None, "feat"),
        P("dom", None, None, None),
        P("dom", None, None),
        P("dom", None, None, None),
        P("dom", None, None, None),
        P("dom", None, None),
        P("dom", None, None, None),
        P(),
        P(),
        P(),
        P(),
    )
    return jax.shard_map(
        on_device,
        mesh=mesh,
        in_specs=placed,
        out_specs=(P("dom", "feat", None), P("dom", None, "feat")),
        check_vma=False,
    )
```

```python
import functools

import jax
import jax.numpy as jnp
from jax import lax
from jax.experimental import pallas as pl
from jax.experimental.pallas import tpu as pltpu
from jax.sharding import PartitionSpec as P

f32 = jnp.float32
bf16 = jnp.bfloat16
VM = pl.BlockSpec(memory_space=pltpu.VMEM)
SM = pl.BlockSpec(memory_space=pltpu.SMEM)
HB = pl.BlockSpec(memory_space=pltpu.HBM)
LAST = (((1,), (1,)), ((), ()))
FIRST = (((0,), (0,)), ((), ()))
EXTRA = 16
PASSED = 5


def call(kernel, out_shape, in_specs, scratch=(), flops=0, size=0, limit=4, out_specs=None):
    run = pl.pallas_call(
        kernel,
        out_shape=out_shape,
        in_specs=in_specs,
        out_specs=out_specs or jax.tree.map(lambda _: VM, out_shape),
        scratch_shapes=list(scratch),
        cost_estimate=pl.CostEstimate(flops=flops, bytes_accessed=size, transcendentals=0),
        compiler_params=pltpu.CompilerParams(vmem_limit_bytes=limit << 20),
    )

    def placed(*operands):
        return run(
            *(
                pltpu.with_memory_space_constraint(value, pltpu.HBM) if spec is HB else value
                for value, spec in zip(operands, in_specs)
            )
        )

    return placed


def dot(left, right, dims):
    return lax.dot_general(left, right, dims, preferred_element_type=f32)


def step_of(groups, k, near=False):
    if near and groups > 2 and k in (1, 2):
        return groups - 3 + k
    return (groups - k) % groups


def whole_lanes(count):
    return -(-count // 128) * 128


def ahead(me, groups, k, near=False):
    step = step_of(groups, k, near)
    return me ^ step if groups & (groups - 1) == 0 else (me + step) % groups


def behind(me, groups, k, near=False):
    step = step_of(groups, k, near)
    return me ^ step if groups & (groups - 1) == 0 else (me + groups - step) % groups


def step_to(a, b, count):
    step = a ^ b if count & (count - 1) == 0 else (b + count - a) % count
    return (count - step) % count


def next_to(a, j, count):
    step = step_of(count, j)
    return a ^ step if count & (count - 1) == 0 else (a + step) % count


def fetch(sems, *pairs):
    copies = [pltpu.make_async_copy(a, b, sems.at[i]) for i, (a, b) in enumerate(pairs)]
    for copy in copies:
        copy.start()
    return copies


def columns_of(values):
    return values.reshape(-1, values.shape[-1]).T


def pick_rows(chunk, other, part_ref, sources_ref, table_ref, out_ref, order, hits, ready):
    chips = out_ref.shape[0]
    _, groups, slots = sources_ref.shape
    lanes, nodes = table_ref.shape[0] - EXTRA, table_ref.shape[1]
    half = groups * slots // 2
    chip, core = part_ref[0] // 2, part_ref[0] % 2
    lane = lax.broadcasted_iota(jnp.int32, (slots, nodes), 1)

    def step(i, last):
        for j in range(chunk):
            order[j] = sources_ref[next_to(chip, i * chunk + j, chips) * 2 + (core ^ other)]
        columns = columns_of(order[...])
        for n in range(chunk * groups):
            hits[n * slots : (n + 1) * slots, :] = jnp.where(
                columns[:, n : n + 1] == lane, 1.0, 0.0
            ).astype(bf16)
        if last:
            ready()
        picked = dot(hits[...], table_ref[:lanes, :], LAST)
        picked = picked.reshape(chunk, groups * slots, lanes)
        tail = picked[:, :, lanes - 128 :]
        left = lax.broadcasted_iota(jnp.int32, (chunk, half, 128), 2) < 64
        tail = jnp.where(left, tail[:, :half], tail[:, half:]).astype(bf16)
        out_ref[pl.ds(i * chunk, chunk), out_ref.shape[1] - half :, :] = tail
        if lanes > 128:
            body = picked[:, :, :128].astype(bf16)
            out_ref[pl.ds(i * chunk, chunk), : 2 * half, :] = body

    if chips == chunk:
        step(0, True)
    else:
        ready()
        lax.fori_loop(0, chips // chunk, lambda i, _: step(i, False), None)


def gather_kernel(chunk, part_ref, sources_hbm, features_hbm, *rest):
    extras, (mate_ref, table_ref, sources_ref, *rest) = rest[:PASSED], rest[PASSED:]
    passed, (order, hits, sems) = rest[:PASSED], rest[PASSED:]
    width, nodes = features_hbm.shape
    indices, table, tail, *others = fetch(
        sems,
        (sources_hbm, sources_ref),
        (features_hbm, table_ref.at[pl.ds(0, width), :]),
        (features_hbm.at[pl.ds(width - 64, 64), :], table_ref.at[pl.ds(width, 64), :]),
        *zip(extras, passed),
    )
    table_ref[width + 64 :, :] = jnp.ones((EXTRA, nodes), bf16)

    def ready():
        table.wait()
        tail.wait()

    indices.wait()
    pick_rows(chunk, 1, part_ref, sources_ref, table_ref, mate_ref, order, hits, ready)
    for copy in others:
        copy.wait()


def local_kernel(
    chunk,
    me_ref,
    part_ref,
    table_ref,
    sources_ref,
    tiles_ref,
    targets_ref,
    weight_ref,
    ids_vmem,
    counts_vmem,
    sums_ref,
    edges_ref,
    band_ref,
    mine_ref,
    *rest,
):
    blocks, (ids_ref, counts_ref, bands_ref, order, hits, sems) = rest[:-6], rest[-6:]
    parts, groups, slots = targets_ref.shape
    rows = edges_ref.shape[3]
    high = sums_ref.shape[1]
    width = high - EXTRA - 64
    copies = fetch(sems, (ids_vmem, ids_ref), (counts_vmem, counts_ref))
    bands_ref[...] = jnp.zeros_like(bands_ref)
    picked = order.shape[0]
    pick_rows(picked, 0, part_ref, sources_ref, table_ref, mine_ref, order, hits, lambda: None)
    for k in range(1, groups):
        group = ahead(me_ref[0], groups, k, True)
        blocks[k - 1][...] = table_ref[:width, pl.ds(pl.multiple_of(group * rows, rows), rows)]
    for copy in copies:
        copy.wait()

    def place(t, _):
        at = pl.multiple_of(ids_ref[1, t] * rows, rows)
        bands_ref[ids_ref[0, t], :, pl.ds(at, rows)] = tiles_ref[t]
        return 0

    lax.fori_loop(0, tiles_ref.shape[0], place, 0, unroll=tiles_ref.shape[0] <= 16)
    for g in range(groups):
        sums_ref[g] = dot(table_ref[:high, :], bands_ref[g], LAST)
    band_ref[...] = bands_ref[me_ref[0]]
    lane = lax.broadcasted_iota(jnp.int32, (slots, rows), 1)
    slot = lax.broadcasted_iota(jnp.int32, (slots, rows), 0)
    chips, chip, core = parts // 2, part_ref[0] // 2, part_ref[0] % 2

    def connect(i, _):
        first = i * chunk
        target = columns_of(targets_ref[pl.ds(first, chunk)])
        weight = columns_of(weight_ref[pl.ds(first, chunk)].astype(f32))
        for g in range(groups):
            degree = jnp.zeros((1, rows), f32)
            for e in range(chunk):
                n, d = e * groups + g, first + e
                at = step_to(d // 2, chip, chips) * 2 + ((d % 2) ^ core)
                hit = (target[:, n : n + 1] == lane) & (slot < counts_ref[g, d])
                values = jnp.where(hit, weight[:, n : n + 1], 0.0)
                edges_ref[g, at] = values.astype(bf16)
                degree = degree + jnp.sum(values, axis=0, keepdims=True)
            sums_ref[g, high - EXTRA : high - EXTRA + 1, :] += degree
        return 0

    if parts == chunk:
        connect(0, 0)
    else:
        lax.fori_loop(0, parts // chunk, connect, 0)


def hits_kernel(after, me_ref, part_ref, sources_hbm, hits_ref, sources_ref, sem):
    del after
    copy = pltpu.make_async_copy(sources_hbm, sources_ref, sem)
    copy.start()
    parts, groups, slots = sources_ref.shape
    chips, chip, core = parts // 2, part_ref[0] // 2, part_ref[0] % 2
    mine = lax.broadcasted_iota(jnp.int32, sources_ref.shape, 1) == me_ref[0]
    copy.wait()
    picks = jnp.sum(jnp.where(mine, sources_ref[...], 0), axis=1).T
    lane = lax.broadcasted_iota(jnp.int32, (slots, hits_ref.shape[1]), 1)
    for d in range(parts):
        to = ((d % 2) ^ core) * chips + step_to(chip, d // 2, chips)
        hits_ref[pl.ds(pl.multiple_of(to * slots, slots), slots), :] = jnp.where(
            picks[:, d : d + 1] == lane, 1.0, 0.0
        ).astype(bf16)


def mean_kernel(first, me_ref, sums_ref, edges_ref, *rest):
    groups, parts, slots, rows = edges_ref.shape
    arrived, outs = rest[: parts // 2], rest[parts // 2 :]
    width, high = outs[0].shape[0], sums_ref.shape[1] - EXTRA
    body, half = width - 64, groups // 2
    for k, out in enumerate(outs, first):
        group = ahead(me_ref[0], groups, k)
        edges = edges_ref[group].reshape(parts * slots, rows)

        def boundary(row):
            span = pl.ds(pl.multiple_of(row * slots, slots), slots)
            far = [x[:, span, :].reshape(2 * slots, 128) for x in arrived]
            return dot(jnp.concatenate(far, axis=0), edges, FIRST)

        tail = boundary((groups if body else 0) + group % half)
        tail = jnp.where(group < half, tail[:64], tail[64:])
        degree = sums_ref[group, high : high + 1, :]
        out[body:, :] = ((sums_ref[group, body:width, :] + tail) / degree).astype(bf16)
        if body:
            total = sums_ref[group, :body, :] + boundary(group)
            out[:body, :] = (total / degree).astype(bf16)


def own_mean_kernel(after, *rest):
    del after
    mean_kernel(0, *rest)


def rows_from(me, groups, k, width, near=False):
    return pl.ds(pl.multiple_of(behind(me, groups, k, near) * width, width), width)


def self_kernel(me_ref, features_hbm, weight_hbm, *rest):
    blocks, (out_ref, own_ref, weight_ref, sems) = rest[:-4], rest[-4:]
    groups, (width, rows) = len(blocks) + 1, own_ref.shape
    me = me_ref[0]
    spans = [rows_from(me, groups, k, width, True) for k in range(groups)]
    own, *weights = fetch(
        sems,
        (features_hbm.at[:, pl.ds(pl.multiple_of(me * rows, rows), rows)], own_ref),
        *[(weight_hbm.at[span, :], weight_ref.at[span, :]) for span in spans],
    )
    own.wait()
    total = jnp.zeros(out_ref.shape, f32)
    for block, span, weight in zip((own_ref, *blocks), spans, weights):
        weight.wait()
        total = total + dot(block[...], weight_ref[span, :], FIRST)
    out_ref[...] = total


def add_blocks(total, me, groups, first, blocks, weight_ref):
    width = blocks[0].shape[0]
    for k, block in enumerate(blocks, first):
        total = total + dot(block[...], weight_ref[rows_from(me, groups, k, width), :], FIRST)
    return total


def early_kernel(groups, me_ref, weight_ref, own_ref, *rest):
    blocks, out_ref = rest[:-1], rest[-1]
    out_ref[...] = add_blocks(own_ref[...], me_ref[0], groups, 0, blocks, weight_ref)


def hidden_kernel(groups, me_ref, weight_ref, out_weight_ref, early_ref, *rest):
    blocks, (hidden_ref, *copies) = rest[: groups - 2], rest[groups - 2 :]
    total = add_blocks(early_ref[...], me_ref[0], groups, 2, blocks, weight_ref)
    hidden = jnp.maximum(total, 0.0).astype(bf16)
    hidden_ref[...] = hidden
    projected = dot(out_weight_ref[...], hidden, LAST).astype(bf16)
    for copy in copies:
        copy[...] = projected


def own_kernel(hidden_ref, weight_ref, out_ref, hidden_out, sem):
    copy = pltpu.make_async_copy(hidden_ref, hidden_out, sem)
    copy.start()
    out_ref[...] = dot(weight_ref[...], hidden_ref[...], LAST)
    copy.wait()


def pick_blocks(groups, first, me_ref, hits_ref, blocks):
    rows = blocks[0].shape[1]
    total = None
    for k, block in enumerate(blocks, first):
        at = pl.multiple_of(behind(me_ref[0], groups, k) * rows, rows)
        term = dot(hits_ref[:, pl.ds(at, rows)], block[...], LAST)
        total = term if total is None else total + term
    return total


def early_pick_kernel(groups, me_ref, hits_ref, *rest):
    rest[-1][...] = pick_blocks(groups, 0, me_ref, hits_ref, rest[:-1])


def pick_kernel(groups, me_ref, hits_ref, early_ref, *rest):
    projected, (mine_ref, mate_ref) = rest[:-2], rest[-2:]
    total = early_ref[...] + pick_blocks(groups, 2, me_ref, hits_ref, projected)
    gap = mine_ref.shape[2] - total.shape[1]
    total = jnp.concatenate([total, jnp.zeros((total.shape[0], gap), f32)], axis=1).astype(bf16)
    half = total.shape[0] // 2
    mine_ref[...] = total[:half].reshape(mine_ref.shape)
    mate_ref[...] = total[half:].reshape(mate_ref.shape)


def pair_kernel(after, mine_ref, got_ref, *rest):
    del after
    chips = mine_ref.shape[0]
    held = (len(rest) - chips) // 2
    for j, out in enumerate(rest[held : held + chips]):
        out[0] = mine_ref[j]
        out[1] = got_ref[j]
    for block, out in zip(rest[:held], rest[held + chips :]):
        out[...] = block[...]


def near_kernel(me_ref, own_ref, sums_ref, band_ref, *rest):
    projected, out_ref = rest[:-1], rest[-1]
    groups, rows = len(projected), projected[0].shape[1]
    me, width = me_ref[0], sums_ref.shape[1] - EXTRA
    total = None
    for k in range(groups):
        at = pl.multiple_of(behind(me, groups, k) * rows, rows)
        term = dot(projected[k][...], band_ref[:, pl.ds(at, rows)], LAST)
        total = term if total is None else total + term
    out_ref[...] = own_ref[...] + total / sums_ref[me, width : width + 1, :]


def last_kernel(first, me_ref, near_ref, edges_ref, sums_ref, *rest):
    arrived, out_ref = rest[:-1], rest[-1]
    _, _, slots, rows = edges_ref.shape
    me, width = me_ref[0], sums_ref.shape[1] - EXTRA
    count = 2 * len(arrived)
    arrived = jnp.concatenate([x[...].reshape(2 * slots, -1) for x in arrived], axis=0)
    edges = edges_ref[me, 2 * first : 2 * first + count].reshape(count * slots, rows)
    far = dot(arrived, edges, FIRST)[: near_ref.shape[0]]
    out_ref[...] = near_ref[...] + far / sums_ref[me, width : width + 1, :]


def scores_kernel(first, me_ref, *rest):
    rest, (out_hbm, scores_ref, sem) = rest[:-3], rest[-3:]
    last_kernel(first, me_ref, *rest, scores_ref)
    copy = pltpu.make_async_copy(scores_ref, out_hbm.at[:, 0, :], sem)
    copy.start()
    copy.wait()


def on_device(
    features,
    tiles,
    tile_ids,
    sources,
    targets,
    counts,
    edge_weight,
    self_one,
    neigh_one,
    self_out,
    neigh_out,
):
    feature_rows, tile_contents = features[0].T, tiles[0]
    groups, parts = lax.axis_size("feat"), lax.axis_size("dom")
    me = lax.axis_index("feat").astype(jnp.int32).reshape(1)
    part = lax.axis_index("dom").astype(jnp.int32).reshape(1)
    width, nodes = feature_rows.shape
    rows, slots = nodes // groups, sources.shape[3]
    hid, classes = self_one.shape[1], self_out.shape[1]
    chips = parts // 2
    chunk = max(1, min(parts, 512 // (groups * slots)))

    def shape(*dims, dtype=bf16):
        return jax.ShapeDtypeStruct(dims, dtype)

    def shift(blocks, near=False):
        return [
            lax.ppermute(block, "feat", [(i, ahead(i, groups, k, near)) for i in range(groups)])
            for k, block in enumerate(blocks, 1)
        ]

    def to_mate(value):
        return lax.ppermute(value, "dom", [(d, d ^ 1) for d in range(parts)])

    def to_chips(blocks):
        return [blocks[0]] + [
            lax.ppermute(
                blocks[j],
                "dom",
                [(d, next_to(d // 2, j, chips) * 2 + d % 2) for d in range(parts)],
            )
            for j in range(1, chips)
        ]

    picked = min(chips, chunk)
    lanes = whole_lanes(width)
    folded = groups * slots // 2 * (3 if width > 64 else 1)
    extras = (tile_contents, targets[0], edge_weight[0], tile_ids[0].T, counts[0].T)
    picking = [
        pltpu.VMEM((picked, groups, slots), jnp.int32),
        pltpu.VMEM((picked * groups * slots, nodes), bf16),
    ]
    mate, table, *passed = call(
        functools.partial(gather_kernel, picked),
        (
            shape(chips, folded, 128),
            shape(lanes + EXTRA, nodes),
            shape(parts, groups, slots, dtype=jnp.int32),
        )
        + tuple(shape(*value.shape, dtype=value.dtype) for value in extras),
        [SM, HB, HB] + [HB] * PASSED,
        picking + [pltpu.SemaphoreType.DMA((3 + PASSED,))],
        2 * nodes * nodes * width,
        1 << 20,
    )(part, sources[0], feature_rows, *extras)
    mate = to_mate(mate)
    sums, edges, band, mine, *feature_blocks = call(
        functools.partial(local_kernel, chunk),
        (
            shape(groups, lanes + EXTRA, rows, dtype=f32),
            shape(groups, parts, slots, rows),
            shape(rows, nodes),
            shape(chips, folded, 128),
        )
        + (shape(width, rows),) * (groups - 1),
        [SM, SM, VM, VM] + [VM] * PASSED,
        [
            pltpu.SMEM(tile_ids.shape[:0:-1], jnp.int32),
            pltpu.SMEM(counts.shape[:0:-1], jnp.int32),
            pltpu.VMEM((groups, rows, nodes), bf16),
        ]
        + picking
        + [pltpu.SemaphoreType.DMA((2,))],
        2 * nodes * nodes * width,
        1 << 20,
        4 if groups <= 4 else 16,
    )(me, part, table, *passed)
    paired = call(
        pair_kernel,
        (shape(2, folded, 128),) * chips + (shape(width, rows),) * (groups - 1),
        [VM] * (2 + groups),
        (),
        0,
        1 << 20,
    )(band, mine, mate, *feature_blocks)
    arrived = to_chips(paired[:chips])
    feature_blocks = shift(paired[chips:], near=True)
    means = call(
        functools.partial(mean_kernel, 1),
        (shape(width, rows),) * (groups - 1),
        [SM] + [VM] * (2 + chips),
        (),
        2 * nodes * parts * slots * width,
        1 << 20,
    )(me, sums, edges, *arrived)
    means = shift(means)
    own = call(
        self_kernel,
        shape(rows, hid, dtype=f32),
        [SM, HB, HB] + [VM] * (groups - 1),
        [
            pltpu.VMEM((width, rows), bf16),
            pltpu.VMEM(self_one.shape, bf16),
            pltpu.SemaphoreType.DMA((1 + groups,)),
        ],
        2 * rows * hid * groups * width,
        2 << 20,
    )(me, feature_rows, self_one, *feature_blocks)
    own_mean = call(
        own_mean_kernel,
        (shape(width, rows),),
        [VM, SM] + [VM] * (2 + chips),
        (),
        2 * rows * parts * slots * width,
        1 << 18,
    )(own, me, sums, edges, *arrived)
    means = [*own_mean, *means]
    early = call(
        functools.partial(early_kernel, groups),
        shape(rows, hid, dtype=f32),
        [SM] + [VM] * 4,
        (),
        rows * hid * groups * width,
        2 << 20,
    )(me, neigh_one, own, *means[:2])
    hidden, *projected = call(
        functools.partial(hidden_kernel, groups),
        (shape(rows, hid),) + (shape(classes, rows),) * groups,
        [SM] + [VM] * (1 + groups),
        (),
        rows * hid * groups * width,
        2 << 20,
    )(me, neigh_one, neigh_out.T, early, *means[2:])
    hits = call(
        hits_kernel,
        shape(parts * slots, nodes),
        [VM, SM, SM, HB],
        [pltpu.VMEM((parts, groups, slots), jnp.int32), pltpu.SemaphoreType.DMA],
        0,
        1 << 19,
    )(projected[0], me, part, sources[0])
    projected = projected[:1] + shift(projected[1:])
    early = call(
        functools.partial(early_pick_kernel, groups),
        shape(parts * slots, classes, dtype=f32),
        [SM] + [VM] * 3,
        (),
        parts * slots * nodes * classes,
        1 << 18,
    )(me, hits, *projected[:2])
    mine, mate = call(
        functools.partial(pick_kernel, groups),
        (shape(chips, slots, whole_lanes(classes)),) * 2,
        [SM] + [VM] * groups,
        (),
        parts * slots * nodes * classes,
        1 << 18,
    )(me, hits, early, *projected[2:])
    mate = to_mate(mate)
    arrived = to_chips(
        call(pair_kernel, (shape(2, slots, whole_lanes(classes)),) * chips, [VM] * 3, (), 0, 1 << 19)(
            hits, mine, mate
        )
    )
    own, hidden = call(
        own_kernel,
        (shape(classes, rows, dtype=f32), shape(rows, hid)),
        [VM, VM],
        [pltpu.SemaphoreType.DMA],
        2 * rows * hid * classes,
        1 << 20,
        out_specs=(VM, HB),
    )(hidden, self_out.T)
    near = call(
        near_kernel,
        shape(classes, rows, dtype=f32),
        [SM] + [VM] * (3 + groups),
        (),
        2 * rows * nodes * classes,
        1 << 19,
    )(me, own, sums, band, *projected)
    half = chips // 2
    near = call(
        functools.partial(last_kernel, 0),
        shape(classes, rows, dtype=f32),
        [SM] + [VM] * (3 + half),
        (),
        rows * parts * slots * classes,
        1 << 18,
    )(me, near, edges, sums, *arrived[:half])
    logits = call(
        functools.partial(scores_kernel, half),
        shape(classes, 1, rows, dtype=f32),
        [SM] + [VM] * (3 + chips - half),
        [pltpu.VMEM((classes, rows), f32), pltpu.SemaphoreType.DMA],
        rows * parts * slots * classes,
        1 << 19,
        out_specs=HB,
    )(me, near, edges, sums, *arrived[half:])
    return hidden[None], logits.transpose(1, 0, 2)


def solution(mesh):
    placed = (
        P("dom", None, "feat"),
        P("dom", None, None, None),
        P("dom", None, None),
        P("dom", None, None, None),
        P("dom", None, None, None),
        P("dom", None, None),
        P("dom", None, None, None),
        P(),
        P(),
        P(),
        P(),
    )
    return jax.shard_map(
        on_device,
        mesh=mesh,
        in_specs=placed,
        out_specs=(P("dom", "feat", None), P("dom", None, "feat")),
        check_vma=False,
    )
```

```python
import functools

import jax
import jax.numpy as jnp
from jax import lax
from jax.experimental import pallas as pl
from jax.experimental.pallas import tpu as pltpu
from jax.sharding import PartitionSpec as P

f32 = jnp.float32
bf16 = jnp.bfloat16
VM = pl.BlockSpec(memory_space=pltpu.VMEM)
SM = pl.BlockSpec(memory_space=pltpu.SMEM)
HB = pl.BlockSpec(memory_space=pltpu.HBM)
LAST = (((1,), (1,)), ((), ()))
FIRST = (((0,), (0,)), ((), ()))
EXTRA = 16
PASSED = 5


def call(kernel, out_shape, in_specs, scratch=(), flops=0, size=0, limit=4, out_specs=None):
    run = pl.pallas_call(
        kernel,
        out_shape=out_shape,
        in_specs=in_specs,
        out_specs=out_specs or jax.tree.map(lambda _: VM, out_shape),
        scratch_shapes=list(scratch),
        cost_estimate=pl.CostEstimate(flops=flops, bytes_accessed=size, transcendentals=0),
        compiler_params=pltpu.CompilerParams(vmem_limit_bytes=limit << 20),
    )

    def placed(*operands):
        return run(
            *(
                pltpu.with_memory_space_constraint(value, pltpu.HBM) if spec is HB else value
                for value, spec in zip(operands, in_specs)
            )
        )

    return placed


def dot(left, right, dims):
    return lax.dot_general(left, right, dims, preferred_element_type=f32)


def step_of(groups, k, near=False):
    if near and groups > 2 and k in (1, 2):
        return groups - 3 + k
    return (groups - k) % groups


def whole_lanes(count):
    return -(-count // 128) * 128


def ahead(me, groups, k, near=False):
    step = step_of(groups, k, near)
    return me ^ step if groups & (groups - 1) == 0 else (me + step) % groups


def behind(me, groups, k, near=False):
    step = step_of(groups, k, near)
    return me ^ step if groups & (groups - 1) == 0 else (me + groups - step) % groups


def gray(a):
    return a ^ (a >> 1)


def swapped(j):
    return (j >> 1) | ((j & 1) << 1)


def step_to(a, b, count):
    if count == 4:
        return swapped((gray(b) + count - gray(a)) % count)
    step = a ^ b if count & (count - 1) == 0 else (b + count - a) % count
    return (count - step) % count


def next_to(a, j, count):
    if count == 4:
        return gray((gray(a) + swapped(j)) % count)
    step = step_of(count, j)
    return a ^ step if count & (count - 1) == 0 else (a + step) % count


def fetch(sems, *pairs):
    copies = [pltpu.make_async_copy(a, b, sems.at[i]) for i, (a, b) in enumerate(pairs)]
    for copy in copies:
        copy.start()
    return copies


def columns_of(values):
    return values.reshape(-1, values.shape[-1]).T


def pick_rows(chunk, other, part_ref, sources_ref, table_ref, out_ref, order, hits, ready):
    chips, lanes = out_ref.shape[0], out_ref.shape[2]
    _, groups, slots = sources_ref.shape
    nodes = table_ref.shape[1]
    chip, core = part_ref[0] // 2, part_ref[0] % 2
    lane = lax.broadcasted_iota(jnp.int32, (slots, nodes), 1)

    def step(i, last):
        for j in range(chunk):
            order[j] = sources_ref[next_to(chip, i * chunk + j, chips) * 2 + (core ^ other)]
        columns = columns_of(order[...])
        for n in range(chunk * groups):
            hits[n * slots : (n + 1) * slots, :] = jnp.where(
                columns[:, n : n + 1] == lane, 1.0, 0.0
            ).astype(bf16)
        if last:
            ready()
        picked = dot(hits[...], table_ref[:lanes, :], LAST).astype(bf16)
        out_ref[pl.ds(i * chunk, chunk)] = picked.reshape(chunk, groups * slots, -1)

    if chips == chunk:
        step(0, True)
    else:
        ready()
        lax.fori_loop(0, chips // chunk, lambda i, _: step(i, False), None)


def gather_kernel(chunk, part_ref, sources_hbm, features_hbm, *rest):
    extras, (mate_ref, table_ref, sources_ref, *rest) = rest[:PASSED], rest[PASSED:]
    passed, (order, hits, sems) = rest[:PASSED], rest[PASSED:]
    width, nodes = features_hbm.shape
    indices, table, *others = fetch(
        sems,
        (sources_hbm, sources_ref),
        (features_hbm, table_ref.at[pl.ds(0, width), :]),
        *zip(extras, passed),
    )
    table_ref[width : width + EXTRA, :] = jnp.ones((EXTRA, nodes), bf16)
    if table_ref.shape[0] > width + EXTRA:
        table_ref[width + EXTRA :, :] = jnp.zeros(
            (table_ref.shape[0] - width - EXTRA, nodes), bf16
        )
    indices.wait()
    pick_rows(chunk, 1, part_ref, sources_ref, table_ref, mate_ref, order, hits, table.wait)
    for copy in others:
        copy.wait()


def local_kernel(
    chunk,
    me_ref,
    part_ref,
    table_ref,
    sources_ref,
    tiles_ref,
    targets_ref,
    weight_ref,
    ids_vmem,
    counts_vmem,
    sums_ref,
    edges_ref,
    band_ref,
    mine_ref,
    *rest,
):
    blocks, (ids_ref, counts_ref, bands_ref, order, hits, sems) = rest[:-6], rest[-6:]
    parts, groups, slots = targets_ref.shape
    rows = edges_ref.shape[3]
    high = sums_ref.shape[1]
    width = high - EXTRA
    copies = fetch(sems, (ids_vmem, ids_ref), (counts_vmem, counts_ref))
    bands_ref[...] = jnp.zeros_like(bands_ref)
    picked = order.shape[0]
    pick_rows(picked, 0, part_ref, sources_ref, table_ref, mine_ref, order, hits, lambda: None)
    for k in range(1, groups):
        group = ahead(me_ref[0], groups, k, True)
        blocks[k - 1][...] = table_ref[:width, pl.ds(pl.multiple_of(group * rows, rows), rows)]
    for copy in copies:
        copy.wait()

    def place(t, _):
        at = pl.multiple_of(ids_ref[1, t] * rows, rows)
        bands_ref[ids_ref[0, t], :, pl.ds(at, rows)] = tiles_ref[t]
        return 0

    lax.fori_loop(0, tiles_ref.shape[0], place, 0, unroll=tiles_ref.shape[0] <= 16)
    for g in range(groups):
        sums_ref[g] = dot(table_ref[:high, :], bands_ref[g], LAST)
    band_ref[...] = bands_ref[me_ref[0]]
    lane = lax.broadcasted_iota(jnp.int32, (slots, rows), 1)
    slot = lax.broadcasted_iota(jnp.int32, (slots, rows), 0)
    chips, chip, core = parts // 2, part_ref[0] // 2, part_ref[0] % 2

    def connect(i, _):
        first = i * chunk
        target = columns_of(targets_ref[pl.ds(first, chunk)])
        weight = columns_of(weight_ref[pl.ds(first, chunk)].astype(f32))
        for g in range(groups):
            degree = jnp.zeros((1, rows), f32)
            for e in range(chunk):
                n, d = e * groups + g, first + e
                at = step_to(d // 2, chip, chips) * 2 + ((d % 2) ^ core)
                hit = (target[:, n : n + 1] == lane) & (slot < counts_ref[g, d])
                values = jnp.where(hit, weight[:, n : n + 1], 0.0)
                edges_ref[g, at] = values.astype(bf16)
                degree = degree + jnp.sum(values, axis=0, keepdims=True)
            sums_ref[g, width : width + 1, :] += degree
        return 0

    if parts == chunk:
        connect(0, 0)
    else:
        lax.fori_loop(0, parts // chunk, connect, 0)


def hits_kernel(after, me_ref, part_ref, sources_hbm, hits_ref, sources_ref, sem):
    del after
    copy = pltpu.make_async_copy(sources_hbm, sources_ref, sem)
    copy.start()
    parts, groups, slots = sources_ref.shape
    chips, chip, core = parts // 2, part_ref[0] // 2, part_ref[0] % 2
    mine = lax.broadcasted_iota(jnp.int32, sources_ref.shape, 1) == me_ref[0]
    copy.wait()
    picks = jnp.sum(jnp.where(mine, sources_ref[...], 0), axis=1).T
    lane = lax.broadcasted_iota(jnp.int32, (slots, hits_ref.shape[1]), 1)
    for d in range(parts):
        to = ((d % 2) ^ core) * chips + step_to(chip, d // 2, chips)
        hits_ref[pl.ds(pl.multiple_of(to * slots, slots), slots), :] = jnp.where(
            picks[:, d : d + 1] == lane, 1.0, 0.0
        ).astype(bf16)


def mean_kernel(first, me_ref, sums_ref, edges_ref, *rest):
    groups, parts, slots, rows = edges_ref.shape
    arrived, outs = rest[: parts // 2], rest[parts // 2 :]
    width = outs[0].shape[0]
    for k, out in enumerate(outs, first):
        group = ahead(me_ref[0], groups, k)
        span = pl.ds(pl.multiple_of(group * slots, slots), slots)
        far = jnp.concatenate([x[:, span, :].reshape(2 * slots, -1) for x in arrived], axis=0)
        far = dot(far, edges_ref[group].reshape(parts * slots, rows), FIRST)
        total = sums_ref[group, :width, :] + far[:width]
        out[...] = (total / sums_ref[group, width : width + 1, :]).astype(bf16)


def own_mean_kernel(after, *rest):
    del after
    mean_kernel(0, *rest)


def rows_from(me, groups, k, width, near=False):
    return pl.ds(pl.multiple_of(behind(me, groups, k, near) * width, width), width)


def self_kernel(me_ref, features_hbm, weight_hbm, *rest):
    blocks, (out_ref, own_ref, weight_ref, sems) = rest[:-4], rest[-4:]
    groups, (width, rows) = len(blocks) + 1, own_ref.shape
    me = me_ref[0]
    spans = [rows_from(me, groups, k, width, True) for k in range(groups)]
    own, *weights = fetch(
        sems,
        (features_hbm.at[:, pl.ds(pl.multiple_of(me * rows, rows), rows)], own_ref),
        *[(weight_hbm.at[span, :], weight_ref.at[span, :]) for span in spans],
    )
    own.wait()
    total = jnp.zeros(out_ref.shape, f32)
    for block, span, weight in zip((own_ref, *blocks), spans, weights):
        weight.wait()
        total = total + dot(block[...], weight_ref[span, :], FIRST)
    out_ref[...] = total


def add_blocks(total, me, groups, first, blocks, weight_ref):
    width = blocks[0].shape[0]
    for k, block in enumerate(blocks, first):
        total = total + dot(block[...], weight_ref[rows_from(me, groups, k, width), :], FIRST)
    return total


def early_kernel(groups, me_ref, weight_ref, own_ref, *rest):
    blocks, out_ref = rest[:-1], rest[-1]
    out_ref[...] = add_blocks(own_ref[...], me_ref[0], groups, 0, blocks, weight_ref)


def hidden_kernel(groups, me_ref, weight_ref, out_weight_ref, early_ref, *rest):
    blocks, (hidden_ref, *copies) = rest[: groups - 2], rest[groups - 2 :]
    total = add_blocks(early_ref[...], me_ref[0], groups, 2, blocks, weight_ref)
    hidden = jnp.maximum(total, 0.0).astype(bf16)
    hidden_ref[...] = hidden
    projected = dot(out_weight_ref[...], hidden, LAST).astype(bf16)
    for copy in copies:
        copy[...] = projected


def own_kernel(hidden_ref, weight_ref, out_ref, hidden_out, sem):
    copy = pltpu.make_async_copy(hidden_ref, hidden_out, sem)
    copy.start()
    out_ref[...] = dot(weight_ref[...], hidden_ref[...], LAST)
    copy.wait()


def pick_blocks(groups, first, me_ref, hits_ref, blocks):
    rows = blocks[0].shape[1]
    total = None
    for k, block in enumerate(blocks, first):
        at = pl.multiple_of(behind(me_ref[0], groups, k) * rows, rows)
        term = dot(hits_ref[:, pl.ds(at, rows)], block[...], LAST)
        total = term if total is None else total + term
    return total


def early_pick_kernel(groups, me_ref, hits_ref, *rest):
    rest[-1][...] = pick_blocks(groups, 0, me_ref, hits_ref, rest[:-1])


def pick_kernel(groups, me_ref, hits_ref, early_ref, *rest):
    projected, (mine_ref, mate_ref) = rest[:-2], rest[-2:]
    total = early_ref[...] + pick_blocks(groups, 2, me_ref, hits_ref, projected)
    gap = mine_ref.shape[2] - total.shape[1]
    total = jnp.concatenate([total, jnp.zeros((total.shape[0], gap), f32)], axis=1).astype(bf16)
    half = total.shape[0] // 2
    mine_ref[...] = total[:half].reshape(mine_ref.shape)
    mate_ref[...] = total[half:].reshape(mate_ref.shape)


def pair_kernel(after, mine_ref, got_ref, *rest):
    del after
    chips = mine_ref.shape[0]
    held = (len(rest) - chips) // 2
    for j, out in enumerate(rest[held : held + chips]):
        out[0] = mine_ref[j]
        out[1] = got_ref[j]
    for block, out in zip(rest[:held], rest[held + chips :]):
        out[...] = block[...]


def near_kernel(me_ref, own_ref, sums_ref, band_ref, *rest):
    projected, out_ref = rest[:-1], rest[-1]
    groups, rows = len(projected), projected[0].shape[1]
    me, width = me_ref[0], sums_ref.shape[1] - EXTRA
    total = None
    for k in range(groups):
        at = pl.multiple_of(behind(me, groups, k) * rows, rows)
        term = dot(projected[k][...], band_ref[:, pl.ds(at, rows)], LAST)
        total = term if total is None else total + term
    out_ref[...] = own_ref[...] + total / sums_ref[me, width : width + 1, :]


def last_kernel(first, me_ref, near_ref, edges_ref, sums_ref, *rest):
    arrived, out_ref = rest[:-1], rest[-1]
    _, _, slots, rows = edges_ref.shape
    me, width = me_ref[0], sums_ref.shape[1] - EXTRA
    count = 2 * len(arrived)
    arrived = jnp.concatenate([x[...].reshape(2 * slots, -1) for x in arrived], axis=0)
    edges = edges_ref[me, 2 * first : 2 * first + count].reshape(count * slots, rows)
    far = dot(arrived, edges, FIRST)[: near_ref.shape[0]]
    out_ref[...] = near_ref[...] + far / sums_ref[me, width : width + 1, :]


def scores_kernel(first, me_ref, *rest):
    rest, (out_hbm, scores_ref, sem) = rest[:-3], rest[-3:]
    last_kernel(first, me_ref, *rest, scores_ref)
    copy = pltpu.make_async_copy(scores_ref, out_hbm.at[:, 0, :], sem)
    copy.start()
    copy.wait()


def on_device(
    features,
    tiles,
    tile_ids,
    sources,
    targets,
    counts,
    edge_weight,
    self_one,
    neigh_one,
    self_out,
    neigh_out,
):
    feature_rows, tile_contents = features[0].T, tiles[0]
    groups, parts = lax.axis_size("feat"), lax.axis_size("dom")
    me = lax.axis_index("feat").astype(jnp.int32).reshape(1)
    part = lax.axis_index("dom").astype(jnp.int32).reshape(1)
    width, nodes = feature_rows.shape
    rows, slots = nodes // groups, sources.shape[3]
    hid, classes = self_one.shape[1], self_out.shape[1]
    chips = parts // 2
    chunk = max(1, min(parts, 512 // (groups * slots)))

    def shape(*dims, dtype=bf16):
        return jax.ShapeDtypeStruct(dims, dtype)

    def shift(blocks, near=False):
        return [
            lax.ppermute(block, "feat", [(i, ahead(i, groups, k, near)) for i in range(groups)])
            for k, block in enumerate(blocks, 1)
        ]

    def to_mate(value):
        return lax.ppermute(value, "dom", [(d, d ^ 1) for d in range(parts)])

    def to_chips(blocks):
        return [blocks[0]] + [
            lax.ppermute(
                blocks[j],
                "dom",
                [(d, next_to(d // 2, j, chips) * 2 + d % 2) for d in range(parts)],
            )
            for j in range(1, chips)
        ]

    picked = min(chips, chunk)
    lanes = whole_lanes(width)
    table_rows = max(lanes, width + EXTRA)
    extras = (tile_contents, targets[0], edge_weight[0], tile_ids[0].T, counts[0].T)
    picking = [
        pltpu.VMEM((picked, groups, slots), jnp.int32),
        pltpu.VMEM((picked * groups * slots, nodes), bf16),
    ]
    mate, table, *passed = call(
        functools.partial(gather_kernel, picked),
        (
            shape(chips, groups * slots, lanes),
            shape(table_rows, nodes),
            shape(parts, groups, slots, dtype=jnp.int32),
        )
        + tuple(shape(*value.shape, dtype=value.dtype) for value in extras),
        [SM, HB, HB] + [HB] * PASSED,
        picking + [pltpu.SemaphoreType.DMA((2 + PASSED,))],
        2 * nodes * nodes * width,
        1 << 20,
    )(part, sources[0], feature_rows, *extras)
    mate = to_mate(mate)
    sums, edges, band, mine, *feature_blocks = call(
        functools.partial(local_kernel, chunk),
        (
            shape(groups, width + EXTRA, rows, dtype=f32),
            shape(groups, parts, slots, rows),
            shape(rows, nodes),
            shape(chips, groups * slots, lanes),
        )
        + (shape(width, rows),) * (groups - 1),
        [SM, SM, VM, VM] + [VM] * PASSED,
        [
            pltpu.SMEM(tile_ids.shape[:0:-1], jnp.int32),
            pltpu.SMEM(counts.shape[:0:-1], jnp.int32),
            pltpu.VMEM((groups, rows, nodes), bf16),
        ]
        + picking
        + [pltpu.SemaphoreType.DMA((2,))],
        2 * nodes * nodes * width,
        1 << 20,
        4 if groups <= 4 else 16,
    )(me, part, table, *passed)
    paired = call(
        pair_kernel,
        (shape(2, groups * slots, lanes),) * chips + (shape(width, rows),) * (groups - 1),
        [VM] * (2 + groups),
        (),
        0,
        1 << 20,
    )(band, mine, mate, *feature_blocks)
    arrived = to_chips(paired[:chips])
    feature_blocks = shift(paired[chips:], near=True)
    means = call(
        functools.partial(mean_kernel, 1),
        (shape(width, rows),) * (groups - 1),
        [SM] + [VM] * (2 + chips),
        (),
        2 * nodes * parts * slots * width,
        1 << 20,
    )(me, sums, edges, *arrived)
    means = shift(means)
    own = call(
        self_kernel,
        shape(rows, hid, dtype=f32),
        [SM, HB, HB] + [VM] * (groups - 1),
        [
            pltpu.VMEM((width, rows), bf16),
            pltpu.VMEM(self_one.shape, bf16),
            pltpu.SemaphoreType.DMA((1 + groups,)),
        ],
        2 * rows * hid * groups * width,
        2 << 20,
    )(me, feature_rows, self_one, *feature_blocks)
    own_mean = call(
        own_mean_kernel,
        (shape(width, rows),),
        [VM, SM] + [VM] * (2 + chips),
        (),
        2 * rows * parts * slots * width,
        1 << 18,
    )(own, me, sums, edges, *arrived)
    means = [*own_mean, *means]
    early = call(
        functools.partial(early_kernel, groups),
        shape(rows, hid, dtype=f32),
        [SM] + [VM] * 4,
        (),
        rows * hid * groups * width,
        2 << 20,
    )(me, neigh_one, own, *means[:2])
    hidden, *projected = call(
        functools.partial(hidden_kernel, groups),
        (shape(rows, hid),) + (shape(classes, rows),) * groups,
        [SM] + [VM] * (1 + groups),
        (),
        rows * hid * groups * width,
        2 << 20,
    )(me, neigh_one, neigh_out.T, early, *means[2:])
    hits = call(
        hits_kernel,
        shape(parts * slots, nodes),
        [VM, SM, SM, HB],
        [pltpu.VMEM((parts, groups, slots), jnp.int32), pltpu.SemaphoreType.DMA],
        0,
        1 << 19,
    )(projected[0], me, part, sources[0])
    projected = projected[:1] + shift(projected[1:])
    early = call(
        functools.partial(early_pick_kernel, groups),
        shape(parts * slots, classes, dtype=f32),
        [SM] + [VM] * 3,
        (),
        parts * slots * nodes * classes,
        1 << 18,
    )(me, hits, *projected[:2])
    mine, mate = call(
        functools.partial(pick_kernel, groups),
        (shape(chips, slots, whole_lanes(classes)),) * 2,
        [SM] + [VM] * groups,
        (),
        parts * slots * nodes * classes,
        1 << 18,
    )(me, hits, early, *projected[2:])
    mate = to_mate(mate)
    arrived = to_chips(
        call(pair_kernel, (shape(2, slots, whole_lanes(classes)),) * chips, [VM] * 3, (), 0, 1 << 19)(
            hits, mine, mate
        )
    )
    own, hidden = call(
        own_kernel,
        (shape(classes, rows, dtype=f32), shape(rows, hid)),
        [VM, VM],
        [pltpu.SemaphoreType.DMA],
        2 * rows * hid * classes,
        1 << 20,
        out_specs=(VM, HB),
    )(hidden, self_out.T)
    near = call(
        near_kernel,
        shape(classes, rows, dtype=f32),
        [SM] + [VM] * (3 + groups),
        (),
        2 * rows * nodes * classes,
        1 << 19,
    )(me, own, sums, band, *projected)
    half = chips // 2
    near = call(
        functools.partial(last_kernel, 0),
        shape(classes, rows, dtype=f32),
        [SM] + [VM] * (3 + half),
        (),
        rows * parts * slots * classes,
        1 << 18,
    )(me, near, edges, sums, *arrived[:half])
    logits = call(
        functools.partial(scores_kernel, half),
        shape(classes, 1, rows, dtype=f32),
        [SM] + [VM] * (3 + chips - half),
        [pltpu.VMEM((classes, rows), f32), pltpu.SemaphoreType.DMA],
        rows * parts * slots * classes,
        1 << 19,
        out_specs=HB,
    )(me, near, edges, sums, *arrived[half:])
    return hidden[None], logits.transpose(1, 0, 2)


def solution(mesh):
    placed = (
        P("dom", None, "feat"),
        P("dom", None, None, None),
        P("dom", None, None),
        P("dom", None, None, None),
        P("dom", None, None, None),
        P("dom", None, None),
        P("dom", None, None, None),
        P(),
        P(),
        P(),
        P(),
    )
    return jax.shard_map(
        on_device,
        mesh=mesh,
        in_specs=placed,
        out_specs=(P("dom", "feat", None), P("dom", None, "feat")),
        check_vma=False,
    )
```

```python
import functools

import jax
import jax.numpy as jnp
from jax import lax
from jax.experimental import pallas as pl
from jax.experimental.pallas import tpu as pltpu
from jax.sharding import PartitionSpec as P

f32 = jnp.float32
bf16 = jnp.bfloat16
VM = pl.BlockSpec(memory_space=pltpu.VMEM)
SM = pl.BlockSpec(memory_space=pltpu.SMEM)
HB = pl.BlockSpec(memory_space=pltpu.HBM)
LAST = (((1,), (1,)), ((), ()))
FIRST = (((0,), (0,)), ((), ()))
EXTRA = 16
PASSED = 5


def call(kernel, out_shape, in_specs, scratch=(), flops=0, size=0, limit=4, out_specs=None):
    run = pl.pallas_call(
        kernel,
        out_shape=out_shape,
        in_specs=in_specs,
        out_specs=out_specs or jax.tree.map(lambda _: VM, out_shape),
        scratch_shapes=list(scratch),
        cost_estimate=pl.CostEstimate(flops=flops, bytes_accessed=size, transcendentals=0),
        compiler_params=pltpu.CompilerParams(vmem_limit_bytes=limit << 20),
    )

    def placed(*operands):
        return run(
            *(
                pltpu.with_memory_space_constraint(value, pltpu.HBM) if spec is HB else value
                for value, spec in zip(operands, in_specs)
            )
        )

    return placed


def dot(left, right, dims):
    return lax.dot_general(left, right, dims, preferred_element_type=f32)


def step_of(groups, k, near=False):
    if near and groups > 2 and k in (1, 2):
        return groups - 3 + k
    return (groups - k) % groups


def whole_lanes(count):
    return -(-count // 128) * 128


def ahead(me, groups, k, near=False):
    step = step_of(groups, k, near)
    return me ^ step if groups & (groups - 1) == 0 else (me + step) % groups


def behind(me, groups, k, near=False):
    step = step_of(groups, k, near)
    return me ^ step if groups & (groups - 1) == 0 else (me + groups - step) % groups


def gray(a):
    return a ^ (a >> 1)


def swapped(j):
    return (j >> 1) | ((j & 1) << 1)


def step_to(a, b, count, square=False):
    if square and count == 4:
        return swapped((gray(b) + count - gray(a)) % count)
    step = a ^ b if count & (count - 1) == 0 else (b + count - a) % count
    return (count - step) % count


def next_to(a, j, count, square=False):
    if square and count == 4:
        return gray((gray(a) + swapped(j)) % count)
    step = step_of(count, j)
    return a ^ step if count & (count - 1) == 0 else (a + step) % count


def pair_at(chip, j, count):
    if count == 4:
        return step_to(gray((gray(chip) + count - swapped(j)) % count), chip, count)
    return j


def fetch(sems, *pairs):
    copies = [pltpu.make_async_copy(a, b, sems.at[i]) for i, (a, b) in enumerate(pairs)]
    for copy in copies:
        copy.start()
    return copies


def columns_of(values):
    return values.reshape(-1, values.shape[-1]).T


def pick_rows(chunk, other, part_ref, sources_ref, table_ref, out_ref, order, hits, ready):
    chips, lanes = out_ref.shape[0], out_ref.shape[2]
    _, groups, slots = sources_ref.shape
    nodes = table_ref.shape[1]
    chip, core = part_ref[0] // 2, part_ref[0] % 2
    lane = lax.broadcasted_iota(jnp.int32, (slots, nodes), 1)

    def step(i, last):
        for j in range(chunk):
            order[j] = sources_ref[next_to(chip, i * chunk + j, chips) * 2 + (core ^ other)]
        columns = columns_of(order[...])
        for n in range(chunk * groups):
            hits[n * slots : (n + 1) * slots, :] = jnp.where(
                columns[:, n : n + 1] == lane, 1.0, 0.0
            ).astype(bf16)
        if last:
            ready()
        picked = dot(hits[...], table_ref[:lanes, :], LAST).astype(bf16)
        out_ref[pl.ds(i * chunk, chunk)] = picked.reshape(chunk, groups * slots, -1)

    if chips == chunk:
        step(0, True)
    else:
        ready()
        lax.fori_loop(0, chips // chunk, lambda i, _: step(i, False), None)


def gather_kernel(chunk, part_ref, sources_hbm, features_hbm, *rest):
    extras, (mate_ref, table_ref, sources_ref, *rest) = rest[:PASSED], rest[PASSED:]
    passed, (order, hits, sems) = rest[:PASSED], rest[PASSED:]
    width, nodes = features_hbm.shape
    indices, table, *others = fetch(
        sems,
        (sources_hbm, sources_ref),
        (features_hbm, table_ref.at[pl.ds(0, width), :]),
        *zip(extras, passed),
    )
    table_ref[width : width + EXTRA, :] = jnp.ones((EXTRA, nodes), bf16)
    if table_ref.shape[0] > width + EXTRA:
        table_ref[width + EXTRA :, :] = jnp.zeros(
            (table_ref.shape[0] - width - EXTRA, nodes), bf16
        )
    indices.wait()
    pick_rows(chunk, 1, part_ref, sources_ref, table_ref, mate_ref, order, hits, table.wait)
    for copy in others:
        copy.wait()


def local_kernel(
    chunk,
    me_ref,
    part_ref,
    table_ref,
    sources_ref,
    tiles_ref,
    targets_ref,
    weight_ref,
    ids_vmem,
    counts_vmem,
    sums_ref,
    edges_ref,
    band_ref,
    mine_ref,
    *rest,
):
    blocks, (ids_ref, counts_ref, bands_ref, order, hits, sems) = rest[:-6], rest[-6:]
    parts, groups, slots = targets_ref.shape
    rows = edges_ref.shape[3]
    high = sums_ref.shape[1]
    width = high - EXTRA
    copies = fetch(sems, (ids_vmem, ids_ref), (counts_vmem, counts_ref))
    bands_ref[...] = jnp.zeros_like(bands_ref)
    picked = order.shape[0]
    pick_rows(picked, 0, part_ref, sources_ref, table_ref, mine_ref, order, hits, lambda: None)
    for k in range(1, groups):
        group = ahead(me_ref[0], groups, k, True)
        blocks[k - 1][...] = table_ref[:width, pl.ds(pl.multiple_of(group * rows, rows), rows)]
    for copy in copies:
        copy.wait()

    def place(t, _):
        at = pl.multiple_of(ids_ref[1, t] * rows, rows)
        bands_ref[ids_ref[0, t], :, pl.ds(at, rows)] = tiles_ref[t]
        return 0

    lax.fori_loop(0, tiles_ref.shape[0], place, 0, unroll=tiles_ref.shape[0] <= 16)
    for g in range(groups):
        sums_ref[g] = dot(table_ref[:high, :], bands_ref[g], LAST)
    band_ref[...] = bands_ref[me_ref[0]]
    lane = lax.broadcasted_iota(jnp.int32, (slots, rows), 1)
    slot = lax.broadcasted_iota(jnp.int32, (slots, rows), 0)
    chips, chip, core = parts // 2, part_ref[0] // 2, part_ref[0] % 2

    def connect(i, _):
        first = i * chunk
        target = columns_of(targets_ref[pl.ds(first, chunk)])
        weight = columns_of(weight_ref[pl.ds(first, chunk)].astype(f32))
        for g in range(groups):
            degree = jnp.zeros((1, rows), f32)
            for e in range(chunk):
                n, d = e * groups + g, first + e
                at = step_to(d // 2, chip, chips) * 2 + ((d % 2) ^ core)
                hit = (target[:, n : n + 1] == lane) & (slot < counts_ref[g, d])
                values = jnp.where(hit, weight[:, n : n + 1], 0.0)
                edges_ref[g, at] = values.astype(bf16)
                degree = degree + jnp.sum(values, axis=0, keepdims=True)
            sums_ref[g, width : width + 1, :] += degree
        return 0

    if parts == chunk:
        connect(0, 0)
    else:
        lax.fori_loop(0, parts // chunk, connect, 0)


def hits_kernel(after, me_ref, part_ref, sources_hbm, hits_ref, sources_ref, sem):
    del after
    copy = pltpu.make_async_copy(sources_hbm, sources_ref, sem)
    copy.start()
    parts, groups, slots = sources_ref.shape
    chips, chip, core = parts // 2, part_ref[0] // 2, part_ref[0] % 2
    mine = lax.broadcasted_iota(jnp.int32, sources_ref.shape, 1) == me_ref[0]
    copy.wait()
    picks = jnp.sum(jnp.where(mine, sources_ref[...], 0), axis=1).T
    lane = lax.broadcasted_iota(jnp.int32, (slots, hits_ref.shape[1]), 1)
    for d in range(parts):
        to = ((d % 2) ^ core) * chips + step_to(chip, d // 2, chips, True)
        hits_ref[pl.ds(pl.multiple_of(to * slots, slots), slots), :] = jnp.where(
            picks[:, d : d + 1] == lane, 1.0, 0.0
        ).astype(bf16)


def mean_kernel(first, me_ref, sums_ref, edges_ref, *rest):
    groups, parts, slots, rows = edges_ref.shape
    arrived, outs = rest[: parts // 2], rest[parts // 2 :]
    width = outs[0].shape[0]
    for k, out in enumerate(outs, first):
        group = ahead(me_ref[0], groups, k)
        span = pl.ds(pl.multiple_of(group * slots, slots), slots)
        far = jnp.concatenate([x[:, span, :].reshape(2 * slots, -1) for x in arrived], axis=0)
        far = dot(far, edges_ref[group].reshape(parts * slots, rows), FIRST)
        total = sums_ref[group, :width, :] + far[:width]
        out[...] = (total / sums_ref[group, width : width + 1, :]).astype(bf16)


def own_mean_kernel(after, *rest):
    del after
    mean_kernel(0, *rest)


def rows_from(me, groups, k, width, near=False):
    return pl.ds(pl.multiple_of(behind(me, groups, k, near) * width, width), width)


def self_kernel(me_ref, features_hbm, weight_hbm, *rest):
    blocks, (out_ref, own_ref, weight_ref, sems) = rest[:-4], rest[-4:]
    groups, (width, rows) = len(blocks) + 1, own_ref.shape
    me = me_ref[0]
    spans = [rows_from(me, groups, k, width, True) for k in range(groups)]
    own, *weights = fetch(
        sems,
        (features_hbm.at[:, pl.ds(pl.multiple_of(me * rows, rows), rows)], own_ref),
        *[(weight_hbm.at[span, :], weight_ref.at[span, :]) for span in spans],
    )
    own.wait()
    total = jnp.zeros(out_ref.shape, f32)
    for block, span, weight in zip((own_ref, *blocks), spans, weights):
        weight.wait()
        total = total + dot(block[...], weight_ref[span, :], FIRST)
    out_ref[...] = total


def add_blocks(total, me, groups, first, blocks, weight_ref):
    width = blocks[0].shape[0]
    for k, block in enumerate(blocks, first):
        total = total + dot(block[...], weight_ref[rows_from(me, groups, k, width), :], FIRST)
    return total


def early_kernel(groups, me_ref, weight_ref, own_ref, *rest):
    blocks, out_ref = rest[:-1], rest[-1]
    out_ref[...] = add_blocks(own_ref[...], me_ref[0], groups, 0, blocks, weight_ref)


def hidden_kernel(groups, me_ref, weight_ref, out_weight_ref, early_ref, *rest):
    blocks, (hidden_ref, *copies) = rest[: groups - 2], rest[groups - 2 :]
    total = add_blocks(early_ref[...], me_ref[0], groups, 2, blocks, weight_ref)
    hidden = jnp.maximum(total, 0.0).astype(bf16)
    hidden_ref[...] = hidden
    projected = dot(out_weight_ref[...], hidden, LAST).astype(bf16)
    for copy in copies:
        copy[...] = projected


def own_kernel(hidden_ref, weight_ref, out_ref, hidden_out, sem):
    copy = pltpu.make_async_copy(hidden_ref, hidden_out, sem)
    copy.start()
    out_ref[...] = dot(weight_ref[...], hidden_ref[...], LAST)
    copy.wait()


def pick_blocks(groups, first, me_ref, hits_ref, blocks):
    rows = blocks[0].shape[1]
    total = None
    for k, block in enumerate(blocks, first):
        at = pl.multiple_of(behind(me_ref[0], groups, k) * rows, rows)
        term = dot(hits_ref[:, pl.ds(at, rows)], block[...], LAST)
        total = term if total is None else total + term
    return total


def early_pick_kernel(groups, me_ref, hits_ref, *rest):
    rest[-1][...] = pick_blocks(groups, 0, me_ref, hits_ref, rest[:-1])


def pick_kernel(groups, me_ref, hits_ref, early_ref, *rest):
    projected, (mine_ref, mate_ref) = rest[:-2], rest[-2:]
    total = early_ref[...] + pick_blocks(groups, 2, me_ref, hits_ref, projected)
    gap = mine_ref.shape[2] - total.shape[1]
    total = jnp.concatenate([total, jnp.zeros((total.shape[0], gap), f32)], axis=1).astype(bf16)
    half = total.shape[0] // 2
    mine_ref[...] = total[:half].reshape(mine_ref.shape)
    mate_ref[...] = total[half:].reshape(mate_ref.shape)


def pair_kernel(after, mine_ref, got_ref, *rest):
    del after
    chips = mine_ref.shape[0]
    held = (len(rest) - chips) // 2
    for j, out in enumerate(rest[held : held + chips]):
        out[0] = mine_ref[j]
        out[1] = got_ref[j]
    for block, out in zip(rest[:held], rest[held + chips :]):
        out[...] = block[...]


def near_kernel(me_ref, own_ref, sums_ref, band_ref, *rest):
    projected, out_ref = rest[:-1], rest[-1]
    groups, rows = len(projected), projected[0].shape[1]
    me, width = me_ref[0], sums_ref.shape[1] - EXTRA
    total = None
    for k in range(groups):
        at = pl.multiple_of(behind(me, groups, k) * rows, rows)
        term = dot(projected[k][...], band_ref[:, pl.ds(at, rows)], LAST)
        total = term if total is None else total + term
    out_ref[...] = own_ref[...] + total / sums_ref[me, width : width + 1, :]


def last_kernel(first, part_ref, me_ref, near_ref, edges_ref, sums_ref, *rest):
    arrived, out_ref = rest[:-1], rest[-1]
    _, parts, slots, rows = edges_ref.shape
    chip = part_ref[0] // 2
    me, width = me_ref[0], sums_ref.shape[1] - EXTRA
    count = 2 * len(arrived)
    arrived = jnp.concatenate([x[...].reshape(2 * slots, -1) for x in arrived], axis=0)
    spans = [pl.ds(2 * pair_at(chip, first + i, parts // 2), 2) for i in range(count // 2)]
    edges = jnp.concatenate([edges_ref[me, x].reshape(2 * slots, rows) for x in spans], axis=0)
    far = dot(arrived, edges, FIRST)[: near_ref.shape[0]]
    out_ref[...] = near_ref[...] + far / sums_ref[me, width : width + 1, :]


def scores_kernel(first, part_ref, me_ref, *rest):
    rest, (out_hbm, scores_ref, sem) = rest[:-3], rest[-3:]
    last_kernel(first, part_ref, me_ref, *rest, scores_ref)
    copy = pltpu.make_async_copy(scores_ref, out_hbm.at[:, 0, :], sem)
    copy.start()
    copy.wait()


def on_device(
    features,
    tiles,
    tile_ids,
    sources,
    targets,
    counts,
    edge_weight,
    self_one,
    neigh_one,
    self_out,
    neigh_out,
):
    feature_rows, tile_contents = features[0].T, tiles[0]
    groups, parts = lax.axis_size("feat"), lax.axis_size("dom")
    me = lax.axis_index("feat").astype(jnp.int32).reshape(1)
    part = lax.axis_index("dom").astype(jnp.int32).reshape(1)
    width, nodes = feature_rows.shape
    rows, slots = nodes // groups, sources.shape[3]
    hid, classes = self_one.shape[1], self_out.shape[1]
    chips = parts // 2
    chunk = max(1, min(parts, 512 // (groups * slots)))

    def shape(*dims, dtype=bf16):
        return jax.ShapeDtypeStruct(dims, dtype)

    def shift(blocks, near=False):
        return [
            lax.ppermute(block, "feat", [(i, ahead(i, groups, k, near)) for i in range(groups)])
            for k, block in enumerate(blocks, 1)
        ]

    def to_mate(value):
        return lax.ppermute(value, "dom", [(d, d ^ 1) for d in range(parts)])

    def to_chips(blocks, square=False):
        return [blocks[0]] + [
            lax.ppermute(
                blocks[j],
                "dom",
                [(d, next_to(d // 2, j, chips, square) * 2 + d % 2) for d in range(parts)],
            )
            for j in range(1, chips)
        ]

    picked = min(chips, chunk)
    lanes = whole_lanes(width)
    table_rows = max(lanes, width + EXTRA)
    extras = (tile_contents, targets[0], edge_weight[0], tile_ids[0].T, counts[0].T)
    picking = [
        pltpu.VMEM((picked, groups, slots), jnp.int32),
        pltpu.VMEM((picked * groups * slots, nodes), bf16),
    ]
    mate, table, *passed = call(
        functools.partial(gather_kernel, picked),
        (
            shape(chips, groups * slots, lanes),
            shape(table_rows, nodes),
            shape(parts, groups, slots, dtype=jnp.int32),
        )
        + tuple(shape(*value.shape, dtype=value.dtype) for value in extras),
        [SM, HB, HB] + [HB] * PASSED,
        picking + [pltpu.SemaphoreType.DMA((2 + PASSED,))],
        2 * nodes * nodes * width,
        1 << 20,
    )(part, sources[0], feature_rows, *extras)
    mate = to_mate(mate)
    sums, edges, band, mine, *feature_blocks = call(
        functools.partial(local_kernel, chunk),
        (
            shape(groups, width + EXTRA, rows, dtype=f32),
            shape(groups, parts, slots, rows),
            shape(rows, nodes),
            shape(chips, groups * slots, lanes),
        )
        + (shape(width, rows),) * (groups - 1),
        [SM, SM, VM, VM] + [VM] * PASSED,
        [
            pltpu.SMEM(tile_ids.shape[:0:-1], jnp.int32),
            pltpu.SMEM(counts.shape[:0:-1], jnp.int32),
            pltpu.VMEM((groups, rows, nodes), bf16),
        ]
        + picking
        + [pltpu.SemaphoreType.DMA((2,))],
        2 * nodes * nodes * width,
        1 << 20,
        4 if groups <= 4 else 16,
    )(me, part, table, *passed)
    paired = call(
        pair_kernel,
        (shape(2, groups * slots, lanes),) * chips + (shape(width, rows),) * (groups - 1),
        [VM] * (2 + groups),
        (),
        0,
        1 << 20,
    )(band, mine, mate, *feature_blocks)
    arrived = to_chips(paired[:chips])
    feature_blocks = shift(paired[chips:], near=True)
    means = call(
        functools.partial(mean_kernel, 1),
        (shape(width, rows),) * (groups - 1),
        [SM] + [VM] * (2 + chips),
        (),
        2 * nodes * parts * slots * width,
        1 << 20,
    )(me, sums, edges, *arrived)
    means = shift(means)
    own = call(
        self_kernel,
        shape(rows, hid, dtype=f32),
        [SM, HB, HB] + [VM] * (groups - 1),
        [
            pltpu.VMEM((width, rows), bf16),
            pltpu.VMEM(self_one.shape, bf16),
            pltpu.SemaphoreType.DMA((1 + groups,)),
        ],
        2 * rows * hid * groups * width,
        2 << 20,
    )(me, feature_rows, self_one, *feature_blocks)
    own_mean = call(
        own_mean_kernel,
        (shape(width, rows),),
        [VM, SM] + [VM] * (2 + chips),
        (),
        2 * rows * parts * slots * width,
        1 << 18,
    )(own, me, sums, edges, *arrived)
    means = [*own_mean, *means]
    early = call(
        functools.partial(early_kernel, groups),
        shape(rows, hid, dtype=f32),
        [SM] + [VM] * 4,
        (),
        rows * hid * groups * width,
        2 << 20,
    )(me, neigh_one, own, *means[:2])
    hidden, *projected = call(
        functools.partial(hidden_kernel, groups),
        (shape(rows, hid),) + (shape(classes, rows),) * groups,
        [SM] + [VM] * (1 + groups),
        (),
        rows * hid * groups * width,
        2 << 20,
    )(me, neigh_one, neigh_out.T, early, *means[2:])
    hits = call(
        hits_kernel,
        shape(parts * slots, nodes),
        [VM, SM, SM, HB],
        [pltpu.VMEM((parts, groups, slots), jnp.int32), pltpu.SemaphoreType.DMA],
        0,
        1 << 19,
    )(projected[0], me, part, sources[0])
    projected = projected[:1] + shift(projected[1:])
    early = call(
        functools.partial(early_pick_kernel, groups),
        shape(parts * slots, classes, dtype=f32),
        [SM] + [VM] * 3,
        (),
        parts * slots * nodes * classes,
        1 << 18,
    )(me, hits, *projected[:2])
    mine, mate = call(
        functools.partial(pick_kernel, groups),
        (shape(chips, slots, whole_lanes(classes)),) * 2,
        [SM] + [VM] * groups,
        (),
        parts * slots * nodes * classes,
        1 << 18,
    )(me, hits, early, *projected[2:])
    mate = to_mate(mate)
    arrived = to_chips(
        call(pair_kernel, (shape(2, slots, whole_lanes(classes)),) * chips, [VM] * 3, (), 0, 1 << 19)(
            hits, mine, mate
        ),
        True,
    )
    own, hidden = call(
        own_kernel,
        (shape(classes, rows, dtype=f32), shape(rows, hid)),
        [VM, VM],
        [pltpu.SemaphoreType.DMA],
        2 * rows * hid * classes,
        1 << 20,
        out_specs=(VM, HB),
    )(hidden, self_out.T)
    near = call(
        near_kernel,
        shape(classes, rows, dtype=f32),
        [SM] + [VM] * (3 + groups),
        (),
        2 * rows * nodes * classes,
        1 << 19,
    )(me, own, sums, band, *projected)
    half = chips // 2
    near = call(
        functools.partial(last_kernel, 0),
        shape(classes, rows, dtype=f32),
        [SM, SM] + [VM] * (3 + half),
        (),
        rows * parts * slots * classes,
        1 << 18,
    )(part, me, near, edges, sums, *arrived[:half])
    logits = call(
        functools.partial(scores_kernel, half),
        shape(classes, 1, rows, dtype=f32),
        [SM, SM] + [VM] * (3 + chips - half),
        [pltpu.VMEM((classes, rows), f32), pltpu.SemaphoreType.DMA],
        rows * parts * slots * classes,
        1 << 19,
        out_specs=HB,
    )(part, me, near, edges, sums, *arrived[half:])
    return hidden[None], logits.transpose(1, 0, 2)


def solution(mesh):
    placed = (
        P("dom", None, "feat"),
        P("dom", None, None, None),
        P("dom", None, None),
        P("dom", None, None, None),
        P("dom", None, None, None),
        P("dom", None, None),
        P("dom", None, None, None),
        P(),
        P(),
        P(),
        P(),
    )
    return jax.shard_map(
        on_device,
        mesh=mesh,
        in_specs=placed,
        out_specs=(P("dom", "feat", None), P("dom", None, "feat")),
        check_vma=False,
    )
```
